32 devices in a mesh: len: 8 (over z, y), pipe: 4 (over x, core).
Axes of the slice: x: 2, y: 2, z: 4, core: 2. Of those that a mesh axis runs over, the one named last changes fastest.
Arguments:
- inputs: bfloat16 [32, 2048, 256], P(('len', 'pipe')), may hold values from -6 to 6
- cotangent: bfloat16 [32, 2048, 256], P(('len', 'pipe')), may hold values from -6 to 6
- point_weight: bfloat16 [256, 256], replicated, may hold values from -0.375 to 0.375
- point_bias: float32 [256], replicated, may hold values from -3 to 3
- spec_real: bfloat16 [128, 256, 256], P('len'), may hold values from -0.25 to 0.25
- spec_imag: bfloat16 [128, 256, 256], P('len'), may hold values from -0.25 to 0.25
- junc_weight: bfloat16 [256, 256], replicated, may hold values from -0.375 to 0.375
- junc_bias: float32 [256], replicated, may hold values from -3 to 3
- inlet_ids: int32 [32], replicated, may hold values from 0 to 31
- outlet_ids: int32 [32], replicated, may hold values from 0 to 31
Outputs:
- outputs: bfloat16 [32, 2048, 256], P(('len', 'pipe'))
- grad_inputs: bfloat16 [32, 2048, 256], P(('len', 'pipe'))
- grad_real: float32 [128, 256, 256], P('len')
- grad_imag: float32 [128, 256, 256], P('len')
The draws below stay inside these ranges and needn't reach their ends.
All inputs are finite; a program needn't handle non-finite values.
Results may differ from the reference program's by a relative error of at most 0.015.
Values may be sent and summed in bfloat16 or wider, within the bound.
No kernel may reach another device: no remote copies, remote signals or barrier semaphores. Data moves between devices by JAX's collectives and lax.ppermute only.
A program may use at most 64 MiB of HBM per device.

```python
import math
import jax
import jax.numpy as jnp
from jax import lax

C = 256
MODES = 128
CELLS = 2048
PIPES = 32
JUNCS = 32


def touch_ends(drawn, stream_key, low, top_value):
    shape = drawn.shape
    spot = [jax.random.randint(jax.random.fold_in(stream_key, axis), (), 0, shape[axis]) for axis in range(len(shape))]
    drawn = drawn.at[tuple(spot)].set(low)
    longest = shape.index(max(shape))
    spot[longest] = (spot[longest] + 1) % shape[longest]
    return drawn.at[tuple(spot)].set(top_value)


def shard_levels(own_key, extent, pieces, least, high):
    loudness, own = 1.0, jax.random.fold_in(own_key, 6)
    for axis_at, shards_of in pieces:
        heights = jnp.exp(jax.random.uniform(jax.random.fold_in(own, axis_at), (shards_of,), jnp.float32, least / len(pieces), high / len(pieces)))
        loudness = loudness * jnp.repeat(heights, extent[axis_at] // shards_of).reshape([-1 if axis == axis_at else 1 for axis in range(len(extent))])
    return loudness


def bell_draw(stream_key, shape, width, limit, shards=(), dtype=jnp.bfloat16):
    level = shard_levels(stream_key, shape, shards, -0.22, 0.18) if shards else 1.0
    entries = jax.random.normal(stream_key, shape, jnp.float32) * width * level
    return jnp.minimum(jnp.maximum(entries, -limit), limit).astype(dtype)


def setup_inputs(seed: int = 0) -> dict:
    splits = jax.random.split(jax.random.key(seed), 11)
    inputs = bell_draw(splits[0], (PIPES, CELLS, C), 1.0, 6.0, ((0, 32),))
    cotangent = bell_draw(splits[1], (PIPES, CELLS, C), 1.0, 6.0, ((0, 32),))
    point_weight = bell_draw(splits[2], (C, C), C ** -0.5, 0.375)
    point_bias = bell_draw(splits[3], (C,), 0.5, 3.0, (), jnp.float32)
    spec_real = bell_draw(splits[4], (MODES, C, C), (2 * C) ** -0.5, 0.25, ((0, 8),))
    spec_imag = bell_draw(splits[5], (MODES, C, C), (2 * C) ** -0.5, 0.25, ((0, 8),))
    junc_weight = bell_draw(splits[6], (C, C), C ** -0.5, 0.375)
    junc_bias = bell_draw(splits[7], (C,), 0.5, 3.0, (), jnp.float32)
    inlet_ids = touch_ends(jax.random.randint(splits[8], (PIPES,), 0, JUNCS), jax.random.fold_in(splits[8], 1), 0, JUNCS - 1).astype(jnp.int32)
    outlet_ids = touch_ends(jax.random.randint(splits[9], (PIPES,), 0, JUNCS), jax.random.fold_in(splits[9], 1), 0, JUNCS - 1).astype(jnp.int32)
    return dict(inputs=inputs, cotangent=cotangent, point_weight=point_weight, point_bias=point_bias, spec_real=spec_real, spec_imag=spec_imag, junc_weight=junc_weight, junc_bias=junc_bias, inlet_ids=inlet_ids, outlet_ids=outlet_ids)


COUPLING = 0.125

def tables(cell_count, mode_count):
    position = lax.broadcasted_iota(jnp.int32, (mode_count, cell_count), 1)
    frequency = lax.broadcasted_iota(jnp.int32, (mode_count, cell_count), 0)
    product_index = frequency * position % cell_count
    angles = product_index.astype(jnp.float32) * (2.0 * math.pi / cell_count)
    norm_scale = 1.0 / math.sqrt(cell_count)
    cosine = jnp.cos(angles) * norm_scale
    sine_table = jnp.sin(angles) * norm_scale
    doubled = jnp.where(frequency == 0, 1.0, 2.0)
    forward = jnp.stack([cosine, -sine_table], axis=1).reshape(2 * mode_count, cell_count).astype(jnp.bfloat16)
    inverse = jnp.transpose(jnp.stack([doubled * cosine, -doubled * sine_table], axis=1).reshape(2 * mode_count, cell_count)).astype(jnp.bfloat16)
    return (forward, inverse)

def spectral_blocks(spec_real, spec_imag):
    upper = jnp.concatenate([spec_real, spec_imag], axis=2)
    lower = jnp.concatenate([-spec_imag, spec_real], axis=2)
    return jnp.concatenate([upper, lower], axis=1)

def activate(values):
    return jax.nn.gelu(values, approximate=True)

def silu_slope(values):
    sigmoid_part = jax.nn.sigmoid(values)
    return sigmoid_part * (1.0 + values * (1.0 - sigmoid_part))

def reference(inputs, cotangent, point_weight, point_bias, spec_real, spec_imag, junc_weight, junc_bias, inlet_ids, outlet_ids):
    forward, inverse = tables(CELLS, MODES)
    forward_wide = forward.astype(jnp.float32)
    inverse_wide = inverse.astype(jnp.float32)
    blocks = spectral_blocks(spec_real, spec_imag).astype(jnp.float32)
    pipe_blocks = inputs.reshape(-1, 16, CELLS, C)

    def transform(block):
        return jnp.einsum('kl,plc->pkc', forward_wide, block.astype(jnp.float32)).astype(jnp.bfloat16)
    spectra = lax.map(transform, pipe_blocks).reshape(PIPES, MODES, 2 * C)
    mixed = jnp.einsum('pmk,mkn->pmn', spectra.astype(jnp.float32), blocks).astype(jnp.bfloat16)
    junction_iota = lax.broadcasted_iota(jnp.int32, (PIPES, JUNCS), 1)
    in_hot = (inlet_ids[:, None] == junction_iota).astype(jnp.bfloat16)
    out_hot = (outlet_ids[:, None] == junction_iota).astype(jnp.bfloat16)
    partial_value = jnp.dot(in_hot.T, inputs[:, 0, :], preferred_element_type=jnp.float32) + jnp.dot(out_hot.T, inputs[:, -1, :], preferred_element_type=jnp.float32)
    junc_act = jnp.dot(partial_value.astype(jnp.bfloat16), junc_weight, preferred_element_type=jnp.float32) + junc_bias
    junc_rows = jax.nn.silu(junc_act).astype(jnp.bfloat16)
    cond = COUPLING * (jnp.dot(in_hot, junc_rows, preferred_element_type=jnp.float32) + jnp.dot(out_hot, junc_rows, preferred_element_type=jnp.float32))
    mixed_blocks = mixed.reshape(-1, 16, 2 * MODES, C)
    cond_blocks = cond.reshape(-1, 16, C)
    cot_blocks = cotangent.reshape(-1, 16, CELLS, C)

    def forward_block(items):
        block, mode_rows, cond_rows, cot_rows = items
        spectral = jnp.einsum('lk,pkc->plc', inverse_wide, mode_rows.astype(jnp.float32))
        pre = (spectral + cond_rows[:, None, :]).astype(jnp.bfloat16)
        pointwise = jnp.dot(block.reshape(-1, C), point_weight, preferred_element_type=jnp.float32).reshape(block.shape)
        summed = pointwise + point_bias + pre.astype(jnp.float32)
        result, pullback = jax.vjp(activate, summed)
        grad_total = pullback(cot_rows.astype(jnp.float32))[0].astype(jnp.bfloat16)
        grad_spec = jnp.einsum('lk,plc->pkc', inverse_wide, grad_total.astype(jnp.float32)).astype(jnp.bfloat16)
        grad_cond = lax.optimization_barrier(jnp.sum(grad_total.astype(jnp.float32), axis=1))
        return (result.astype(jnp.bfloat16), grad_total, grad_spec, grad_cond)
    outputs, grad_total, grad_spec, grad_cond = lax.map(forward_block, (pipe_blocks, mixed_blocks, cond_blocks, cot_blocks))
    outputs = outputs.reshape(PIPES, CELLS, C)
    grad_modes = grad_spec.reshape(PIPES, MODES, 2 * C).astype(jnp.float32)
    grad_cond = grad_cond.reshape(PIPES, C)
    weight_terms = jnp.einsum('pmk,pmn->mkn', spectra.astype(jnp.float32), grad_modes)
    grad_real = weight_terms[:, :C, :C] + weight_terms[:, C:, C:]
    grad_imag = weight_terms[:, :C, C:] - weight_terms[:, C:, :C]
    grad_mixed = jnp.einsum('pmn,mkn->pmk', grad_modes, blocks).astype(jnp.bfloat16).reshape(-1, 16, 2 * MODES, C)
    in_wide = in_hot.astype(jnp.float32)
    out_wide = out_hot.astype(jnp.float32)
    junc_grad = COUPLING * (jnp.dot(in_wide.T, grad_cond, precision=lax.Precision.HIGHEST) + jnp.dot(out_wide.T, grad_cond, precision=lax.Precision.HIGHEST))
    act_grad = (junc_grad * silu_slope(junc_act)).astype(jnp.bfloat16)
    sums_grad = jnp.dot(act_grad, junc_weight.T, preferred_element_type=jnp.float32).astype(jnp.bfloat16)
    end_first = jnp.dot(in_hot, sums_grad, preferred_element_type=jnp.float32).reshape(-1, 16, C)
    end_last = jnp.dot(out_hot, sums_grad, preferred_element_type=jnp.float32).reshape(-1, 16, C)

    def backward_block(items):
        grad_rows, first_rows, last_rows, total_rows = items
        grad_cells = jnp.einsum('kl,pkc->plc', forward_wide, grad_rows.astype(jnp.float32))
        grad_cells = grad_cells.at[:, 0, :].add(first_rows).at[:, -1, :].add(last_rows)
        spread = grad_cells.astype(jnp.bfloat16)
        grad_local = jnp.dot(total_rows.reshape(-1, C), point_weight.T, preferred_element_type=jnp.float32).reshape(total_rows.shape)
        return (grad_local + spread.astype(jnp.float32)).astype(jnp.bfloat16)
    grad_inputs = lax.map(backward_block, (grad_mixed, end_first, end_last, grad_total)).reshape(PIPES, CELLS, C)
    return (outputs, grad_inputs, grad_real, grad_imag)
```

```python
import functools
import math

import jax
import jax.numpy as jnp
import ml_dtypes
import numpy as np
from jax import lax
from jax.experimental import pallas as pl
from jax.experimental.pallas import tpu as pltpu
from jax.sharding import PartitionSpec as P

COUPLING = 0.125
TILE = 256
LANES = 128
GELU_S = math.sqrt(2.0 / math.pi)
GELU_C = 0.044715
VMEM = pl.BlockSpec(memory_space=pltpu.VMEM)
SMEM = pl.BlockSpec(memory_space=pltpu.SMEM)


def forward_table(cell_count, mode_count, groups):
    product_index = np.arange(mode_count)[:, None] * np.arange(cell_count)[None, :] % cell_count
    angles = product_index.astype(np.float32) * np.float32(2.0 * math.pi / cell_count)
    norm_scale = np.float32(1.0 / math.sqrt(cell_count))
    cosine = (np.cos(angles) * norm_scale).reshape(groups, -1, cell_count)
    sine = (np.sin(angles) * norm_scale).reshape(groups, -1, cell_count)
    table = np.concatenate([cosine, -sine], axis=1).reshape(2 * mode_count, cell_count)
    return table.astype(ml_dtypes.bfloat16)


def dot(left, right, left_dim=1, right_dim=0):
    return lax.dot_general(
        left,
        right,
        (((left_dim,), (right_dim,)), ((), ())),
        preferred_element_type=jnp.float32,
    )


def put(ref, at, value):
    for lane in range(ref.shape[0]):
        ref[lane, at, :] = value[:, lane * LANES : (lane + 1) * LANES]


def take(ref, at):
    return jnp.concatenate([ref[lane, at, :] for lane in range(ref.shape[0])], axis=1)


def spectrum_kernel(groups, x_ref, f_ref, msg_ref):
    span = f_ref.shape[0] // groups
    cells = x_ref.shape[0]
    spectra = dot(f_ref[...], x_ref[...]).astype(jnp.bfloat16)
    ends = jnp.concatenate([x_ref[0:1, :], x_ref[cells - 1 : cells, :]], axis=0)
    for owner in range(groups):
        msg_ref[owner, 0:span, :] = spectra[owner * span : (owner + 1) * span]
        msg_ref[owner, span : span + 2, :] = ends


def mix_kernel(backward, r_ref, real_ref, imag_ref, out_ref, x_ref, y_ref):
    groups = r_ref.shape[0]
    modes = real_ref.shape[0]
    span = 2 * modes
    for source in range(groups):
        put(x_ref, pl.ds(source * span, span), r_ref[source, 0:span, :].astype(jnp.float32))
    for mode in range(modes):
        first = pl.ds(mode, groups, stride=span)
        second = pl.ds(modes + mode, groups, stride=span)
        rows = jnp.concatenate([take(x_ref, first), take(x_ref, second)], axis=0).astype(jnp.bfloat16)
        dim = 1 if backward else 0
        by_real = dot(rows, real_ref[mode], 1, dim)
        by_imag = dot(rows, imag_ref[mode], 1, dim)
        if backward:
            put(y_ref, first, by_real[:groups] + by_imag[groups:])
            put(y_ref, second, by_real[groups:] - by_imag[:groups])
        else:
            put(y_ref, first, by_real[:groups] - by_imag[groups:])
            put(y_ref, second, by_imag[:groups] + by_real[groups:])
    for source in range(groups):
        out_ref[source] = take(y_ref, pl.ds(source * span, span)).astype(jnp.bfloat16)


def junction_forward_kernel(pipes, *refs):
    msgs, (inlet_ref, outlet_ref, where_ref, weight_ref, bias_ref, cond_ref, slope_ref) = (
        refs[:pipes],
        refs[pipes:],
    )
    groups, rows = msgs[0].shape[0], msgs[0].shape[1]
    channels = msgs[0].shape[2]
    me, column = where_ref[0], where_ref[1]
    own_in, own_out = inlet_ref[me], outlet_ref[me]
    is_first = lax.broadcasted_iota(jnp.int32, (2, channels), 0) == 0

    def matches(pipe, junction):
        first = (inlet_ref[pipe] == junction).astype(jnp.float32)
        last = (outlet_ref[pipe] == junction).astype(jnp.float32)
        return jnp.where(is_first, first, last)

    totals = (jnp.zeros((2, channels), jnp.float32),) * 2
    for step in range(pipes):
        source = lax.rem(column + step, pipes)

        def add(group, carried, step=step, source=source):
            pipe = group * pipes + source
            ends = msgs[step][group, rows - 2 : rows, :].astype(jnp.float32)
            return (
                carried[0] + ends * matches(pipe, own_in),
                carried[1] + ends * matches(pipe, own_out),
            )

        totals = lax.fori_loop(0, groups, add, totals, unroll=min(groups, 8))
    sums = jnp.concatenate(
        [
            jnp.sum(totals[0], axis=0, keepdims=True),
            jnp.sum(totals[1], axis=0, keepdims=True),
            jnp.zeros((6, channels), jnp.float32),
        ],
        axis=0,
    )
    act = dot(sums.astype(jnp.bfloat16), weight_ref[...]) + bias_ref[...]
    sigmoid_part = jax.nn.sigmoid(act)
    junc_rows = (act * sigmoid_part).astype(jnp.bfloat16).astype(jnp.float32)
    cond_ref[...] = COUPLING * (junc_rows[0:1] + junc_rows[1:2])
    slope_ref[...] = sigmoid_part * (1.0 + act * (1.0 - sigmoid_part))


def junction_backward_kernel(pipes, *refs):
    msgs, (inlet_ref, outlet_ref, where_ref, weight_ref, slope_ref, rows_ref) = (
        refs[:pipes],
        refs[pipes:],
    )
    groups, rows = msgs[0].shape[0], msgs[0].shape[1]
    channels = msgs[0].shape[2]
    me, column = where_ref[0], where_ref[1]
    own_in, own_out = inlet_ref[me], outlet_ref[me]

    def matches(pipe, junction):
        return (inlet_ref[pipe] == junction).astype(jnp.float32) + (
            outlet_ref[pipe] == junction
        ).astype(jnp.float32)

    totals = (jnp.zeros((2, channels), jnp.float32),) * 2
    for step in range(pipes):
        source = lax.rem(column + step, pipes)

        def add(group, carried, step=step, source=source):
            pipe = group * pipes + source
            parts = msgs[step][group, rows - 2 : rows, :].astype(jnp.float32)
            return (
                carried[0] + parts * matches(pipe, own_in),
                carried[1] + parts * matches(pipe, own_out),
            )

        totals = lax.fori_loop(0, groups, add, totals, unroll=min(groups, 8))
    junc_grad = COUPLING * jnp.concatenate(
        [
            jnp.sum(totals[0], axis=0, keepdims=True),
            jnp.sum(totals[1], axis=0, keepdims=True),
            jnp.zeros((6, channels), jnp.float32),
        ],
        axis=0,
    )
    act_grad = (junc_grad * slope_ref[...]).astype(jnp.bfloat16)
    sums_grad = dot(act_grad, weight_ref[...], 1, 1).astype(jnp.bfloat16)
    rows_ref[...] = sums_grad.astype(jnp.float32)


def layer_kernel(
    groups,
    x_ref,
    cot_ref,
    weight_ref,
    bias_ref,
    modes_ref,
    cond_ref,
    f_ref,
    ft_ref,
    out_ref,
    total_ref,
    msg_ref,
    acc_ref,
):
    cells, channels = x_ref.shape
    all_rows = f_ref.shape[0]
    span = all_rows // groups
    row = lax.broadcasted_iota(jnp.int32, (all_rows, channels), 0)
    doubled = jnp.where((row == 0) | (row == span // 2), 1.0, 2.0).astype(jnp.float32)
    modes = (modes_ref[...].astype(jnp.float32) * doubled).astype(jnp.bfloat16)
    weight = weight_ref[...]
    cond = cond_ref[...]
    bias = bias_ref[...]
    for tile in range(cells // TILE):
        at = pl.ds(tile * TILE, TILE)
        spectral = dot(ft_ref[at, :], modes)
        pre = (spectral + cond).astype(jnp.bfloat16).astype(jnp.float32)
        summed = dot(x_ref[at, :], weight) + bias + pre
        square = summed * summed
        half = 0.5 + 0.5 * jnp.tanh(summed * (GELU_S + (GELU_S * GELU_C) * square))
        result = summed * half
        out_ref[at, :] = result.astype(jnp.bfloat16)
        slope = half + result * (1.0 - half) * (2.0 * GELU_S + (6.0 * GELU_S * GELU_C) * square)
        total = (cot_ref[at, :].astype(jnp.float32) * slope).astype(jnp.bfloat16)
        total_ref[at, :] = total
        part = dot(f_ref[:, at], total)
        if tile == 0:
            acc_ref[...] = part
        else:
            acc_ref[...] += part
    grad_cond = acc_ref[0:1, :] * (1.0 / f_ref[0:1, 0:1].astype(jnp.float32))
    high = grad_cond.astype(jnp.bfloat16)
    low = (grad_cond - high.astype(jnp.float32)).astype(jnp.bfloat16)
    extra = jnp.concatenate([high, low], axis=0)
    grad_spec = (acc_ref[...] * doubled).astype(jnp.bfloat16)
    for owner in range(groups):
        msg_ref[owner, 0:span, :] = grad_spec[owner * span : (owner + 1) * span]
        msg_ref[owner, span : span + 2, :] = extra


def local_grad_kernel(total_ref, weight_ref, out_ref):
    out_ref[...] = dot(total_ref[...], weight_ref[...], 1, 1)


def input_grad_kernel(modes_ref, ft_ref, local_ref, rows_ref, out_ref):
    cells, channels = out_ref.shape
    modes = modes_ref[...]
    row = lax.broadcasted_iota(jnp.int32, (TILE, channels), 0)
    tiles = cells // TILE
    for tile in range(tiles):
        at = pl.ds(tile * TILE, TILE)
        grad_cells = dot(ft_ref[at, :], modes)
        if tile == 0:
            grad_cells = grad_cells + jnp.where(row == 0, rows_ref[0:1, :], 0.0)
        if tile == tiles - 1:
            grad_cells = grad_cells + jnp.where(row == TILE - 1, rows_ref[1:2, :], 0.0)
        spread = grad_cells.astype(jnp.bfloat16).astype(jnp.float32)
        out_ref[at, :] = (local_ref[at, :] + spread).astype(jnp.bfloat16)


def weight_grad_kernel(pipes, per_step, modes, *refs):
    fields, grads = refs[:pipes], refs[pipes : 2 * pipes]
    real_ref, imag_ref, x_ref, g_ref = refs[2 * pipes :]
    groups = fields[0].shape[0]
    span = 2 * modes

    @pl.when(pl.program_id(0) == 0)
    def _():
        for step in range(pipes):
            for source in range(groups):
                at = pl.ds((step * groups + source) * span, span)
                put(x_ref, at, fields[step][source, 0:span, :].astype(jnp.float32))
                put(g_ref, at, grads[step][source, 0:span, :].astype(jnp.float32))

    count = pipes * groups
    for offset in range(per_step):
        mode = pl.program_id(0) * per_step + offset
        first = pl.ds(mode, count, stride=span)
        second = pl.ds(modes + mode, count, stride=span)
        a, b = take(x_ref, first), take(x_ref, second)
        u, v = take(g_ref, first), take(g_ref, second)
        left = jnp.concatenate([a, b], axis=0).astype(jnp.bfloat16)
        real_ref[offset] = dot(left, jnp.concatenate([u, v], axis=0).astype(jnp.bfloat16), 0, 0)
        imag_ref[offset] = dot(left, jnp.concatenate([v, -u], axis=0).astype(jnp.bfloat16), 0, 0)


def rows_of(count, channels):
    return pltpu.VMEM((channels // LANES, count, LANES), jnp.float32)


def call(kernel, outs, specs, scratch=(), out_specs=None, name=None):
    return pl.pallas_call(
        kernel,
        out_shape=outs,
        in_specs=specs,
        out_specs=out_specs if out_specs is not None else [VMEM] * len(outs),
        scratch_shapes=list(scratch),
        compiler_params=pltpu.CompilerParams(vmem_limit_bytes=16 * 1024 * 1024),
        name=name,
    )


def body(
    inputs,
    cotangent,
    point_weight,
    point_bias,
    spec_real,
    spec_imag,
    junc_weight,
    junc_bias,
    inlet_ids,
    outlet_ids,
):
    per_dev, cell_count, channels = inputs.shape
    assert per_dev == 1
    groups, pipes = lax.axis_size("len"), lax.axis_size("pipe")
    modes = spec_real.shape[0]
    span = 2 * modes
    table = forward_table(cell_count, modes * groups, groups)
    f_table = jnp.asarray(table)
    ft_table = jnp.asarray(np.ascontiguousarray(table.T))
    column = lax.axis_index("pipe")
    where = jnp.stack([lax.axis_index("len") * pipes + column, column]).astype(jnp.int32)
    field = inputs.reshape(cell_count, channels)
    cot = cotangent.reshape(cell_count, channels)
    bias_row = point_bias.reshape(1, channels)
    junc_bias_row = junc_bias.reshape(1, channels)
    shape = jax.ShapeDtypeStruct
    message = shape((groups, span + 2, channels), jnp.bfloat16)
    chunk = shape((groups, span, channels), jnp.bfloat16)

    def exchange(value):
        return lax.all_to_all(value, "len", split_axis=0, concat_axis=0, tiled=True)

    def gather(value):
        return [value] + [
            lax.ppermute(value, "pipe", [(i, (i - step) % pipes) for i in range(pipes)])
            for step in range(1, pipes)
        ]

    def mix(backward, value):
        return call(
            functools.partial(mix_kernel, backward),
            [chunk],
            [VMEM] * 3,
            [rows_of(groups * span, channels)] * 2,
            name="mix_grad" if backward else "mix",
        )(value, spec_real, spec_imag)[0]

    (sent,) = call(
        functools.partial(spectrum_kernel, groups), [message], [VMEM] * 2, name="spectrum"
    )(field, f_table)
    received = exchange(sent)
    fields = gather(received)
    returned = exchange(mix(False, received)).reshape(groups * span, channels)
    cond, slope = call(
        functools.partial(junction_forward_kernel, pipes),
        [shape((1, channels), jnp.float32), shape((8, channels), jnp.float32)],
        [VMEM] * pipes + [SMEM] * 3 + [VMEM] * 2,
        name="junction",
    )(*fields, inlet_ids, outlet_ids, where, junc_weight, junc_bias_row)
    outputs, total, sent = call(
        functools.partial(layer_kernel, groups),
        [shape(field.shape, jnp.bfloat16), shape(field.shape, jnp.bfloat16), message],
        [VMEM] * 8,
        [pltpu.VMEM((groups * span, channels), jnp.float32)],
        name="layer",
    )(field, cot, point_weight, bias_row, returned, cond, f_table, ft_table)
    received = exchange(sent)
    grads = gather(received)
    returned = exchange(mix(True, received)).reshape(groups * span, channels)
    (local,) = call(
        local_grad_kernel, [shape(field.shape, jnp.float32)], [VMEM] * 2, name="local_grad"
    )(total, point_weight)
    (rows,) = call(
        functools.partial(junction_backward_kernel, pipes),
        [shape((8, channels), jnp.float32)],
        [VMEM] * pipes + [SMEM] * 3 + [VMEM] * 2,
        name="junction_grad",
    )(*grads, inlet_ids, outlet_ids, where, junc_weight, slope)
    per_step = math.gcd(modes, 4)
    big = shape((modes, channels, channels), jnp.float32)
    whole = pl.BlockSpec(message.shape, lambda i: (0, 0, 0))
    part = pl.BlockSpec((per_step, channels, channels), lambda i: (i, 0, 0))
    grad_real, grad_imag = pl.pallas_call(
        functools.partial(weight_grad_kernel, pipes, per_step, modes),
        grid=(modes // per_step,),
        out_shape=[big, big],
        in_specs=[whole] * (2 * pipes),
        out_specs=[part, part],
        scratch_shapes=[rows_of(pipes * groups * span, channels)] * 2,
        compiler_params=pltpu.CompilerParams(vmem_limit_bytes=24 * 1024 * 1024),
        name="weight_grad",
    )(*fields, *grads)
    (grad_inputs,) = call(
        input_grad_kernel, [shape(field.shape, jnp.bfloat16)], [VMEM] * 4, name="input_grad"
    )(returned, ft_table, local, rows)
    return (
        outputs.reshape(inputs.shape),
        grad_inputs.reshape(inputs.shape),
        grad_real,
        grad_imag,
    )


def solution(mesh):
    placed = (
        P(("len", "pipe"), None, None),
        P(("len", "pipe"), None, None),
        P(),
        P(),
        P("len", None, None),
        P("len", None, None),
        P(),
        P(),
        P(),
        P(),
    )
    return jax.shard_map(
        body,
        mesh=mesh,
        in_specs=placed,
        out_specs=(
            P(("len", "pipe"), None, None),
            P(("len", "pipe"), None, None),
            P("len", None, None),
            P("len", None, None),
        ),
        check_vma=False,
    )
```

```python
import functools
import math

import jax
import jax.numpy as jnp
import ml_dtypes
import numpy as np
from jax import lax
from jax.experimental import pallas as pl
from jax.experimental.pallas import tpu as pltpu
from jax.sharding import PartitionSpec as P

COUPLING = 0.125
TILE = 256
LANES = 128
PAIRWISE = 8
GELU_S = math.sqrt(2.0 / math.pi)
GELU_C = 0.044715
VMEM = pl.BlockSpec(memory_space=pltpu.VMEM)
SMEM = pl.BlockSpec(memory_space=pltpu.SMEM)
HBM = pl.BlockSpec(memory_space=pltpu.HBM)
MIB = 1024 * 1024


def forward_table(cell_count, mode_count, groups):
    product_index = np.arange(mode_count)[:, None] * np.arange(cell_count)[None, :] % cell_count
    angles = product_index.astype(np.float32) * np.float32(2.0 * math.pi / cell_count)
    norm_scale = np.float32(1.0 / math.sqrt(cell_count))
    cosine = (np.cos(angles) * norm_scale).reshape(groups, -1, cell_count)
    sine = (np.sin(angles) * norm_scale).reshape(groups, -1, cell_count)
    table = np.concatenate([cosine, -sine], axis=1).reshape(2 * mode_count, cell_count)
    return table.astype(ml_dtypes.bfloat16)


def dot(left, right, left_dim=1, right_dim=0):
    return lax.dot_general(
        left,
        right,
        (((left_dim,), (right_dim,)), ((), ())),
        preferred_element_type=jnp.float32,
    )


def put(ref, at, value):
    for lane in range(ref.shape[0]):
        ref[lane, at, :] = value[:, lane * LANES : (lane + 1) * LANES]


def take(ref, at):
    return jnp.concatenate([ref[lane, at, :] for lane in range(ref.shape[0])], axis=1)


def chunk(refs, at):
    return refs[at] if len(refs) > 1 else refs[0].at[at]


def rows_at(refs, me, at, span):
    if len(refs) == 1:
        return pl.ds(at * span, span)
    return pl.ds(pl.multiple_of(lax.bitwise_xor(me, at) * span, span), span)


def spectrum_kernel(groups, parts, x_ref, f_ref, *refs):
    out_refs, (x_tiles, f_tiles, rows_ref, x_sems, f_sems) = refs[:parts], refs[parts:]
    me = lax.axis_index("len")
    tiles, all_rows, tile = f_ref.shape
    span = all_rows // groups
    copies = []
    for at in range(tiles):
        copies.append(
            (
                pltpu.make_async_copy(
                    x_ref.at[pl.ds(at * tile, tile)], x_tiles.at[at], x_sems.at[at]
                ),
                pltpu.make_async_copy(f_ref.at[at], f_tiles.at[at], f_sems.at[at]),
            )
        )
    for pair in copies:
        pair[0].start()
        pair[1].start()
    total = None
    for at, pair in enumerate(copies):
        pair[0].wait()
        pair[1].wait()
        part = dot(f_tiles[at], x_tiles[at])
        total = part if total is None else total + part
    rows_ref[...] = total.astype(jnp.bfloat16)
    ends = jnp.concatenate([x_tiles[0, 0:1, :], x_tiles[tiles - 1, tile - 1 : tile, :]], axis=0)
    for at in range(groups):
        out = chunk(out_refs, at)
        out[0:span, :] = rows_ref[rows_at(out_refs, me, at, span), :]
        out[span : span + 2, :] = ends


def pack_kernel(parts, *refs):
    for at in range(refs[parts].shape[0]):
        refs[parts][at] = chunk(refs[:parts], at)[...]


def mix_kernel(backward, parts, groups, *refs):
    ins, (real_ref, imag_ref) = refs[:parts], refs[parts : parts + 2]
    outs, (x_ref, y_ref) = refs[parts + 2 : 2 * parts + 2], refs[2 * parts + 2 :]
    modes = real_ref.shape[0]
    span = 2 * modes
    for source in range(groups):
        rows = chunk(ins, source)[0:span, :].astype(jnp.float32)
        put(x_ref, pl.ds(source * span, span), rows)
    for mode in range(modes):
        first = pl.ds(mode, groups, stride=span)
        second = pl.ds(modes + mode, groups, stride=span)
        rows = jnp.concatenate([take(x_ref, first), take(x_ref, second)], axis=0).astype(
            jnp.bfloat16
        )
        dim = 1 if backward else 0
        by_real = dot(rows, real_ref[mode], 1, dim)
        by_imag = dot(rows, imag_ref[mode], 1, dim)
        if backward:
            put(y_ref, first, by_real[:groups] + by_imag[groups:])
            put(y_ref, second, by_real[groups:] - by_imag[:groups])
        else:
            put(y_ref, first, by_real[:groups] - by_imag[groups:])
            put(y_ref, second, by_imag[:groups] + by_real[groups:])
    for source in range(groups):
        rows = take(y_ref, pl.ds(source * span, span))
        chunk(outs, source)[...] = rows.astype(jnp.bfloat16)


def pipe_index(groups, pipes, group, step):
    source = lax.bitwise_xor(lax.axis_index("pipe"), step)
    if groups <= PAIRWISE:
        group = lax.bitwise_xor(lax.axis_index("len"), group)
    return group * pipes + source


def own_pipe(pipes):
    return lax.axis_index("len") * pipes + lax.axis_index("pipe")


def two_rows(totals, channels):
    return jnp.concatenate(
        [
            jnp.sum(totals[0], axis=0, keepdims=True),
            jnp.sum(totals[1], axis=0, keepdims=True),
            jnp.zeros((6, channels), jnp.float32),
        ],
        axis=0,
    )


def junction_sums(pipes, msgs, inlet_ref, outlet_ref, both):
    groups, rows, channels = msgs[0].shape
    me = own_pipe(pipes)
    own_in, own_out = inlet_ref[me], outlet_ref[me]
    is_first = lax.broadcasted_iota(jnp.int32, (2, channels), 0) == 0

    def matches(pipe, junction):
        first = (inlet_ref[pipe] == junction).astype(jnp.float32)
        last = (outlet_ref[pipe] == junction).astype(jnp.float32)
        return first + last if both else jnp.where(is_first, first, last)

    totals = (jnp.zeros((2, channels), jnp.float32),) * 2
    for step in range(pipes):

        def add(group, carried, step=step):
            pipe = pipe_index(groups, pipes, group, step)
            ends = msgs[step][group, rows - 2 : rows, :].astype(jnp.float32)
            return (
                carried[0] + ends * matches(pipe, own_in),
                carried[1] + ends * matches(pipe, own_out),
            )

        totals = lax.fori_loop(0, groups, add, totals, unroll=min(groups, 8))
    return two_rows(totals, channels)


def junction_forward_kernel(pipes, *refs):
    msgs, (inlet_ref, outlet_ref, weight_ref, bias_ref, cond_ref, slope_ref) = (
        refs[:pipes],
        refs[pipes:],
    )
    sums = junction_sums(pipes, msgs, inlet_ref, outlet_ref, False)
    act = dot(sums.astype(jnp.bfloat16), weight_ref[...]) + bias_ref[...]
    sigmoid_part = jax.nn.sigmoid(act)
    junc_rows = (act * sigmoid_part).astype(jnp.bfloat16).astype(jnp.float32)
    cond_ref[...] = COUPLING * (junc_rows[0:1] + junc_rows[1:2])
    slope_ref[...] = sigmoid_part * (1.0 + act * (1.0 - sigmoid_part))


def junction_backward_kernel(pipes, *refs):
    msgs, (inlet_ref, outlet_ref, weight_ref, slope_ref, rows_ref) = refs[:pipes], refs[pipes:]
    junc_grad = COUPLING * junction_sums(pipes, msgs, inlet_ref, outlet_ref, True)
    act_grad = (junc_grad * slope_ref[...]).astype(jnp.bfloat16)
    sums_grad = dot(act_grad, weight_ref[...], 1, 1).astype(jnp.bfloat16)
    rows_ref[...] = sums_grad.astype(jnp.float32)


def layer_kernel(
    groups, parts, x_ref, cot_ref, weight_ref, bias_ref, cond_ref, f_ref, ft_ref, *refs
):
    mode_refs, (out_ref, total_ref) = refs[:parts], refs[parts : parts + 2]
    msg_refs, (modes_ref, acc_ref, rows_ref) = refs[parts + 2 : 2 * parts + 2], refs[2 * parts + 2 :]
    me = lax.axis_index("len")
    cells, channels = x_ref.shape
    tiles, all_rows, tile = f_ref.shape
    span = all_rows // groups
    row = lax.broadcasted_iota(jnp.int32, (all_rows, channels), 0)
    doubled = jnp.where((row == 0) | (row == span // 2), 1.0, 2.0).astype(jnp.float32)
    for at in range(groups):
        modes_ref[rows_at(mode_refs, me, at, span), :] = chunk(mode_refs, at)[...]
    modes = (modes_ref[...].astype(jnp.float32) * doubled).astype(jnp.bfloat16)
    weight = weight_ref[...]
    cond = cond_ref[...]
    bias = bias_ref[...]
    for step in range(tiles):
        at = pl.ds(step * tile, tile)
        spectral = dot(ft_ref[at, :], modes)
        pre = (spectral + cond).astype(jnp.bfloat16).astype(jnp.float32)
        summed = dot(x_ref[at, :], weight) + bias + pre
        square = summed * summed
        half = 0.5 + 0.5 * jnp.tanh(summed * (GELU_S + (GELU_S * GELU_C) * square))
        result = summed * half
        out_ref[at, :] = result.astype(jnp.bfloat16)
        slope = half + result * (1.0 - half) * (2.0 * GELU_S + (6.0 * GELU_S * GELU_C) * square)
        total = (cot_ref[at, :].astype(jnp.float32) * slope).astype(jnp.bfloat16)
        total_ref[at, :] = total
        part = dot(f_ref[step], total)
        if step == 0:
            acc_ref[...] = part
        else:
            acc_ref[...] += part
    grad_cond = acc_ref[0:1, :] * (1.0 / f_ref[0, 0:1, 0:1].astype(jnp.float32))
    high = grad_cond.astype(jnp.bfloat16)
    low = (grad_cond - high.astype(jnp.float32)).astype(jnp.bfloat16)
    extra = jnp.concatenate([high, low], axis=0)
    rows_ref[...] = (acc_ref[...] * doubled).astype(jnp.bfloat16)
    for at in range(groups):
        out = chunk(msg_refs, at)
        out[0:span, :] = rows_ref[rows_at(msg_refs, me, at, span), :]
        out[span : span + 2, :] = extra


def local_grad_kernel(total_ref, weight_ref, out_ref, grad_ref, copied_ref, sem):
    copy = pltpu.make_async_copy(out_ref, copied_ref, sem)
    copy.start()
    grad_ref[...] = dot(total_ref[...], weight_ref[...], 1, 1)
    copy.wait()


def input_grad_kernel(groups, parts, ft_ref, local_ref, rows_ref, *refs):
    mode_refs, (out_ref, modes_ref, tiles_ref, sems) = refs[:parts], refs[parts:]
    me = lax.axis_index("len")
    span = ft_ref.shape[1] // groups
    for at in range(groups):
        modes_ref[rows_at(mode_refs, me, at, span), :] = chunk(mode_refs, at)[...]
    modes = modes_ref[...]
    tiles, tile, channels = tiles_ref.shape
    row = lax.broadcasted_iota(jnp.int32, (tile, channels), 0)
    copies = []
    for step in range(tiles):
        at = pl.ds(step * tile, tile)
        grad_cells = dot(ft_ref[at, :], modes)
        if step == 0:
            grad_cells = grad_cells + jnp.where(row == 0, rows_ref[0:1, :], 0.0)
        if step == tiles - 1:
            grad_cells = grad_cells + jnp.where(row == tile - 1, rows_ref[1:2, :], 0.0)
        spread = grad_cells.astype(jnp.bfloat16).astype(jnp.float32)
        tiles_ref[step] = (local_ref[at, :] + spread).astype(jnp.bfloat16)
        copies.append(pltpu.make_async_copy(tiles_ref.at[step], out_ref.at[at], sems.at[step]))
        copies[-1].start()
    for copy in copies:
        copy.wait()


def weight_grad_kernel(pipes, modes, *refs):
    fields, grads = refs[:pipes], refs[pipes : 2 * pipes]
    real_out, imag_out, x_ref, g_ref, real_ref, imag_ref, real_sems, imag_sems = refs[2 * pipes :]
    groups = fields[0].shape[0]
    span = 2 * modes
    for step in range(pipes):
        for source in range(groups):
            at = pl.ds((step * groups + source) * span, span)
            put(x_ref, at, fields[step][source, 0:span, :].astype(jnp.float32))
            put(g_ref, at, grads[step][source, 0:span, :].astype(jnp.float32))
    count = pipes * groups
    copies = []
    for mode in range(modes):
        first = pl.ds(mode, count, stride=span)
        second = pl.ds(modes + mode, count, stride=span)
        a, b = take(x_ref, first), take(x_ref, second)
        u, v = take(g_ref, first), take(g_ref, second)
        left = jnp.concatenate([a, b], axis=0).astype(jnp.bfloat16)
        real_ref[mode] = dot(left, jnp.concatenate([u, v], axis=0).astype(jnp.bfloat16), 0, 0)
        imag_ref[mode] = dot(left, jnp.concatenate([v, -u], axis=0).astype(jnp.bfloat16), 0, 0)
        copies.append(pltpu.make_async_copy(real_ref.at[mode], real_out.at[mode], real_sems.at[mode]))
        copies.append(pltpu.make_async_copy(imag_ref.at[mode], imag_out.at[mode], imag_sems.at[mode]))
        copies[-2].start()
        copies[-1].start()
    for copy in copies:
        copy.wait()


def rows_of(count, channels):
    return pltpu.VMEM((channels // LANES, count, LANES), jnp.float32)


def call(kernel, outs, specs, scratch=(), out_specs=None, name=None, limit=8):
    return pl.pallas_call(
        kernel,
        out_shape=outs,
        in_specs=specs,
        out_specs=out_specs if out_specs is not None else [VMEM] * len(outs),
        scratch_shapes=list(scratch),
        compiler_params=pltpu.CompilerParams(vmem_limit_bytes=limit * MIB),
        name=name,
    )


def body(
    inputs,
    cotangent,
    point_weight,
    point_bias,
    spec_real,
    spec_imag,
    junc_weight,
    junc_bias,
    inlet_ids,
    outlet_ids,
):
    per_dev, cell_count, channels = inputs.shape
    assert per_dev == 1
    groups, pipes = lax.axis_size("len"), lax.axis_size("pipe")
    assert pipes == 4
    modes = spec_real.shape[0]
    span = 2 * modes
    all_rows = span * groups
    tiles = cell_count // TILE
    table = forward_table(cell_count, modes * groups, groups)
    tiled = table.reshape(all_rows, tiles, TILE).transpose(1, 0, 2)
    f_table = jnp.asarray(np.ascontiguousarray(tiled))
    ft_table = jnp.asarray(np.ascontiguousarray(table.T))
    field = inputs.reshape(cell_count, channels)
    cot = cotangent.reshape(cell_count, channels)
    bias_row = point_bias.reshape(1, channels)
    junc_bias_row = junc_bias.reshape(1, channels)
    shape = jax.ShapeDtypeStruct
    bf16, f32 = jnp.bfloat16, jnp.float32
    pairwise = groups <= PAIRWISE
    parts = groups if pairwise else 1

    def chunks(rows):
        if pairwise:
            return [shape((rows, channels), bf16)] * groups
        return [shape((groups, rows, channels), bf16)]

    def exchange(values):
        if not pairwise:
            return [lax.all_to_all(values[0], "len", split_axis=0, concat_axis=0, tiled=True)]
        moved = {
            step: lax.ppermute(values[step], "len", [(i, i ^ step) for i in range(groups)])
            for step in reversed(range(1, groups))
        }
        return [values[0]] + [moved[step] for step in range(1, groups)]

    def swap(value, step):
        return lax.ppermute(value, "pipe", [(i, i ^ step) for i in range(pipes)])

    def gather(values):
        if pairwise:
            whole = shape((groups, span + 2, channels), bf16)
            (own,) = call(
                functools.partial(pack_kernel, parts), [whole], [VMEM] * parts, name="pack"
            )(*values)
        else:
            own = values[0]
        across = swap(own, 2)
        return [own, swap(own, 1), across, swap(across, 1)]

    def mix(backward, values):
        return call(
            functools.partial(mix_kernel, backward, parts, groups),
            chunks(span),
            [VMEM] * (parts + 2),
            [rows_of(all_rows, channels)] * 2,
            name="mix_grad" if backward else "mix",
        )(*values, spec_real, spec_imag)

    sent = call(
        functools.partial(spectrum_kernel, groups, parts),
        chunks(span + 2),
        [HBM] * 2,
        [
            pltpu.VMEM((tiles, TILE, channels), bf16),
            pltpu.VMEM((tiles, all_rows, TILE), bf16),
            pltpu.VMEM((all_rows, channels), bf16),
            pltpu.SemaphoreType.DMA((tiles,)),
            pltpu.SemaphoreType.DMA((tiles,)),
        ],
        name="spectrum",
    )(field, f_table)
    received = exchange(sent)
    returned = exchange(mix(False, received))
    fields = gather(received)
    cond, slope = call(
        functools.partial(junction_forward_kernel, pipes),
        [shape((1, channels), f32), shape((8, channels), f32)],
        [VMEM] * pipes + [SMEM] * 2 + [VMEM] * 2,
        name="junction",
    )(*fields, inlet_ids, outlet_ids, junc_weight, junc_bias_row)
    early, total, *sent = call(
        functools.partial(layer_kernel, groups, parts),
        [shape(field.shape, bf16), shape(field.shape, bf16)] + chunks(span + 2),
        [VMEM] * (7 + parts),
        [
            pltpu.VMEM((all_rows, channels), bf16),
            pltpu.VMEM((all_rows, channels), f32),
            pltpu.VMEM((all_rows, channels), bf16),
        ],
        name="layer",
    )(field, cot, point_weight, bias_row, cond, f_table, ft_table, *returned)
    received = exchange(sent)
    returned = exchange(mix(True, received))
    grads = gather(received)
    local, outputs = call(
        local_grad_kernel,
        [shape(field.shape, f32), shape(field.shape, bf16)],
        [VMEM] * 3,
        [pltpu.SemaphoreType.DMA],
        out_specs=[VMEM, HBM],
        name="local_grad",
    )(total, point_weight, early)
    (rows,) = call(
        functools.partial(junction_backward_kernel, pipes),
        [shape((8, channels), f32)],
        [VMEM] * pipes + [SMEM] * 2 + [VMEM] * 2,
        name="junction_grad",
    )(*grads, inlet_ids, outlet_ids, junc_weight, slope)
    big = shape((modes, channels, channels), f32)
    grad_real, grad_imag = call(
        functools.partial(weight_grad_kernel, pipes, modes),
        [big, big],
        [VMEM] * (2 * pipes),
        [rows_of(pipes * all_rows, channels)] * 2
        + [pltpu.VMEM(big.shape, f32)] * 2
        + [pltpu.SemaphoreType.DMA((modes,))] * 2,
        out_specs=[HBM, HBM],
        name="weight_grad",
        limit=16,
    )(*fields, *grads)
    (grad_inputs,) = call(
        functools.partial(input_grad_kernel, groups, parts),
        [shape(field.shape, bf16)],
        [VMEM] * (3 + parts),
        [
            pltpu.VMEM((all_rows, channels), bf16),
            pltpu.VMEM((tiles, TILE, channels), bf16),
            pltpu.SemaphoreType.DMA((tiles,)),
        ],
        out_specs=[HBM],
        name="input_grad",
    )(ft_table, local, rows, *returned)
    return (
        outputs.reshape(inputs.shape),
        grad_inputs.reshape(inputs.shape),
        grad_real,
        grad_imag,
    )


def solution(mesh):
    placed = (
        P(("len", "pipe"), None, None),
        P(("len", "pipe"), None, None),
        P(),
        P(),
        P("len", None, None),
        P("len", None, None),
        P(),
        P(),
        P(),
        P(),
    )
    return jax.shard_map(
        body,
        mesh=mesh,
        in_specs=placed,
        out_specs=(
            P(("len", "pipe"), None, None),
            P(("len", "pipe"), None, None),
            P("len", None, None),
            P("len", None, None),
        ),
        check_vma=False,
    )
```

```python
import functools
import math

import jax
import jax.numpy as jnp
import ml_dtypes
import numpy as np
from jax import lax
from jax.experimental import pallas as pl
from jax.experimental.pallas import tpu as pltpu
from jax.sharding import PartitionSpec as P

COUPLING = 0.125
TILE = 256
LANES = 128
GELU_S = math.sqrt(2.0 / math.pi)
GELU_C = 0.044715
VMEM = pl.BlockSpec(memory_space=pltpu.VMEM)
SMEM = pl.BlockSpec(memory_space=pltpu.SMEM)
HBM = pl.BlockSpec(memory_space=pltpu.HBM)
MIB = 1024 * 1024


def forward_table(cell_count, mode_count, groups):
    product_index = np.arange(mode_count)[:, None] * np.arange(cell_count)[None, :] % cell_count
    angles = product_index.astype(np.float32) * np.float32(2.0 * math.pi / cell_count)
    norm_scale = np.float32(1.0 / math.sqrt(cell_count))
    cosine = (np.cos(angles) * norm_scale).reshape(groups, -1, cell_count)
    sine = (np.sin(angles) * norm_scale).reshape(groups, -1, cell_count)
    table = np.concatenate([cosine, -sine], axis=1).reshape(2 * mode_count, cell_count)
    return table.astype(ml_dtypes.bfloat16)


def dot(left, right, left_dim=1, right_dim=0):
    return lax.dot_general(
        left,
        right,
        (((left_dim,), (right_dim,)), ((), ())),
        preferred_element_type=jnp.float32,
    )


def put(ref, at, value):
    for lane in range(ref.shape[0]):
        ref[lane, at, :] = value[:, lane * LANES : (lane + 1) * LANES]


def take(ref, at):
    return jnp.concatenate([ref[lane, at, :] for lane in range(ref.shape[0])], axis=1)


def spectrum_kernel(x_ref, f_ref, msg_ref, x_tiles, f_tiles, x_sems, f_sems):
    groups, rows = msg_ref.shape[0], msg_ref.shape[1]
    tiles, all_rows, tile = f_ref.shape
    channels = x_ref.shape[1]
    span = all_rows // groups
    copies = []
    for at in range(tiles):
        rows_in = pl.ds(at * tile, tile)
        copies.append(
            (
                pltpu.make_async_copy(x_ref.at[rows_in], x_tiles.at[at], x_sems.at[at]),
                pltpu.make_async_copy(f_ref.at[at], f_tiles.at[at], f_sems.at[at]),
            )
        )
    for pair in copies:
        pair[0].start()
        pair[1].start()
    total = None
    for at, pair in enumerate(copies):
        pair[0].wait()
        pair[1].wait()
        part = dot(f_tiles[at], x_tiles[at])
        total = part if total is None else total + part
    spectra = total.astype(jnp.bfloat16)
    ends = extra_rows(
        x_tiles[0, 0:1, :], x_tiles[tiles - 1, tile - 1 : tile, :], rows - span, channels
    )
    for at in range(groups):
        msg_ref[at, 0:span, :] = spectra[at * span : (at + 1) * span]
        msg_ref[at, span:rows, :] = ends


def extra_rows(first, second, count, channels):
    parts = [first.astype(jnp.float32), second.astype(jnp.float32)]
    if count > 2:
        parts.append(jnp.zeros((count - 2, channels), jnp.float32))
    return jnp.concatenate(parts, axis=0).astype(jnp.bfloat16)


def mix_kernel(backward, r_ref, real_ref, imag_ref, out_ref, ends_ref, *refs):
    x_ref, y_ref = refs[-2:]
    groups, modes = r_ref.shape[0], real_ref.shape[0]
    span = 2 * modes
    for source in range(groups):
        rows = r_ref[source].astype(jnp.float32)
        put(x_ref, pl.ds(source * span, span), rows[0:span])
        if backward:
            ends_ref[source : source + 1, :] = rows[span : span + 1] + rows[span + 1 : span + 2]
        else:
            ends_ref[source : source + 1, :] = rows[span : span + 1]
            ends_ref[groups + source : groups + source + 1, :] = rows[span + 1 : span + 2]
    for mode in range(modes):
        first = pl.ds(mode, groups, stride=span)
        second = pl.ds(modes + mode, groups, stride=span)
        rows = jnp.concatenate([take(x_ref, first), take(x_ref, second)], axis=0).astype(
            jnp.bfloat16
        )
        dim = 1 if backward else 0
        by_real = dot(rows, real_ref[mode], 1, dim)
        by_imag = dot(rows, imag_ref[mode], 1, dim)
        if backward:
            put(y_ref, first, by_real[:groups] + by_imag[groups:])
            put(y_ref, second, by_real[groups:] - by_imag[:groups])
        else:
            refs[0][mode] = rows
            put(y_ref, first, by_real[:groups] - by_imag[groups:])
            put(y_ref, second, by_imag[:groups] + by_real[groups:])
    for source in range(groups):
        rows = take(y_ref, pl.ds(source * span, span))
        out_ref[source] = rows.astype(jnp.bfloat16)


def own_pipe(pipes):
    return lax.axis_index("len") * pipes + lax.axis_index("pipe")


def two_rows(first, second, channels):
    return jnp.concatenate([first, second, jnp.zeros((6, channels), jnp.float32)], axis=0)


def junction_sums(pipes, ends, inlet_ref, outlet_ref, both):
    channels = ends[0].shape[1]
    groups = ends[0].shape[0] if both else ends[0].shape[0] // 2
    column = lax.axis_index("pipe")
    me = own_pipe(pipes)
    owns = inlet_ref[me], outlet_ref[me]

    def add(group, carried):
        for step in range(pipes):
            pipe = group * pipes + lax.bitwise_xor(column, step)
            first = ends[step][pl.ds(group, 1), :]
            last = first if both else ends[step][pl.ds(groups + group, 1), :]
            carried = tuple(
                total
                + first * (inlet_ref[pipe] == own).astype(jnp.float32)
                + last * (outlet_ref[pipe] == own).astype(jnp.float32)
                for total, own in zip(carried, owns)
            )
        return carried

    zero = jnp.zeros((1, channels), jnp.float32)
    totals = lax.fori_loop(0, groups, add, (zero, zero), unroll=min(groups, 8))
    return two_rows(totals[0], totals[1], channels)


def junction_forward_kernel(pipes, *refs):
    ends, (inlet_ref, outlet_ref, weight_ref, bias_ref, cond_ref, slope_ref) = (
        refs[:pipes],
        refs[pipes:],
    )
    sums = junction_sums(pipes, ends, inlet_ref, outlet_ref, False)
    act = dot(sums.astype(jnp.bfloat16), weight_ref[...]) + bias_ref[...]
    sigmoid_part = jax.nn.sigmoid(act)
    junc_rows = (act * sigmoid_part).astype(jnp.bfloat16).astype(jnp.float32)
    cond_ref[...] = COUPLING * (junc_rows[0:1] + junc_rows[1:2])
    slope_ref[...] = sigmoid_part * (1.0 + act * (1.0 - sigmoid_part))


def junction_backward_kernel(pipes, *refs):
    ends, (inlet_ref, outlet_ref, weight_ref, slope_ref, rows_ref) = refs[:pipes], refs[pipes:]
    junc_grad = COUPLING * junction_sums(pipes, ends, inlet_ref, outlet_ref, True)
    act_grad = (junc_grad * slope_ref[...]).astype(jnp.bfloat16)
    sums_grad = dot(act_grad, weight_ref[...], 1, 1).astype(jnp.bfloat16)
    rows_ref[...] = sums_grad.astype(jnp.float32)


def layer_kernel(
    x_ref,
    cot_ref,
    weight_ref,
    bias_ref,
    cond_ref,
    f_ref,
    ft_ref,
    modes_ref,
    out_ref,
    total_ref,
    msg_ref,
    acc_ref,
):
    channels = x_ref.shape[1]
    groups, rows = msg_ref.shape[0], msg_ref.shape[1]
    tiles, all_rows, tile = f_ref.shape
    span = all_rows // groups
    row = lax.broadcasted_iota(jnp.int32, (all_rows, channels), 0)
    doubled = jnp.where((row == 0) | (row == span // 2), 1.0, 2.0).astype(jnp.float32)
    modes = (modes_ref[...].astype(jnp.float32) * doubled).astype(jnp.bfloat16)
    weight = weight_ref[...]
    cond = cond_ref[...]
    bias = bias_ref[...]
    for step in range(tiles):
        at = pl.ds(step * tile, tile)
        spectral = dot(ft_ref[at, :], modes)
        pre = (spectral + cond).astype(jnp.bfloat16).astype(jnp.float32)
        summed = dot(x_ref[at, :], weight) + bias + pre
        square = summed * summed
        half = 0.5 + 0.5 * jnp.tanh(summed * (GELU_S + (GELU_S * GELU_C) * square))
        result = summed * half
        out_ref[at, :] = result.astype(jnp.bfloat16)
        slope = half + result * (1.0 - half) * (2.0 * GELU_S + (6.0 * GELU_S * GELU_C) * square)
        total = (cot_ref[at, :].astype(jnp.float32) * slope).astype(jnp.bfloat16)
        total_ref[at, :] = total
        part = dot(f_ref[step], total)
        if step == 0:
            acc_ref[...] = part
        else:
            acc_ref[...] += part
    grad_cond = acc_ref[0:1, :] * (1.0 / f_ref[0, 0:1, 0:1].astype(jnp.float32))
    high = grad_cond.astype(jnp.bfloat16).astype(jnp.float32)
    extra = extra_rows(high, grad_cond - high, rows - span, channels)
    grad_spec = (acc_ref[...] * doubled).astype(jnp.bfloat16)
    for at in range(groups):
        msg_ref[at, 0:span, :] = grad_spec[at * span : (at + 1) * span]
        msg_ref[at, span:rows, :] = extra


def local_grad_kernel(total_ref, weight_ref, out_ref, grad_ref, copied_ref, sem):
    copy = pltpu.make_async_copy(out_ref, copied_ref, sem)
    copy.start()
    grad_ref[...] = dot(total_ref[...], weight_ref[...], 1, 1)
    copy.wait()


def input_grad_kernel(ft_ref, local_ref, rows_ref, modes_ref, out_ref, tiles_ref, sems):
    modes = modes_ref[...]
    tiles, tile, channels = tiles_ref.shape
    row = lax.broadcasted_iota(jnp.int32, (tile, channels), 0)
    copies = []
    for step in range(tiles):
        at = pl.ds(step * tile, tile)
        grad_cells = dot(ft_ref[at, :], modes)
        if step == 0:
            grad_cells = grad_cells + jnp.where(row == 0, rows_ref[0:1, :], 0.0)
        if step == tiles - 1:
            grad_cells = grad_cells + jnp.where(row == tile - 1, rows_ref[1:2, :], 0.0)
        spread = grad_cells.astype(jnp.bfloat16).astype(jnp.float32)
        tiles_ref[step] = (local_ref[at, :] + spread).astype(jnp.bfloat16)
        copies.append(pltpu.make_async_copy(tiles_ref.at[step], out_ref.at[at], sems.at[step]))
        copies[-1].start()
    for copy in copies:
        copy.wait()


def weight_grad_kernel(pipes, *refs):
    fields, grads = refs[:pipes], refs[pipes : 2 * pipes]
    real_out, imag_out, g_ref, real_ref, imag_ref, real_sems, imag_sems = refs[2 * pipes :]
    groups, modes = grads[0].shape[0], fields[0].shape[0]
    span = 2 * modes
    for step in range(pipes):
        for source in range(groups):
            at = pl.ds((step * groups + source) * span, span)
            put(g_ref, at, grads[step][source, 0:span, :].astype(jnp.float32))
    copies = []
    for mode in range(modes):
        plain, turned = [], []
        for step in range(pipes):
            base = step * groups * span + mode
            u = take(g_ref, pl.ds(base, groups, stride=span))
            v = take(g_ref, pl.ds(base + modes, groups, stride=span))
            plain += [u, v]
            turned += [v, -u]
        left = jnp.concatenate([fields[step][mode] for step in range(pipes)], axis=0)
        real_ref[mode] = dot(left, jnp.concatenate(plain, axis=0).astype(jnp.bfloat16), 0, 0)
        imag_ref[mode] = dot(left, jnp.concatenate(turned, axis=0).astype(jnp.bfloat16), 0, 0)
        copies.append(pltpu.make_async_copy(real_ref.at[mode], real_out.at[mode], real_sems.at[mode]))
        copies.append(pltpu.make_async_copy(imag_ref.at[mode], imag_out.at[mode], imag_sems.at[mode]))
        copies[-2].start()
        copies[-1].start()
    for copy in copies:
        copy.wait()


def rows_of(count, channels):
    return pltpu.VMEM((channels // LANES, count, LANES), jnp.float32)


def call(kernel, outs, specs, scratch=(), out_specs=None, name=None, limit=8):
    return pl.pallas_call(
        kernel,
        out_shape=outs,
        in_specs=specs,
        out_specs=out_specs if out_specs is not None else [VMEM] * len(outs),
        scratch_shapes=list(scratch),
        compiler_params=pltpu.CompilerParams(vmem_limit_bytes=limit * MIB),
        name=name,
    )


def body(
    inputs,
    cotangent,
    point_weight,
    point_bias,
    spec_real,
    spec_imag,
    junc_weight,
    junc_bias,
    inlet_ids,
    outlet_ids,
):
    per_dev, cell_count, channels = inputs.shape
    assert per_dev == 1
    groups, pipes = lax.axis_size("len"), lax.axis_size("pipe")
    assert pipes == 4
    modes = spec_real.shape[0]
    span = 2 * modes
    all_rows = span * groups
    tiles = cell_count // TILE
    table = forward_table(cell_count, modes * groups, groups)
    tiled = table.reshape(all_rows, tiles, TILE).transpose(1, 0, 2)
    f_table = jnp.asarray(np.ascontiguousarray(tiled))
    ft_table = jnp.asarray(np.ascontiguousarray(table.T))
    field = inputs.reshape(cell_count, channels)
    cot = cotangent.reshape(cell_count, channels)
    bias_row = point_bias.reshape(1, channels)
    junc_bias_row = junc_bias.reshape(1, channels)
    shape = jax.ShapeDtypeStruct
    bf16, f32 = jnp.bfloat16, jnp.float32
    message = shape((groups, span + (16 if span % 16 == 0 else 2), channels), bf16)
    chunks = shape((groups, span, channels), bf16)

    def exchange(value):
        return lax.all_to_all(value, "len", split_axis=0, concat_axis=0, tiled=True)

    def gather(value):
        return [value] + [
            lax.ppermute(value, "pipe", [(i, i ^ step) for i in range(pipes)])
            for step in range(1, pipes)
        ]

    def mix(backward, value):
        outs = [chunks, shape((groups if backward else 2 * groups, channels), f32)]
        if not backward:
            outs.append(shape((modes, 2 * groups, channels), bf16))
        return call(
            functools.partial(mix_kernel, backward),
            outs,
            [VMEM] * 3,
            [rows_of(all_rows, channels)] * 2,
            name="mix_grad" if backward else "mix",
        )(value, spec_real, spec_imag)

    (sent,) = call(
        spectrum_kernel,
        [message],
        [HBM] * 2,
        [
            pltpu.VMEM((tiles, TILE, channels), bf16),
            pltpu.VMEM((tiles, all_rows, TILE), bf16),
            pltpu.SemaphoreType.DMA((tiles,)),
            pltpu.SemaphoreType.DMA((tiles,)),
        ],
        name="spectrum",
        limit=60,
    )(field, f_table)
    received = exchange(sent)
    mixed, ends, rows = mix(False, received)
    returned = exchange(mixed).reshape(all_rows, channels)
    ends = gather(ends)
    fields = gather(rows)
    cond, slope = call(
        functools.partial(junction_forward_kernel, pipes),
        [shape((1, channels), f32), shape((8, channels), f32)],
        [VMEM] * pipes + [SMEM] * 2 + [VMEM] * 2,
        name="junction",
    )(*ends, inlet_ids, outlet_ids, junc_weight, junc_bias_row)
    early, total, sent = call(
        layer_kernel,
        [shape(field.shape, bf16), shape(field.shape, bf16), message],
        [VMEM] * 8,
        [pltpu.VMEM((all_rows, channels), f32)],
        name="layer",
    )(field, cot, point_weight, bias_row, cond, f_table, ft_table, returned)
    received = exchange(sent)
    grads = gather(received)
    mixed, ends = mix(True, received)
    returned = exchange(mixed).reshape(all_rows, channels)
    ends = gather(ends)
    local, outputs = call(
        local_grad_kernel,
        [shape(field.shape, f32), shape(field.shape, bf16)],
        [VMEM] * 3,
        [pltpu.SemaphoreType.DMA],
        out_specs=[VMEM, HBM],
        name="local_grad",
    )(total, point_weight, early)
    (rows,) = call(
        functools.partial(junction_backward_kernel, pipes),
        [shape((8, channels), f32)],
        [VMEM] * pipes + [SMEM] * 2 + [VMEM] * 2,
        name="junction_grad",
    )(*ends, inlet_ids, outlet_ids, junc_weight, slope)
    big = shape((modes, channels, channels), f32)
    grad_real, grad_imag = call(
        functools.partial(weight_grad_kernel, pipes),
        [big, big],
        [VMEM] * (2 * pipes),
        [rows_of(pipes * all_rows, channels)]
        + [pltpu.VMEM(big.shape, f32)] * 2
        + [pltpu.SemaphoreType.DMA((modes,))] * 2,
        out_specs=[HBM, HBM],
        name="weight_grad",
        limit=16,
    )(*fields, *grads)
    (grad_inputs,) = call(
        input_grad_kernel,
        [shape(field.shape, bf16)],
        [VMEM] * 4,
        [pltpu.VMEM((tiles, TILE, channels), bf16), pltpu.SemaphoreType.DMA((tiles,))],
        out_specs=[HBM],
        name="input_grad",
    )(ft_table, local, rows, returned)
    return (
        outputs.reshape(inputs.shape),
        grad_inputs.reshape(inputs.shape),
        grad_real,
        grad_imag,
    )


def solution(mesh):
    placed = (
        P(("len", "pipe"), None, None),
        P(("len", "pipe"), None, None),
        P(),
        P(),
        P("len", None, None),
        P("len", None, None),
        P(),
        P(),
        P(),
        P(),
    )
    return jax.shard_map(
        body,
        mesh=mesh,
        in_specs=placed,
        out_specs=(
            P(("len", "pipe"), None, None),
            P(("len", "pipe"), None, None),
            P("len", None, None),
            P("len", None, None),
        ),
        check_vma=False,
    )
```

```python
import functools
import math

import jax
import jax.numpy as jnp
import ml_dtypes
import numpy as np
from jax import lax
from jax.experimental import pallas as pl
from jax.experimental.pallas import tpu as pltpu
from jax.sharding import PartitionSpec as P

COUPLING = 0.125
TILE = 256
LANES = 128
GELU_S = math.sqrt(2.0 / math.pi)
GELU_C = 0.044715
VMEM = pl.BlockSpec(memory_space=pltpu.VMEM)
SMEM = pl.BlockSpec(memory_space=pltpu.SMEM)
HBM = pl.BlockSpec(memory_space=pltpu.HBM)
MIB = 1024 * 1024


def forward_table(cell_count, mode_count, groups):
    product_index = np.arange(mode_count)[:, None] * np.arange(cell_count)[None, :] % cell_count
    angles = product_index.astype(np.float32) * np.float32(2.0 * math.pi / cell_count)
    norm_scale = np.float32(1.0 / math.sqrt(cell_count))
    cosine = (np.cos(angles) * norm_scale).reshape(groups, -1, cell_count)
    sine = (np.sin(angles) * norm_scale).reshape(groups, -1, cell_count)
    table = np.concatenate([cosine, -sine], axis=1).reshape(2 * mode_count, cell_count)
    return table.astype(ml_dtypes.bfloat16)


def dot(left, right, left_dim=1, right_dim=0):
    return lax.dot_general(
        left,
        right,
        (((left_dim,), (right_dim,)), ((), ())),
        preferred_element_type=jnp.float32,
    )


def put(ref, at, value):
    for lane in range(ref.shape[0]):
        ref[lane, at, :] = value[:, lane * LANES : (lane + 1) * LANES]


def take(ref, at):
    return jnp.concatenate([ref[lane, at, :] for lane in range(ref.shape[0])], axis=1)


def spectrum_kernel(x_ref, f_ref, msg_ref, x_tiles, f_tiles, x_sems, f_sems):
    groups, rows = msg_ref.shape[0], msg_ref.shape[1]
    tiles, all_rows, tile = f_ref.shape
    channels = x_ref.shape[1]
    span = all_rows // groups
    copies = []
    for at in range(tiles):
        rows_in = pl.ds(at * tile, tile)
        copies.append(
            (
                pltpu.make_async_copy(x_ref.at[rows_in], x_tiles.at[at], x_sems.at[at]),
                pltpu.make_async_copy(f_ref.at[at], f_tiles.at[at], f_sems.at[at]),
            )
        )
    for pair in copies:
        pair[0].start()
        pair[1].start()
    total = None
    for at, pair in enumerate(copies):
        pair[0].wait()
        pair[1].wait()
        part = dot(f_tiles[at], x_tiles[at])
        total = part if total is None else total + part
    spectra = total.astype(jnp.bfloat16)
    ends = extra_rows(
        x_tiles[0, 0:1, :], x_tiles[tiles - 1, tile - 1 : tile, :], rows - span, channels
    )
    for at in range(groups):
        msg_ref[at, 0:span, :] = spectra[at * span : (at + 1) * span]
        msg_ref[at, span:rows, :] = ends


def extra_rows(first, second, count, channels):
    parts = [first.astype(jnp.float32), second.astype(jnp.float32)]
    if count > 2:
        parts.append(jnp.zeros((count - 2, channels), jnp.float32))
    return jnp.concatenate(parts, axis=0).astype(jnp.bfloat16)


def mix_kernel(backward, r_ref, real_ref, imag_ref, out_ref, x_ref, y_ref):
    groups, modes = r_ref.shape[0], real_ref.shape[0]
    span = 2 * modes
    for source in range(groups):
        put(x_ref, pl.ds(source * span, span), r_ref[source, 0:span, :].astype(jnp.float32))
    for mode in range(modes):
        first = pl.ds(mode, groups, stride=span)
        second = pl.ds(modes + mode, groups, stride=span)
        rows = jnp.concatenate([take(x_ref, first), take(x_ref, second)], axis=0).astype(
            jnp.bfloat16
        )
        dim = 1 if backward else 0
        by_real = dot(rows, real_ref[mode], 1, dim)
        by_imag = dot(rows, imag_ref[mode], 1, dim)
        if backward:
            put(y_ref, first, by_real[:groups] + by_imag[groups:])
            put(y_ref, second, by_real[groups:] - by_imag[:groups])
        else:
            put(y_ref, first, by_real[:groups] - by_imag[groups:])
            put(y_ref, second, by_imag[:groups] + by_real[groups:])
    for source in range(groups):
        rows = take(y_ref, pl.ds(source * span, span))
        out_ref[source] = rows.astype(jnp.bfloat16)


def own_pipe(pipes):
    return lax.axis_index("len") * pipes + lax.axis_index("pipe")


def two_rows(first, second, channels):
    return jnp.concatenate([first, second, jnp.zeros((6, channels), jnp.float32)], axis=0)


def junction_sums(pipes, msgs, inlet_ref, outlet_ref, both):
    groups, rows, channels = msgs[0].shape
    column = lax.axis_index("pipe")
    me = own_pipe(pipes)
    owns = inlet_ref[me], outlet_ref[me]
    is_first = lax.broadcasted_iota(jnp.int32, (2, channels), 0) == 0

    def matches(pipe, junction):
        first = (inlet_ref[pipe] == junction).astype(jnp.float32)
        last = (outlet_ref[pipe] == junction).astype(jnp.float32)
        return first + last if both else jnp.where(is_first, first, last)

    def add(group, carried):
        for step in range(pipes):
            pipe = group * pipes + lax.bitwise_xor(column, step)
            ends = msgs[step][group, rows - 2 : rows, :].astype(jnp.float32)
            carried = tuple(
                total + ends * matches(pipe, own) for total, own in zip(carried, owns)
            )
        return carried

    zero = jnp.zeros((2, channels), jnp.float32)
    totals = lax.fori_loop(0, groups, add, (zero, zero), unroll=min(groups, 8))
    return two_rows(
        jnp.sum(totals[0], axis=0, keepdims=True),
        jnp.sum(totals[1], axis=0, keepdims=True),
        channels,
    )


def started(copies):
    for copy in copies:
        copy.start()
    return copies


def wait(copies):
    for copy in copies:
        copy.wait()


def brought(pairs, sems, base=0):
    return started(
        [
            pltpu.make_async_copy(source, target, sems.at[base + place])
            for place, (source, target) in enumerate(pairs)
        ]
    )


def layer_kernel(pipes, *refs):
    msgs, refs = refs[:pipes], refs[pipes:]
    (x_ref, cot_ref, f_ref, ft_ref), refs = refs[:4], refs[4:]
    small, refs = refs[:7], refs[7:]
    (out_ref, total_ref, msg_ref, slope_ref), refs = refs[:4], refs[4:]
    x_tiles, cot_tiles, f_tiles, ft_tiles, out_tiles, total_tiles, acc_ref = refs[:7]
    msg_bufs, refs = refs[7 : 7 + pipes], refs[7 + pipes :]
    small_bufs, (first_sems, in_sems, out_sems) = refs[:7], refs[7:]
    inlet, outlet, junc_weight, junc_bias, weight_ref, bias_ref, modes_ref = small_bufs
    channels = x_ref.shape[1]
    groups, rows = msg_ref.shape[0], msg_ref.shape[1]
    tiles, all_rows, tile = f_ref.shape
    span = all_rows // groups
    junction = brought(list(zip(small[:4], small_bufs[:4])) + list(zip(msgs, msg_bufs)), first_sems)
    shared = brought(zip(small[4:], small_bufs[4:]), first_sems, 4 + pipes)
    coming = []
    for step in range(tiles):
        at = pl.ds(step * tile, tile)
        coming.append(
            brought(
                [
                    (ft_ref.at[at], ft_tiles.at[step]),
                    (x_ref.at[at], x_tiles.at[step]),
                    (cot_ref.at[at], cot_tiles.at[step]),
                    (f_ref.at[step], f_tiles.at[step]),
                ],
                in_sems,
                4 * step,
            )
        )
    wait(junction)
    sums = junction_sums(pipes, msg_bufs, inlet, outlet, False)
    act = dot(sums.astype(jnp.bfloat16), junc_weight[...]) + junc_bias[...]
    sigmoid_part = jax.nn.sigmoid(act)
    junc_rows = (act * sigmoid_part).astype(jnp.bfloat16).astype(jnp.float32)
    cond = COUPLING * (junc_rows[0:1] + junc_rows[1:2])
    slope_ref[...] = sigmoid_part * (1.0 + act * (1.0 - sigmoid_part))
    wait(shared)
    row = lax.broadcasted_iota(jnp.int32, (all_rows, channels), 0)
    doubled = jnp.where((row == 0) | (row == span // 2), 1.0, 2.0).astype(jnp.float32)
    modes = (modes_ref[...].astype(jnp.float32) * doubled).astype(jnp.bfloat16)
    weight = weight_ref[...]
    bias = bias_ref[...]
    going = []
    for step in range(tiles):
        at = pl.ds(step * tile, tile)
        wait(coming[step])
        spectral = dot(ft_tiles[step], modes)
        pre = (spectral + cond).astype(jnp.bfloat16).astype(jnp.float32)
        summed = dot(x_tiles[step], weight) + bias + pre
        square = summed * summed
        half = 0.5 + 0.5 * jnp.tanh(summed * (GELU_S + (GELU_S * GELU_C) * square))
        result = summed * half
        out_tiles[step] = result.astype(jnp.bfloat16)
        slope = half + result * (1.0 - half) * (2.0 * GELU_S + (6.0 * GELU_S * GELU_C) * square)
        total = (cot_tiles[step].astype(jnp.float32) * slope).astype(jnp.bfloat16)
        total_tiles[step] = total
        going += brought(
            [(out_tiles.at[step], out_ref.at[at]), (total_tiles.at[step], total_ref.at[at])],
            out_sems,
            2 * step,
        )
        part = dot(f_tiles[step], total)
        if step == 0:
            acc_ref[...] = part
        else:
            acc_ref[...] += part
    grad_cond = acc_ref[0:1, :] * (1.0 / f_tiles[0, 0:1, 0:1].astype(jnp.float32))
    high = grad_cond.astype(jnp.bfloat16).astype(jnp.float32)
    extra = extra_rows(high, grad_cond - high, rows - span, channels)
    grad_spec = (acc_ref[...] * doubled).astype(jnp.bfloat16)
    for at in range(groups):
        msg_ref[at, 0:span, :] = grad_spec[at * span : (at + 1) * span]
        msg_ref[at, span:rows, :] = extra
    wait(going)


def input_grad_kernel(pipes, *refs):
    msgs, refs = refs[:pipes], refs[pipes:]
    (total_ref, ft_ref), small, out_ref = refs[:2], refs[2:8], refs[8]
    total_tiles, ft_tiles, out_tiles = refs[9:12]
    msg_bufs, refs = refs[12 : 12 + pipes], refs[12 + pipes :]
    small_bufs, (first_sems, in_sems, out_sems) = refs[:6], refs[6:]
    inlet, outlet, junc_weight, slope_ref, weight_ref, modes_ref = small_bufs
    tiles, tile, channels = out_tiles.shape
    shared = brought(zip(small[4:], small_bufs[4:]), first_sems)
    order = list(range(1, tiles - 1)) + [0, tiles - 1]
    coming = {}
    for step in order:
        at = pl.ds(step * tile, tile)
        coming[step] = brought(
            [(ft_ref.at[at], ft_tiles.at[step]), (total_ref.at[at], total_tiles.at[step])],
            in_sems,
            2 * step,
        )
    junction = brought(
        list(zip(small[:4], small_bufs[:4])) + list(zip(msgs, msg_bufs)), first_sems, 2
    )
    wait(shared)
    modes = modes_ref[...]
    weight = weight_ref[...]
    row = lax.broadcasted_iota(jnp.int32, (tile, channels), 0)
    going = []
    for step in order:
        at = pl.ds(step * tile, tile)
        if step == 0:
            wait(junction)
            junc_grad = COUPLING * junction_sums(pipes, msg_bufs, inlet, outlet, True)
            act_grad = (junc_grad * slope_ref[...]).astype(jnp.bfloat16)
            sums_grad = dot(act_grad, junc_weight[...], 1, 1)
            sums_grad = sums_grad.astype(jnp.bfloat16).astype(jnp.float32)
        wait(coming[step])
        grad_cells = dot(ft_tiles[step], modes)
        if step == 0:
            grad_cells = grad_cells + jnp.where(row == 0, sums_grad[0:1, :], 0.0)
        if step == tiles - 1:
            grad_cells = grad_cells + jnp.where(row == tile - 1, sums_grad[1:2, :], 0.0)
        spread = grad_cells.astype(jnp.bfloat16).astype(jnp.float32)
        local = dot(total_tiles[step], weight, 1, 1)
        out_tiles[step] = (local + spread).astype(jnp.bfloat16)
        going += brought([(out_tiles.at[step], out_ref.at[at])], out_sems, step)
    wait(going)


def weight_grad_kernel(pipes, modes, *refs):
    fields, grads = refs[:pipes], refs[pipes : 2 * pipes]
    real_out, imag_out, x_ref, g_ref, real_ref, imag_ref, sems = refs[2 * pipes :]
    groups = fields[0].shape[0]
    span = 2 * modes
    for step in range(pipes):
        for source in range(groups):
            at = pl.ds((step * groups + source) * span, span)
            put(x_ref, at, fields[step][source, 0:span, :].astype(jnp.float32))
            put(g_ref, at, grads[step][source, 0:span, :].astype(jnp.float32))
    count = pipes * groups
    going = []
    for mode in range(modes):
        first = pl.ds(mode, count, stride=span)
        second = pl.ds(modes + mode, count, stride=span)
        a, b = take(x_ref, first), take(x_ref, second)
        u, v = take(g_ref, first), take(g_ref, second)
        left = jnp.concatenate([a, b], axis=0).astype(jnp.bfloat16)
        real_ref[mode] = dot(left, jnp.concatenate([u, v], axis=0).astype(jnp.bfloat16), 0, 0)
        imag_ref[mode] = dot(left, jnp.concatenate([v, -u], axis=0).astype(jnp.bfloat16), 0, 0)
        going += started(
            [
                pltpu.make_async_copy(real_ref.at[mode], real_out.at[mode], sems.at[mode, 0]),
                pltpu.make_async_copy(imag_ref.at[mode], imag_out.at[mode], sems.at[mode, 1]),
            ]
        )
    wait(going)


def rows_of(count, channels):
    return pltpu.VMEM((channels // LANES, count, LANES), jnp.float32)


def call(kernel, outs, specs, scratch=(), out_specs=None, name=None, limit=8):
    return pl.pallas_call(
        kernel,
        out_shape=outs,
        in_specs=specs,
        out_specs=out_specs if out_specs is not None else [VMEM] * len(outs),
        scratch_shapes=list(scratch),
        compiler_params=pltpu.CompilerParams(vmem_limit_bytes=limit * MIB),
        name=name,
    )


def body(
    inputs,
    cotangent,
    point_weight,
    point_bias,
    spec_real,
    spec_imag,
    junc_weight,
    junc_bias,
    inlet_ids,
    outlet_ids,
):
    per_dev, cell_count, channels = inputs.shape
    assert per_dev == 1
    groups, pipes = lax.axis_size("len"), lax.axis_size("pipe")
    assert pipes == 4
    modes = spec_real.shape[0]
    span = 2 * modes
    all_rows = span * groups
    tiles = cell_count // TILE
    table = forward_table(cell_count, modes * groups, groups)
    tiled = table.reshape(all_rows, tiles, TILE).transpose(1, 0, 2)
    f_table = jnp.asarray(np.ascontiguousarray(tiled))
    ft_table = jnp.asarray(np.ascontiguousarray(table.T))
    field = inputs.reshape(cell_count, channels)
    cot = cotangent.reshape(cell_count, channels)
    bias_row = point_bias.reshape(1, channels)
    junc_bias_row = junc_bias.reshape(1, channels)
    shape = jax.ShapeDtypeStruct
    bf16, f32 = jnp.bfloat16, jnp.float32
    message = shape((groups, span + 2, channels), bf16)
    chunks = shape((groups, span, channels), bf16)
    cell_tiles = pltpu.VMEM((tiles, TILE, channels), bf16)
    table_tiles = pltpu.VMEM((tiles, all_rows, TILE), bf16)
    back_tiles = pltpu.VMEM((tiles, TILE, all_rows), bf16)
    dma = pltpu.SemaphoreType.DMA

    def exchange(value):
        return lax.all_to_all(value, "len", split_axis=0, concat_axis=0, tiled=True)

    def swap(value, step):
        return lax.ppermute(value, "pipe", [(i, i ^ step) for i in range(pipes)])

    def gather(own, behind):
        across = swap(own, 2)
        tied, tied_across, _ = lax.optimization_barrier((own, across, behind))
        return [own, swap(tied, 1), across, swap(tied_across, 1)]

    def mix(backward, value):
        return call(
            functools.partial(mix_kernel, backward),
            [chunks],
            [VMEM] * 3,
            [rows_of(all_rows, channels)] * 2,
            name="mix_grad" if backward else "mix",
        )(value, spec_real, spec_imag)[0]

    (sent,) = call(
        spectrum_kernel,
        [message],
        [HBM] * 2,
        [cell_tiles, table_tiles, dma((tiles,)), dma((tiles,))],
        name="spectrum",
        limit=60,
    )(field, f_table)
    received = exchange(sent)
    mixed = mix(False, received)
    returned = exchange(mixed).reshape(all_rows, channels)
    fields = gather(received, mixed)
    ids = pltpu.SMEM(inlet_ids.shape, jnp.int32)
    square = pltpu.VMEM((channels, channels), bf16)
    flat = pltpu.VMEM((1, channels), f32)
    modes_buf = pltpu.VMEM((all_rows, channels), bf16)
    msg_bufs = [pltpu.VMEM(message.shape, bf16)] * pipes
    outputs, total, sent, slope = call(
        functools.partial(layer_kernel, pipes),
        [shape(field.shape, bf16)] * 2 + [message, shape((8, channels), f32)],
        [HBM] * (pipes + 11),
        [cell_tiles, cell_tiles, table_tiles, back_tiles, cell_tiles, cell_tiles]
        + [pltpu.VMEM((all_rows, channels), f32)]
        + msg_bufs
        + [ids, ids, square, flat, square, flat, modes_buf]
        + [dma((pipes + 7,)), dma((4 * tiles,)), dma((2 * tiles,))],
        out_specs=[HBM, HBM, VMEM, VMEM],
        name="layer",
        limit=60,
    )(
        *fields,
        field,
        cot,
        f_table,
        ft_table,
        inlet_ids,
        outlet_ids,
        junc_weight,
        junc_bias_row,
        point_weight,
        bias_row,
        returned,
    )
    received = exchange(sent)
    mixed = mix(True, received)
    returned = exchange(mixed).reshape(all_rows, channels)
    grads = gather(received, mixed)
    big = shape((modes, channels, channels), f32)
    grad_real, grad_imag = call(
        functools.partial(weight_grad_kernel, pipes, modes),
        [big, big],
        [VMEM] * (2 * pipes),
        [rows_of(pipes * all_rows, channels)] * 2
        + [pltpu.VMEM(big.shape, f32)] * 2
        + [dma((modes, 2))],
        out_specs=[HBM, HBM],
        name="weight_grad",
        limit=16,
    )(*fields, *grads)
    (grad_inputs,) = call(
        functools.partial(input_grad_kernel, pipes),
        [shape(field.shape, bf16)],
        [HBM] * (pipes + 8),
        [cell_tiles, back_tiles, cell_tiles]
        + msg_bufs
        + [ids, ids, square, pltpu.VMEM((8, channels), f32), square, modes_buf]
        + [dma((pipes + 6,)), dma((2 * tiles,)), dma((tiles,))],
        out_specs=[HBM],
        name="input_grad",
        limit=60,
    )(
        *grads,
        total,
        ft_table,
        inlet_ids,
        outlet_ids,
        junc_weight,
        slope,
        point_weight,
        returned,
    )
    return (
        outputs.reshape(inputs.shape),
        grad_inputs.reshape(inputs.shape),
        grad_real,
        grad_imag,
    )


def solution(mesh):
    placed = (
        P(("len", "pipe"), None, None),
        P(("len", "pipe"), None, None),
        P(),
        P(),
        P("len", None, None),
        P("len", None, None),
        P(),
        P(),
        P(),
        P(),
    )
    return jax.shard_map(
        body,
        mesh=mesh,
        in_specs=placed,
        out_specs=(
            P(("len", "pipe"), None, None),
            P(("len", "pipe"), None, None),
            P("len", None, None),
            P("len", None, None),
        ),
        check_vma=False,
    )
```

```python
import functools
import math

import jax
import jax.numpy as jnp
import ml_dtypes
import numpy as np
from jax import lax
from jax.experimental import pallas as pl
from jax.experimental.pallas import tpu as pltpu
from jax.sharding import PartitionSpec as P

COUPLING = 0.125
TILE = 256
LANES = 128
GELU_S = math.sqrt(2.0 / math.pi)
GELU_C = 0.044715
VMEM = pl.BlockSpec(memory_space=pltpu.VMEM)
SMEM = pl.BlockSpec(memory_space=pltpu.SMEM)
HBM = pl.BlockSpec(memory_space=pltpu.HBM)
MIB = 1024 * 1024


def forward_table(cell_count, mode_count, groups):
    product_index = np.arange(mode_count)[:, None] * np.arange(cell_count)[None, :] % cell_count
    angles = product_index.astype(np.float32) * np.float32(2.0 * math.pi / cell_count)
    norm_scale = np.float32(1.0 / math.sqrt(cell_count))
    cosine = (np.cos(angles) * norm_scale).reshape(groups, -1, cell_count)
    sine = (np.sin(angles) * norm_scale).reshape(groups, -1, cell_count)
    table = np.concatenate([cosine, -sine], axis=1).reshape(2 * mode_count, cell_count)
    return table.astype(ml_dtypes.bfloat16)


def dot(left, right, left_dim=1, right_dim=0):
    return lax.dot_general(
        left,
        right,
        (((left_dim,), (right_dim,)), ((), ())),
        preferred_element_type=jnp.float32,
    )


def put(ref, at, value):
    for lane in range(ref.shape[0]):
        ref[lane, at, :] = value[:, lane * LANES : (lane + 1) * LANES]


def take(ref, at):
    return jnp.concatenate([ref[lane, at, :] for lane in range(ref.shape[0])], axis=1)


def spectrum_kernel(x_ref, f_ref, msg_ref):
    groups, rows = msg_ref.shape[0], msg_ref.shape[1]
    tiles, all_rows, tile = f_ref.shape
    cells, channels = x_ref.shape
    span = all_rows // groups
    total = None
    for step in range(tiles):
        part = dot(f_ref[step], x_ref[step * tile : (step + 1) * tile, :])
        total = part if total is None else total + part
    spectra = total.astype(jnp.bfloat16)
    ends = extra_rows(x_ref[0:1, :], x_ref[cells - 1 : cells, :], rows - span, channels)
    for at in range(groups):
        msg_ref[at, 0:span, :] = spectra[at * span : (at + 1) * span]
        msg_ref[at, span:rows, :] = ends


def extra_rows(first, second, count, channels):
    parts = [first.astype(jnp.float32), second.astype(jnp.float32)]
    if count > 2:
        parts.append(jnp.zeros((count - 2, channels), jnp.float32))
    return jnp.concatenate(parts, axis=0).astype(jnp.bfloat16)


def mix_kernel(backward, r_ref, real_ref, imag_ref, *refs):
    x_ref, y_ref = refs[-2:]
    groups, modes = r_ref.shape[0], real_ref.shape[0]
    span = 2 * modes
    if backward:
        early_ref, out_ref, copied_ref, sem = refs[:4]
        copy = pltpu.make_async_copy(early_ref, copied_ref, sem)
        copy.start()
    else:
        out_ref = refs[0]
    for source in range(groups):
        put(x_ref, pl.ds(source * span, span), r_ref[source, 0:span, :].astype(jnp.float32))
    for mode in range(modes):
        first = pl.ds(mode, groups, stride=span)
        second = pl.ds(modes + mode, groups, stride=span)
        rows = jnp.concatenate([take(x_ref, first), take(x_ref, second)], axis=0).astype(
            jnp.bfloat16
        )
        dim = 1 if backward else 0
        by_real = dot(rows, real_ref[mode], 1, dim)
        by_imag = dot(rows, imag_ref[mode], 1, dim)
        if backward:
            put(y_ref, first, by_real[:groups] + by_imag[groups:])
            put(y_ref, second, by_real[groups:] - by_imag[:groups])
        else:
            put(y_ref, first, by_real[:groups] - by_imag[groups:])
            put(y_ref, second, by_imag[:groups] + by_real[groups:])
    for source in range(groups):
        rows = take(y_ref, pl.ds(source * span, span)).astype(jnp.bfloat16)
        out_ref[source, 0:span, :] = rows
        if out_ref.shape[1] > span:
            out_ref[source, span:, :] = jnp.zeros((2, rows.shape[1]), jnp.bfloat16)
    if backward:
        copy.wait()


def own_pipe(pipes):
    return lax.axis_index("len") * pipes + lax.axis_index("pipe")


def two_rows(first, second, channels):
    return jnp.concatenate([first, second, jnp.zeros((6, channels), jnp.float32)], axis=0)


def junction_sums(pipes, msgs, inlet_ref, outlet_ref, both):
    groups, rows, channels = msgs[0].shape
    column = lax.axis_index("pipe")
    me = own_pipe(pipes)
    owns = inlet_ref[me], outlet_ref[me]
    is_first = lax.broadcasted_iota(jnp.int32, (2, channels), 0) == 0

    def matches(pipe, junction):
        first = (inlet_ref[pipe] == junction).astype(jnp.float32)
        last = (outlet_ref[pipe] == junction).astype(jnp.float32)
        return first + last if both else jnp.where(is_first, first, last)

    def add(group, carried):
        for step in range(pipes):
            pipe = group * pipes + lax.bitwise_xor(column, step)
            ends = msgs[step][group, rows - 2 : rows, :].astype(jnp.float32)
            carried = tuple(
                total + ends * matches(pipe, own) for total, own in zip(carried, owns)
            )
        return carried

    zero = jnp.zeros((2, channels), jnp.float32)
    totals = lax.fori_loop(0, groups, add, (zero, zero), unroll=min(groups, 8))
    return two_rows(
        jnp.sum(totals[0], axis=0, keepdims=True),
        jnp.sum(totals[1], axis=0, keepdims=True),
        channels,
    )


def junction_forward_kernel(pipes, *refs):
    msgs, (inlet_ref, outlet_ref, weight_ref, bias_ref, cond_ref, slope_ref) = (
        refs[:pipes],
        refs[pipes:],
    )
    sums = junction_sums(pipes, msgs, inlet_ref, outlet_ref, False)
    act = dot(sums.astype(jnp.bfloat16), weight_ref[...]) + bias_ref[...]
    sigmoid_part = jax.nn.sigmoid(act)
    junc_rows = (act * sigmoid_part).astype(jnp.bfloat16).astype(jnp.float32)
    cond_ref[...] = COUPLING * (junc_rows[0:1] + junc_rows[1:2])
    slope_ref[...] = sigmoid_part * (1.0 + act * (1.0 - sigmoid_part))


def junction_backward_kernel(pipes, *refs):
    msgs, (inlet_ref, outlet_ref, weight_ref, slope_ref, rows_ref) = refs[:pipes], refs[pipes:]
    junc_grad = COUPLING * junction_sums(pipes, msgs, inlet_ref, outlet_ref, True)
    act_grad = (junc_grad * slope_ref[...]).astype(jnp.bfloat16)
    sums_grad = dot(act_grad, weight_ref[...], 1, 1).astype(jnp.bfloat16)
    rows_ref[...] = sums_grad.astype(jnp.float32)


def started(copies):
    for copy in copies:
        copy.start()
    return copies


def wait(copies):
    for copy in copies:
        copy.wait()


def layer_kernel(
    x_ref,
    cot_ref,
    f_ref,
    ft_ref,
    weight_ref,
    bias_ref,
    cond_ref,
    modes_ref,
    out_ref,
    total_ref,
    msg_ref,
    acc_ref,
):
    channels = x_ref.shape[1]
    groups, rows = msg_ref.shape[0], msg_ref.shape[1]
    tiles, all_rows, tile = f_ref.shape
    span = all_rows // groups
    row = lax.broadcasted_iota(jnp.int32, (all_rows, channels), 0)
    doubled = jnp.where((row == 0) | (row == span // 2), 1.0, 2.0).astype(jnp.float32)
    modes = jnp.concatenate(
        [modes_ref[at, 0:span, :].astype(jnp.float32) for at in range(groups)], axis=0
    )
    modes = (modes * doubled).astype(jnp.bfloat16)
    weight = weight_ref[...]
    cond = cond_ref[...]
    bias = bias_ref[...]
    for step in range(tiles):
        at = pl.ds(step * tile, tile)
        spectral = dot(ft_ref[at, :], modes)
        pre = (spectral + cond).astype(jnp.bfloat16).astype(jnp.float32)
        summed = dot(x_ref[at, :], weight) + bias + pre
        square = summed * summed
        half = 0.5 + 0.5 * jnp.tanh(summed * (GELU_S + (GELU_S * GELU_C) * square))
        result = summed * half
        out_ref[at, :] = result.astype(jnp.bfloat16)
        slope = half + result * (1.0 - half) * (2.0 * GELU_S + (6.0 * GELU_S * GELU_C) * square)
        total = (cot_ref[at, :].astype(jnp.float32) * slope).astype(jnp.bfloat16)
        total_ref[at, :] = total
        part = dot(f_ref[step], total)
        if step == 0:
            acc_ref[...] = part
        else:
            acc_ref[...] += part
    grad_cond = acc_ref[0:1, :] * (1.0 / f_ref[0, 0:1, 0:1].astype(jnp.float32))
    high = grad_cond.astype(jnp.bfloat16).astype(jnp.float32)
    extra = extra_rows(high, grad_cond - high, rows - span, channels)
    grad_spec = (acc_ref[...] * doubled).astype(jnp.bfloat16)
    for at in range(groups):
        msg_ref[at, 0:span, :] = grad_spec[at * span : (at + 1) * span]
        msg_ref[at, span:rows, :] = extra


def input_grad_kernel(
    total_ref, ft_ref, weight_ref, rows_ref, modes_ref, out_ref, tiles_ref, sems
):
    modes = modes_ref[...]
    weight = weight_ref[...]
    tiles, tile, channels = tiles_ref.shape
    row = lax.broadcasted_iota(jnp.int32, (tile, channels), 0)
    going = []
    for step in range(tiles):
        at = pl.ds(step * tile, tile)
        grad_cells = dot(ft_ref[at, :], modes)
        if step == 0:
            grad_cells = grad_cells + jnp.where(row == 0, rows_ref[0:1, :], 0.0)
        if step == tiles - 1:
            grad_cells = grad_cells + jnp.where(row == tile - 1, rows_ref[1:2, :], 0.0)
        spread = grad_cells.astype(jnp.bfloat16).astype(jnp.float32)
        local = dot(total_ref[at, :], weight, 1, 1)
        tiles_ref[step] = (local + spread).astype(jnp.bfloat16)
        going += started(
            [pltpu.make_async_copy(tiles_ref.at[step], out_ref.at[at], sems.at[step])]
        )
    wait(going)


def weight_grad_kernel(pipes, modes, *refs):
    fields, grads = refs[:pipes], refs[pipes : 2 * pipes]
    real_out, imag_out, x_ref, g_ref, real_ref, imag_ref, sems = refs[2 * pipes :]
    groups = fields[0].shape[0]
    span = 2 * modes
    for step in range(pipes):
        for source in range(groups):
            at = pl.ds((step * groups + source) * span, span)
            put(x_ref, at, fields[step][source, 0:span, :].astype(jnp.float32))
            put(g_ref, at, grads[step][source, 0:span, :].astype(jnp.float32))
    count = pipes * groups
    going = []
    for mode in range(modes):
        first = pl.ds(mode, count, stride=span)
        second = pl.ds(modes + mode, count, stride=span)
        a, b = take(x_ref, first), take(x_ref, second)
        u, v = take(g_ref, first), take(g_ref, second)
        left = jnp.concatenate([a, b], axis=0).astype(jnp.bfloat16)
        real_ref[mode] = dot(left, jnp.concatenate([u, v], axis=0).astype(jnp.bfloat16), 0, 0)
        imag_ref[mode] = dot(left, jnp.concatenate([v, -u], axis=0).astype(jnp.bfloat16), 0, 0)
        going += started(
            [
                pltpu.make_async_copy(real_ref.at[mode], real_out.at[mode], sems.at[mode, 0]),
                pltpu.make_async_copy(imag_ref.at[mode], imag_out.at[mode], sems.at[mode, 1]),
            ]
        )
    wait(going)


def rows_of(count, channels):
    return pltpu.VMEM((channels // LANES, count, LANES), jnp.float32)


def call(kernel, outs, specs, scratch=(), out_specs=None, name=None, limit=8, busy=1):
    return pl.pallas_call(
        kernel,
        out_shape=outs,
        in_specs=specs,
        out_specs=out_specs if out_specs is not None else [VMEM] * len(outs),
        scratch_shapes=list(scratch),
        compiler_params=pltpu.CompilerParams(vmem_limit_bytes=limit * MIB),
        cost_estimate=pl.CostEstimate(
            flops=busy * 1_000_000_000, bytes_accessed=busy * MIB, transcendentals=0
        ),
        name=name,
    )


def body(
    inputs,
    cotangent,
    point_weight,
    point_bias,
    spec_real,
    spec_imag,
    junc_weight,
    junc_bias,
    inlet_ids,
    outlet_ids,
):
    per_dev, cell_count, channels = inputs.shape
    assert per_dev == 1
    groups, pipes = lax.axis_size("len"), lax.axis_size("pipe")
    assert pipes == 4
    modes = spec_real.shape[0]
    span = 2 * modes
    all_rows = span * groups
    tiles = cell_count // TILE
    table = forward_table(cell_count, modes * groups, groups)
    tiled = table.reshape(all_rows, tiles, TILE).transpose(1, 0, 2)
    f_table = jnp.asarray(np.ascontiguousarray(tiled))
    ft_table = jnp.asarray(np.ascontiguousarray(table.T))
    field = inputs.reshape(cell_count, channels)
    cot = cotangent.reshape(cell_count, channels)
    bias_row = point_bias.reshape(1, channels)
    junc_bias_row = junc_bias.reshape(1, channels)
    shape = jax.ShapeDtypeStruct
    bf16, f32 = jnp.bfloat16, jnp.float32
    message = shape((groups, span + 2, channels), bf16)
    chunks = shape((groups, span, channels), bf16)
    dma = pltpu.SemaphoreType.DMA

    def exchange(value):
        return lax.all_to_all(value, "len", split_axis=0, concat_axis=0, tiled=True)

    def swap(value, step):
        return lax.ppermute(value, "pipe", [(i, i ^ step) for i in range(pipes)])

    def gather(own, behind):
        across = swap(own, 2)
        tied, tied_across, _ = lax.optimization_barrier((own, across, behind))
        return [own, swap(tied, 1), across, swap(tied_across, 1)]

    def mix(backward, value, *early):
        return call(
            functools.partial(mix_kernel, backward),
            [chunks, early[0]] if backward else [message],
            [VMEM] * (4 if backward else 3),
            ([dma] if backward else []) + [rows_of(all_rows, channels)] * 2,
            out_specs=[VMEM, HBM] if backward else [VMEM],
            name="mix_grad" if backward else "mix",
            busy=12,
        )(value, spec_real, spec_imag, *early)

    (sent,) = call(spectrum_kernel, [message], [VMEM] * 2, name="spectrum", busy=12)(
        field, f_table
    )
    received = exchange(sent)
    (mixed,) = mix(False, received)
    returned = exchange(mixed)
    fields = gather(received, mixed)
    cond, slope = call(
        functools.partial(junction_forward_kernel, pipes),
        [shape((1, channels), f32), shape((8, channels), f32)],
        [VMEM] * pipes + [SMEM] * 2 + [VMEM] * 2,
        name="junction",
    )(*fields, inlet_ids, outlet_ids, junc_weight, junc_bias_row)
    early, total, sent = call(
        layer_kernel,
        [shape(field.shape, bf16), shape(field.shape, bf16), message],
        [VMEM] * 8,
        [pltpu.VMEM((all_rows, channels), f32)],
        name="layer",
        busy=12,
    )(field, cot, f_table, ft_table, point_weight, bias_row, cond, returned)
    received = exchange(sent)
    mixed, outputs = mix(True, received, early)
    returned = exchange(mixed).reshape(all_rows, channels)
    grads = gather(received, mixed)
    (rows,) = call(
        functools.partial(junction_backward_kernel, pipes),
        [shape((8, channels), f32)],
        [VMEM] * pipes + [SMEM] * 2 + [VMEM] * 2,
        name="junction_grad",
    )(*grads, inlet_ids, outlet_ids, junc_weight, slope)
    big = shape((modes, channels, channels), f32)
    grad_real, grad_imag = call(
        functools.partial(weight_grad_kernel, pipes, modes),
        [big, big],
        [VMEM] * (2 * pipes),
        [rows_of(pipes * all_rows, channels)] * 2
        + [pltpu.VMEM(big.shape, f32)] * 2
        + [dma((modes, 2))],
        out_specs=[HBM, HBM],
        name="weight_grad",
        limit=16,
    )(*fields, *grads)
    (grad_inputs,) = call(
        input_grad_kernel,
        [shape(field.shape, bf16)],
        [VMEM] * 5,
        [pltpu.VMEM((tiles, TILE, channels), bf16), dma((tiles,))],
        out_specs=[HBM],
        name="input_grad",
    )(total, ft_table, point_weight, rows, returned)
    return (
        outputs.reshape(inputs.shape),
        grad_inputs.reshape(inputs.shape),
        grad_real,
        grad_imag,
    )


def solution(mesh):
    placed = (
        P(("len", "pipe"), None, None),
        P(("len", "pipe"), None, None),
        P(),
        P(),
        P("len", None, None),
        P("len", None, None),
        P(),
        P(),
        P(),
        P(),
    )
    return jax.shard_map(
        body,
        mesh=mesh,
        in_specs=placed,
        out_specs=(
            P(("len", "pipe"), None, None),
            P(("len", "pipe"), None, None),
            P("len", None, None),
            P("len", None, None),
        ),
        check_vma=False,
    )
```

```python
import functools
import math

import jax
import jax.numpy as jnp
import ml_dtypes
import numpy as np
from jax import lax
from jax.experimental import pallas as pl
from jax.experimental.pallas import tpu as pltpu
from jax.sharding import PartitionSpec as P

COUPLING = 0.125
TILE = 256
LANES = 128
GELU_S = math.sqrt(2.0 / math.pi)
GELU_C = 0.044715
VMEM = pl.BlockSpec(memory_space=pltpu.VMEM)
SMEM = pl.BlockSpec(memory_space=pltpu.SMEM)
HBM = pl.BlockSpec(memory_space=pltpu.HBM)
MIB = 1024 * 1024


def half_table(cell_count, mode_count, groups):
    half = cell_count // 2
    product_index = np.arange(mode_count)[:, None] * np.arange(half)[None, :] % cell_count
    angles = product_index.astype(np.float32) * np.float32(2.0 * math.pi / cell_count)
    norm_scale = np.float32(1.0 / math.sqrt(cell_count))
    cosine = (np.cos(angles) * norm_scale).reshape(groups, -1, half)
    sine = (np.sin(angles) * norm_scale).reshape(groups, -1, half)
    table = np.concatenate([cosine, -sine], axis=1).reshape(2 * mode_count, half)
    return table.astype(ml_dtypes.bfloat16)


def row_signs(all_rows, span, channels):
    row = lax.broadcasted_iota(jnp.int32, (all_rows, channels), 0)
    per_owner = span // 2
    mode = (row // span) * per_owner + lax.rem(row, per_owner)
    return jnp.where(lax.rem(mode, 2) == 0, 1.0, -1.0).astype(jnp.float32)


def dot(left, right, left_dim=1, right_dim=0):
    return lax.dot_general(
        left,
        right,
        (((left_dim,), (right_dim,)), ((), ())),
        preferred_element_type=jnp.float32,
    )


def put(ref, at, value):
    for lane in range(ref.shape[0]):
        ref[lane, at, :] = value[:, lane * LANES : (lane + 1) * LANES]


def take(ref, at):
    return jnp.concatenate([ref[lane, at, :] for lane in range(ref.shape[0])], axis=1)


def spectrum_kernel(x_ref, f_ref, msg_ref):
    groups, rows = msg_ref.shape[0], msg_ref.shape[1]
    steps, all_rows, tile = f_ref.shape
    cells, channels = x_ref.shape
    half = cells // 2
    span = all_rows // groups
    sums = []
    for base in (0, half):
        total = None
        for step in range(steps):
            at = base + step * tile
            part = dot(f_ref[step], x_ref[at : at + tile, :])
            total = part if total is None else total + part
        sums.append(total)
    spectra = (sums[0] + row_signs(all_rows, span, channels) * sums[1]).astype(jnp.bfloat16)
    ends = extra_rows(x_ref[0:1, :], x_ref[cells - 1 : cells, :], rows - span, channels)
    for at in range(groups):
        msg_ref[at, 0:span, :] = spectra[at * span : (at + 1) * span]
        msg_ref[at, span:rows, :] = ends


def extra_rows(first, second, count, channels):
    parts = [first.astype(jnp.float32), second.astype(jnp.float32)]
    if count > 2:
        parts.append(jnp.zeros((count - 2, channels), jnp.float32))
    return jnp.concatenate(parts, axis=0).astype(jnp.bfloat16)


def mix_kernel(backward, r_ref, real_ref, imag_ref, out_ref, x_ref, y_ref):
    groups, modes = r_ref.shape[0], real_ref.shape[0]
    span = 2 * modes
    for source in range(groups):
        put(x_ref, pl.ds(source * span, span), r_ref[source, 0:span, :].astype(jnp.float32))
    for mode in range(modes):
        first = pl.ds(mode, groups, stride=span)
        second = pl.ds(modes + mode, groups, stride=span)
        rows = jnp.concatenate([take(x_ref, first), take(x_ref, second)], axis=0).astype(
            jnp.bfloat16
        )
        dim = 1 if backward else 0
        by_real = dot(rows, real_ref[mode], 1, dim)
        by_imag = dot(rows, imag_ref[mode], 1, dim)
        if backward:
            put(y_ref, first, by_real[:groups] + by_imag[groups:])
            put(y_ref, second, by_real[groups:] - by_imag[:groups])
        else:
            put(y_ref, first, by_real[:groups] - by_imag[groups:])
            put(y_ref, second, by_imag[:groups] + by_real[groups:])
    for source in range(groups):
        rows = take(y_ref, pl.ds(source * span, span))
        out_ref[source] = rows.astype(jnp.bfloat16)


def own_pipe(pipes):
    return lax.axis_index("len") * pipes + lax.axis_index("pipe")


def two_rows(first, second, channels):
    return jnp.concatenate([first, second, jnp.zeros((6, channels), jnp.float32)], axis=0)


def junction_sums(pipes, msgs, inlet_ref, outlet_ref, both):
    groups, rows, channels = msgs[0].shape
    column = lax.axis_index("pipe")
    me = own_pipe(pipes)
    owns = inlet_ref[me], outlet_ref[me]
    is_first = lax.broadcasted_iota(jnp.int32, (2, channels), 0) == 0

    def matches(pipe, junction):
        first = (inlet_ref[pipe] == junction).astype(jnp.float32)
        last = (outlet_ref[pipe] == junction).astype(jnp.float32)
        return first + last if both else jnp.where(is_first, first, last)

    def add(group, carried):
        for step in range(pipes):
            pipe = group * pipes + lax.bitwise_xor(column, step)
            ends = msgs[step][group, rows - 2 : rows, :].astype(jnp.float32)
            carried = tuple(
                total + ends * matches(pipe, own) for total, own in zip(carried, owns)
            )
        return carried

    zero = jnp.zeros((2, channels), jnp.float32)
    totals = lax.fori_loop(0, groups, add, (zero, zero), unroll=min(groups, 8))
    return two_rows(
        jnp.sum(totals[0], axis=0, keepdims=True),
        jnp.sum(totals[1], axis=0, keepdims=True),
        channels,
    )


def junction_forward_kernel(pipes, *refs):
    msgs, (inlet_ref, outlet_ref, weight_ref, bias_ref, cond_ref, slope_ref) = (
        refs[:pipes],
        refs[pipes:],
    )
    sums = junction_sums(pipes, msgs, inlet_ref, outlet_ref, False)
    act = dot(sums.astype(jnp.bfloat16), weight_ref[...]) + bias_ref[...]
    sigmoid_part = jax.nn.sigmoid(act)
    junc_rows = (act * sigmoid_part).astype(jnp.bfloat16).astype(jnp.float32)
    cond_ref[...] = COUPLING * (junc_rows[0:1] + junc_rows[1:2])
    slope_ref[...] = sigmoid_part * (1.0 + act * (1.0 - sigmoid_part))


def junction_backward_kernel(pipes, *refs):
    msgs, (inlet_ref, outlet_ref, weight_ref, slope_ref, rows_ref) = refs[:pipes], refs[pipes:]
    junc_grad = COUPLING * junction_sums(pipes, msgs, inlet_ref, outlet_ref, True)
    act_grad = (junc_grad * slope_ref[...]).astype(jnp.bfloat16)
    sums_grad = dot(act_grad, weight_ref[...], 1, 1).astype(jnp.bfloat16)
    rows_ref[...] = sums_grad.astype(jnp.float32)


def started(copies):
    for copy in copies:
        copy.start()
    return copies


def wait(copies):
    for copy in copies:
        copy.wait()


def brought(pairs, sems, base=0):
    return started(
        [
            pltpu.make_async_copy(source, target, sems.at[base + place])
            for place, (source, target) in enumerate(pairs)
        ]
    )


def layer_kernel(
    x_ref,
    cot_ref,
    f_ref,
    ft_ref,
    weight_ref,
    bias_ref,
    cond_ref,
    modes_ref,
    out_ref,
    total_ref,
    msg_ref,
    x_tiles,
    cot_tiles,
    f_tiles,
    ft_tiles,
    weight_buf,
    bias_buf,
    cond_buf,
    modes_buf,
    summed_tiles,
    out_tiles,
    total_tiles,
    low_ref,
    high_ref,
    small_sems,
    in_sems,
    out_sems,
):
    steps, all_rows, tile = f_ref.shape
    half = steps * tile
    channels = x_ref.shape[1]
    groups, rows = msg_ref.shape[0], msg_ref.shape[1]
    span = all_rows // groups
    low = [pl.ds(step * tile, tile) for step in range(steps)]
    high = [pl.ds(half + step * tile, tile) for step in range(steps)]
    small = brought(
        [
            (modes_ref, modes_buf),
            (weight_ref, weight_buf),
            (bias_ref, bias_buf),
            (cond_ref, cond_buf),
        ],
        small_sems,
    )
    first, second, third = {}, {}, {}

    def bring_first(step):
        first[step] = brought(
            [
                (ft_ref.at[low[step]], ft_tiles.at[step]),
                (x_ref.at[low[step]], x_tiles.at[step, 0]),
                (x_ref.at[high[step]], x_tiles.at[step, 1]),
            ],
            in_sems,
            6 * step,
        )

    def bring_rest(step):
        second[step] = brought(
            [
                (cot_ref.at[low[step]], cot_tiles.at[step, 0]),
                (cot_ref.at[high[step]], cot_tiles.at[step, 1]),
            ],
            in_sems,
            6 * step + 3,
        )
        third[step] = brought([(f_ref.at[step], f_tiles.at[step])], in_sems, 6 * step + 5)

    for step in range(steps + 1):
        if step < steps:
            bring_first(step)
        if step > 0:
            bring_rest(step - 1)
    wait(small)
    row = lax.broadcasted_iota(jnp.int32, (all_rows, channels), 0)
    doubled = jnp.where((row == 0) | (row == span // 2), 1.0, 2.0).astype(jnp.float32)
    signs = row_signs(all_rows, span, channels)
    modes = jnp.concatenate(
        [modes_buf[at, 0:span, :].astype(jnp.float32) for at in range(groups)], axis=0
    )
    modes = modes * doubled
    modes = (modes.astype(jnp.bfloat16), (modes * signs).astype(jnp.bfloat16))
    weight = weight_buf[...]
    cond = cond_buf[...]
    bias = bias_buf[...]
    going = []
    for block in range(steps + 2):
        if block < steps:
            wait(first[block])
        if 1 <= block <= steps:
            wait(second[block - 1])
        if 2 <= block:
            wait(third[block - 2])
        if block < steps:
            for side in range(2):
                spectral = dot(ft_tiles[block], modes[side])
                pre = (spectral + cond).astype(jnp.bfloat16).astype(jnp.float32)
                summed_tiles[block, side] = dot(x_tiles[block, side], weight) + bias + pre
        if 1 <= block <= steps:
            step = block - 1
            for side in range(2):
                summed = summed_tiles[step, side]
                square = summed * summed
                part = 0.5 + 0.5 * jnp.tanh(summed * (GELU_S + (GELU_S * GELU_C) * square))
                result = summed * part
                out_tiles[step, side] = result.astype(jnp.bfloat16)
                slope = part + result * (1.0 - part) * (
                    2.0 * GELU_S + (6.0 * GELU_S * GELU_C) * square
                )
                total = cot_tiles[step, side].astype(jnp.float32) * slope
                total_tiles[step, side] = total.astype(jnp.bfloat16)
        if 2 <= block:
            step = block - 2
            for side, acc_ref in enumerate((low_ref, high_ref)):
                part = dot(f_tiles[step], total_tiles[step, side])
                if step == 0:
                    acc_ref[...] = part
                else:
                    acc_ref[...] += part
        if 1 <= block <= steps:
            step = block - 1
            going += brought(
                [
                    (out_tiles.at[step, 0], out_ref.at[low[step]]),
                    (out_tiles.at[step, 1], out_ref.at[high[step]]),
                    (total_tiles.at[step, 0], total_ref.at[low[step]]),
                    (total_tiles.at[step, 1], total_ref.at[high[step]]),
                ],
                out_sems,
                4 * step,
            )
    acc = low_ref[...] + signs * high_ref[...]
    grad_cond = acc[0:1, :] * (1.0 / f_tiles[0, 0:1, 0:1].astype(jnp.float32))
    upper = grad_cond.astype(jnp.bfloat16).astype(jnp.float32)
    extra = extra_rows(upper, grad_cond - upper, rows - span, channels)
    grad_spec = (acc * doubled).astype(jnp.bfloat16)
    for at in range(groups):
        msg_ref[at, 0:span, :] = grad_spec[at * span : (at + 1) * span]
        msg_ref[at, span:rows, :] = extra
    wait(going)


def input_grad_kernel(
    total_ref,
    ft_ref,
    weight_ref,
    rows_ref,
    modes_ref,
    out_ref,
    total_tiles,
    ft_tiles,
    weight_buf,
    rows_buf,
    modes_buf,
    out_tiles,
    small_sems,
    in_sems,
    out_sems,
):
    steps, tile, all_rows = ft_tiles.shape
    half = steps * tile
    groups, span, channels = modes_ref.shape
    low = [pl.ds(step * tile, tile) for step in range(steps)]
    high = [pl.ds(half + step * tile, tile) for step in range(steps)]
    small = brought(
        [(modes_ref, modes_buf), (weight_ref, weight_buf), (rows_ref, rows_buf)], small_sems
    )
    coming = [
        brought(
            [
                (ft_ref.at[low[step]], ft_tiles.at[step]),
                (total_ref.at[low[step]], total_tiles.at[step, 0]),
                (total_ref.at[high[step]], total_tiles.at[step, 1]),
            ],
            in_sems,
            3 * step,
        )
        for step in range(steps)
    ]
    row = lax.broadcasted_iota(jnp.int32, (tile, channels), 0)
    wait(small)
    modes = jnp.concatenate(
        [modes_buf[at, 0:span, :].astype(jnp.float32) for at in range(groups)], axis=0
    )
    signs = row_signs(all_rows, span, channels)
    modes = (modes.astype(jnp.bfloat16), (modes * signs).astype(jnp.bfloat16))
    weight = weight_buf[...]
    going = []
    for step in range(steps):
        wait(coming[step])
        for side, at in enumerate((low[step], high[step])):
            grad_cells = dot(ft_tiles[step], modes[side])
            if step == 0 and side == 0:
                grad_cells = grad_cells + jnp.where(row == 0, rows_buf[0:1, :], 0.0)
            if step == steps - 1 and side == 1:
                grad_cells = grad_cells + jnp.where(row == tile - 1, rows_buf[1:2, :], 0.0)
            spread = grad_cells.astype(jnp.bfloat16).astype(jnp.float32)
            local = dot(total_tiles[step, side], weight, 1, 1)
            out_tiles[step, side] = (local + spread).astype(jnp.bfloat16)
        going += brought(
            [
                (out_tiles.at[step, 0], out_ref.at[low[step]]),
                (out_tiles.at[step, 1], out_ref.at[high[step]]),
            ],
            out_sems,
            2 * step,
        )
    wait(going)


def weight_grad_kernel(pipes, modes, *refs):
    fields, grads = refs[:pipes], refs[pipes : 2 * pipes]
    real_out, imag_out, x_ref, g_ref, real_ref, imag_ref, sems = refs[2 * pipes :]
    groups = fields[0].shape[0]
    span = 2 * modes
    for step in range(pipes):
        for source in range(groups):
            at = pl.ds((step * groups + source) * span, span)
            put(x_ref, at, fields[step][source, 0:span, :].astype(jnp.float32))
            put(g_ref, at, grads[step][source, 0:span, :].astype(jnp.float32))
    count = pipes * groups
    going = []
    for mode in range(modes):
        first = pl.ds(mode, count, stride=span)
        second = pl.ds(modes + mode, count, stride=span)
        a, b = take(x_ref, first), take(x_ref, second)
        u, v = take(g_ref, first), take(g_ref, second)
        left = jnp.concatenate([a, b], axis=0).astype(jnp.bfloat16)
        real_ref[mode] = dot(left, jnp.concatenate([u, v], axis=0).astype(jnp.bfloat16), 0, 0)
        imag_ref[mode] = dot(left, jnp.concatenate([v, -u], axis=0).astype(jnp.bfloat16), 0, 0)
        going += started(
            [
                pltpu.make_async_copy(real_ref.at[mode], real_out.at[mode], sems.at[mode, 0]),
                pltpu.make_async_copy(imag_ref.at[mode], imag_out.at[mode], sems.at[mode, 1]),
            ]
        )
    wait(going)


def rows_of(count, channels):
    return pltpu.VMEM((channels // LANES, count, LANES), jnp.float32)


def call(kernel, outs, specs, scratch=(), out_specs=None, name=None, limit=8, busy=1):
    return pl.pallas_call(
        kernel,
        out_shape=outs,
        in_specs=specs,
        out_specs=out_specs if out_specs is not None else [VMEM] * len(outs),
        scratch_shapes=list(scratch),
        compiler_params=pltpu.CompilerParams(vmem_limit_bytes=limit * MIB),
        cost_estimate=pl.CostEstimate(
            flops=busy * 1_000_000_000, bytes_accessed=busy * MIB, transcendentals=0
        ),
        name=name,
    )


def body(
    inputs,
    cotangent,
    point_weight,
    point_bias,
    spec_real,
    spec_imag,
    junc_weight,
    junc_bias,
    inlet_ids,
    outlet_ids,
):
    per_dev, cell_count, channels = inputs.shape
    assert per_dev == 1
    groups, pipes = lax.axis_size("len"), lax.axis_size("pipe")
    assert pipes == 4
    modes = spec_real.shape[0]
    span = 2 * modes
    all_rows = span * groups
    steps = cell_count // (2 * TILE)
    table = half_table(cell_count, modes * groups, groups)
    tiled = table.reshape(all_rows, steps, TILE).transpose(1, 0, 2)
    f_table = jnp.asarray(np.ascontiguousarray(tiled))
    ft_table = jnp.asarray(np.ascontiguousarray(table.T))
    field = inputs.reshape(cell_count, channels)
    cot = cotangent.reshape(cell_count, channels)
    bias_row = point_bias.reshape(1, channels)
    junc_bias_row = junc_bias.reshape(1, channels)
    shape = jax.ShapeDtypeStruct
    bf16, f32 = jnp.bfloat16, jnp.float32
    message = shape((groups, span + 2, channels), bf16)
    chunks = shape((groups, span, channels), bf16)
    dma = pltpu.SemaphoreType.DMA

    def exchange(value):
        return lax.all_to_all(value, "len", split_axis=0, concat_axis=0, tiled=True)

    def swap(value, step):
        return lax.ppermute(value, "pipe", [(i, i ^ step) for i in range(pipes)])

    def gather(own, behind):
        across = swap(own, 2)
        tied, tied_across, _ = lax.optimization_barrier((own, across, behind))
        return [own, swap(tied, 1), across, swap(tied_across, 1)]

    def mix(backward, value):
        return call(
            functools.partial(mix_kernel, backward),
            [chunks],
            [VMEM] * 3,
            [rows_of(all_rows, channels)] * 2,
            name="mix_grad" if backward else "mix",
            busy=12,
        )(value, spec_real, spec_imag)[0]

    (sent,) = call(spectrum_kernel, [message], [VMEM] * 2, name="spectrum", busy=12)(
        field, f_table
    )
    received = exchange(sent)
    mixed = mix(False, received)
    returned = exchange(mixed)
    fields = gather(received, mixed)
    cond, slope = call(
        functools.partial(junction_forward_kernel, pipes),
        [shape((1, channels), f32), shape((8, channels), f32)],
        [VMEM] * pipes + [SMEM] * 2 + [VMEM] * 2,
        name="junction",
    )(*fields, inlet_ids, outlet_ids, junc_weight, junc_bias_row)
    sides = pltpu.VMEM((steps, 2, TILE, channels), bf16)
    table_tiles = pltpu.VMEM((steps, all_rows, TILE), bf16)
    back_tiles = pltpu.VMEM((steps, TILE, all_rows), bf16)
    square = pltpu.VMEM((channels, channels), bf16)
    flat = pltpu.VMEM((1, channels), f32)
    outputs, total, sent = call(
        layer_kernel,
        [shape(field.shape, bf16), shape(field.shape, bf16), message],
        [HBM] * 8,
        [sides, sides, table_tiles, back_tiles, square, flat, flat]
        + [pltpu.VMEM(chunks.shape, bf16), pltpu.VMEM((steps, 2, TILE, channels), f32)]
        + [sides, sides]
        + [pltpu.VMEM((all_rows, channels), f32)] * 2
        + [dma((4,)), dma((6 * steps,)), dma((4 * steps,))],
        out_specs=[HBM, HBM, VMEM],
        name="layer",
        busy=12,
        limit=60,
    )(field, cot, f_table, ft_table, point_weight, bias_row, cond, returned)
    received = exchange(sent)
    mixed = mix(True, received)
    returned = exchange(mixed)
    grads = gather(received, mixed)
    (rows,) = call(
        functools.partial(junction_backward_kernel, pipes),
        [shape((8, channels), f32)],
        [VMEM] * pipes + [SMEM] * 2 + [VMEM] * 2,
        name="junction_grad",
    )(*grads, inlet_ids, outlet_ids, junc_weight, slope)
    big = shape((modes, channels, channels), f32)
    grad_real, grad_imag = call(
        functools.partial(weight_grad_kernel, pipes, modes),
        [big, big],
        [VMEM] * (2 * pipes),
        [rows_of(pipes * all_rows, channels)] * 2
        + [pltpu.VMEM(big.shape, f32)] * 2
        + [dma((modes, 2))],
        out_specs=[HBM, HBM],
        name="weight_grad",
        limit=16,
    )(*fields, *grads)
    total, grad_real, grad_imag = lax.optimization_barrier((total, grad_real, grad_imag))
    (grad_inputs,) = call(
        input_grad_kernel,
        [shape(field.shape, bf16)],
        [HBM] * 5,
        [sides, back_tiles, square, pltpu.VMEM((8, channels), f32)]
        + [pltpu.VMEM(chunks.shape, bf16), sides]
        + [dma((3,)), dma((3 * steps,)), dma((2 * steps,))],
        out_specs=[HBM],
        name="input_grad",
        limit=60,
    )(total, ft_table, point_weight, rows, returned)
    return (
        outputs.reshape(inputs.shape),
        grad_inputs.reshape(inputs.shape),
        grad_real,
        grad_imag,
    )


def solution(mesh):
    placed = (
        P(("len", "pipe"), None, None),
        P(("len", "pipe"), None, None),
        P(),
        P(),
        P("len", None, None),
        P("len", None, None),
        P(),
        P(),
        P(),
        P(),
    )
    return jax.shard_map(
        body,
        mesh=mesh,
        in_specs=placed,
        out_specs=(
            P(("len", "pipe"), None, None),
            P(("len", "pipe"), None, None),
            P("len", None, None),
            P("len", None, None),
        ),
        check_vma=False,
    )
```

```python
import functools
import math

import jax
import jax.numpy as jnp
import ml_dtypes
import numpy as np
from jax import lax
from jax.experimental import pallas as pl
from jax.experimental.pallas import tpu as pltpu
from jax.sharding import PartitionSpec as P

COUPLING = 0.125
TILE = 256
LANES = 128
GELU_S = math.sqrt(2.0 / math.pi)
GELU_C = 0.044715
VMEM = pl.BlockSpec(memory_space=pltpu.VMEM)
SMEM = pl.BlockSpec(memory_space=pltpu.SMEM)
HBM = pl.BlockSpec(memory_space=pltpu.HBM)
MIB = 1024 * 1024


def half_table(cell_count, mode_count, groups):
    half = cell_count // 2
    product_index = np.arange(mode_count)[:, None] * np.arange(half)[None, :] % cell_count
    angles = product_index.astype(np.float32) * np.float32(2.0 * math.pi / cell_count)
    norm_scale = np.float32(1.0 / math.sqrt(cell_count))
    cosine = (np.cos(angles) * norm_scale).reshape(groups, -1, half)
    sine = (np.sin(angles) * norm_scale).reshape(groups, -1, half)
    table = np.concatenate([cosine, -sine], axis=1).reshape(2 * mode_count, half)
    return table.astype(ml_dtypes.bfloat16)


def row_signs(all_rows, span, channels):
    row = lax.broadcasted_iota(jnp.int32, (all_rows, channels), 0)
    per_owner = span // 2
    mode = (row // span) * per_owner + lax.rem(row, per_owner)
    return jnp.where(lax.rem(mode, 2) == 0, 1.0, -1.0).astype(jnp.float32)


def dot(left, right, left_dim=1, right_dim=0):
    return lax.dot_general(
        left,
        right,
        (((left_dim,), (right_dim,)), ((), ())),
        preferred_element_type=jnp.float32,
    )


def put(ref, at, value):
    for lane in range(ref.shape[0]):
        ref[lane, at, :] = value[:, lane * LANES : (lane + 1) * LANES]


def take(ref, at):
    return jnp.concatenate([ref[lane, at, :] for lane in range(ref.shape[0])], axis=1)


def spectrum_kernel(x_ref, f_ref, msg_ref):
    groups, rows = msg_ref.shape[0], msg_ref.shape[1]
    steps, all_rows, tile = f_ref.shape
    cells, channels = x_ref.shape
    half = cells // 2
    span = all_rows // groups
    sums = []
    for base in (0, half):
        total = None
        for step in range(steps):
            at = base + step * tile
            part = dot(f_ref[step], x_ref[at : at + tile, :])
            total = part if total is None else total + part
        sums.append(total)
    spectra = (sums[0] + row_signs(all_rows, span, channels) * sums[1]).astype(jnp.bfloat16)
    ends = extra_rows(x_ref[0:1, :], x_ref[cells - 1 : cells, :], rows - span, channels)
    for at in range(groups):
        msg_ref[at, 0:span, :] = spectra[at * span : (at + 1) * span]
        msg_ref[at, span:rows, :] = ends


def extra_rows(first, second, count, channels):
    parts = [first.astype(jnp.float32), second.astype(jnp.float32)]
    if count > 2:
        parts.append(jnp.zeros((count - 2, channels), jnp.float32))
    return jnp.concatenate(parts, axis=0).astype(jnp.bfloat16)


def mix_kernel(backward, r_ref, real_ref, imag_ref, *refs):
    x_ref, y_ref = refs[-2:]
    groups, modes = r_ref.shape[0], real_ref.shape[0]
    span = 2 * modes
    if backward:
        early_ref, out_ref, copied_ref, sem = refs[:4]
        copy = pltpu.make_async_copy(early_ref, copied_ref, sem)
        copy.start()
    else:
        out_ref = refs[0]
    for source in range(groups):
        put(x_ref, pl.ds(source * span, span), r_ref[source, 0:span, :].astype(jnp.float32))
    for mode in range(modes):
        first = pl.ds(mode, groups, stride=span)
        second = pl.ds(modes + mode, groups, stride=span)
        rows = jnp.concatenate([take(x_ref, first), take(x_ref, second)], axis=0).astype(
            jnp.bfloat16
        )
        dim = 1 if backward else 0
        by_real = dot(rows, real_ref[mode], 1, dim)
        by_imag = dot(rows, imag_ref[mode], 1, dim)
        if backward:
            put(y_ref, first, by_real[:groups] + by_imag[groups:])
            put(y_ref, second, by_real[groups:] - by_imag[:groups])
        else:
            put(y_ref, first, by_real[:groups] - by_imag[groups:])
            put(y_ref, second, by_imag[:groups] + by_real[groups:])
    for source in range(groups):
        rows = take(y_ref, pl.ds(source * span, span)).astype(jnp.bfloat16)
        out_ref[source] = rows
    if backward:
        copy.wait()


def own_pipe(pipes):
    return lax.axis_index("len") * pipes + lax.axis_index("pipe")


def two_rows(first, second, channels):
    return jnp.concatenate([first, second, jnp.zeros((6, channels), jnp.float32)], axis=0)


def junction_sums(pipes, msgs, inlet_ref, outlet_ref, both):
    groups, rows, channels = msgs[0].shape
    column = lax.axis_index("pipe")
    me = own_pipe(pipes)
    owns = inlet_ref[me], outlet_ref[me]
    is_first = lax.broadcasted_iota(jnp.int32, (2, channels), 0) == 0

    def matches(pipe, junction):
        first = (inlet_ref[pipe] == junction).astype(jnp.float32)
        last = (outlet_ref[pipe] == junction).astype(jnp.float32)
        return first + last if both else jnp.where(is_first, first, last)

    def add(group, carried):
        for step in range(pipes):
            pipe = group * pipes + lax.bitwise_xor(column, step)
            ends = msgs[step][group, rows - 2 : rows, :].astype(jnp.float32)
            carried = tuple(
                total + ends * matches(pipe, own) for total, own in zip(carried, owns)
            )
        return carried

    zero = jnp.zeros((2, channels), jnp.float32)
    totals = lax.fori_loop(0, groups, add, (zero, zero), unroll=min(groups, 8))
    return two_rows(
        jnp.sum(totals[0], axis=0, keepdims=True),
        jnp.sum(totals[1], axis=0, keepdims=True),
        channels,
    )


def junction_forward(pipes, msgs, inlet_ref, outlet_ref, weight_ref, bias_ref):
    sums = junction_sums(pipes, msgs, inlet_ref, outlet_ref, False)
    act = dot(sums.astype(jnp.bfloat16), weight_ref[...]) + bias_ref[...]
    sigmoid_part = jax.nn.sigmoid(act)
    junc_rows = (act * sigmoid_part).astype(jnp.bfloat16).astype(jnp.float32)
    cond = COUPLING * (junc_rows[0:1] + junc_rows[1:2])
    return cond, sigmoid_part * (1.0 + act * (1.0 - sigmoid_part))


def junction_backward(pipes, msgs, inlet_ref, outlet_ref, weight_ref, slope_ref):
    junc_grad = COUPLING * junction_sums(pipes, msgs, inlet_ref, outlet_ref, True)
    act_grad = (junc_grad * slope_ref[...]).astype(jnp.bfloat16)
    return dot(act_grad, weight_ref[...], 1, 1).astype(jnp.bfloat16).astype(jnp.float32)


def started(copies):
    for copy in copies:
        copy.start()
    return copies


def wait(copies):
    for copy in copies:
        copy.wait()


def brought(pairs, sems, base=0):
    return started(
        [
            pltpu.make_async_copy(source, target, sems.at[base + place])
            for place, (source, target) in enumerate(pairs)
        ]
    )


def layer_kernel(pipes, *refs):
    msgs, refs = refs[:pipes], refs[pipes:]
    (inlet_ref, outlet_ref, junc_weight_ref, junc_bias_ref), refs = refs[:4], refs[4:]
    x_ref, cot_ref, f_ref, ft_ref, weight_ref, bias_ref, modes_ref = refs[:7]
    out_ref, total_ref, msg_ref, slope_ref, low_ref, high_ref = refs[7:]
    steps, all_rows, tile = f_ref.shape
    half = steps * tile
    channels = x_ref.shape[1]
    groups, rows = msg_ref.shape[0], msg_ref.shape[1]
    span = all_rows // groups
    cond, slope = junction_forward(
        pipes, msgs, inlet_ref, outlet_ref, junc_weight_ref, junc_bias_ref
    )
    slope_ref[...] = slope
    row = lax.broadcasted_iota(jnp.int32, (all_rows, channels), 0)
    doubled = jnp.where((row == 0) | (row == span // 2), 1.0, 2.0).astype(jnp.float32)
    signs = row_signs(all_rows, span, channels)
    modes = jnp.concatenate(
        [modes_ref[at, 0:span, :].astype(jnp.float32) for at in range(groups)], axis=0
    )
    modes = modes * doubled
    modes = (modes.astype(jnp.bfloat16), (modes * signs).astype(jnp.bfloat16))
    weight = weight_ref[...]
    bias = bias_ref[...]
    for step in range(steps):
        for side, acc_ref in enumerate((low_ref, high_ref)):
            at = pl.ds(side * half + step * tile, tile)
            pointwise = dot(x_ref[at, :], weight) + bias
            spectral = dot(ft_ref[pl.ds(step * tile, tile), :], modes[side])
            summed = pointwise + (spectral + cond).astype(jnp.bfloat16).astype(jnp.float32)
            square = summed * summed
            part = 0.5 + 0.5 * jnp.tanh(summed * (GELU_S + (GELU_S * GELU_C) * square))
            result = summed * part
            out_ref[at, :] = result.astype(jnp.bfloat16)
            slope = part + result * (1.0 - part) * (
                2.0 * GELU_S + (6.0 * GELU_S * GELU_C) * square
            )
            total = (cot_ref[at, :].astype(jnp.float32) * slope).astype(jnp.bfloat16)
            total_ref[at, :] = total
            term = dot(f_ref[step], total)
            if step == 0:
                acc_ref[...] = term
            else:
                acc_ref[...] += term
    acc = low_ref[...] + signs * high_ref[...]
    grad_cond = acc[0:1, :] * (1.0 / f_ref[0, 0:1, 0:1].astype(jnp.float32))
    upper = grad_cond.astype(jnp.bfloat16).astype(jnp.float32)
    extra = extra_rows(upper, grad_cond - upper, rows - span, channels)
    grad_spec = (acc * doubled).astype(jnp.bfloat16)
    for at in range(groups):
        msg_ref[at, 0:span, :] = grad_spec[at * span : (at + 1) * span]
        msg_ref[at, span:rows, :] = extra


def last_kernel(pipes, modes, per_copy, *refs):
    fields, grads, refs = refs[:pipes], refs[pipes : 2 * pipes], refs[2 * pipes :]
    (inlet_ref, outlet_ref, junc_weight_ref, slope_ref), refs = refs[:4], refs[4:]
    total_ref, ft_ref, weight_ref, modes_ref = refs[:4]
    real_out, imag_out, field_out = refs[4:7]
    x_ref, g_ref, real_ref, imag_ref, tiles_ref, weight_sems, field_sems = refs[7:]
    groups, span, channels = modes_ref.shape
    steps, tile = tiles_ref.shape[0], tiles_ref.shape[2]
    half, all_rows = steps * tile, groups * span
    for step in range(pipes):
        for source in range(groups):
            at = pl.ds((step * groups + source) * span, span)
            put(x_ref, at, fields[step][source, 0:span, :].astype(jnp.float32))
            put(g_ref, at, grads[step][source, 0:span, :].astype(jnp.float32))
    count = pipes * groups
    going = []

    def weight_part(number):
        for mode in range(number * per_copy, (number + 1) * per_copy):
            first = pl.ds(mode, count, stride=span)
            second = pl.ds(modes + mode, count, stride=span)
            a, b = take(x_ref, first), take(x_ref, second)
            u, v = take(g_ref, first), take(g_ref, second)
            left = jnp.concatenate([a, b], axis=0).astype(jnp.bfloat16)
            right = jnp.concatenate([u, v], axis=0).astype(jnp.bfloat16)
            turned = jnp.concatenate([v, -u], axis=0).astype(jnp.bfloat16)
            real_ref[mode] = dot(left, right, 0, 0)
            imag_ref[mode] = dot(left, turned, 0, 0)
        at = pl.ds(number * per_copy, per_copy)
        return started(
            [
                pltpu.make_async_copy(real_ref.at[at], real_out.at[at], weight_sems.at[number, 0]),
                pltpu.make_async_copy(imag_ref.at[at], imag_out.at[at], weight_sems.at[number, 1]),
            ]
        )

    back = jnp.concatenate(
        [modes_ref[at, 0:span, :].astype(jnp.float32) for at in range(groups)], axis=0
    )
    signs = row_signs(all_rows, span, channels)
    back = (back.astype(jnp.bfloat16), (back * signs).astype(jnp.bfloat16))
    weight = weight_ref[...]
    row = lax.broadcasted_iota(jnp.int32, (tile, channels), 0)
    sums_grad = junction_backward(
        pipes, grads, inlet_ref, outlet_ref, junc_weight_ref, slope_ref
    )

    def field_part(step):
        for side in range(2):
            at = pl.ds(side * half + step * tile, tile)
            grad_cells = dot(ft_ref[pl.ds(step * tile, tile), :], back[side])
            if step == 0 and side == 0:
                grad_cells = grad_cells + jnp.where(row == 0, sums_grad[0:1, :], 0.0)
            if step == steps - 1 and side == 1:
                grad_cells = grad_cells + jnp.where(row == tile - 1, sums_grad[1:2, :], 0.0)
            spread = grad_cells.astype(jnp.bfloat16).astype(jnp.float32)
            local = dot(total_ref[at, :], weight, 1, 1)
            tiles_ref[step, side] = (local + spread).astype(jnp.bfloat16)
        copies = []
        for side in range(2):
            at = pl.ds(side * half + step * tile, tile)
            copies.append(
                pltpu.make_async_copy(
                    tiles_ref.at[step, side], field_out.at[at], field_sems.at[step, side]
                )
            )
        return started(copies)

    numbers = modes // per_copy
    for place in range(max(numbers, steps)):
        if place < numbers:
            going += weight_part(place)
        if place < steps:
            going += field_part(place)
    wait(going)


def rows_of(count, channels):
    return pltpu.VMEM((channels // LANES, count, LANES), jnp.float32)


def call(kernel, outs, specs, scratch=(), out_specs=None, name=None, limit=8, busy=1):
    return pl.pallas_call(
        kernel,
        out_shape=outs,
        in_specs=specs,
        out_specs=out_specs if out_specs is not None else [VMEM] * len(outs),
        scratch_shapes=list(scratch),
        compiler_params=pltpu.CompilerParams(vmem_limit_bytes=limit * MIB),
        cost_estimate=pl.CostEstimate(
            flops=busy * 1_000_000_000, bytes_accessed=busy * MIB, transcendentals=0
        ),
        name=name,
    )


def body(
    inputs,
    cotangent,
    point_weight,
    point_bias,
    spec_real,
    spec_imag,
    junc_weight,
    junc_bias,
    inlet_ids,
    outlet_ids,
):
    per_dev, cell_count, channels = inputs.shape
    assert per_dev == 1
    groups, pipes = lax.axis_size("len"), lax.axis_size("pipe")
    assert pipes == 4
    modes = spec_real.shape[0]
    span = 2 * modes
    all_rows = span * groups
    steps = cell_count // (2 * TILE)
    table = half_table(cell_count, modes * groups, groups)
    tiled = table.reshape(all_rows, steps, TILE).transpose(1, 0, 2)
    f_table = jnp.asarray(np.ascontiguousarray(tiled))
    ft_table = jnp.asarray(np.ascontiguousarray(table.T))
    field = inputs.reshape(cell_count, channels)
    cot = cotangent.reshape(cell_count, channels)
    bias_row = point_bias.reshape(1, channels)
    junc_bias_row = junc_bias.reshape(1, channels)
    shape = jax.ShapeDtypeStruct
    bf16, f32 = jnp.bfloat16, jnp.float32
    message = shape((groups, span + 2, channels), bf16)
    chunks = shape((groups, span, channels), bf16)
    dma = pltpu.SemaphoreType.DMA

    def exchange(value):
        return lax.all_to_all(value, "len", split_axis=0, concat_axis=0, tiled=True)

    def swap(value, step):
        return lax.ppermute(value, "pipe", [(i, i ^ step) for i in range(pipes)])

    def gather(own):
        return [own] + [swap(own, step) for step in range(1, pipes)]

    def mix(backward, value, *early):
        return call(
            functools.partial(mix_kernel, backward),
            [chunks, early[0]] if backward else [chunks],
            [VMEM] * (4 if backward else 3),
            ([dma] if backward else []) + [rows_of(all_rows, channels)] * 2,
            out_specs=[VMEM, HBM] if backward else [VMEM],
            name="mix_grad" if backward else "mix",
            busy=12,
        )(value, spec_real, spec_imag, *early)

    (sent,) = call(spectrum_kernel, [message], [VMEM] * 2, name="spectrum", busy=12)(
        field, f_table
    )
    received = exchange(sent)
    fields = gather(received)
    (mixed,) = mix(False, received)
    returned = exchange(mixed)
    early, total, sent, slope = call(
        functools.partial(layer_kernel, pipes),
        [shape(field.shape, bf16)] * 2 + [message, shape((8, channels), f32)],
        [VMEM] * pipes + [SMEM] * 2 + [VMEM] * 9,
        [pltpu.VMEM((all_rows, channels), f32)] * 2,
        name="layer",
        busy=12,
    )(
        *fields,
        inlet_ids,
        outlet_ids,
        junc_weight,
        junc_bias_row,
        field,
        cot,
        f_table,
        ft_table,
        point_weight,
        bias_row,
        returned,
    )
    received = exchange(sent)
    grads = gather(received)
    mixed, outputs = mix(True, received, early)
    returned = exchange(mixed)
    big = shape((modes, channels, channels), f32)
    per_copy = math.gcd(modes, 2)
    grad_real, grad_imag, grad_inputs = call(
        functools.partial(last_kernel, pipes, modes, per_copy),
        [big, big, shape(field.shape, bf16)],
        [VMEM] * (2 * pipes) + [SMEM] * 2 + [VMEM] * 6,
        [rows_of(pipes * all_rows, channels)] * 2
        + [pltpu.VMEM(big.shape, f32)] * 2
        + [pltpu.VMEM((steps, 2, TILE, channels), bf16)]
        + [dma((modes // per_copy, 2)), dma((steps, 2))],
        out_specs=[HBM] * 3,
        name="last",
        limit=20,
    )(
        *fields,
        *grads,
        inlet_ids,
        outlet_ids,
        junc_weight,
        slope,
        total,
        ft_table,
        point_weight,
        returned,
    )
    return (
        outputs.reshape(inputs.shape),
        grad_inputs.reshape(inputs.shape),
        grad_real,
        grad_imag,
    )


def solution(mesh):
    placed = (
        P(("len", "pipe"), None, None),
        P(("len", "pipe"), None, None),
        P(),
        P(),
        P("len", None, None),
        P("len", None, None),
        P(),
        P(),
        P(),
        P(),
    )
    return jax.shard_map(
        body,
        mesh=mesh,
        in_specs=placed,
        out_specs=(
            P(("len", "pipe"), None, None),
            P(("len", "pipe"), None, None),
            P("len", None, None),
            P("len", None, None),
        ),
        check_vma=False,
    )
```

```python
import functools
import math

import jax
import jax.numpy as jnp
import ml_dtypes
import numpy as np
from jax import lax
from jax.experimental import pallas as pl
from jax.experimental.pallas import tpu as pltpu
from jax.sharding import PartitionSpec as P

COUPLING = 0.125
TILE = 256
LANES = 128
GELU_S = math.sqrt(2.0 / math.pi)
GELU_C = 0.044715
VMEM = pl.BlockSpec(memory_space=pltpu.VMEM)
SMEM = pl.BlockSpec(memory_space=pltpu.SMEM)
HBM = pl.BlockSpec(memory_space=pltpu.HBM)
MIB = 1024 * 1024


def half_table(cell_count, mode_count, groups):
    half = cell_count // 2
    product_index = np.arange(mode_count)[:, None] * np.arange(half)[None, :] % cell_count
    angles = product_index.astype(np.float32) * np.float32(2.0 * math.pi / cell_count)
    norm_scale = np.float32(1.0 / math.sqrt(cell_count))
    cosine = (np.cos(angles) * norm_scale).reshape(groups, -1, half)
    sine = (np.sin(angles) * norm_scale).reshape(groups, -1, half)
    table = np.concatenate([cosine, -sine], axis=1).reshape(2 * mode_count, half)
    return table.astype(ml_dtypes.bfloat16)


def row_signs(all_rows, span, channels):
    row = lax.broadcasted_iota(jnp.int32, (all_rows, channels), 0)
    per_owner = span // 2
    mode = (row // span) * per_owner + lax.rem(row, per_owner)
    return jnp.where(lax.rem(mode, 2) == 0, 1.0, -1.0).astype(jnp.float32)


def dot(left, right, left_dim=1, right_dim=0):
    return lax.dot_general(
        left,
        right,
        (((left_dim,), (right_dim,)), ((), ())),
        preferred_element_type=jnp.float32,
    )


def put(ref, at, value):
    for lane in range(ref.shape[0]):
        ref[lane, at, :] = value[:, lane * LANES : (lane + 1) * LANES]


def take(ref, at):
    return jnp.concatenate([ref[lane, at, :] for lane in range(ref.shape[0])], axis=1)


def spectrum_kernel(x_ref, f_ref, msg_ref):
    groups, rows = msg_ref.shape[0], msg_ref.shape[1]
    steps, all_rows, tile = f_ref.shape
    cells, channels = x_ref.shape
    half = cells // 2
    span = all_rows // groups
    sums = []
    for base in (0, half):
        total = None
        for step in range(steps):
            at = base + step * tile
            part = dot(f_ref[step], x_ref[at : at + tile, :])
            total = part if total is None else total + part
        sums.append(total)
    spectra = (sums[0] + row_signs(all_rows, span, channels) * sums[1]).astype(jnp.bfloat16)
    ends = extra_rows(x_ref[0:1, :], x_ref[cells - 1 : cells, :], rows - span, channels)
    for at in range(groups):
        msg_ref[at, 0:span, :] = spectra[at * span : (at + 1) * span]
        msg_ref[at, span:rows, :] = ends


def extra_rows(first, second, count, channels):
    parts = [first.astype(jnp.float32), second.astype(jnp.float32)]
    if count > 2:
        parts.append(jnp.zeros((count - 2, channels), jnp.float32))
    return jnp.concatenate(parts, axis=0).astype(jnp.bfloat16)


def mix_kernel(backward, r_ref, real_ref, imag_ref, *refs):
    x_ref, y_ref = refs[-2:]
    groups, modes = r_ref.shape[0], real_ref.shape[0]
    span = 2 * modes
    if backward:
        early_ref, out_ref, copied_ref, sem = refs[:4]
        copy = pltpu.make_async_copy(early_ref, copied_ref, sem)
        copy.start()
    else:
        out_ref = refs[0]
    for source in range(groups):
        put(x_ref, pl.ds(source * span, span), r_ref[source, 0:span, :].astype(jnp.float32))
    for mode in range(modes):
        first = pl.ds(mode, groups, stride=span)
        second = pl.ds(modes + mode, groups, stride=span)
        rows = jnp.concatenate([take(x_ref, first), take(x_ref, second)], axis=0).astype(
            jnp.bfloat16
        )
        dim = 1 if backward else 0
        by_real = dot(rows, real_ref[mode], 1, dim)
        by_imag = dot(rows, imag_ref[mode], 1, dim)
        if backward:
            put(y_ref, first, by_real[:groups] + by_imag[groups:])
            put(y_ref, second, by_real[groups:] - by_imag[:groups])
        else:
            put(y_ref, first, by_real[:groups] - by_imag[groups:])
            put(y_ref, second, by_imag[:groups] + by_real[groups:])
    for source in range(groups):
        rows = take(y_ref, pl.ds(source * span, span)).astype(jnp.bfloat16)
        out_ref[source] = rows
    if backward:
        copy.wait()


def own_pipe(pipes):
    return lax.axis_index("len") * pipes + lax.axis_index("pipe")


def selection(inlet_ref, outlet_ref, pipes, groups, both):
    me = own_pipe(pipes)
    shape = (8, 2 * pipes * groups)
    lane = lax.broadcasted_iota(jnp.int32, shape, 1)
    row = lax.broadcasted_iota(jnp.int32, shape, 0)
    own = jnp.where(row == 0, inlet_ref[me], outlet_ref[me])
    first = jnp.full(shape, -1, jnp.int32)
    last = jnp.full(shape, -1, jnp.int32)
    for column in range(pipes):
        for group in range(groups):
            base = 2 * (column * groups + group)
            pipe = group * pipes + column
            here, there = lane == base, lane == base + 1
            if both:
                here = there = here | there
            first = jnp.where(here, inlet_ref[pipe], first)
            last = jnp.where(there, outlet_ref[pipe], last)
    picked = (first == own).astype(jnp.float32) + (last == own).astype(jnp.float32)
    return picked.astype(jnp.bfloat16)


def junction_sums(ends_ref, inlet_ref, outlet_ref, both):
    pipes, twice, channels = ends_ref.shape
    picked = selection(inlet_ref, outlet_ref, pipes, twice // 2, both)
    ends = ends_ref[...].reshape(pipes * twice, channels).astype(jnp.bfloat16)
    return dot(picked, ends)


def ends_kernel(r_ref, ends_ref):
    groups, rows = r_ref.shape[0], r_ref.shape[1]
    for group in range(groups):
        ends_ref[2 * group : 2 * group + 2, :] = r_ref[group, rows - 2 : rows, :].astype(
            jnp.float32
        )


def started(copies):
    for copy in copies:
        copy.start()
    return copies


def wait(copies):
    for copy in copies:
        copy.wait()


def brought(pairs, sems, base=0):
    return started(
        [
            pltpu.make_async_copy(source, target, sems.at[base + place])
            for place, (source, target) in enumerate(pairs)
        ]
    )


def layer_kernel(pipes, *refs):
    ends, refs = refs[:pipes], refs[pipes:]
    (inlet_ref, outlet_ref, junc_weight_ref, junc_bias_ref), refs = refs[:4], refs[4:]
    x_ref, cot_ref, f_ref, ft_ref, weight_ref, bias_ref, modes_ref = refs[:7]
    out_ref, total_ref, msg_ref, slope_ref, low_ref, high_ref, ends_ref = refs[7:]
    steps, all_rows, tile = f_ref.shape
    half = steps * tile
    channels = x_ref.shape[1]
    groups, rows = msg_ref.shape[0], msg_ref.shape[1]
    span = all_rows // groups
    column = lax.axis_index("pipe")
    for step in range(pipes):
        ends_ref[lax.bitwise_xor(column, step)] = ends[step][...]
    sums = junction_sums(ends_ref, inlet_ref, outlet_ref, False)
    act = dot(sums.astype(jnp.bfloat16), junc_weight_ref[...]) + junc_bias_ref[...]
    sigmoid_part = jax.nn.sigmoid(act)
    junc_rows = (act * sigmoid_part).astype(jnp.bfloat16).astype(jnp.float32)
    cond = COUPLING * (junc_rows[0:1] + junc_rows[1:2])
    slope_ref[...] = sigmoid_part * (1.0 + act * (1.0 - sigmoid_part))
    row = lax.broadcasted_iota(jnp.int32, (all_rows, channels), 0)
    doubled = jnp.where((row == 0) | (row == span // 2), 1.0, 2.0).astype(jnp.float32)
    signs = row_signs(all_rows, span, channels)
    modes = jnp.concatenate(
        [modes_ref[at, 0:span, :].astype(jnp.float32) for at in range(groups)], axis=0
    )
    modes = modes * doubled
    modes = (modes.astype(jnp.bfloat16), (modes * signs).astype(jnp.bfloat16))
    weight = weight_ref[...]
    bias = bias_ref[...]
    for step in range(steps):
        for side, acc_ref in enumerate((low_ref, high_ref)):
            at = pl.ds(side * half + step * tile, tile)
            pointwise = dot(x_ref[at, :], weight) + bias
            spectral = dot(ft_ref[pl.ds(step * tile, tile), :], modes[side])
            summed = pointwise + (spectral + cond).astype(jnp.bfloat16).astype(jnp.float32)
            square = summed * summed
            part = 0.5 + 0.5 * jnp.tanh(summed * (GELU_S + (GELU_S * GELU_C) * square))
            result = summed * part
            out_ref[at, :] = result.astype(jnp.bfloat16)
            slope = part + result * (1.0 - part) * (
                2.0 * GELU_S + (6.0 * GELU_S * GELU_C) * square
            )
            total = (cot_ref[at, :].astype(jnp.float32) * slope).astype(jnp.bfloat16)
            total_ref[at, :] = total
            term = dot(f_ref[step], total)
            if step == 0:
                acc_ref[...] = term
            else:
                acc_ref[...] += term
    acc = low_ref[...] + signs * high_ref[...]
    grad_cond = acc[0:1, :] * (1.0 / f_ref[0, 0:1, 0:1].astype(jnp.float32))
    upper = grad_cond.astype(jnp.bfloat16).astype(jnp.float32)
    extra = extra_rows(upper, grad_cond - upper, rows - span, channels)
    grad_spec = (acc * doubled).astype(jnp.bfloat16)
    for at in range(groups):
        msg_ref[at, 0:span, :] = grad_spec[at * span : (at + 1) * span]
        msg_ref[at, span:rows, :] = extra


def weight_grad_kernel(pipes, modes, per_copy, *refs):
    fields, grads, refs = refs[:pipes], refs[pipes : 2 * pipes], refs[2 * pipes :]
    (inlet_ref, outlet_ref, junc_weight_ref, slope_ref), refs = refs[:4], refs[4:]
    real_out, imag_out, rows_ref, x_ref, g_ref, real_ref, imag_ref, ends_ref, sems = refs
    groups, rows = fields[0].shape[0], fields[0].shape[1]
    span = 2 * modes
    for step in range(pipes):
        for source in range(groups):
            at = pl.ds((step * groups + source) * span, span)
            put(x_ref, at, fields[step][source, 0:span, :].astype(jnp.float32))
            put(g_ref, at, grads[step][source, 0:span, :].astype(jnp.float32))
    count = pipes * groups
    going = []
    for number in range(modes // per_copy):
        for mode in range(number * per_copy, (number + 1) * per_copy):
            first = pl.ds(mode, count, stride=span)
            second = pl.ds(modes + mode, count, stride=span)
            a, b = take(x_ref, first), take(x_ref, second)
            u, v = take(g_ref, first), take(g_ref, second)
            left = jnp.concatenate([a, b], axis=0).astype(jnp.bfloat16)
            right = jnp.concatenate([u, v], axis=0).astype(jnp.bfloat16)
            turned = jnp.concatenate([v, -u], axis=0).astype(jnp.bfloat16)
            real_ref[mode] = dot(left, right, 0, 0)
            imag_ref[mode] = dot(left, turned, 0, 0)
        at = pl.ds(number * per_copy, per_copy)
        going += started(
            [
                pltpu.make_async_copy(real_ref.at[at], real_out.at[at], sems.at[number, 0]),
                pltpu.make_async_copy(imag_ref.at[at], imag_out.at[at], sems.at[number, 1]),
            ]
        )
    column = lax.axis_index("pipe")
    for step in range(pipes):
        place = lax.bitwise_xor(column, step)
        for group in range(groups):
            parts = grads[step][group, rows - 2 : rows, :].astype(jnp.float32)
            ends_ref[place, 2 * group : 2 * group + 2, :] = parts
    junc_grad = COUPLING * junction_sums(ends_ref, inlet_ref, outlet_ref, True)
    act_grad = (junc_grad * slope_ref[...]).astype(jnp.bfloat16)
    sums_grad = dot(act_grad, junc_weight_ref[...], 1, 1)
    rows_ref[...] = sums_grad.astype(jnp.bfloat16).astype(jnp.float32)
    wait(going)


def input_grad_kernel(
    total_ref, ft_ref, weight_ref, rows_ref, modes_ref, out_ref, tiles_ref, sems
):
    groups, span, channels = modes_ref.shape
    steps, tile = tiles_ref.shape[0], tiles_ref.shape[2]
    half, all_rows = steps * tile, groups * span
    back = jnp.concatenate(
        [modes_ref[at, 0:span, :].astype(jnp.float32) for at in range(groups)], axis=0
    )
    signs = row_signs(all_rows, span, channels)
    back = (back.astype(jnp.bfloat16), (back * signs).astype(jnp.bfloat16))
    weight = weight_ref[...]
    row = lax.broadcasted_iota(jnp.int32, (tile, channels), 0)
    going = []
    for step in range(steps):
        for side in range(2):
            at = pl.ds(side * half + step * tile, tile)
            grad_cells = dot(ft_ref[pl.ds(step * tile, tile), :], back[side])
            if step == 0 and side == 0:
                grad_cells = grad_cells + jnp.where(row == 0, rows_ref[0:1, :], 0.0)
            if step == steps - 1 and side == 1:
                grad_cells = grad_cells + jnp.where(row == tile - 1, rows_ref[1:2, :], 0.0)
            spread = grad_cells.astype(jnp.bfloat16).astype(jnp.float32)
            local = dot(total_ref[at, :], weight, 1, 1)
            tiles_ref[step, side] = (local + spread).astype(jnp.bfloat16)
            going += started(
                [
                    pltpu.make_async_copy(
                        tiles_ref.at[step, side], out_ref.at[at], sems.at[step, side]
                    )
                ]
            )
    wait(going)


def rows_of(count, channels):
    return pltpu.VMEM((channels // LANES, count, LANES), jnp.float32)


def call(kernel, outs, specs, scratch=(), out_specs=None, name=None, limit=8, busy=1):
    return pl.pallas_call(
        kernel,
        out_shape=outs,
        in_specs=specs,
        out_specs=out_specs if out_specs is not None else [VMEM] * len(outs),
        scratch_shapes=list(scratch),
        compiler_params=pltpu.CompilerParams(vmem_limit_bytes=limit * MIB),
        cost_estimate=pl.CostEstimate(
            flops=busy * 1_000_000_000, bytes_accessed=busy * MIB, transcendentals=0
        ),
        name=name,
    )


def body(
    inputs,
    cotangent,
    point_weight,
    point_bias,
    spec_real,
    spec_imag,
    junc_weight,
    junc_bias,
    inlet_ids,
    outlet_ids,
):
    per_dev, cell_count, channels = inputs.shape
    assert per_dev == 1
    groups, pipes = lax.axis_size("len"), lax.axis_size("pipe")
    assert pipes == 4
    modes = spec_real.shape[0]
    span = 2 * modes
    all_rows = span * groups
    steps = cell_count // (2 * TILE)
    table = half_table(cell_count, modes * groups, groups)
    tiled = table.reshape(all_rows, steps, TILE).transpose(1, 0, 2)
    f_table = jnp.asarray(np.ascontiguousarray(tiled))
    ft_table = jnp.asarray(np.ascontiguousarray(table.T))
    field = inputs.reshape(cell_count, channels)
    cot = cotangent.reshape(cell_count, channels)
    bias_row = point_bias.reshape(1, channels)
    junc_bias_row = junc_bias.reshape(1, channels)
    shape = jax.ShapeDtypeStruct
    bf16, f32 = jnp.bfloat16, jnp.float32
    message = shape((groups, span + 2, channels), bf16)
    chunks = shape((groups, span, channels), bf16)
    dma = pltpu.SemaphoreType.DMA

    def exchange(value):
        return lax.all_to_all(value, "len", split_axis=0, concat_axis=0, tiled=True)

    def swap(value, step):
        return lax.ppermute(value, "pipe", [(i, i ^ step) for i in range(pipes)])

    def gather(own):
        across = swap(own, 2)
        return [own, swap(own, 1), across, swap(across, 1)]

    def mix(backward, value, *early):
        return call(
            functools.partial(mix_kernel, backward),
            [chunks, early[0]] if backward else [chunks],
            [VMEM] * (4 if backward else 3),
            ([dma] if backward else []) + [rows_of(all_rows, channels)] * 2,
            out_specs=[VMEM, HBM] if backward else [VMEM],
            name="mix_grad" if backward else "mix",
            busy=12,
        )(value, spec_real, spec_imag, *early)

    (sent,) = call(spectrum_kernel, [message], [VMEM] * 2, name="spectrum", busy=12)(
        field, f_table
    )
    received = exchange(sent)
    (ends,) = call(
        ends_kernel, [shape((2 * groups, channels), f32)], [VMEM], name="pipe_ends"
    )(received)
    ends = [ends] + [swap(ends, step) for step in range(1, pipes)]
    (mixed,) = mix(False, received)
    mixed, *ends = lax.optimization_barrier((mixed, *ends))
    returned = exchange(mixed)
    spectra = received
    ends_buf = pltpu.VMEM((pipes, 2 * groups, channels), f32)
    early, total, sent, slope = call(
        functools.partial(layer_kernel, pipes),
        [shape(field.shape, bf16)] * 2 + [message, shape((8, channels), f32)],
        [VMEM] * pipes + [SMEM] * 2 + [VMEM] * 9,
        [pltpu.VMEM((all_rows, channels), f32)] * 2 + [ends_buf],
        name="layer",
        busy=12,
    )(
        *ends,
        inlet_ids,
        outlet_ids,
        junc_weight,
        junc_bias_row,
        field,
        cot,
        f_table,
        ft_table,
        point_weight,
        bias_row,
        returned,
    )
    received = exchange(sent)
    received, spectra = lax.optimization_barrier((received, spectra))
    fields = gather(spectra)
    grads = gather(received)
    mixed, outputs = mix(True, received, early)
    returned = exchange(mixed)
    big = shape((modes, channels, channels), f32)
    per_copy = math.gcd(modes, 2)
    grad_real, grad_imag, rows = call(
        functools.partial(weight_grad_kernel, pipes, modes, per_copy),
        [big, big, shape((8, channels), f32)],
        [VMEM] * (2 * pipes) + [SMEM] * 2 + [VMEM] * 2,
        [rows_of(pipes * all_rows, channels)] * 2
        + [pltpu.VMEM(big.shape, f32)] * 2
        + [ends_buf, dma((modes // per_copy, 2))],
        out_specs=[HBM, HBM, VMEM],
        name="weight_grad",
        limit=16,
    )(*fields, *grads, inlet_ids, outlet_ids, junc_weight, slope)
    (grad_inputs,) = call(
        input_grad_kernel,
        [shape(field.shape, bf16)],
        [VMEM] * 5,
        [pltpu.VMEM((steps, 2, TILE, channels), bf16), dma((steps, 2))],
        out_specs=[HBM],
        name="input_grad",
    )(total, ft_table, point_weight, rows, returned)
    return (
        outputs.reshape(inputs.shape),
        grad_inputs.reshape(inputs.shape),
        grad_real,
        grad_imag,
    )


def solution(mesh):
    placed = (
        P(("len", "pipe"), None, None),
        P(("len", "pipe"), None, None),
        P(),
        P(),
        P("len", None, None),
        P("len", None, None),
        P(),
        P(),
        P(),
        P(),
    )
    return jax.shard_map(
        body,
        mesh=mesh,
        in_specs=placed,
        out_specs=(
            P(("len", "pipe"), None, None),
            P(("len", "pipe"), None, None),
            P("len", None, None),
            P("len", None, None),
        ),
        check_vma=False,
    )
```

```python
import functools
import math

import jax
import jax.numpy as jnp
import ml_dtypes
import numpy as np
from jax import lax
from jax.experimental import pallas as pl
from jax.experimental.pallas import tpu as pltpu
from jax.sharding import PartitionSpec as P

COUPLING = 0.125
TILE = 256
LANES = 128
GELU_S = math.sqrt(2.0 / math.pi)
GELU_C = 0.044715
VMEM = pl.BlockSpec(memory_space=pltpu.VMEM)
HBM = pl.BlockSpec(memory_space=pltpu.HBM)
MIB = 1024 * 1024


def half_table(cell_count, mode_count, groups):
    half = cell_count // 2
    product_index = np.arange(mode_count)[:, None] * np.arange(half)[None, :] % cell_count
    angles = product_index.astype(np.float32) * np.float32(2.0 * math.pi / cell_count)
    norm_scale = np.float32(1.0 / math.sqrt(cell_count))
    cosine = (np.cos(angles) * norm_scale).reshape(groups, -1, half)
    sine = (np.sin(angles) * norm_scale).reshape(groups, -1, half)
    table = np.concatenate([cosine, -sine], axis=1).reshape(2 * mode_count, half)
    return table.astype(ml_dtypes.bfloat16)


def row_signs(all_rows, span, channels):
    row = lax.broadcasted_iota(jnp.int32, (all_rows, channels), 0)
    per_owner = span // 2
    mode = (row // span) * per_owner + lax.rem(row, per_owner)
    return jnp.where(lax.rem(mode, 2) == 0, 1.0, -1.0).astype(jnp.float32)


def dot(left, right, left_dim=1, right_dim=0):
    return lax.dot_general(
        left,
        right,
        (((left_dim,), (right_dim,)), ((), ())),
        preferred_element_type=jnp.float32,
    )


def put(ref, at, value):
    for lane in range(ref.shape[0]):
        ref[lane, at, :] = value[:, lane * LANES : (lane + 1) * LANES]


def take(ref, at):
    return jnp.concatenate([ref[lane, at, :] for lane in range(ref.shape[0])], axis=1)


def spectrum_kernel(x_ref, f_ref, msg_ref):
    groups, rows = msg_ref.shape[0], msg_ref.shape[1]
    steps, all_rows, tile = f_ref.shape
    cells, channels = x_ref.shape
    half = cells // 2
    span = all_rows // groups
    sums = []
    for base in (0, half):
        total = None
        for step in range(steps):
            at = base + step * tile
            part = dot(f_ref[step], x_ref[at : at + tile, :])
            total = part if total is None else total + part
        sums.append(total)
    spectra = (sums[0] + row_signs(all_rows, span, channels) * sums[1]).astype(jnp.bfloat16)
    ends = extra_rows(x_ref[0:1, :], x_ref[cells - 1 : cells, :], rows - span, channels)
    for at in range(groups):
        msg_ref[at, 0:span, :] = spectra[at * span : (at + 1) * span]
        msg_ref[at, span:rows, :] = ends


def extra_rows(first, second, count, channels):
    parts = [first.astype(jnp.float32), second.astype(jnp.float32)]
    if count > 2:
        parts.append(jnp.zeros((count - 2, channels), jnp.float32))
    return jnp.concatenate(parts, axis=0).astype(jnp.bfloat16)


def mix_kernel(backward, r_ref, real_ref, imag_ref, *refs):
    x_ref, y_ref = refs[-2:]
    groups, modes = r_ref.shape[0], real_ref.shape[0]
    span = 2 * modes
    if backward:
        early_ref, out_ref, copied_ref, sem = refs[:4]
        copy = pltpu.make_async_copy(early_ref, copied_ref, sem)
        copy.start()
    else:
        out_ref = refs[0]
    for source in range(groups):
        put(x_ref, pl.ds(source * span, span), r_ref[source, 0:span, :].astype(jnp.float32))
    for mode in range(modes):
        first = pl.ds(mode, groups, stride=span)
        second = pl.ds(modes + mode, groups, stride=span)
        rows = jnp.concatenate([take(x_ref, first), take(x_ref, second)], axis=0).astype(
            jnp.bfloat16
        )
        dim = 1 if backward else 0
        by_real = dot(rows, real_ref[mode], 1, dim)
        by_imag = dot(rows, imag_ref[mode], 1, dim)
        if backward:
            put(y_ref, first, by_real[:groups] + by_imag[groups:])
            put(y_ref, second, by_real[groups:] - by_imag[:groups])
        else:
            put(y_ref, first, by_real[:groups] - by_imag[groups:])
            put(y_ref, second, by_imag[:groups] + by_real[groups:])
    for source in range(groups):
        rows = take(y_ref, pl.ds(source * span, span)).astype(jnp.bfloat16)
        out_ref[source] = rows
    if backward:
        copy.wait()


def own_pipe(pipes):
    return lax.axis_index("len") * pipes + lax.axis_index("pipe")


def selection(inlet_ref, outlet_ref, pipes):
    count = inlet_ref.shape[1]
    lane = lax.broadcasted_iota(jnp.int32, (8, count), 1)
    row = lax.broadcasted_iota(jnp.int32, (8, count), 0)
    inlets = jnp.broadcast_to(inlet_ref[...], (8, count)).astype(jnp.float32)
    outlets = jnp.broadcast_to(outlet_ref[...], (8, count)).astype(jnp.float32)
    mine = jnp.where(row == 0, inlets, outlets)
    own = jnp.sum(jnp.where(lane == own_pipe(pipes), mine, 0.0), axis=1, keepdims=True)
    return (inlets == own).astype(jnp.bfloat16), (outlets == own).astype(jnp.bfloat16)


def whole(ref):
    return take(ref, pl.ds(0, ref.shape[1])).astype(jnp.bfloat16)


def ends_kernel(r_ref, ends_ref):
    groups, rows = r_ref.shape[0], r_ref.shape[1]
    for group in range(groups):
        ends = r_ref[group, rows - 2 : rows, :].astype(jnp.float32)
        ends_ref[group : group + 1, :] = ends[0:1]
        ends_ref[groups + group : groups + group + 1, :] = ends[1:2]


def started(copies):
    for copy in copies:
        copy.start()
    return copies


def wait(copies):
    for copy in copies:
        copy.wait()


def brought(pairs, sems, base=0):
    return started(
        [
            pltpu.make_async_copy(source, target, sems.at[base + place])
            for place, (source, target) in enumerate(pairs)
        ]
    )


def layer_kernel(pipes, *refs):
    ends, refs = refs[:pipes], refs[pipes:]
    (inlet_ref, outlet_ref, junc_weight_ref, junc_bias_ref), refs = refs[:4], refs[4:]
    x_ref, cot_ref, f_ref, ft_ref, weight_ref, bias_ref, modes_ref = refs[:7]
    out_ref, total_ref, msg_ref, slope_ref, low_ref, high_ref, first_ref, last_ref = refs[7:]
    steps, all_rows, tile = f_ref.shape
    half = steps * tile
    channels = x_ref.shape[1]
    groups, rows = msg_ref.shape[0], msg_ref.shape[1]
    span = all_rows // groups
    column = lax.axis_index("pipe")
    for step in range(pipes):
        at = pl.ds(lax.bitwise_xor(column, step), groups, stride=pipes)
        put(first_ref, at, ends[step][0:groups, :])
        put(last_ref, at, ends[step][groups : 2 * groups, :])
    picked_in, picked_out = selection(inlet_ref, outlet_ref, pipes)
    sums = dot(picked_in, whole(first_ref)) + dot(picked_out, whole(last_ref))
    act = dot(sums.astype(jnp.bfloat16), junc_weight_ref[...]) + junc_bias_ref[...]
    sigmoid_part = jax.nn.sigmoid(act)
    junc_rows = (act * sigmoid_part).astype(jnp.bfloat16).astype(jnp.float32)
    cond = COUPLING * (junc_rows[0:1] + junc_rows[1:2])
    slope_ref[...] = sigmoid_part * (1.0 + act * (1.0 - sigmoid_part))
    row = lax.broadcasted_iota(jnp.int32, (all_rows, channels), 0)
    doubled = jnp.where((row == 0) | (row == span // 2), 1.0, 2.0).astype(jnp.float32)
    signs = row_signs(all_rows, span, channels)
    modes = jnp.concatenate(
        [modes_ref[at, 0:span, :].astype(jnp.float32) for at in range(groups)], axis=0
    )
    modes = modes * doubled
    modes = (modes.astype(jnp.bfloat16), (modes * signs).astype(jnp.bfloat16))
    weight = weight_ref[...]
    bias = bias_ref[...]
    for step in range(steps):
        for side, acc_ref in enumerate((low_ref, high_ref)):
            at = pl.ds(side * half + step * tile, tile)
            pointwise = dot(x_ref[at, :], weight) + bias
            spectral = dot(ft_ref[pl.ds(step * tile, tile), :], modes[side])
            summed = pointwise + (spectral + cond).astype(jnp.bfloat16).astype(jnp.float32)
            square = summed * summed
            part = 0.5 + 0.5 * jnp.tanh(summed * (GELU_S + (GELU_S * GELU_C) * square))
            result = summed * part
            out_ref[at, :] = result.astype(jnp.bfloat16)
            slope = part + result * (1.0 - part) * (
                2.0 * GELU_S + (6.0 * GELU_S * GELU_C) * square
            )
            total = (cot_ref[at, :].astype(jnp.float32) * slope).astype(jnp.bfloat16)
            total_ref[at, :] = total
            term = dot(f_ref[step], total)
            if step == 0:
                acc_ref[...] = term
            else:
                acc_ref[...] += term
    acc = low_ref[...] + signs * high_ref[...]
    grad_cond = acc[0:1, :] * (1.0 / f_ref[0, 0:1, 0:1].astype(jnp.float32))
    upper = grad_cond.astype(jnp.bfloat16).astype(jnp.float32)
    extra = extra_rows(upper, grad_cond - upper, rows - span, channels)
    grad_spec = (acc * doubled).astype(jnp.bfloat16)
    for at in range(groups):
        msg_ref[at, 0:span, :] = grad_spec[at * span : (at + 1) * span]
        msg_ref[at, span:rows, :] = extra


def weight_grad_kernel(pipes, modes, per_copy, *refs):
    fields, grads, refs = refs[:pipes], refs[pipes : 2 * pipes], refs[2 * pipes :]
    (inlet_ref, outlet_ref, junc_weight_ref, slope_ref), refs = refs[:4], refs[4:]
    real_out, imag_out, rows_ref, x_ref, g_ref, real_ref, imag_ref = refs[:7]
    first_ref, last_ref, upper_ref, lower_ref, sems = refs[7:]
    groups, rows = fields[0].shape[0], fields[0].shape[1]
    span = 2 * modes
    for step in range(pipes):
        for source in range(groups):
            at = pl.ds((step * groups + source) * span, span)
            put(x_ref, at, fields[step][source, 0:span, :].astype(jnp.float32))
            put(g_ref, at, grads[step][source, 0:span, :].astype(jnp.float32))
    count = pipes * groups
    going = []
    for number in range(modes // per_copy):
        for mode in range(number * per_copy, (number + 1) * per_copy):
            first = pl.ds(mode, count, stride=span)
            second = pl.ds(modes + mode, count, stride=span)
            a, b = take(x_ref, first), take(x_ref, second)
            u, v = take(g_ref, first), take(g_ref, second)
            left = jnp.concatenate([a, b], axis=0).astype(jnp.bfloat16)
            right = jnp.concatenate([u, v], axis=0).astype(jnp.bfloat16)
            turned = jnp.concatenate([v, -u], axis=0).astype(jnp.bfloat16)
            real_ref[mode] = dot(left, right, 0, 0)
            imag_ref[mode] = dot(left, turned, 0, 0)
        at = pl.ds(number * per_copy, per_copy)
        going += started(
            [
                pltpu.make_async_copy(real_ref.at[at], real_out.at[at], sems.at[number, 0]),
                pltpu.make_async_copy(imag_ref.at[at], imag_out.at[at], sems.at[number, 1]),
            ]
        )
    column = lax.axis_index("pipe")
    for step in range(pipes):
        for group in range(groups):
            parts = grads[step][group, rows - 2 : rows, :].astype(jnp.float32)
            upper_ref[group : group + 1, :] = parts[0:1]
            lower_ref[group : group + 1, :] = parts[1:2]
        at = pl.ds(lax.bitwise_xor(column, step), groups, stride=pipes)
        put(first_ref, at, upper_ref[...])
        put(last_ref, at, lower_ref[...])
    picked_in, picked_out = selection(inlet_ref, outlet_ref, pipes)
    picked = picked_in + picked_out
    junc_grad = COUPLING * (dot(picked, whole(first_ref)) + dot(picked, whole(last_ref)))
    act_grad = (junc_grad * slope_ref[...]).astype(jnp.bfloat16)
    sums_grad = dot(act_grad, junc_weight_ref[...], 1, 1)
    rows_ref[...] = sums_grad.astype(jnp.bfloat16).astype(jnp.float32)
    wait(going)


def input_grad_kernel(
    total_ref, ft_ref, weight_ref, rows_ref, modes_ref, out_ref, tiles_ref, sems
):
    groups, span, channels = modes_ref.shape
    steps, tile = tiles_ref.shape[0], tiles_ref.shape[2]
    half, all_rows = steps * tile, groups * span
    back = jnp.concatenate(
        [modes_ref[at, 0:span, :].astype(jnp.float32) for at in range(groups)], axis=0
    )
    signs = row_signs(all_rows, span, channels)
    back = (back.astype(jnp.bfloat16), (back * signs).astype(jnp.bfloat16))
    weight = weight_ref[...]
    row = lax.broadcasted_iota(jnp.int32, (tile, channels), 0)
    going = []
    for step in range(steps):
        for side in range(2):
            at = pl.ds(side * half + step * tile, tile)
            grad_cells = dot(ft_ref[pl.ds(step * tile, tile), :], back[side])
            if step == 0 and side == 0:
                grad_cells = grad_cells + jnp.where(row == 0, rows_ref[0:1, :], 0.0)
            if step == steps - 1 and side == 1:
                grad_cells = grad_cells + jnp.where(row == tile - 1, rows_ref[1:2, :], 0.0)
            spread = grad_cells.astype(jnp.bfloat16).astype(jnp.float32)
            local = dot(total_ref[at, :], weight, 1, 1)
            tiles_ref[step, side] = (local + spread).astype(jnp.bfloat16)
            going += started(
                [
                    pltpu.make_async_copy(
                        tiles_ref.at[step, side], out_ref.at[at], sems.at[step, side]
                    )
                ]
            )
    wait(going)


def rows_of(count, channels):
    return pltpu.VMEM((channels // LANES, count, LANES), jnp.float32)


def call(kernel, outs, specs, scratch=(), out_specs=None, name=None, limit=8, busy=0):
    return pl.pallas_call(
        kernel,
        out_shape=outs,
        in_specs=specs,
        out_specs=out_specs if out_specs is not None else [VMEM] * len(outs),
        scratch_shapes=list(scratch),
        compiler_params=pltpu.CompilerParams(vmem_limit_bytes=limit * MIB),
        cost_estimate=pl.CostEstimate(
            flops=busy * 1_000_000_000, bytes_accessed=busy * MIB, transcendentals=0
        )
        if busy
        else None,
        name=name,
    )


def body(
    inputs,
    cotangent,
    point_weight,
    point_bias,
    spec_real,
    spec_imag,
    junc_weight,
    junc_bias,
    inlet_ids,
    outlet_ids,
):
    per_dev, cell_count, channels = inputs.shape
    assert per_dev == 1
    groups, pipes = lax.axis_size("len"), lax.axis_size("pipe")
    assert pipes == 4
    modes = spec_real.shape[0]
    span = 2 * modes
    all_rows = span * groups
    steps = cell_count // (2 * TILE)
    table = half_table(cell_count, modes * groups, groups)
    tiled = table.reshape(all_rows, steps, TILE).transpose(1, 0, 2)
    f_table = jnp.asarray(np.ascontiguousarray(tiled))
    ft_table = jnp.asarray(np.ascontiguousarray(table.T))
    field = inputs.reshape(cell_count, channels)
    cot = cotangent.reshape(cell_count, channels)
    bias_row = point_bias.reshape(1, channels)
    junc_bias_row = junc_bias.reshape(1, channels)
    shape = jax.ShapeDtypeStruct
    bf16, f32 = jnp.bfloat16, jnp.float32
    message = shape((groups, span + 2, channels), bf16)
    chunks = shape((groups, span, channels), bf16)
    dma = pltpu.SemaphoreType.DMA

    def exchange(value):
        return lax.all_to_all(value, "len", split_axis=0, concat_axis=0, tiled=True)

    def swap(value, step):
        return lax.ppermute(value, "pipe", [(i, i ^ step) for i in range(pipes)])

    def gather(own, behind):
        across = swap(own, 2)
        tied, tied_across, _ = lax.optimization_barrier((own, across, behind))
        return [own, swap(tied, 1), across, swap(tied_across, 1)]

    def mix(backward, value, *early):
        return call(
            functools.partial(mix_kernel, backward),
            [chunks, early[0]] if backward else [chunks],
            [VMEM] * (4 if backward else 3),
            ([dma] if backward else []) + [rows_of(all_rows, channels)] * 2,
            out_specs=[VMEM, HBM] if backward else [VMEM],
            name="mix_grad" if backward else "mix",
            busy=12,
        )(value, spec_real, spec_imag, *early)

    (sent,) = call(spectrum_kernel, [message], [VMEM] * 2, name="spectrum", busy=12)(
        field, f_table
    )
    received = exchange(sent)
    (ends,) = call(
        ends_kernel, [shape((2 * groups, channels), f32)], [VMEM], name="pipe_ends"
    )(received)
    ends = [ends] + [swap(ends, step) for step in range(1, pipes)]
    (mixed,) = mix(False, received)
    mixed, *ends = lax.optimization_barrier((mixed, *ends))
    returned = exchange(mixed)
    spectra = received
    pipe_rows = [rows_of(pipes * groups, channels)] * 2
    inlet_row = inlet_ids.reshape(1, -1)
    outlet_row = outlet_ids.reshape(1, -1)
    early, total, sent, slope = call(
        functools.partial(layer_kernel, pipes),
        [shape(field.shape, bf16)] * 2 + [message, shape((8, channels), f32)],
        [VMEM] * (pipes + 11),
        [pltpu.VMEM((all_rows, channels), f32)] * 2 + pipe_rows,
        name="layer",
        busy=12,
    )(
        *ends,
        inlet_row,
        outlet_row,
        junc_weight,
        junc_bias_row,
        field,
        cot,
        f_table,
        ft_table,
        point_weight,
        bias_row,
        returned,
    )
    received = exchange(sent)
    received, spectra = lax.optimization_barrier((received, spectra))
    mixed, outputs = mix(True, received, early)
    fields = gather(spectra, mixed)
    grads = gather(received, mixed)
    returned = exchange(mixed)
    big = shape((modes, channels, channels), f32)
    per_copy = math.gcd(modes, 2)
    grad_real, grad_imag, rows = call(
        functools.partial(weight_grad_kernel, pipes, modes, per_copy),
        [big, big, shape((8, channels), f32)],
        [VMEM] * (2 * pipes + 4),
        [rows_of(pipes * all_rows, channels)] * 2
        + [pltpu.VMEM(big.shape, f32)] * 2
        + pipe_rows
        + [pltpu.VMEM((groups, channels), f32)] * 2
        + [dma((modes // per_copy, 2))],
        out_specs=[HBM, HBM, VMEM],
        name="weight_grad",
        limit=16,
    )(*fields, *grads, inlet_row, outlet_row, junc_weight, slope)
    (grad_inputs,) = call(
        input_grad_kernel,
        [shape(field.shape, bf16)],
        [VMEM] * 5,
        [pltpu.VMEM((steps, 2, TILE, channels), bf16), dma((steps, 2))],
        out_specs=[HBM],
        name="input_grad",
    )(total, ft_table, point_weight, rows, returned)
    return (
        outputs.reshape(inputs.shape),
        grad_inputs.reshape(inputs.shape),
        grad_real,
        grad_imag,
    )


def solution(mesh):
    placed = (
        P(("len", "pipe"), None, None),
        P(("len", "pipe"), None, None),
        P(),
        P(),
        P("len", None, None),
        P("len", None, None),
        P(),
        P(),
        P(),
        P(),
    )
    return jax.shard_map(
        body,
        mesh=mesh,
        in_specs=placed,
        out_specs=(
            P(("len", "pipe"), None, None),
            P(("len", "pipe"), None, None),
            P("len", None, None),
            P("len", None, None),
        ),
        check_vma=False,
    )
```

```python
import functools
import math

import jax
import jax.numpy as jnp
import ml_dtypes
import numpy as np
from jax import lax
from jax.experimental import pallas as pl
from jax.experimental.pallas import tpu as pltpu
from jax.sharding import PartitionSpec as P

COUPLING = 0.125
TILE = 256
LANES = 128
GELU_S = math.sqrt(2.0 / math.pi)
GELU_C = 0.044715
VMEM = pl.BlockSpec(memory_space=pltpu.VMEM)
HBM = pl.BlockSpec(memory_space=pltpu.HBM)
MIB = 1024 * 1024


def half_table(cell_count, mode_count, groups):
    half = cell_count // 2
    product_index = np.arange(mode_count)[:, None] * np.arange(half)[None, :] % cell_count
    angles = product_index.astype(np.float32) * np.float32(2.0 * math.pi / cell_count)
    norm_scale = np.float32(1.0 / math.sqrt(cell_count))
    cosine = (np.cos(angles) * norm_scale).reshape(groups, -1, half)
    sine = (np.sin(angles) * norm_scale).reshape(groups, -1, half)
    table = np.concatenate([cosine, -sine], axis=1).reshape(2 * mode_count, half)
    return table.astype(ml_dtypes.bfloat16)


def factors_kernel(span, signs_ref, doubled_ref):
    row = lax.broadcasted_iota(jnp.int32, signs_ref.shape, 0)
    per_owner = span // 2
    mode = (row // span) * per_owner + lax.rem(row, per_owner)
    signs_ref[...] = jnp.where(lax.rem(mode, 2) == 0, 1.0, -1.0).astype(jnp.float32)
    doubled_ref[...] = jnp.where(mode == 0, 1.0, 2.0).astype(jnp.float32)


def dot(left, right, left_dim=1, right_dim=0):
    return lax.dot_general(
        left,
        right,
        (((left_dim,), (right_dim,)), ((), ())),
        preferred_element_type=jnp.float32,
    )


def put(ref, at, value):
    for lane in range(ref.shape[0]):
        ref[lane, at, :] = value[:, lane * LANES : (lane + 1) * LANES]


def take(ref, at):
    return jnp.concatenate([ref[lane, at, :] for lane in range(ref.shape[0])], axis=1)


def spectrum_kernel(x_ref, f_ref, signs_ref, msg_ref):
    groups, rows = msg_ref.shape[0], msg_ref.shape[1]
    steps, all_rows, tile = f_ref.shape
    cells, channels = x_ref.shape
    half = cells // 2
    span = all_rows // groups
    sums = []
    for base in (0, half):
        total = None
        for step in range(steps):
            at = base + step * tile
            part = dot(f_ref[step], x_ref[at : at + tile, :])
            total = part if total is None else total + part
        sums.append(total)
    spectra = (sums[0] + signs_ref[...] * sums[1]).astype(jnp.bfloat16)
    ends = extra_rows(x_ref[0:1, :], x_ref[cells - 1 : cells, :], rows - span, channels)
    for at in range(groups):
        msg_ref[at, 0:span, :] = spectra[at * span : (at + 1) * span]
        msg_ref[at, span:rows, :] = ends


def extra_rows(first, second, count, channels):
    parts = [first.astype(jnp.float32), second.astype(jnp.float32)]
    if count > 2:
        parts.append(jnp.zeros((count - 2, channels), jnp.float32))
    return jnp.concatenate(parts, axis=0).astype(jnp.bfloat16)


def mix_kernel(backward, r_ref, real_ref, imag_ref, *refs):
    x_ref, y_ref = refs[-2:]
    groups, modes = r_ref.shape[0], real_ref.shape[0]
    span = 2 * modes
    if backward:
        early_ref, out_ref, copied_ref, sem = refs[:4]
        copy = pltpu.make_async_copy(early_ref, copied_ref, sem)
        copy.start()
    else:
        out_ref = refs[0]
    for source in range(groups):
        put(x_ref, pl.ds(source * span, span), r_ref[source, 0:span, :].astype(jnp.float32))
    for mode in range(modes):
        first = pl.ds(mode, groups, stride=span)
        second = pl.ds(modes + mode, groups, stride=span)
        rows = jnp.concatenate([take(x_ref, first), take(x_ref, second)], axis=0).astype(
            jnp.bfloat16
        )
        dim = 1 if backward else 0
        by_real = dot(rows, real_ref[mode], 1, dim)
        by_imag = dot(rows, imag_ref[mode], 1, dim)
        if backward:
            put(y_ref, first, by_real[:groups] + by_imag[groups:])
            put(y_ref, second, by_real[groups:] - by_imag[:groups])
        else:
            put(y_ref, first, by_real[:groups] - by_imag[groups:])
            put(y_ref, second, by_imag[:groups] + by_real[groups:])
    for source in range(groups):
        rows = take(y_ref, pl.ds(source * span, span)).astype(jnp.bfloat16)
        out_ref[source] = rows
    if backward:
        copy.wait()


def own_pipe(pipes):
    return lax.axis_index("len") * pipes + lax.axis_index("pipe")


def selection(inlet_ref, outlet_ref, pipes):
    count = inlet_ref.shape[1]
    lane = lax.broadcasted_iota(jnp.int32, (8, count), 1)
    row = lax.broadcasted_iota(jnp.int32, (8, count), 0)
    inlets = jnp.broadcast_to(inlet_ref[...], (8, count)).astype(jnp.float32)
    outlets = jnp.broadcast_to(outlet_ref[...], (8, count)).astype(jnp.float32)
    mine = jnp.where(row == 0, inlets, outlets)
    own = jnp.sum(jnp.where(lane == own_pipe(pipes), mine, 0.0), axis=1, keepdims=True)
    return (inlets == own).astype(jnp.bfloat16), (outlets == own).astype(jnp.bfloat16)


def whole(ref):
    return take(ref, pl.ds(0, ref.shape[1])).astype(jnp.bfloat16)


def ends_kernel(r_ref, ends_ref):
    groups, rows = r_ref.shape[0], r_ref.shape[1]
    for group in range(groups):
        ends = r_ref[group, rows - 2 : rows, :].astype(jnp.float32)
        ends_ref[group : group + 1, :] = ends[0:1]
        ends_ref[groups + group : groups + group + 1, :] = ends[1:2]


def started(copies):
    for copy in copies:
        copy.start()
    return copies


def wait(copies):
    for copy in copies:
        copy.wait()


def brought(pairs, sems, base=0):
    return started(
        [
            pltpu.make_async_copy(source, target, sems.at[base + place])
            for place, (source, target) in enumerate(pairs)
        ]
    )


def layer_kernel(pipes, *refs):
    ends, refs = refs[:pipes], refs[pipes:]
    (inlet_ref, outlet_ref, junc_weight_ref, junc_bias_ref), refs = refs[:4], refs[4:]
    x_ref, cot_ref, f_ref, ft_ref, weight_ref, bias_ref, modes_ref = refs[:7]
    (signs_ref, doubled_ref), refs = refs[7:9], refs[9:]
    out_ref, total_ref, msg_ref, slope_ref, low_ref, high_ref, first_ref, last_ref = refs
    steps, all_rows, tile = f_ref.shape
    half = steps * tile
    channels = x_ref.shape[1]
    groups, rows = msg_ref.shape[0], msg_ref.shape[1]
    span = all_rows // groups
    column = lax.axis_index("pipe")
    for step in range(pipes):
        at = pl.ds(lax.bitwise_xor(column, step), groups, stride=pipes)
        put(first_ref, at, ends[step][0:groups, :])
        put(last_ref, at, ends[step][groups : 2 * groups, :])
    picked_in, picked_out = selection(inlet_ref, outlet_ref, pipes)
    sums = dot(picked_in, whole(first_ref)) + dot(picked_out, whole(last_ref))
    act = dot(sums.astype(jnp.bfloat16), junc_weight_ref[...]) + junc_bias_ref[...]
    sigmoid_part = jax.nn.sigmoid(act)
    junc_rows = (act * sigmoid_part).astype(jnp.bfloat16).astype(jnp.float32)
    cond = COUPLING * (junc_rows[0:1] + junc_rows[1:2])
    slope_ref[...] = sigmoid_part * (1.0 + act * (1.0 - sigmoid_part))
    doubled = doubled_ref[...]
    signs = signs_ref[...]
    modes = jnp.concatenate(
        [modes_ref[at, 0:span, :].astype(jnp.float32) for at in range(groups)], axis=0
    )
    modes = modes * doubled
    modes = (modes.astype(jnp.bfloat16), (modes * signs).astype(jnp.bfloat16))
    weight = weight_ref[...]
    bias = bias_ref[...]
    for step in range(steps):
        for side, acc_ref in enumerate((low_ref, high_ref)):
            at = pl.ds(side * half + step * tile, tile)
            pointwise = dot(x_ref[at, :], weight) + bias
            spectral = dot(ft_ref[pl.ds(step * tile, tile), :], modes[side])
            summed = pointwise + (spectral + cond).astype(jnp.bfloat16).astype(jnp.float32)
            square = summed * summed
            part = 0.5 + 0.5 * jnp.tanh(summed * (GELU_S + (GELU_S * GELU_C) * square))
            result = summed * part
            out_ref[at, :] = result.astype(jnp.bfloat16)
            slope = part + result * (1.0 - part) * (
                2.0 * GELU_S + (6.0 * GELU_S * GELU_C) * square
            )
            total = (cot_ref[at, :].astype(jnp.float32) * slope).astype(jnp.bfloat16)
            total_ref[at, :] = total
            term = dot(f_ref[step], total)
            if step == 0:
                acc_ref[...] = term
            else:
                acc_ref[...] += term
    acc = low_ref[...] + signs * high_ref[...]
    grad_cond = acc[0:1, :] * (1.0 / f_ref[0, 0:1, 0:1].astype(jnp.float32))
    upper = grad_cond.astype(jnp.bfloat16).astype(jnp.float32)
    extra = extra_rows(upper, grad_cond - upper, rows - span, channels)
    grad_spec = (acc * doubled).astype(jnp.bfloat16)
    for at in range(groups):
        msg_ref[at, 0:span, :] = grad_spec[at * span : (at + 1) * span]
        msg_ref[at, span:rows, :] = extra


def weight_grad_kernel(pipes, modes, per_copy, *refs):
    both, refs = refs[:pipes], refs[pipes:]
    (inlet_ref, outlet_ref, junc_weight_ref, slope_ref), refs = refs[:4], refs[4:]
    real_out, imag_out, rows_ref, x_ref, g_ref, real_ref, imag_ref = refs[:7]
    first_ref, last_ref, upper_ref, lower_ref, sems = refs[7:]
    groups, rows = both[0].shape[0] // 2, both[0].shape[1]
    span = 2 * modes
    for step in range(pipes):
        for source in range(groups):
            at = pl.ds((step * groups + source) * span, span)
            put(x_ref, at, both[step][source, 0:span, :].astype(jnp.float32))
            put(g_ref, at, both[step][groups + source, 0:span, :].astype(jnp.float32))
    count = pipes * groups
    going = []
    for number in range(modes // per_copy):
        for mode in range(number * per_copy, (number + 1) * per_copy):
            first = pl.ds(mode, count, stride=span)
            second = pl.ds(modes + mode, count, stride=span)
            a, b = take(x_ref, first), take(x_ref, second)
            u, v = take(g_ref, first), take(g_ref, second)
            left = jnp.concatenate([a, b], axis=0).astype(jnp.bfloat16)
            right = jnp.concatenate([u, v], axis=0).astype(jnp.bfloat16)
            turned = jnp.concatenate([v, -u], axis=0).astype(jnp.bfloat16)
            real_ref[mode] = dot(left, right, 0, 0)
            imag_ref[mode] = dot(left, turned, 0, 0)
        at = pl.ds(number * per_copy, per_copy)
        going += started(
            [
                pltpu.make_async_copy(real_ref.at[at], real_out.at[at], sems.at[number, 0]),
                pltpu.make_async_copy(imag_ref.at[at], imag_out.at[at], sems.at[number, 1]),
            ]
        )
    column = lax.axis_index("pipe")
    for step in range(pipes):
        for group in range(groups):
            parts = both[step][groups + group, rows - 2 : rows, :].astype(jnp.float32)
            upper_ref[group : group + 1, :] = parts[0:1]
            lower_ref[group : group + 1, :] = parts[1:2]
        at = pl.ds(lax.bitwise_xor(column, step), groups, stride=pipes)
        put(first_ref, at, upper_ref[...])
        put(last_ref, at, lower_ref[...])
    picked_in, picked_out = selection(inlet_ref, outlet_ref, pipes)
    picked = picked_in + picked_out
    junc_grad = COUPLING * (dot(picked, whole(first_ref)) + dot(picked, whole(last_ref)))
    act_grad = (junc_grad * slope_ref[...]).astype(jnp.bfloat16)
    sums_grad = dot(act_grad, junc_weight_ref[...], 1, 1)
    rows_ref[...] = sums_grad.astype(jnp.bfloat16).astype(jnp.float32)
    wait(going)


def pack_kernel(first_ref, second_ref, out_ref):
    groups = first_ref.shape[0]
    out_ref[0:groups] = first_ref[...]
    out_ref[groups : 2 * groups] = second_ref[...]


def input_grad_kernel(
    total_ref, ft_ref, weight_ref, rows_ref, signs_ref, modes_ref, out_ref, tiles_ref, sems
):
    groups, span, channels = modes_ref.shape
    steps, tile = tiles_ref.shape[0], tiles_ref.shape[2]
    half = steps * tile
    back = jnp.concatenate(
        [modes_ref[at, 0:span, :].astype(jnp.float32) for at in range(groups)], axis=0
    )
    signs = signs_ref[...]
    back = (back.astype(jnp.bfloat16), (back * signs).astype(jnp.bfloat16))
    weight = weight_ref[...]
    row = lax.broadcasted_iota(jnp.int32, (tile, channels), 0)
    going = []
    for step in range(steps):
        for side in range(2):
            at = pl.ds(side * half + step * tile, tile)
            grad_cells = dot(ft_ref[pl.ds(step * tile, tile), :], back[side])
            if step == 0 and side == 0:
                grad_cells = grad_cells + jnp.where(row == 0, rows_ref[0:1, :], 0.0)
            if step == steps - 1 and side == 1:
                grad_cells = grad_cells + jnp.where(row == tile - 1, rows_ref[1:2, :], 0.0)
            spread = grad_cells.astype(jnp.bfloat16).astype(jnp.float32)
            local = dot(total_ref[at, :], weight, 1, 1)
            tiles_ref[step, side] = (local + spread).astype(jnp.bfloat16)
            going += started(
                [
                    pltpu.make_async_copy(
                        tiles_ref.at[step, side], out_ref.at[at], sems.at[step, side]
                    )
                ]
            )
    wait(going)


def rows_of(count, channels):
    return pltpu.VMEM((channels // LANES, count, LANES), jnp.float32)


def call(kernel, outs, specs, scratch=(), out_specs=None, name=None, limit=8, busy=0):
    return pl.pallas_call(
        kernel,
        out_shape=outs,
        in_specs=specs,
        out_specs=out_specs if out_specs is not None else [VMEM] * len(outs),
        scratch_shapes=list(scratch),
        compiler_params=pltpu.CompilerParams(vmem_limit_bytes=limit * MIB),
        cost_estimate=pl.CostEstimate(
            flops=busy * 1_000_000_000, bytes_accessed=busy * MIB, transcendentals=0
        )
        if busy
        else None,
        name=name,
    )


def body(
    inputs,
    cotangent,
    point_weight,
    point_bias,
    spec_real,
    spec_imag,
    junc_weight,
    junc_bias,
    inlet_ids,
    outlet_ids,
):
    per_dev, cell_count, channels = inputs.shape
    assert per_dev == 1
    groups, pipes = lax.axis_size("len"), lax.axis_size("pipe")
    assert pipes == 4
    modes = spec_real.shape[0]
    span = 2 * modes
    all_rows = span * groups
    steps = cell_count // (2 * TILE)
    table = half_table(cell_count, modes * groups, groups)
    tiled = table.reshape(all_rows, steps, TILE).transpose(1, 0, 2)
    f_table = jnp.asarray(np.ascontiguousarray(tiled))
    ft_table = jnp.asarray(np.ascontiguousarray(table.T))
    field = inputs.reshape(cell_count, channels)
    cot = cotangent.reshape(cell_count, channels)
    bias_row = point_bias.reshape(1, channels)
    junc_bias_row = junc_bias.reshape(1, channels)
    shape = jax.ShapeDtypeStruct
    bf16, f32 = jnp.bfloat16, jnp.float32
    message = shape((groups, span + 2, channels), bf16)
    chunks = shape((groups, span, channels), bf16)
    dma = pltpu.SemaphoreType.DMA

    def exchange(value):
        return lax.all_to_all(value, "len", split_axis=0, concat_axis=0, tiled=True)

    def swap(value, step):
        return lax.ppermute(value, "pipe", [(i, i ^ step) for i in range(pipes)])

    def gather(own, behind):
        across = swap(own, 2)
        tied, tied_across, _ = lax.optimization_barrier((own, across, behind))
        return [own, swap(tied, 1), across, swap(tied_across, 1)]

    def mix(backward, value, *early):
        return call(
            functools.partial(mix_kernel, backward),
            [chunks, early[0]] if backward else [chunks],
            [VMEM] * (4 if backward else 3),
            ([dma] if backward else []) + [rows_of(all_rows, channels)] * 2,
            out_specs=[VMEM, HBM] if backward else [VMEM],
            name="mix_grad" if backward else "mix",
            busy=12,
        )(value, spec_real, spec_imag, *early)

    signs, doubled = call(
        functools.partial(factors_kernel, span),
        [shape((all_rows, channels), f32)] * 2,
        [],
        name="factors",
        busy=1,
    )()
    (sent,) = call(spectrum_kernel, [message], [VMEM] * 3, name="spectrum", busy=12)(
        field, f_table, signs
    )
    received = exchange(sent)
    (ends,) = call(
        ends_kernel, [shape((2 * groups, channels), f32)], [VMEM], name="pipe_ends"
    )(received)
    ends = [ends] + [swap(ends, step) for step in range(1, pipes)]
    (mixed,) = mix(False, received)
    mixed, *ends = lax.optimization_barrier((mixed, *ends))
    returned = exchange(mixed)
    spectra = received
    pipe_rows = [rows_of(pipes * groups, channels)] * 2
    inlet_row = inlet_ids.reshape(1, -1)
    outlet_row = outlet_ids.reshape(1, -1)
    early, total, sent, slope = call(
        functools.partial(layer_kernel, pipes),
        [shape(field.shape, bf16)] * 2 + [message, shape((8, channels), f32)],
        [VMEM] * (pipes + 13),
        [pltpu.VMEM((all_rows, channels), f32)] * 2 + pipe_rows,
        name="layer",
        busy=12,
    )(
        *ends,
        inlet_row,
        outlet_row,
        junc_weight,
        junc_bias_row,
        field,
        cot,
        f_table,
        ft_table,
        point_weight,
        bias_row,
        returned,
        signs,
        doubled,
    )
    received = exchange(sent)
    received, spectra = lax.optimization_barrier((received, spectra))
    (both,) = call(
        pack_kernel,
        [shape((2 * groups, span + 2, channels), bf16)],
        [VMEM] * 2,
        name="pack",
    )(spectra, received)
    mixed, outputs = mix(True, received, early)
    both = gather(both, mixed)
    returned = exchange(mixed)
    big = shape((modes, channels, channels), f32)
    per_copy = math.gcd(modes, 2)
    grad_real, grad_imag, rows = call(
        functools.partial(weight_grad_kernel, pipes, modes, per_copy),
        [big, big, shape((8, channels), f32)],
        [VMEM] * (pipes + 4),
        [rows_of(pipes * all_rows, channels)] * 2
        + [pltpu.VMEM(big.shape, f32)] * 2
        + pipe_rows
        + [pltpu.VMEM((groups, channels), f32)] * 2
        + [dma((modes // per_copy, 2))],
        out_specs=[HBM, HBM, VMEM],
        name="weight_grad",
        limit=16,
    )(*both, inlet_row, outlet_row, junc_weight, slope)
    (grad_inputs,) = call(
        input_grad_kernel,
        [shape(field.shape, bf16)],
        [VMEM] * 6,
        [pltpu.VMEM((steps, 2, TILE, channels), bf16), dma((steps, 2))],
        out_specs=[HBM],
        name="input_grad",
    )(total, ft_table, point_weight, rows, signs, returned)
    return (
        outputs.reshape(inputs.shape),
        grad_inputs.reshape(inputs.shape),
        grad_real,
        grad_imag,
    )


def solution(mesh):
    placed = (
        P(("len", "pipe"), None, None),
        P(("len", "pipe"), None, None),
        P(),
        P(),
        P("len", None, None),
        P("len", None, None),
        P(),
        P(),
        P(),
        P(),
    )
    return jax.shard_map(
        body,
        mesh=mesh,
        in_specs=placed,
        out_specs=(
            P(("len", "pipe"), None, None),
            P(("len", "pipe"), None, None),
            P("len", None, None),
            P("len", None, None),
        ),
        check_vma=False,
    )
```

```python
import functools
import math

import jax
import jax.numpy as jnp
import ml_dtypes
import numpy as np
from jax import lax
from jax.experimental import pallas as pl
from jax.experimental.pallas import tpu as pltpu
from jax.sharding import PartitionSpec as P

COUPLING = 0.125
TILE = 256
LANES = 128
GELU_S = math.sqrt(2.0 / math.pi)
GELU_C = 0.044715
VMEM = pl.BlockSpec(memory_space=pltpu.VMEM)
HBM = pl.BlockSpec(memory_space=pltpu.HBM)
MIB = 1024 * 1024


def half_table(cell_count, mode_count, groups):
    half = cell_count // 2
    product_index = np.arange(mode_count)[:, None] * np.arange(half)[None, :] % cell_count
    angles = product_index.astype(np.float32) * np.float32(2.0 * math.pi / cell_count)
    norm_scale = np.float32(1.0 / math.sqrt(cell_count))
    cosine = (np.cos(angles) * norm_scale).reshape(groups, -1, half)
    sine = (np.sin(angles) * norm_scale).reshape(groups, -1, half)
    table = np.concatenate([cosine, -sine], axis=1).reshape(2 * mode_count, half)
    return table.astype(ml_dtypes.bfloat16)


def row_signs(all_rows, span, channels):
    row = lax.broadcasted_iota(jnp.int32, (all_rows, channels), 0)
    per_owner = span // 2
    mode = (row // span) * per_owner + lax.rem(row, per_owner)
    return jnp.where(lax.rem(mode, 2) == 0, 1.0, -1.0).astype(jnp.float32)


def dot(left, right, left_dim=1, right_dim=0):
    return lax.dot_general(
        left,
        right,
        (((left_dim,), (right_dim,)), ((), ())),
        preferred_element_type=jnp.float32,
    )


def put(ref, at, value):
    for lane in range(ref.shape[0]):
        ref[lane, at, :] = value[:, lane * LANES : (lane + 1) * LANES]


def take(ref, at):
    return jnp.concatenate([ref[lane, at, :] for lane in range(ref.shape[0])], axis=1)


def spectrum_kernel(x_ref, f_ref, msg_ref):
    groups, rows = msg_ref.shape[0], msg_ref.shape[1]
    steps, all_rows, tile = f_ref.shape
    cells, channels = x_ref.shape
    half = cells // 2
    span = all_rows // groups
    sums = []
    for base in (0, half):
        total = None
        for step in range(steps):
            at = base + step * tile
            part = dot(f_ref[step], x_ref[at : at + tile, :])
            total = part if total is None else total + part
        sums.append(total)
    spectra = (sums[0] + row_signs(all_rows, span, channels) * sums[1]).astype(jnp.bfloat16)
    ends = extra_rows(x_ref[0:1, :], x_ref[cells - 1 : cells, :], rows - span, channels)
    for at in range(groups):
        msg_ref[at, 0:span, :] = spectra[at * span : (at + 1) * span]
        msg_ref[at, span:rows, :] = ends


def extra_rows(first, second, count, channels):
    parts = [first.astype(jnp.float32), second.astype(jnp.float32)]
    if count > 2:
        parts.append(jnp.zeros((count - 2, channels), jnp.float32))
    return jnp.concatenate(parts, axis=0).astype(jnp.bfloat16)


def mix_kernel(backward, r_ref, real_ref, imag_ref, *refs):
    x_ref, y_ref = refs[-2:]
    groups, modes = r_ref.shape[0], real_ref.shape[0]
    span = 2 * modes
    if backward:
        early_ref, out_ref, copied_ref, sem = refs[:4]
        copy = pltpu.make_async_copy(early_ref, copied_ref, sem)
        copy.start()
    else:
        out_ref = refs[0]
    for source in range(groups):
        put(x_ref, pl.ds(source * span, span), r_ref[source, 0:span, :].astype(jnp.float32))
    for mode in range(modes):
        first = pl.ds(mode, groups, stride=span)
        second = pl.ds(modes + mode, groups, stride=span)
        rows = jnp.concatenate([take(x_ref, first), take(x_ref, second)], axis=0).astype(
            jnp.bfloat16
        )
        dim = 1 if backward else 0
        by_real = dot(rows, real_ref[mode], 1, dim)
        by_imag = dot(rows, imag_ref[mode], 1, dim)
        if backward:
            put(y_ref, first, by_real[:groups] + by_imag[groups:])
            put(y_ref, second, by_real[groups:] - by_imag[:groups])
        else:
            put(y_ref, first, by_real[:groups] - by_imag[groups:])
            put(y_ref, second, by_imag[:groups] + by_real[groups:])
    for source in range(groups):
        rows = take(y_ref, pl.ds(source * span, span)).astype(jnp.bfloat16)
        out_ref[source] = rows
    if backward:
        copy.wait()


def own_pipe(pipes):
    return lax.axis_index("len") * pipes + lax.axis_index("pipe")


def selection(inlet_ref, outlet_ref, pipes):
    count = inlet_ref.shape[1]
    lane = lax.broadcasted_iota(jnp.int32, (8, count), 1)
    row = lax.broadcasted_iota(jnp.int32, (8, count), 0)
    inlets = jnp.broadcast_to(inlet_ref[...], (8, count)).astype(jnp.float32)
    outlets = jnp.broadcast_to(outlet_ref[...], (8, count)).astype(jnp.float32)
    mine = jnp.where(row == 0, inlets, outlets)
    own = jnp.sum(jnp.where(lane == own_pipe(pipes), mine, 0.0), axis=1, keepdims=True)
    return (inlets == own).astype(jnp.bfloat16), (outlets == own).astype(jnp.bfloat16)


def whole(ref):
    return take(ref, pl.ds(0, ref.shape[1])).astype(jnp.bfloat16)


def ends_kernel(r_ref, ends_ref):
    groups, rows = r_ref.shape[0], r_ref.shape[1]
    for group in range(groups):
        ends = r_ref[group, rows - 2 : rows, :].astype(jnp.float32)
        ends_ref[group : group + 1, :] = ends[0:1]
        ends_ref[groups + group : groups + group + 1, :] = ends[1:2]


def started(copies):
    for copy in copies:
        copy.start()
    return copies


def wait(copies):
    for copy in copies:
        copy.wait()


def brought(pairs, sems, base=0):
    return started(
        [
            pltpu.make_async_copy(source, target, sems.at[base + place])
            for place, (source, target) in enumerate(pairs)
        ]
    )


def layer_kernel(pipes, *refs):
    ends, refs = refs[:pipes], refs[pipes:]
    (inlet_ref, outlet_ref, junc_weight_ref, junc_bias_ref), refs = refs[:4], refs[4:]
    x_ref, cot_ref, f_ref, ft_ref, weight_ref, bias_ref, modes_ref = refs[:7]
    out_ref, total_ref, msg_ref, slope_ref, low_ref, high_ref, first_ref, last_ref = refs[7:]
    steps, all_rows, tile = f_ref.shape
    half = steps * tile
    channels = x_ref.shape[1]
    groups, rows = msg_ref.shape[0], msg_ref.shape[1]
    span = all_rows // groups
    column = lax.axis_index("pipe")
    for step in range(pipes):
        at = pl.ds(lax.bitwise_xor(column, step), groups, stride=pipes)
        put(first_ref, at, ends[step][0:groups, :])
        put(last_ref, at, ends[step][groups : 2 * groups, :])
    picked_in, picked_out = selection(inlet_ref, outlet_ref, pipes)
    sums = dot(picked_in, whole(first_ref)) + dot(picked_out, whole(last_ref))
    act = dot(sums.astype(jnp.bfloat16), junc_weight_ref[...]) + junc_bias_ref[...]
    sigmoid_part = jax.nn.sigmoid(act)
    junc_rows = (act * sigmoid_part).astype(jnp.bfloat16).astype(jnp.float32)
    cond = COUPLING * (junc_rows[0:1] + junc_rows[1:2])
    slope_ref[...] = sigmoid_part * (1.0 + act * (1.0 - sigmoid_part))
    row = lax.broadcasted_iota(jnp.int32, (all_rows, channels), 0)
    doubled = jnp.where((row == 0) | (row == span // 2), 1.0, 2.0).astype(jnp.float32)
    signs = row_signs(all_rows, span, channels)
    modes = jnp.concatenate(
        [modes_ref[at, 0:span, :].astype(jnp.float32) for at in range(groups)], axis=0
    )
    modes = modes * doubled
    modes = (modes.astype(jnp.bfloat16), (modes * signs).astype(jnp.bfloat16))
    weight = weight_ref[...]
    bias = bias_ref[...]
    for step in range(steps):
        for side, acc_ref in enumerate((low_ref, high_ref)):
            at = pl.ds(side * half + step * tile, tile)
            pointwise = dot(x_ref[at, :], weight) + bias
            spectral = dot(ft_ref[pl.ds(step * tile, tile), :], modes[side])
            summed = pointwise + (spectral + cond).astype(jnp.bfloat16).astype(jnp.float32)
            square = summed * summed
            part = 0.5 + 0.5 * jnp.tanh(summed * (GELU_S + (GELU_S * GELU_C) * square))
            result = summed * part
            out_ref[at, :] = result.astype(jnp.bfloat16)
            slope = part + result * (1.0 - part) * (
                2.0 * GELU_S + (6.0 * GELU_S * GELU_C) * square
            )
            total = (cot_ref[at, :].astype(jnp.float32) * slope).astype(jnp.bfloat16)
            total_ref[at, :] = total
            term = dot(f_ref[step], total)
            if step == 0:
                acc_ref[...] = term
            else:
                acc_ref[...] += term
    acc = low_ref[...] + signs * high_ref[...]
    grad_cond = acc[0:1, :] * (1.0 / f_ref[0, 0:1, 0:1].astype(jnp.float32))
    upper = grad_cond.astype(jnp.bfloat16).astype(jnp.float32)
    extra = extra_rows(upper, grad_cond - upper, rows - span, channels)
    grad_spec = (acc * doubled).astype(jnp.bfloat16)
    for at in range(groups):
        msg_ref[at, 0:span, :] = grad_spec[at * span : (at + 1) * span]
        msg_ref[at, span:rows, :] = extra


def weight_grad_kernel(pipes, modes, per_copy, *refs):
    fields, grads, refs = refs[:pipes], refs[pipes : 2 * pipes], refs[2 * pipes :]
    (inlet_ref, outlet_ref, junc_weight_ref, slope_ref), refs = refs[:4], refs[4:]
    real_out, imag_out, rows_ref, x_ref, g_ref, real_ref, imag_ref = refs[:7]
    first_ref, last_ref, upper_ref, lower_ref, sems = refs[7:]
    groups, rows = fields[0].shape[0], fields[0].shape[1]
    span = 2 * modes
    for step in range(pipes):
        for source in range(groups):
            at = pl.ds((step * groups + source) * span, span)
            put(x_ref, at, fields[step][source, 0:span, :].astype(jnp.float32))
            put(g_ref, at, grads[step][source, 0:span, :].astype(jnp.float32))
    count = pipes * groups
    going = []
    for number in range(modes // per_copy):
        for mode in range(number * per_copy, (number + 1) * per_copy):
            first = pl.ds(mode, count, stride=span)
            second = pl.ds(modes + mode, count, stride=span)
            a, b = take(x_ref, first), take(x_ref, second)
            u, v = take(g_ref, first), take(g_ref, second)
            left = jnp.concatenate([a, b], axis=0).astype(jnp.bfloat16)
            right = jnp.concatenate([u, v], axis=0).astype(jnp.bfloat16)
            turned = jnp.concatenate([v, -u], axis=0).astype(jnp.bfloat16)
            real_ref[mode] = dot(left, right, 0, 0)
            imag_ref[mode] = dot(left, turned, 0, 0)
        at = pl.ds(number * per_copy, per_copy)
        going += started(
            [
                pltpu.make_async_copy(real_ref.at[at], real_out.at[at], sems.at[number, 0]),
                pltpu.make_async_copy(imag_ref.at[at], imag_out.at[at], sems.at[number, 1]),
            ]
        )
    column = lax.axis_index("pipe")
    for step in range(pipes):
        for group in range(groups):
            parts = grads[step][group, rows - 2 : rows, :].astype(jnp.float32)
            upper_ref[group : group + 1, :] = parts[0:1]
            lower_ref[group : group + 1, :] = parts[1:2]
        at = pl.ds(lax.bitwise_xor(column, step), groups, stride=pipes)
        put(first_ref, at, upper_ref[...])
        put(last_ref, at, lower_ref[...])
    picked_in, picked_out = selection(inlet_ref, outlet_ref, pipes)
    picked = picked_in + picked_out
    junc_grad = COUPLING * (dot(picked, whole(first_ref)) + dot(picked, whole(last_ref)))
    act_grad = (junc_grad * slope_ref[...]).astype(jnp.bfloat16)
    sums_grad = dot(act_grad, junc_weight_ref[...], 1, 1)
    rows_ref[...] = sums_grad.astype(jnp.bfloat16).astype(jnp.float32)
    wait(going)


def pack_kernel(first_ref, second_ref, out_ref):
    groups = first_ref.shape[0]
    out_ref[0:groups] = first_ref[...]
    out_ref[groups : 2 * groups] = second_ref[...]


def split_kernel(both_ref, first_ref, second_ref):
    groups = first_ref.shape[0]
    first_ref[...] = both_ref[0:groups]
    second_ref[...] = both_ref[groups : 2 * groups]


def input_grad_kernel(
    total_ref, ft_ref, weight_ref, rows_ref, modes_ref, out_ref, tiles_ref, sems
):
    groups, span, channels = modes_ref.shape
    steps, tile = tiles_ref.shape[0], tiles_ref.shape[2]
    half, all_rows = steps * tile, groups * span
    back = jnp.concatenate(
        [modes_ref[at, 0:span, :].astype(jnp.float32) for at in range(groups)], axis=0
    )
    signs = row_signs(all_rows, span, channels)
    back = (back.astype(jnp.bfloat16), (back * signs).astype(jnp.bfloat16))
    weight = weight_ref[...]
    row = lax.broadcasted_iota(jnp.int32, (tile, channels), 0)
    going = []
    for step in range(steps):
        for side in range(2):
            at = pl.ds(side * half + step * tile, tile)
            grad_cells = dot(ft_ref[pl.ds(step * tile, tile), :], back[side])
            if step == 0 and side == 0:
                grad_cells = grad_cells + jnp.where(row == 0, rows_ref[0:1, :], 0.0)
            if step == steps - 1 and side == 1:
                grad_cells = grad_cells + jnp.where(row == tile - 1, rows_ref[1:2, :], 0.0)
            spread = grad_cells.astype(jnp.bfloat16).astype(jnp.float32)
            local = dot(total_ref[at, :], weight, 1, 1)
            tiles_ref[step, side] = (local + spread).astype(jnp.bfloat16)
            going += started(
                [
                    pltpu.make_async_copy(
                        tiles_ref.at[step, side], out_ref.at[at], sems.at[step, side]
                    )
                ]
            )
    wait(going)


def rows_of(count, channels):
    return pltpu.VMEM((channels // LANES, count, LANES), jnp.float32)


def call(kernel, outs, specs, scratch=(), out_specs=None, name=None, limit=8, busy=0):
    return pl.pallas_call(
        kernel,
        out_shape=outs,
        in_specs=specs,
        out_specs=out_specs if out_specs is not None else [VMEM] * len(outs),
        scratch_shapes=list(scratch),
        compiler_params=pltpu.CompilerParams(vmem_limit_bytes=limit * MIB),
        cost_estimate=pl.CostEstimate(
            flops=busy * 1_000_000_000, bytes_accessed=busy * MIB, transcendentals=0
        )
        if busy
        else None,
        name=name,
    )


def body(
    inputs,
    cotangent,
    point_weight,
    point_bias,
    spec_real,
    spec_imag,
    junc_weight,
    junc_bias,
    inlet_ids,
    outlet_ids,
):
    per_dev, cell_count, channels = inputs.shape
    assert per_dev == 1
    groups, pipes = lax.axis_size("len"), lax.axis_size("pipe")
    assert pipes == 4
    modes = spec_real.shape[0]
    span = 2 * modes
    all_rows = span * groups
    steps = cell_count // (2 * TILE)
    table = half_table(cell_count, modes * groups, groups)
    tiled = table.reshape(all_rows, steps, TILE).transpose(1, 0, 2)
    f_table = jnp.asarray(np.ascontiguousarray(tiled))
    ft_table = jnp.asarray(np.ascontiguousarray(table.T))
    field = inputs.reshape(cell_count, channels)
    cot = cotangent.reshape(cell_count, channels)
    bias_row = point_bias.reshape(1, channels)
    junc_bias_row = junc_bias.reshape(1, channels)
    shape = jax.ShapeDtypeStruct
    bf16, f32 = jnp.bfloat16, jnp.float32
    message = shape((groups, span + 2, channels), bf16)
    chunks = shape((groups, span, channels), bf16)
    dma = pltpu.SemaphoreType.DMA

    def exchange(value):
        return lax.all_to_all(value, "len", split_axis=0, concat_axis=0, tiled=True)

    def swap(value, step):
        return lax.ppermute(value, "pipe", [(i, i ^ step) for i in range(pipes)])

    def mix(backward, value, *early):
        return call(
            functools.partial(mix_kernel, backward),
            [chunks, early[0]] if backward else [chunks],
            [VMEM] * (4 if backward else 3),
            ([dma] if backward else []) + [rows_of(all_rows, channels)] * 2,
            out_specs=[VMEM, HBM] if backward else [VMEM],
            name="mix_grad" if backward else "mix",
            busy=12,
        )(value, spec_real, spec_imag, *early)

    (sent,) = call(spectrum_kernel, [message], [VMEM] * 2, name="spectrum", busy=12)(
        field, f_table
    )
    received = exchange(sent)
    (ends,) = call(
        ends_kernel, [shape((2 * groups, channels), f32)], [VMEM], name="pipe_ends"
    )(received)
    ends = [ends] + [swap(ends, step) for step in range(1, pipes)]
    (mixed,) = mix(False, received)
    mixed, *ends = lax.optimization_barrier((mixed, *ends))
    returned = exchange(mixed)
    spectra = received
    pipe_rows = [rows_of(pipes * groups, channels)] * 2
    inlet_row = inlet_ids.reshape(1, -1)
    outlet_row = outlet_ids.reshape(1, -1)
    early, total, sent, slope = call(
        functools.partial(layer_kernel, pipes),
        [shape(field.shape, bf16)] * 2 + [message, shape((8, channels), f32)],
        [VMEM] * (pipes + 11),
        [pltpu.VMEM((all_rows, channels), f32)] * 2 + pipe_rows,
        name="layer",
        busy=12,
    )(
        *ends,
        inlet_row,
        outlet_row,
        junc_weight,
        junc_bias_row,
        field,
        cot,
        f_table,
        ft_table,
        point_weight,
        bias_row,
        returned,
    )
    received = exchange(sent)
    received, spectra = lax.optimization_barrier((received, spectra))
    (both,) = call(
        pack_kernel,
        [shape((2 * groups, span + 2, channels), bf16)],
        [VMEM] * 2,
        name="pack",
    )(spectra, received)
    mixed, outputs = mix(True, received, early)
    both, behind = lax.optimization_barrier((swap(both, 2), mixed))
    across = call(split_kernel, [message] * 2, [VMEM], name="split")(both)
    spectra, received, _ = lax.optimization_barrier((spectra, received, behind))
    fields = [spectra, swap(spectra, 1), across[0], swap(across[0], 1)]
    grads = [received, swap(received, 1), across[1], swap(across[1], 1)]
    returned = exchange(mixed)
    big = shape((modes, channels, channels), f32)
    per_copy = math.gcd(modes, 2)
    grad_real, grad_imag, rows = call(
        functools.partial(weight_grad_kernel, pipes, modes, per_copy),
        [big, big, shape((8, channels), f32)],
        [VMEM] * (2 * pipes + 4),
        [rows_of(pipes * all_rows, channels)] * 2
        + [pltpu.VMEM(big.shape, f32)] * 2
        + pipe_rows
        + [pltpu.VMEM((groups, channels), f32)] * 2
        + [dma((modes // per_copy, 2))],
        out_specs=[HBM, HBM, VMEM],
        name="weight_grad",
        limit=16,
    )(*fields, *grads, inlet_row, outlet_row, junc_weight, slope)
    (grad_inputs,) = call(
        input_grad_kernel,
        [shape(field.shape, bf16)],
        [VMEM] * 5,
        [pltpu.VMEM((steps, 2, TILE, channels), bf16), dma((steps, 2))],
        out_specs=[HBM],
        name="input_grad",
    )(total, ft_table, point_weight, rows, returned)
    return (
        outputs.reshape(inputs.shape),
        grad_inputs.reshape(inputs.shape),
        grad_real,
        grad_imag,
    )


def solution(mesh):
    placed = (
        P(("len", "pipe"), None, None),
        P(("len", "pipe"), None, None),
        P(),
        P(),
        P("len", None, None),
        P("len", None, None),
        P(),
        P(),
        P(),
        P(),
    )
    return jax.shard_map(
        body,
        mesh=mesh,
        in_specs=placed,
        out_specs=(
            P(("len", "pipe"), None, None),
            P(("len", "pipe"), None, None),
            P("len", None, None),
            P("len", None, None),
        ),
        check_vma=False,
    )
```

```python
import functools
import math

import jax
import jax.numpy as jnp
import ml_dtypes
import numpy as np
from jax import lax
from jax.experimental import pallas as pl
from jax.experimental.pallas import tpu as pltpu
from jax.sharding import PartitionSpec as P

COUPLING = 0.125
TILE = 256
LANES = 128
GELU_S = math.sqrt(2.0 / math.pi)
GELU_C = 0.044715
VMEM = pl.BlockSpec(memory_space=pltpu.VMEM)
HBM = pl.BlockSpec(memory_space=pltpu.HBM)
MIB = 1024 * 1024


def half_table(cell_count, mode_count, groups):
    half = cell_count // 2
    product_index = np.arange(mode_count)[:, None] * np.arange(half)[None, :] % cell_count
    angles = product_index.astype(np.float32) * np.float32(2.0 * math.pi / cell_count)
    norm_scale = np.float32(1.0 / math.sqrt(cell_count))
    cosine = (np.cos(angles) * norm_scale).reshape(groups, -1, half)
    sine = (np.sin(angles) * norm_scale).reshape(groups, -1, half)
    table = np.concatenate([cosine, -sine], axis=1).reshape(2 * mode_count, half)
    return table.astype(ml_dtypes.bfloat16)


def row_signs(all_rows, span, channels):
    row = lax.broadcasted_iota(jnp.int32, (all_rows, channels), 0)
    per_owner = span // 2
    mode = (row // span) * per_owner + lax.rem(row, per_owner)
    return jnp.where(lax.rem(mode, 2) == 0, 1.0, -1.0).astype(jnp.float32)


def position(column, group, groups):
    return jnp.where(lax.rem(column, 2) == 0, group, groups - 1 - group)


def dot(left, right, left_dim=1, right_dim=0):
    return lax.dot_general(
        left,
        right,
        (((left_dim,), (right_dim,)), ((), ())),
        preferred_element_type=jnp.float32,
    )


def put(ref, at, value):
    for lane in range(ref.shape[0]):
        ref[lane, at, :] = value[:, lane * LANES : (lane + 1) * LANES]


def take(ref, at):
    return jnp.concatenate([ref[lane, at, :] for lane in range(ref.shape[0])], axis=1)


def spectrum_kernel(x_ref, f_ref, msg_ref):
    groups, rows = msg_ref.shape[0], msg_ref.shape[1]
    steps, all_rows, tile = f_ref.shape
    cells, channels = x_ref.shape
    half = cells // 2
    span = all_rows // groups
    sums = []
    for base in (0, half):
        total = None
        for step in range(steps):
            at = base + step * tile
            part = dot(f_ref[step], x_ref[at : at + tile, :])
            total = part if total is None else total + part
        sums.append(total)
    spectra = (sums[0] + row_signs(all_rows, span, channels) * sums[1]).astype(jnp.bfloat16)
    ends = extra_rows(x_ref[0:1, :], x_ref[cells - 1 : cells, :], rows - span, channels)
    column = lax.axis_index("pipe")
    for at in range(groups):
        to = position(column, at, groups)
        msg_ref[to, 0:span, :] = spectra[at * span : (at + 1) * span]
        msg_ref[to, span:rows, :] = ends


def extra_rows(first, second, count, channels):
    parts = [first.astype(jnp.float32), second.astype(jnp.float32)]
    if count > 2:
        parts.append(jnp.zeros((count - 2, channels), jnp.float32))
    return jnp.concatenate(parts, axis=0).astype(jnp.bfloat16)


def mix_kernel(backward, r_ref, real_ref, imag_ref, *refs):
    x_ref, y_ref = refs[-2:]
    groups, modes = r_ref.shape[0], real_ref.shape[0]
    span = 2 * modes
    if backward:
        early_ref, out_ref, copied_ref, sem = refs[:4]
        copy = pltpu.make_async_copy(early_ref, copied_ref, sem)
        copy.start()
    else:
        out_ref = refs[0]
    for source in range(groups):
        put(x_ref, pl.ds(source * span, span), r_ref[source, 0:span, :].astype(jnp.float32))
    for mode in range(modes):
        first = pl.ds(mode, groups, stride=span)
        second = pl.ds(modes + mode, groups, stride=span)
        rows = jnp.concatenate([take(x_ref, first), take(x_ref, second)], axis=0).astype(
            jnp.bfloat16
        )
        dim = 1 if backward else 0
        by_real = dot(rows, real_ref[mode], 1, dim)
        by_imag = dot(rows, imag_ref[mode], 1, dim)
        if backward:
            put(y_ref, first, by_real[:groups] + by_imag[groups:])
            put(y_ref, second, by_real[groups:] - by_imag[:groups])
        else:
            put(y_ref, first, by_real[:groups] - by_imag[groups:])
            put(y_ref, second, by_imag[:groups] + by_real[groups:])
    for source in range(groups):
        rows = take(y_ref, pl.ds(source * span, span)).astype(jnp.bfloat16)
        out_ref[source] = rows
    if backward:
        copy.wait()


def own_pipe(pipes):
    return lax.axis_index("len") * pipes + lax.axis_index("pipe")


def selection(inlet_ref, outlet_ref, pipes):
    count = inlet_ref.shape[1]
    lane = lax.broadcasted_iota(jnp.int32, (8, count), 1)
    row = lax.broadcasted_iota(jnp.int32, (8, count), 0)
    inlets = jnp.broadcast_to(inlet_ref[...], (8, count)).astype(jnp.float32)
    outlets = jnp.broadcast_to(outlet_ref[...], (8, count)).astype(jnp.float32)
    mine = jnp.where(row == 0, inlets, outlets)
    own = jnp.sum(jnp.where(lane == own_pipe(pipes), mine, 0.0), axis=1, keepdims=True)
    return (inlets == own).astype(jnp.bfloat16), (outlets == own).astype(jnp.bfloat16)


def whole(ref):
    return take(ref, pl.ds(0, ref.shape[1])).astype(jnp.bfloat16)


def ends_kernel(r_ref, ends_ref):
    groups, rows = r_ref.shape[0], r_ref.shape[1]
    column = lax.axis_index("pipe")
    for group in range(groups):
        ends = r_ref[position(column, group, groups), rows - 2 : rows, :].astype(jnp.float32)
        ends_ref[group : group + 1, :] = ends[0:1]
        ends_ref[groups + group : groups + group + 1, :] = ends[1:2]


def started(copies):
    for copy in copies:
        copy.start()
    return copies


def wait(copies):
    for copy in copies:
        copy.wait()


def brought(pairs, sems, base=0):
    return started(
        [
            pltpu.make_async_copy(source, target, sems.at[base + place])
            for place, (source, target) in enumerate(pairs)
        ]
    )


def layer_kernel(pipes, *refs):
    ends, refs = refs[:pipes], refs[pipes:]
    (inlet_ref, outlet_ref, junc_weight_ref, junc_bias_ref), refs = refs[:4], refs[4:]
    x_ref, cot_ref, f_ref, ft_ref, weight_ref, bias_ref, modes_ref = refs[:7]
    out_ref, total_ref, msg_ref, slope_ref, low_ref, high_ref, first_ref, last_ref = refs[7:]
    steps, all_rows, tile = f_ref.shape
    half = steps * tile
    channels = x_ref.shape[1]
    groups, rows = msg_ref.shape[0], msg_ref.shape[1]
    span = all_rows // groups
    column = lax.axis_index("pipe")
    for step in range(pipes):
        at = pl.ds(lax.bitwise_xor(column, step), groups, stride=pipes)
        put(first_ref, at, ends[step][0:groups, :])
        put(last_ref, at, ends[step][groups : 2 * groups, :])
    picked_in, picked_out = selection(inlet_ref, outlet_ref, pipes)
    sums = dot(picked_in, whole(first_ref)) + dot(picked_out, whole(last_ref))
    act = dot(sums.astype(jnp.bfloat16), junc_weight_ref[...]) + junc_bias_ref[...]
    sigmoid_part = jax.nn.sigmoid(act)
    junc_rows = (act * sigmoid_part).astype(jnp.bfloat16).astype(jnp.float32)
    cond = COUPLING * (junc_rows[0:1] + junc_rows[1:2])
    slope_ref[...] = sigmoid_part * (1.0 + act * (1.0 - sigmoid_part))
    row = lax.broadcasted_iota(jnp.int32, (all_rows, channels), 0)
    doubled = jnp.where((row == 0) | (row == span // 2), 1.0, 2.0).astype(jnp.float32)
    signs = row_signs(all_rows, span, channels)
    order = [position(column, at, groups) for at in range(groups)]
    modes = jnp.concatenate([modes_ref[at].astype(jnp.float32) for at in order], axis=0)
    modes = modes * doubled
    modes = (modes.astype(jnp.bfloat16), (modes * signs).astype(jnp.bfloat16))
    weight = weight_ref[...]
    bias = bias_ref[...]
    for step in range(steps):
        for side, acc_ref in enumerate((low_ref, high_ref)):
            at = pl.ds(side * half + step * tile, tile)
            pointwise = dot(x_ref[at, :], weight) + bias
            spectral = dot(ft_ref[pl.ds(step * tile, tile), :], modes[side])
            summed = pointwise + (spectral + cond).astype(jnp.bfloat16).astype(jnp.float32)
            square = summed * summed
            part = 0.5 + 0.5 * jnp.tanh(summed * (GELU_S + (GELU_S * GELU_C) * square))
            result = summed * part
            out_ref[at, :] = result.astype(jnp.bfloat16)
            slope = part + result * (1.0 - part) * (
                2.0 * GELU_S + (6.0 * GELU_S * GELU_C) * square
            )
            total = (cot_ref[at, :].astype(jnp.float32) * slope).astype(jnp.bfloat16)
            total_ref[at, :] = total
            term = dot(f_ref[step], total)
            if step == 0:
                acc_ref[...] = term
            else:
                acc_ref[...] += term
    acc = low_ref[...] + signs * high_ref[...]
    grad_cond = acc[0:1, :] * (1.0 / f_ref[0, 0:1, 0:1].astype(jnp.float32))
    upper = grad_cond.astype(jnp.bfloat16).astype(jnp.float32)
    extra = extra_rows(upper, grad_cond - upper, rows - span, channels)
    grad_spec = (acc * doubled).astype(jnp.bfloat16)
    for at in range(groups):
        msg_ref[order[at], 0:span, :] = grad_spec[at * span : (at + 1) * span]
        msg_ref[order[at], span:rows, :] = extra


def weight_grad_kernel(pipes, modes, per_copy, *refs):
    fields, grads, refs = refs[:pipes], refs[pipes : 2 * pipes], refs[2 * pipes :]
    (inlet_ref, outlet_ref, junc_weight_ref, slope_ref), refs = refs[:4], refs[4:]
    real_out, imag_out, rows_ref, x_ref, g_ref, real_ref, imag_ref = refs[:7]
    first_ref, last_ref, upper_ref, lower_ref, sems = refs[7:]
    groups, rows = fields[0].shape[0], fields[0].shape[1]
    span = 2 * modes
    for step in range(pipes):
        for source in range(groups):
            at = pl.ds((step * groups + source) * span, span)
            put(x_ref, at, fields[step][source, 0:span, :].astype(jnp.float32))
            put(g_ref, at, grads[step][source, 0:span, :].astype(jnp.float32))
    count = pipes * groups
    going = []
    for number in range(modes // per_copy):
        for mode in range(number * per_copy, (number + 1) * per_copy):
            first = pl.ds(mode, count, stride=span)
            second = pl.ds(modes + mode, count, stride=span)
            a, b = take(x_ref, first), take(x_ref, second)
            u, v = take(g_ref, first), take(g_ref, second)
            left = jnp.concatenate([a, b], axis=0).astype(jnp.bfloat16)
            right = jnp.concatenate([u, v], axis=0).astype(jnp.bfloat16)
            turned = jnp.concatenate([v, -u], axis=0).astype(jnp.bfloat16)
            real_ref[mode] = dot(left, right, 0, 0)
            imag_ref[mode] = dot(left, turned, 0, 0)
        at = pl.ds(number * per_copy, per_copy)
        going += started(
            [
                pltpu.make_async_copy(real_ref.at[at], real_out.at[at], sems.at[number, 0]),
                pltpu.make_async_copy(imag_ref.at[at], imag_out.at[at], sems.at[number, 1]),
            ]
        )
    column = lax.axis_index("pipe")
    for step in range(pipes):
        for group in range(groups):
            at = position(lax.bitwise_xor(column, step), group, groups)
            parts = grads[step][at, rows - 2 : rows, :].astype(jnp.float32)
            upper_ref[group : group + 1, :] = parts[0:1]
            lower_ref[group : group + 1, :] = parts[1:2]
        at = pl.ds(lax.bitwise_xor(column, step), groups, stride=pipes)
        put(first_ref, at, upper_ref[...])
        put(last_ref, at, lower_ref[...])
    picked_in, picked_out = selection(inlet_ref, outlet_ref, pipes)
    picked = picked_in + picked_out
    junc_grad = COUPLING * (dot(picked, whole(first_ref)) + dot(picked, whole(last_ref)))
    act_grad = (junc_grad * slope_ref[...]).astype(jnp.bfloat16)
    sums_grad = dot(act_grad, junc_weight_ref[...], 1, 1)
    rows_ref[...] = sums_grad.astype(jnp.bfloat16).astype(jnp.float32)
    wait(going)


def pack_kernel(first_ref, second_ref, out_ref):
    groups = first_ref.shape[0]
    out_ref[0:groups] = first_ref[...]
    out_ref[groups : 2 * groups] = second_ref[...]


def split_kernel(both_ref, first_ref, second_ref):
    groups = first_ref.shape[0]
    first_ref[...] = both_ref[0:groups]
    second_ref[...] = both_ref[groups : 2 * groups]


def input_grad_kernel(
    total_ref, ft_ref, weight_ref, rows_ref, modes_ref, out_ref, tiles_ref, sems
):
    groups, span, channels = modes_ref.shape
    steps, tile = tiles_ref.shape[0], tiles_ref.shape[2]
    half, all_rows = steps * tile, groups * span
    column = lax.axis_index("pipe")
    order = [position(column, at, groups) for at in range(groups)]
    back = jnp.concatenate([modes_ref[at].astype(jnp.float32) for at in order], axis=0)
    signs = row_signs(all_rows, span, channels)
    back = (back.astype(jnp.bfloat16), (back * signs).astype(jnp.bfloat16))
    weight = weight_ref[...]
    row = lax.broadcasted_iota(jnp.int32, (tile, channels), 0)
    going = []
    for step in range(steps):
        for side in range(2):
            at = pl.ds(side * half + step * tile, tile)
            grad_cells = dot(ft_ref[pl.ds(step * tile, tile), :], back[side])
            if step == 0 and side == 0:
                grad_cells = grad_cells + jnp.where(row == 0, rows_ref[0:1, :], 0.0)
            if step == steps - 1 and side == 1:
                grad_cells = grad_cells + jnp.where(row == tile - 1, rows_ref[1:2, :], 0.0)
            spread = grad_cells.astype(jnp.bfloat16).astype(jnp.float32)
            local = dot(total_ref[at, :], weight, 1, 1)
            tiles_ref[step, side] = (local + spread).astype(jnp.bfloat16)
            going += started(
                [
                    pltpu.make_async_copy(
                        tiles_ref.at[step, side], out_ref.at[at], sems.at[step, side]
                    )
                ]
            )
    wait(going)


def rows_of(count, channels):
    return pltpu.VMEM((channels // LANES, count, LANES), jnp.float32)


def call(kernel, outs, specs, scratch=(), out_specs=None, name=None, limit=8, busy=0):
    return pl.pallas_call(
        kernel,
        out_shape=outs,
        in_specs=specs,
        out_specs=out_specs if out_specs is not None else [VMEM] * len(outs),
        scratch_shapes=list(scratch),
        compiler_params=pltpu.CompilerParams(vmem_limit_bytes=limit * MIB),
        cost_estimate=pl.CostEstimate(
            flops=busy * 1_000_000_000, bytes_accessed=busy * MIB, transcendentals=0
        )
        if busy
        else None,
        name=name,
    )


def body(
    inputs,
    cotangent,
    point_weight,
    point_bias,
    spec_real,
    spec_imag,
    junc_weight,
    junc_bias,
    inlet_ids,
    outlet_ids,
):
    per_dev, cell_count, channels = inputs.shape
    assert per_dev == 1
    groups, pipes = lax.axis_size("len"), lax.axis_size("pipe")
    assert pipes == 4
    modes = spec_real.shape[0]
    span = 2 * modes
    all_rows = span * groups
    steps = cell_count // (2 * TILE)
    table = half_table(cell_count, modes * groups, groups)
    tiled = table.reshape(all_rows, steps, TILE).transpose(1, 0, 2)
    f_table = jnp.asarray(np.ascontiguousarray(tiled))
    ft_table = jnp.asarray(np.ascontiguousarray(table.T))
    field = inputs.reshape(cell_count, channels)
    cot = cotangent.reshape(cell_count, channels)
    bias_row = point_bias.reshape(1, channels)
    junc_bias_row = junc_bias.reshape(1, channels)
    shape = jax.ShapeDtypeStruct
    bf16, f32 = jnp.bfloat16, jnp.float32
    message = shape((groups, span + 2, channels), bf16)
    chunks = shape((groups, span, channels), bf16)
    dma = pltpu.SemaphoreType.DMA

    ranks = [
        [
            (groups - 1 - group if column % 2 else group) * pipes + column
            for group in range(groups)
        ]
        for column in range(pipes)
    ]

    def exchange(value):
        return lax.all_to_all(
            value,
            ("len", "pipe"),
            split_axis=0,
            concat_axis=0,
            tiled=True,
            axis_index_groups=ranks,
        )

    def swap(value, step):
        return lax.ppermute(value, "pipe", [(i, i ^ step) for i in range(pipes)])

    def mix(backward, value, *early):
        return call(
            functools.partial(mix_kernel, backward),
            [chunks, early[0]] if backward else [chunks],
            [VMEM] * (4 if backward else 3),
            ([dma] if backward else []) + [rows_of(all_rows, channels)] * 2,
            out_specs=[VMEM, HBM] if backward else [VMEM],
            name="mix_grad" if backward else "mix",
            busy=12,
        )(value, spec_real, spec_imag, *early)

    (sent,) = call(spectrum_kernel, [message], [VMEM] * 2, name="spectrum", busy=12)(
        field, f_table
    )
    received = exchange(sent)
    (ends,) = call(
        ends_kernel, [shape((2 * groups, channels), f32)], [VMEM], name="pipe_ends"
    )(received)
    ends = [ends] + [swap(ends, step) for step in range(1, pipes)]
    (mixed,) = mix(False, received)
    mixed, *ends = lax.optimization_barrier((mixed, *ends))
    returned = exchange(mixed)
    spectra = received
    pipe_rows = [rows_of(pipes * groups, channels)] * 2
    inlet_row = inlet_ids.reshape(1, -1)
    outlet_row = outlet_ids.reshape(1, -1)
    early, total, sent, slope = call(
        functools.partial(layer_kernel, pipes),
        [shape(field.shape, bf16)] * 2 + [message, shape((8, channels), f32)],
        [VMEM] * (pipes + 11),
        [pltpu.VMEM((all_rows, channels), f32)] * 2 + pipe_rows,
        name="layer",
        busy=12,
    )(
        *ends,
        inlet_row,
        outlet_row,
        junc_weight,
        junc_bias_row,
        field,
        cot,
        f_table,
        ft_table,
        point_weight,
        bias_row,
        returned,
    )
    received = exchange(sent)
    received, spectra = lax.optimization_barrier((received, spectra))
    (both,) = call(
        pack_kernel,
        [shape((2 * groups, span + 2, channels), bf16)],
        [VMEM] * 2,
        name="pack",
    )(spectra, received)
    mixed, outputs = mix(True, received, early)
    both, behind = lax.optimization_barrier((swap(both, 2), mixed))
    across = call(split_kernel, [message] * 2, [VMEM], name="split")(both)
    spectra, received, _ = lax.optimization_barrier((spectra, received, behind))
    fields = [spectra, swap(spectra, 1), across[0], swap(across[0], 1)]
    grads = [received, swap(received, 1), across[1], swap(across[1], 1)]
    returned = exchange(mixed)
    big = shape((modes, channels, channels), f32)
    per_copy = math.gcd(modes, 2)
    grad_real, grad_imag, rows = call(
        functools.partial(weight_grad_kernel, pipes, modes, per_copy),
        [big, big, shape((8, channels), f32)],
        [VMEM] * (2 * pipes + 4),
        [rows_of(pipes * all_rows, channels)] * 2
        + [pltpu.VMEM(big.shape, f32)] * 2
        + pipe_rows
        + [pltpu.VMEM((groups, channels), f32)] * 2
        + [dma((modes // per_copy, 2))],
        out_specs=[HBM, HBM, VMEM],
        name="weight_grad",
        limit=16,
    )(*fields, *grads, inlet_row, outlet_row, junc_weight, slope)
    (grad_inputs,) = call(
        input_grad_kernel,
        [shape(field.shape, bf16)],
        [VMEM] * 5,
        [pltpu.VMEM((steps, 2, TILE, channels), bf16), dma((steps, 2))],
        out_specs=[HBM],
        name="input_grad",
    )(total, ft_table, point_weight, rows, returned)
    return (
        outputs.reshape(inputs.shape),
        grad_inputs.reshape(inputs.shape),
        grad_real,
        grad_imag,
    )


def solution(mesh):
    placed = (
        P(("len", "pipe"), None, None),
        P(("len", "pipe"), None, None),
        P(),
        P(),
        P("len", None, None),
        P("len", None, None),
        P(),
        P(),
        P(),
        P(),
    )
    return jax.shard_map(
        body,
        mesh=mesh,
        in_specs=placed,
        out_specs=(
            P(("len", "pipe"), None, None),
            P(("len", "pipe"), None, None),
            P("len", None, None),
            P("len", None, None),
        ),
        check_vma=False,
    )
```

```python
import functools
import math

import jax
import jax.numpy as jnp
import ml_dtypes
import numpy as np
from jax import lax
from jax.experimental import pallas as pl
from jax.experimental.pallas import tpu as pltpu
from jax.sharding import PartitionSpec as P

COUPLING = 0.125
TILE = 256
LANES = 128
GELU_S = math.sqrt(2.0 / math.pi)
GELU_C = 0.044715
VMEM = pl.BlockSpec(memory_space=pltpu.VMEM)
HBM = pl.BlockSpec(memory_space=pltpu.HBM)
MIB = 1024 * 1024


def half_table(cell_count, mode_count, groups):
    half = cell_count // 2
    product_index = np.arange(mode_count)[:, None] * np.arange(half)[None, :] % cell_count
    angles = product_index.astype(np.float32) * np.float32(2.0 * math.pi / cell_count)
    norm_scale = np.float32(1.0 / math.sqrt(cell_count))
    cosine = (np.cos(angles) * norm_scale).reshape(groups, -1, half)
    sine = (np.sin(angles) * norm_scale).reshape(groups, -1, half)
    table = np.concatenate([cosine, -sine], axis=1).reshape(2 * mode_count, half)
    return table.astype(ml_dtypes.bfloat16)


def row_signs(all_rows, span, channels):
    row = lax.broadcasted_iota(jnp.int32, (all_rows, channels), 0)
    per_owner = span // 2
    mode = (row // span) * per_owner + lax.rem(row, per_owner)
    return jnp.where(lax.rem(mode, 2) == 0, 1.0, -1.0).astype(jnp.float32)


def dot(left, right, left_dim=1, right_dim=0):
    return lax.dot_general(
        left,
        right,
        (((left_dim,), (right_dim,)), ((), ())),
        preferred_element_type=jnp.float32,
    )


def put(ref, at, value):
    for lane in range(ref.shape[0]):
        ref[lane, at, :] = value[:, lane * LANES : (lane + 1) * LANES]


def take(ref, at):
    return jnp.concatenate([ref[lane, at, :] for lane in range(ref.shape[0])], axis=1)


def ends_kernel(x_ref, ends_ref):
    cells, channels = x_ref.shape
    ends = [x_ref[0:1, :], x_ref[cells - 1 : cells, :], jnp.zeros((6, channels), x_ref.dtype)]
    ends_ref[...] = jnp.concatenate([part.astype(jnp.float32) for part in ends], axis=0)


def spectrum_kernel(x_ref, f_ref, spectra_ref):
    steps, all_rows, tile = f_ref.shape
    half = x_ref.shape[0] // 2
    groups, span, channels = spectra_ref.shape
    sums = []
    for base in (0, half):
        total = None
        for step in range(steps):
            at = base + step * tile
            part = dot(f_ref[step], x_ref[at : at + tile, :])
            total = part if total is None else total + part
        sums.append(total)
    spectra = sums[0] + row_signs(all_rows, span, channels) * sums[1]
    spectra = spectra.astype(jnp.bfloat16)
    for at in range(groups):
        spectra_ref[at] = spectra[at * span : (at + 1) * span]


def message_kernel(pipes, spectra_ref, *refs):
    groups, span = spectra_ref.shape[0], spectra_ref.shape[1]
    msg_ref = refs[pipes]
    ends = jnp.concatenate([refs[step][0:2, :] for step in range(pipes)], axis=0)
    ends = ends.astype(jnp.bfloat16)
    for at in range(groups):
        msg_ref[at, 0:span, :] = spectra_ref[at]
        msg_ref[at, span:, :] = ends


def extra_rows(first, second, count, channels):
    parts = [first.astype(jnp.float32), second.astype(jnp.float32)]
    if count > 2:
        parts.append(jnp.zeros((count - 2, channels), jnp.float32))
    return jnp.concatenate(parts, axis=0).astype(jnp.bfloat16)


def mix_rows(backward, r_ref, real_ref, imag_ref, out_ref, x_ref, y_ref):
    groups, modes = r_ref.shape[0], real_ref.shape[0]
    span = 2 * modes
    for source in range(groups):
        put(x_ref, pl.ds(source * span, span), r_ref[source, 0:span, :].astype(jnp.float32))
    for mode in range(modes):
        first = pl.ds(mode, groups, stride=span)
        second = pl.ds(modes + mode, groups, stride=span)
        rows = jnp.concatenate([take(x_ref, first), take(x_ref, second)], axis=0).astype(
            jnp.bfloat16
        )
        dim = 1 if backward else 0
        by_real = dot(rows, real_ref[mode], 1, dim)
        by_imag = dot(rows, imag_ref[mode], 1, dim)
        if backward:
            put(y_ref, first, by_real[:groups] + by_imag[groups:])
            put(y_ref, second, by_real[groups:] - by_imag[:groups])
        else:
            put(y_ref, first, by_real[:groups] - by_imag[groups:])
            put(y_ref, second, by_imag[:groups] + by_real[groups:])
    for source in range(groups):
        rows = take(y_ref, pl.ds(source * span, span)).astype(jnp.bfloat16)
        out_ref[source] = rows


def mix_kernel(
    pipes,
    r_ref,
    real_ref,
    imag_ref,
    inlet_ref,
    outlet_ref,
    junc_weight_ref,
    junc_bias_ref,
    out_ref,
    cond_ref,
    slope_ref,
    x_ref,
    y_ref,
    first_ref,
    last_ref,
):
    groups, rows = r_ref.shape[0], r_ref.shape[1]
    span = rows - 2 * pipes
    column = lax.axis_index("pipe")
    ends = [r_ref[group, span:rows, :].astype(jnp.float32) for group in range(groups)]
    for step in range(pipes):
        at = pl.ds(lax.bitwise_xor(column, step), groups, stride=pipes)
        for side, ref in enumerate((first_ref, last_ref)):
            row = 2 * step + side
            put(ref, at, jnp.concatenate([part[row : row + 1] for part in ends], axis=0))
    picked_in, picked_out = selection(inlet_ref, outlet_ref, pipes)
    sums = dot(picked_in, whole(first_ref)) + dot(picked_out, whole(last_ref))
    act = dot(sums.astype(jnp.bfloat16), junc_weight_ref[...]) + junc_bias_ref[...]
    sigmoid_part = jax.nn.sigmoid(act)
    junc_rows = (act * sigmoid_part).astype(jnp.bfloat16).astype(jnp.float32)
    cond_ref[...] = COUPLING * (junc_rows[0:1] + junc_rows[1:2])
    slope_ref[...] = sigmoid_part * (1.0 + act * (1.0 - sigmoid_part))
    mix_rows(False, r_ref, real_ref, imag_ref, out_ref, x_ref, y_ref)


def mix_grad_kernel(
    r_ref, real_ref, imag_ref, early_ref, out_ref, copied_ref, sem, x_ref, y_ref
):
    copy = pltpu.make_async_copy(early_ref, copied_ref, sem)
    copy.start()
    mix_rows(True, r_ref, real_ref, imag_ref, out_ref, x_ref, y_ref)
    copy.wait()


def own_pipe(pipes):
    return lax.axis_index("len") * pipes + lax.axis_index("pipe")


def selection(inlet_ref, outlet_ref, pipes):
    count = inlet_ref.shape[1]
    lane = lax.broadcasted_iota(jnp.int32, (8, count), 1)
    row = lax.broadcasted_iota(jnp.int32, (8, count), 0)
    inlets = jnp.broadcast_to(inlet_ref[...], (8, count)).astype(jnp.float32)
    outlets = jnp.broadcast_to(outlet_ref[...], (8, count)).astype(jnp.float32)
    mine = jnp.where(row == 0, inlets, outlets)
    own = jnp.sum(jnp.where(lane == own_pipe(pipes), mine, 0.0), axis=1, keepdims=True)
    return (inlets == own).astype(jnp.bfloat16), (outlets == own).astype(jnp.bfloat16)


def whole(ref):
    return take(ref, pl.ds(0, ref.shape[1])).astype(jnp.bfloat16)


def started(copies):
    for copy in copies:
        copy.start()
    return copies


def wait(copies):
    for copy in copies:
        copy.wait()


def brought(pairs, sems, base=0):
    return started(
        [
            pltpu.make_async_copy(source, target, sems.at[base + place])
            for place, (source, target) in enumerate(pairs)
        ]
    )


def layer_kernel(
    x_ref,
    cot_ref,
    f_ref,
    ft_ref,
    weight_ref,
    bias_ref,
    cond_ref,
    modes_ref,
    out_ref,
    total_ref,
    msg_ref,
    low_ref,
    high_ref,
):
    steps, all_rows, tile = f_ref.shape
    half = steps * tile
    channels = x_ref.shape[1]
    groups, rows = msg_ref.shape[0], msg_ref.shape[1]
    span = all_rows // groups
    cond = cond_ref[...]
    row = lax.broadcasted_iota(jnp.int32, (all_rows, channels), 0)
    doubled = jnp.where((row == 0) | (row == span // 2), 1.0, 2.0).astype(jnp.float32)
    signs = row_signs(all_rows, span, channels)
    modes = jnp.concatenate(
        [modes_ref[at, 0:span, :].astype(jnp.float32) for at in range(groups)], axis=0
    )
    modes = modes * doubled
    modes = (modes.astype(jnp.bfloat16), (modes * signs).astype(jnp.bfloat16))
    weight = weight_ref[...]
    bias = bias_ref[...]
    for step in range(steps):
        for side, acc_ref in enumerate((low_ref, high_ref)):
            at = pl.ds(side * half + step * tile, tile)
            pointwise = dot(x_ref[at, :], weight) + bias
            spectral = dot(ft_ref[pl.ds(step * tile, tile), :], modes[side])
            summed = pointwise + (spectral + cond).astype(jnp.bfloat16).astype(jnp.float32)
            square = summed * summed
            part = 0.5 + 0.5 * jnp.tanh(summed * (GELU_S + (GELU_S * GELU_C) * square))
            result = summed * part
            out_ref[at, :] = result.astype(jnp.bfloat16)
            slope = part + result * (1.0 - part) * (
                2.0 * GELU_S + (6.0 * GELU_S * GELU_C) * square
            )
            total = (cot_ref[at, :].astype(jnp.float32) * slope).astype(jnp.bfloat16)
            total_ref[at, :] = total
            term = dot(f_ref[step], total)
            if step == 0:
                acc_ref[...] = term
            else:
                acc_ref[...] += term
    acc = low_ref[...] + signs * high_ref[...]
    grad_cond = acc[0:1, :] * (1.0 / f_ref[0, 0:1, 0:1].astype(jnp.float32))
    upper = grad_cond.astype(jnp.bfloat16).astype(jnp.float32)
    extra = extra_rows(upper, grad_cond - upper, rows - span, channels)
    grad_spec = (acc * doubled).astype(jnp.bfloat16)
    for at in range(groups):
        msg_ref[at, 0:span, :] = grad_spec[at * span : (at + 1) * span]
        msg_ref[at, span:rows, :] = extra


def weight_grad_kernel(pipes, modes, per_copy, *refs):
    fields, grads, refs = refs[:pipes], refs[pipes : 2 * pipes], refs[2 * pipes :]
    (inlet_ref, outlet_ref, junc_weight_ref, slope_ref), refs = refs[:4], refs[4:]
    real_out, imag_out, rows_ref, x_ref, g_ref, real_ref, imag_ref = refs[:7]
    first_ref, last_ref, upper_ref, lower_ref, sems = refs[7:]
    groups, rows = grads[0].shape[0], grads[0].shape[1]
    span = 2 * modes
    for step in range(pipes):
        for source in range(groups):
            at = pl.ds((step * groups + source) * span, span)
            put(x_ref, at, fields[step][source, 0:span, :].astype(jnp.float32))
            put(g_ref, at, grads[step][source, 0:span, :].astype(jnp.float32))
    count = pipes * groups
    going = []
    for number in range(modes // per_copy):
        for mode in range(number * per_copy, (number + 1) * per_copy):
            first = pl.ds(mode, count, stride=span)
            second = pl.ds(modes + mode, count, stride=span)
            a, b = take(x_ref, first), take(x_ref, second)
            u, v = take(g_ref, first), take(g_ref, second)
            left = jnp.concatenate([a, b], axis=0).astype(jnp.bfloat16)
            right = jnp.concatenate([u, v], axis=0).astype(jnp.bfloat16)
            turned = jnp.concatenate([v, -u], axis=0).astype(jnp.bfloat16)
            real_ref[mode] = dot(left, right, 0, 0)
            imag_ref[mode] = dot(left, turned, 0, 0)
        at = pl.ds(number * per_copy, per_copy)
        going += started(
            [
                pltpu.make_async_copy(real_ref.at[at], real_out.at[at], sems.at[number, 0]),
                pltpu.make_async_copy(imag_ref.at[at], imag_out.at[at], sems.at[number, 1]),
            ]
        )
    column = lax.axis_index("pipe")
    for step in range(pipes):
        for group in range(groups):
            parts = grads[step][group, rows - 2 : rows, :].astype(jnp.float32)
            upper_ref[group : group + 1, :] = parts[0:1]
            lower_ref[group : group + 1, :] = parts[1:2]
        at = pl.ds(lax.bitwise_xor(column, step), groups, stride=pipes)
        put(first_ref, at, upper_ref[...])
        put(last_ref, at, lower_ref[...])
    picked_in, picked_out = selection(inlet_ref, outlet_ref, pipes)
    picked = picked_in + picked_out
    junc_grad = COUPLING * (dot(picked, whole(first_ref)) + dot(picked, whole(last_ref)))
    act_grad = (junc_grad * slope_ref[...]).astype(jnp.bfloat16)
    sums_grad = dot(act_grad, junc_weight_ref[...], 1, 1)
    rows_ref[...] = sums_grad.astype(jnp.bfloat16).astype(jnp.float32)
    wait(going)


def pack_kernel(first_ref, second_ref, out_ref):
    groups, rows = second_ref.shape[0], second_ref.shape[1]
    out_ref[0:groups] = first_ref[:, 0:rows, :]
    out_ref[groups : 2 * groups] = second_ref[...]


def split_kernel(both_ref, first_ref, second_ref):
    groups = first_ref.shape[0]
    first_ref[...] = both_ref[0:groups]
    second_ref[...] = both_ref[groups : 2 * groups]


def input_grad_kernel(
    total_ref, ft_ref, weight_ref, rows_ref, modes_ref, out_ref, tiles_ref, sems
):
    groups, span, channels = modes_ref.shape
    steps, tile = tiles_ref.shape[0], tiles_ref.shape[2]
    half, all_rows = steps * tile, groups * span
    back = jnp.concatenate(
        [modes_ref[at, 0:span, :].astype(jnp.float32) for at in range(groups)], axis=0
    )
    signs = row_signs(all_rows, span, channels)
    back = (back.astype(jnp.bfloat16), (back * signs).astype(jnp.bfloat16))
    weight = weight_ref[...]
    row = lax.broadcasted_iota(jnp.int32, (tile, channels), 0)
    going = []
    for step in range(steps):
        for side in range(2):
            at = pl.ds(side * half + step * tile, tile)
            grad_cells = dot(ft_ref[pl.ds(step * tile, tile), :], back[side])
            if step == 0 and side == 0:
                grad_cells = grad_cells + jnp.where(row == 0, rows_ref[0:1, :], 0.0)
            if step == steps - 1 and side == 1:
                grad_cells = grad_cells + jnp.where(row == tile - 1, rows_ref[1:2, :], 0.0)
            spread = grad_cells.astype(jnp.bfloat16).astype(jnp.float32)
            local = dot(total_ref[at, :], weight, 1, 1)
            tiles_ref[step, side] = (local + spread).astype(jnp.bfloat16)
            going += started(
                [
                    pltpu.make_async_copy(
                        tiles_ref.at[step, side], out_ref.at[at], sems.at[step, side]
                    )
                ]
            )
    wait(going)


def rows_of(count, channels):
    return pltpu.VMEM((channels // LANES, count, LANES), jnp.float32)


def call(kernel, outs, specs, scratch=(), out_specs=None, name=None, limit=8, busy=0):
    return pl.pallas_call(
        kernel,
        out_shape=outs,
        in_specs=specs,
        out_specs=out_specs if out_specs is not None else [VMEM] * len(outs),
        scratch_shapes=list(scratch),
        compiler_params=pltpu.CompilerParams(vmem_limit_bytes=limit * MIB),
        cost_estimate=pl.CostEstimate(
            flops=busy * 1_000_000_000, bytes_accessed=busy * MIB, transcendentals=0
        )
        if busy
        else None,
        name=name,
    )


def body(
    inputs,
    cotangent,
    point_weight,
    point_bias,
    spec_real,
    spec_imag,
    junc_weight,
    junc_bias,
    inlet_ids,
    outlet_ids,
):
    per_dev, cell_count, channels = inputs.shape
    assert per_dev == 1
    groups, pipes = lax.axis_size("len"), lax.axis_size("pipe")
    assert pipes == 4
    modes = spec_real.shape[0]
    span = 2 * modes
    all_rows = span * groups
    steps = cell_count // (2 * TILE)
    table = half_table(cell_count, modes * groups, groups)
    tiled = table.reshape(all_rows, steps, TILE).transpose(1, 0, 2)
    f_table = jnp.asarray(np.ascontiguousarray(tiled))
    ft_table = jnp.asarray(np.ascontiguousarray(table.T))
    field = inputs.reshape(cell_count, channels)
    cot = cotangent.reshape(cell_count, channels)
    bias_row = point_bias.reshape(1, channels)
    junc_bias_row = junc_bias.reshape(1, channels)
    shape = jax.ShapeDtypeStruct
    bf16, f32 = jnp.bfloat16, jnp.float32
    message = shape((groups, span + 2, channels), bf16)
    chunks = shape((groups, span, channels), bf16)
    dma = pltpu.SemaphoreType.DMA

    def exchange(value):
        return lax.all_to_all(value, "len", split_axis=0, concat_axis=0, tiled=True)

    def swap(value, step):
        return lax.ppermute(value, "pipe", [(i, i ^ step) for i in range(pipes)])

    mix_bufs = [rows_of(all_rows, channels)] * 2
    pipe_rows = [rows_of(pipes * groups, channels)] * 2
    inlet_row = inlet_ids.reshape(1, -1)
    outlet_row = outlet_ids.reshape(1, -1)
    (ends,) = call(
        ends_kernel, [shape((8, channels), f32)], [VMEM], name="pipe_ends", busy=4
    )(field)
    ends = [ends] + [swap(ends, step) for step in range(1, pipes)]
    (spectra,) = call(spectrum_kernel, [chunks], [VMEM] * 2, name="spectrum", busy=12)(
        field, f_table
    )
    (sent,) = call(
        functools.partial(message_kernel, pipes),
        [shape((groups, span + 2 * pipes, channels), bf16)],
        [VMEM] * (1 + pipes),
        name="message",
    )(spectra, *ends)
    received = exchange(sent)
    mixed, cond, slope = call(
        functools.partial(mix_kernel, pipes),
        [chunks, shape((1, channels), f32), shape((8, channels), f32)],
        [VMEM] * 7,
        mix_bufs + pipe_rows,
        name="mix",
        busy=12,
    )(received, spec_real, spec_imag, inlet_row, outlet_row, junc_weight, junc_bias_row)
    returned = exchange(mixed)
    spectra = received
    early, total, sent = call(
        layer_kernel,
        [shape(field.shape, bf16)] * 2 + [message],
        [VMEM] * 8,
        [pltpu.VMEM((all_rows, channels), f32)] * 2,
        name="layer",
        busy=12,
    )(field, cot, f_table, ft_table, point_weight, bias_row, cond, returned)
    received = exchange(sent)
    received, spectra = lax.optimization_barrier((received, spectra))
    (both,) = call(
        pack_kernel,
        [shape((2 * groups, span + 2, channels), bf16)],
        [VMEM] * 2,
        name="pack",
    )(spectra, received)
    mixed, outputs = call(
        mix_grad_kernel,
        [chunks, early],
        [VMEM] * 4,
        [dma] + mix_bufs,
        out_specs=[VMEM, HBM],
        name="mix_grad",
        busy=12,
    )(received, spec_real, spec_imag, early)
    both, behind = lax.optimization_barrier((swap(both, 2), mixed))
    across = call(split_kernel, [message] * 2, [VMEM], name="split")(both)
    spectra, received, _ = lax.optimization_barrier((spectra, received, behind))
    fields = [spectra, swap(spectra, 1), across[0], swap(across[0], 1)]
    grads = [received, swap(received, 1), across[1], swap(across[1], 1)]
    returned = exchange(mixed)
    big = shape((modes, channels, channels), f32)
    per_copy = math.gcd(modes, 2)
    grad_real, grad_imag, rows = call(
        functools.partial(weight_grad_kernel, pipes, modes, per_copy),
        [big, big, shape((8, channels), f32)],
        [VMEM] * (2 * pipes + 4),
        [rows_of(pipes * all_rows, channels)] * 2
        + [pltpu.VMEM(big.shape, f32)] * 2
        + pipe_rows
        + [pltpu.VMEM((groups, channels), f32)] * 2
        + [dma((modes // per_copy, 2))],
        out_specs=[HBM, HBM, VMEM],
        name="weight_grad",
        limit=16,
    )(*fields, *grads, inlet_row, outlet_row, junc_weight, slope)
    (grad_inputs,) = call(
        input_grad_kernel,
        [shape(field.shape, bf16)],
        [VMEM] * 5,
        [pltpu.VMEM((steps, 2, TILE, channels), bf16), dma((steps, 2))],
        out_specs=[HBM],
        name="input_grad",
    )(total, ft_table, point_weight, rows, returned)
    return (
        outputs.reshape(inputs.shape),
        grad_inputs.reshape(inputs.shape),
        grad_real,
        grad_imag,
    )


def solution(mesh):
    placed = (
        P(("len", "pipe"), None, None),
        P(("len", "pipe"), None, None),
        P(),
        P(),
        P("len", None, None),
        P("len", None, None),
        P(),
        P(),
        P(),
        P(),
    )
    return jax.shard_map(
        body,
        mesh=mesh,
        in_specs=placed,
        out_specs=(
            P(("len", "pipe"), None, None),
            P(("len", "pipe"), None, None),
            P("len", None, None),
            P("len", None, None),
        ),
        check_vma=False,
    )
```

```python
import functools
import math

import jax
import jax.numpy as jnp
import ml_dtypes
import numpy as np
from jax import lax
from jax.experimental import pallas as pl
from jax.experimental.pallas import tpu as pltpu
from jax.sharding import PartitionSpec as P

COUPLING = 0.125
TILE = 256
LANES = 128
GELU_S = math.sqrt(2.0 / math.pi)
GELU_C = 0.044715
VMEM = pl.BlockSpec(memory_space=pltpu.VMEM)
HBM = pl.BlockSpec(memory_space=pltpu.HBM)
MIB = 1024 * 1024


def half_table(cell_count, mode_count, groups):
    half = cell_count // 2
    product_index = np.arange(mode_count)[:, None] * np.arange(half)[None, :] % cell_count
    angles = product_index.astype(np.float32) * np.float32(2.0 * math.pi / cell_count)
    norm_scale = np.float32(1.0 / math.sqrt(cell_count))
    cosine = (np.cos(angles) * norm_scale).reshape(groups, -1, half)
    sine = (np.sin(angles) * norm_scale).reshape(groups, -1, half)
    table = np.concatenate([cosine, -sine], axis=1).reshape(2 * mode_count, half)
    return table.astype(ml_dtypes.bfloat16)


def row_signs(all_rows, span, channels):
    row = lax.broadcasted_iota(jnp.int32, (all_rows, channels), 0)
    per_owner = span // 2
    mode = (row // span) * per_owner + lax.rem(row, per_owner)
    return jnp.where(lax.rem(mode, 2) == 0, 1.0, -1.0).astype(jnp.float32)


def dot(left, right, left_dim=1, right_dim=0):
    return lax.dot_general(
        left,
        right,
        (((left_dim,), (right_dim,)), ((), ())),
        preferred_element_type=jnp.float32,
    )


def put(ref, at, value):
    for lane in range(ref.shape[0]):
        ref[lane, at, :] = value[:, lane * LANES : (lane + 1) * LANES]


def take(ref, at):
    return jnp.concatenate([ref[lane, at, :] for lane in range(ref.shape[0])], axis=1)


def ends_kernel(x_ref, ends_ref):
    cells, channels = x_ref.shape
    ends = [x_ref[0:1, :], x_ref[cells - 1 : cells, :], jnp.zeros((6, channels), x_ref.dtype)]
    ends_ref[...] = jnp.concatenate([part.astype(jnp.float32) for part in ends], axis=0)


def spectrum_kernel(x_ref, f_ref, spectra_ref):
    steps, all_rows, tile = f_ref.shape
    half = x_ref.shape[0] // 2
    groups, span, channels = spectra_ref.shape
    sums = []
    for base in (0, half):
        total = None
        for step in range(steps):
            at = base + step * tile
            part = dot(f_ref[step], x_ref[at : at + tile, :])
            total = part if total is None else total + part
        sums.append(total)
    spectra = sums[0] + row_signs(all_rows, span, channels) * sums[1]
    spectra = spectra.astype(jnp.bfloat16)
    for at in range(groups):
        spectra_ref[at] = spectra[at * span : (at + 1) * span]


def message_kernel(pipes, spectra_ref, *refs):
    groups, span = spectra_ref.shape[0], spectra_ref.shape[1]
    msg_ref = refs[pipes]
    ends = jnp.concatenate([refs[step][0:2, :] for step in range(pipes)], axis=0)
    ends = ends.astype(jnp.bfloat16)
    for at in range(groups):
        msg_ref[at, 0:span, :] = spectra_ref[at]
        msg_ref[at, span:, :] = ends


def extra_rows(first, second, count, channels):
    parts = [first.astype(jnp.float32), second.astype(jnp.float32)]
    if count > 2:
        parts.append(jnp.zeros((count - 2, channels), jnp.float32))
    return jnp.concatenate(parts, axis=0).astype(jnp.bfloat16)


def mix_rows(backward, r_ref, real_ref, imag_ref, out_ref, x_ref, y_ref):
    groups, modes = r_ref.shape[0], real_ref.shape[0]
    span = 2 * modes
    for source in range(groups):
        put(x_ref, pl.ds(source * span, span), r_ref[source, 0:span, :].astype(jnp.float32))
    for mode in range(modes):
        first = pl.ds(mode, groups, stride=span)
        second = pl.ds(modes + mode, groups, stride=span)
        rows = jnp.concatenate([take(x_ref, first), take(x_ref, second)], axis=0).astype(
            jnp.bfloat16
        )
        dim = 1 if backward else 0
        by_real = dot(rows, real_ref[mode], 1, dim)
        by_imag = dot(rows, imag_ref[mode], 1, dim)
        if backward:
            put(y_ref, first, by_real[:groups] + by_imag[groups:])
            put(y_ref, second, by_real[groups:] - by_imag[:groups])
        else:
            put(y_ref, first, by_real[:groups] - by_imag[groups:])
            put(y_ref, second, by_imag[:groups] + by_real[groups:])
    for source in range(groups):
        rows = take(y_ref, pl.ds(source * span, span)).astype(jnp.bfloat16)
        out_ref[source] = rows


def mix_kernel(
    pipes,
    r_ref,
    real_ref,
    imag_ref,
    inlet_ref,
    outlet_ref,
    junc_weight_ref,
    junc_bias_ref,
    out_ref,
    cond_ref,
    slope_ref,
    x_ref,
    y_ref,
    first_ref,
    last_ref,
):
    groups, rows = r_ref.shape[0], r_ref.shape[1]
    span = rows - 2 * pipes
    column = lax.axis_index("pipe")
    ends = [r_ref[group, span:rows, :].astype(jnp.float32) for group in range(groups)]
    for step in range(pipes):
        at = pl.ds(lax.bitwise_xor(column, step), groups, stride=pipes)
        for side, ref in enumerate((first_ref, last_ref)):
            row = 2 * step + side
            put(ref, at, jnp.concatenate([part[row : row + 1] for part in ends], axis=0))
    picked_in, picked_out = selection(inlet_ref, outlet_ref, pipes)
    sums = dot(picked_in, whole(first_ref)) + dot(picked_out, whole(last_ref))
    act = dot(sums.astype(jnp.bfloat16), junc_weight_ref[...]) + junc_bias_ref[...]
    sigmoid_part = jax.nn.sigmoid(act)
    junc_rows = (act * sigmoid_part).astype(jnp.bfloat16).astype(jnp.float32)
    cond_ref[...] = COUPLING * (junc_rows[0:1] + junc_rows[1:2])
    slope_ref[...] = sigmoid_part * (1.0 + act * (1.0 - sigmoid_part))
    mix_rows(False, r_ref, real_ref, imag_ref, out_ref, x_ref, y_ref)


def mix_grad_kernel(
    r_ref, real_ref, imag_ref, early_ref, out_ref, copied_ref, sem, x_ref, y_ref
):
    copy = pltpu.make_async_copy(early_ref, copied_ref, sem)
    copy.start()
    mix_rows(True, r_ref, real_ref, imag_ref, out_ref, x_ref, y_ref)
    copy.wait()


def own_pipe(pipes):
    return lax.axis_index("len") * pipes + lax.axis_index("pipe")


def selection(inlet_ref, outlet_ref, pipes):
    count = inlet_ref.shape[1]
    lane = lax.broadcasted_iota(jnp.int32, (8, count), 1)
    row = lax.broadcasted_iota(jnp.int32, (8, count), 0)
    inlets = jnp.broadcast_to(inlet_ref[...], (8, count)).astype(jnp.float32)
    outlets = jnp.broadcast_to(outlet_ref[...], (8, count)).astype(jnp.float32)
    mine = jnp.where(row == 0, inlets, outlets)
    own = jnp.sum(jnp.where(lane == own_pipe(pipes), mine, 0.0), axis=1, keepdims=True)
    return (inlets == own).astype(jnp.bfloat16), (outlets == own).astype(jnp.bfloat16)


def whole(ref):
    return take(ref, pl.ds(0, ref.shape[1])).astype(jnp.bfloat16)


def started(copies):
    for copy in copies:
        copy.start()
    return copies


def wait(copies):
    for copy in copies:
        copy.wait()


def brought(pairs, sems, base=0):
    return started(
        [
            pltpu.make_async_copy(source, target, sems.at[base + place])
            for place, (source, target) in enumerate(pairs)
        ]
    )


def layer_kernel(
    x_ref,
    cot_ref,
    f_ref,
    ft_ref,
    weight_ref,
    bias_ref,
    cond_ref,
    modes_ref,
    out_ref,
    total_ref,
    msg_ref,
    low_ref,
    high_ref,
):
    steps, all_rows, tile = f_ref.shape
    half = steps * tile
    channels = x_ref.shape[1]
    groups, rows = msg_ref.shape[0], msg_ref.shape[1]
    span = all_rows // groups
    cond = cond_ref[...]
    row = lax.broadcasted_iota(jnp.int32, (all_rows, channels), 0)
    doubled = jnp.where((row == 0) | (row == span // 2), 1.0, 2.0).astype(jnp.float32)
    signs = row_signs(all_rows, span, channels)
    modes = jnp.concatenate(
        [modes_ref[at, 0:span, :].astype(jnp.float32) for at in range(groups)], axis=0
    )
    modes = modes * doubled
    modes = (modes.astype(jnp.bfloat16), (modes * signs).astype(jnp.bfloat16))
    weight = weight_ref[...]
    bias = bias_ref[...]
    for side, acc_ref in enumerate((low_ref, high_ref)):
        for step in range(steps):
            at = pl.ds(side * half + step * tile, tile)
            pointwise = dot(x_ref[at, :], weight) + bias
            spectral = dot(ft_ref[pl.ds(step * tile, tile), :], modes[side])
            summed = pointwise + (spectral + cond).astype(jnp.bfloat16).astype(jnp.float32)
            square = summed * summed
            part = 0.5 + 0.5 * jnp.tanh(summed * (GELU_S + (GELU_S * GELU_C) * square))
            result = summed * part
            out_ref[at, :] = result.astype(jnp.bfloat16)
            slope = part + result * (1.0 - part) * (
                2.0 * GELU_S + (6.0 * GELU_S * GELU_C) * square
            )
            total = (cot_ref[at, :].astype(jnp.float32) * slope).astype(jnp.bfloat16)
            total_ref[at, :] = total
            term = dot(f_ref[step], total)
            if step == 0:
                acc_ref[...] = term
            else:
                acc_ref[...] += term
    acc = low_ref[...] + signs * high_ref[...]
    grad_cond = acc[0:1, :] * (1.0 / f_ref[0, 0:1, 0:1].astype(jnp.float32))
    upper = grad_cond.astype(jnp.bfloat16).astype(jnp.float32)
    extra = extra_rows(upper, grad_cond - upper, rows - span, channels)
    grad_spec = (acc * doubled).astype(jnp.bfloat16)
    for at in range(groups):
        msg_ref[at, 0:span, :] = grad_spec[at * span : (at + 1) * span]
        msg_ref[at, span:rows, :] = extra


def weight_grad_kernel(pipes, modes, per_copy, *refs):
    fields, grads, refs = refs[:pipes], refs[pipes : 2 * pipes], refs[2 * pipes :]
    (inlet_ref, outlet_ref, junc_weight_ref, slope_ref), refs = refs[:4], refs[4:]
    real_out, imag_out, rows_ref, x_ref, g_ref, real_ref, imag_ref = refs[:7]
    first_ref, last_ref, upper_ref, lower_ref, sems = refs[7:]
    groups, rows = grads[0].shape[0], grads[0].shape[1]
    span = 2 * modes
    for step in range(pipes):
        for source in range(groups):
            at = pl.ds((step * groups + source) * span, span)
            put(x_ref, at, fields[step][source, 0:span, :].astype(jnp.float32))
            put(g_ref, at, grads[step][source, 0:span, :].astype(jnp.float32))
    count = pipes * groups
    going = []
    for number in range(modes // per_copy):
        for mode in range(number * per_copy, (number + 1) * per_copy):
            first = pl.ds(mode, count, stride=span)
            second = pl.ds(modes + mode, count, stride=span)
            a, b = take(x_ref, first), take(x_ref, second)
            u, v = take(g_ref, first), take(g_ref, second)
            left = jnp.concatenate([a, b], axis=0).astype(jnp.bfloat16)
            right = jnp.concatenate([u, v], axis=0).astype(jnp.bfloat16)
            turned = jnp.concatenate([v, -u], axis=0).astype(jnp.bfloat16)
            real_ref[mode] = dot(left, right, 0, 0)
            imag_ref[mode] = dot(left, turned, 0, 0)
        at = pl.ds(number * per_copy, per_copy)
        going += started(
            [
                pltpu.make_async_copy(real_ref.at[at], real_out.at[at], sems.at[number, 0]),
                pltpu.make_async_copy(imag_ref.at[at], imag_out.at[at], sems.at[number, 1]),
            ]
        )
    column = lax.axis_index("pipe")
    for step in range(pipes):
        for group in range(groups):
            parts = grads[step][group, rows - 2 : rows, :].astype(jnp.float32)
            upper_ref[group : group + 1, :] = parts[0:1]
            lower_ref[group : group + 1, :] = parts[1:2]
        at = pl.ds(lax.bitwise_xor(column, step), groups, stride=pipes)
        put(first_ref, at, upper_ref[...])
        put(last_ref, at, lower_ref[...])
    picked_in, picked_out = selection(inlet_ref, outlet_ref, pipes)
    picked = picked_in + picked_out
    junc_grad = COUPLING * (dot(picked, whole(first_ref)) + dot(picked, whole(last_ref)))
    act_grad = (junc_grad * slope_ref[...]).astype(jnp.bfloat16)
    sums_grad = dot(act_grad, junc_weight_ref[...], 1, 1)
    rows_ref[...] = sums_grad.astype(jnp.bfloat16).astype(jnp.float32)
    wait(going)


def pack_kernel(first_ref, second_ref, out_ref):
    groups, rows = second_ref.shape[0], second_ref.shape[1]
    out_ref[0:groups] = first_ref[:, 0:rows, :]
    out_ref[groups : 2 * groups] = second_ref[...]


def split_kernel(both_ref, first_ref, second_ref):
    groups = first_ref.shape[0]
    first_ref[...] = both_ref[0:groups]
    second_ref[...] = both_ref[groups : 2 * groups]


def input_grad_kernel(
    total_ref, ft_ref, weight_ref, rows_ref, modes_ref, out_ref, tiles_ref, sems
):
    groups, span, channels = modes_ref.shape
    steps, tile = tiles_ref.shape[0], tiles_ref.shape[2]
    half, all_rows = steps * tile, groups * span
    back = jnp.concatenate(
        [modes_ref[at, 0:span, :].astype(jnp.float32) for at in range(groups)], axis=0
    )
    signs = row_signs(all_rows, span, channels)
    back = (back.astype(jnp.bfloat16), (back * signs).astype(jnp.bfloat16))
    weight = weight_ref[...]
    row = lax.broadcasted_iota(jnp.int32, (tile, channels), 0)
    going = []
    for side in range(2):
        for step in range(steps):
            at = pl.ds(side * half + step * tile, tile)
            grad_cells = dot(ft_ref[pl.ds(step * tile, tile), :], back[side])
            if step == 0 and side == 0:
                grad_cells = grad_cells + jnp.where(row == 0, rows_ref[0:1, :], 0.0)
            if step == steps - 1 and side == 1:
                grad_cells = grad_cells + jnp.where(row == tile - 1, rows_ref[1:2, :], 0.0)
            spread = grad_cells.astype(jnp.bfloat16).astype(jnp.float32)
            local = dot(total_ref[at, :], weight, 1, 1)
            tiles_ref[step, side] = (local + spread).astype(jnp.bfloat16)
            going += started(
                [
                    pltpu.make_async_copy(
                        tiles_ref.at[step, side], out_ref.at[at], sems.at[step, side]
                    )
                ]
            )
    wait(going)


def rows_of(count, channels):
    return pltpu.VMEM((channels // LANES, count, LANES), jnp.float32)


def call(kernel, outs, specs, scratch=(), out_specs=None, name=None, limit=8, busy=0):
    return pl.pallas_call(
        kernel,
        out_shape=outs,
        in_specs=specs,
        out_specs=out_specs if out_specs is not None else [VMEM] * len(outs),
        scratch_shapes=list(scratch),
        compiler_params=pltpu.CompilerParams(vmem_limit_bytes=limit * MIB),
        cost_estimate=pl.CostEstimate(
            flops=busy * 1_000_000_000, bytes_accessed=busy * MIB, transcendentals=0
        )
        if busy
        else None,
        name=name,
    )


def body(
    inputs,
    cotangent,
    point_weight,
    point_bias,
    spec_real,
    spec_imag,
    junc_weight,
    junc_bias,
    inlet_ids,
    outlet_ids,
):
    per_dev, cell_count, channels = inputs.shape
    assert per_dev == 1
    groups, pipes = lax.axis_size("len"), lax.axis_size("pipe")
    assert pipes == 4
    modes = spec_real.shape[0]
    span = 2 * modes
    all_rows = span * groups
    steps = cell_count // (2 * TILE)
    table = half_table(cell_count, modes * groups, groups)
    tiled = table.reshape(all_rows, steps, TILE).transpose(1, 0, 2)
    f_table = jnp.asarray(np.ascontiguousarray(tiled))
    ft_table = jnp.asarray(np.ascontiguousarray(table.T))
    field = inputs.reshape(cell_count, channels)
    cot = cotangent.reshape(cell_count, channels)
    bias_row = point_bias.reshape(1, channels)
    junc_bias_row = junc_bias.reshape(1, channels)
    shape = jax.ShapeDtypeStruct
    bf16, f32 = jnp.bfloat16, jnp.float32
    message = shape((groups, span + 2, channels), bf16)
    chunks = shape((groups, span, channels), bf16)
    dma = pltpu.SemaphoreType.DMA

    def exchange(value):
        return lax.all_to_all(value, "len", split_axis=0, concat_axis=0, tiled=True)

    def swap(value, step):
        return lax.ppermute(value, "pipe", [(i, i ^ step) for i in range(pipes)])

    mix_bufs = [rows_of(all_rows, channels)] * 2
    pipe_rows = [rows_of(pipes * groups, channels)] * 2
    inlet_row = inlet_ids.reshape(1, -1)
    outlet_row = outlet_ids.reshape(1, -1)
    (ends,) = call(
        ends_kernel, [shape((8, channels), f32)], [VMEM], name="pipe_ends", busy=4
    )(field)
    ends = [ends] + [swap(ends, step) for step in range(1, pipes)]
    (spectra,) = call(spectrum_kernel, [chunks], [VMEM] * 2, name="spectrum", busy=12)(
        field, f_table
    )
    (sent,) = call(
        functools.partial(message_kernel, pipes),
        [shape((groups, span + 2 * pipes, channels), bf16)],
        [VMEM] * (1 + pipes),
        name="message",
    )(spectra, *ends)
    received = exchange(sent)
    mixed, cond, slope = call(
        functools.partial(mix_kernel, pipes),
        [chunks, shape((1, channels), f32), shape((8, channels), f32)],
        [VMEM] * 7,
        mix_bufs + pipe_rows,
        name="mix",
        busy=12,
    )(received, spec_real, spec_imag, inlet_row, outlet_row, junc_weight, junc_bias_row)
    returned = exchange(mixed)
    spectra = received
    early, total, sent = call(
        layer_kernel,
        [shape(field.shape, bf16)] * 2 + [message],
        [VMEM] * 8,
        [pltpu.VMEM((all_rows, channels), f32)] * 2,
        name="layer",
        busy=12,
    )(field, cot, f_table, ft_table, point_weight, bias_row, cond, returned)
    received = exchange(sent)
    received, spectra = lax.optimization_barrier((received, spectra))
    (both,) = call(
        pack_kernel,
        [shape((2 * groups, span + 2, channels), bf16)],
        [VMEM] * 2,
        name="pack",
    )(spectra, received)
    mixed, outputs = call(
        mix_grad_kernel,
        [chunks, early],
        [VMEM] * 4,
        [dma] + mix_bufs,
        out_specs=[VMEM, HBM],
        name="mix_grad",
        busy=12,
    )(received, spec_real, spec_imag, early)
    both, behind = lax.optimization_barrier((swap(both, 2), mixed))
    across = call(split_kernel, [message] * 2, [VMEM], name="split")(both)
    spectra, received, _ = lax.optimization_barrier((spectra, received, behind))
    fields = [spectra, swap(spectra, 1), across[0], swap(across[0], 1)]
    grads = [received, swap(received, 1), across[1], swap(across[1], 1)]
    returned = exchange(mixed)
    big = shape((modes, channels, channels), f32)
    per_copy = math.gcd(modes, 2)
    grad_real, grad_imag, rows = call(
        functools.partial(weight_grad_kernel, pipes, modes, per_copy),
        [big, big, shape((8, channels), f32)],
        [VMEM] * (2 * pipes + 4),
        [rows_of(pipes * all_rows, channels)] * 2
        + [pltpu.VMEM(big.shape, f32)] * 2
        + pipe_rows
        + [pltpu.VMEM((groups, channels), f32)] * 2
        + [dma((modes // per_copy, 2))],
        out_specs=[HBM, HBM, VMEM],
        name="weight_grad",
        limit=16,
    )(*fields, *grads, inlet_row, outlet_row, junc_weight, slope)
    (grad_inputs,) = call(
        input_grad_kernel,
        [shape(field.shape, bf16)],
        [VMEM] * 5,
        [pltpu.VMEM((steps, 2, TILE, channels), bf16), dma((steps, 2))],
        out_specs=[HBM],
        name="input_grad",
    )(total, ft_table, point_weight, rows, returned)
    return (
        outputs.reshape(inputs.shape),
        grad_inputs.reshape(inputs.shape),
        grad_real,
        grad_imag,
    )


def solution(mesh):
    placed = (
        P(("len", "pipe"), None, None),
        P(("len", "pipe"), None, None),
        P(),
        P(),
        P("len", None, None),
        P("len", None, None),
        P(),
        P(),
        P(),
        P(),
    )
    return jax.shard_map(
        body,
        mesh=mesh,
        in_specs=placed,
        out_specs=(
            P(("len", "pipe"), None, None),
            P(("len", "pipe"), None, None),
            P("len", None, None),
            P("len", None, None),
        ),
        check_vma=False,
    )
```

```python
import functools
import math

import jax
import jax.numpy as jnp
import ml_dtypes
import numpy as np
from jax import lax
from jax.experimental import pallas as pl
from jax.experimental.pallas import tpu as pltpu
from jax.sharding import PartitionSpec as P

COUPLING = 0.125
TILE = 256
LANES = 128
PIECE = 64
GELU_S = math.sqrt(2.0 / math.pi)
GELU_C = 0.044715
VMEM = pl.BlockSpec(memory_space=pltpu.VMEM)
HBM = pl.BlockSpec(memory_space=pltpu.HBM)
MIB = 1024 * 1024


def half_table(cell_count, mode_count, groups):
    half = cell_count // 2
    product_index = np.arange(mode_count)[:, None] * np.arange(half)[None, :] % cell_count
    angles = product_index.astype(np.float32) * np.float32(2.0 * math.pi / cell_count)
    norm_scale = np.float32(1.0 / math.sqrt(cell_count))
    cosine = (np.cos(angles) * norm_scale).reshape(groups, -1, half)
    sine = (np.sin(angles) * norm_scale).reshape(groups, -1, half)
    table = np.concatenate([cosine, -sine], axis=1).reshape(2 * mode_count, half)
    return table.astype(ml_dtypes.bfloat16)


def row_signs(all_rows, span, channels):
    row = lax.broadcasted_iota(jnp.int32, (all_rows, channels), 0)
    per_owner = span // 2
    mode = (row // span) * per_owner + lax.rem(row, per_owner)
    return jnp.where(lax.rem(mode, 2) == 0, 1.0, -1.0).astype(jnp.float32)


def dot(left, right, left_dim=1, right_dim=0):
    return lax.dot_general(
        left,
        right,
        (((left_dim,), (right_dim,)), ((), ())),
        preferred_element_type=jnp.float32,
    )


def put(ref, at, value):
    for lane in range(ref.shape[0]):
        ref[lane, at, :] = value[:, lane * LANES : (lane + 1) * LANES]


def take(ref, at):
    return jnp.concatenate([ref[lane, at, :] for lane in range(ref.shape[0])], axis=1)


def ends_kernel(x_ref, ends_ref, edges_ref, sems):
    cells, channels = x_ref.shape
    rows = edges_ref.shape[1]
    copies = [
        pltpu.make_async_copy(x_ref.at[pl.ds(start, rows)], edges_ref.at[side], sems.at[side])
        for side, start in enumerate((0, cells - rows))
    ]
    for copy in copies:
        copy.start()
    for copy in copies:
        copy.wait()
    ends = [edges_ref[0, 0:1, :], edges_ref[1, rows - 1 : rows, :]]
    ends = [part.astype(jnp.float32) for part in ends]
    ends_ref[...] = jnp.concatenate(ends + [jnp.zeros((6, channels), jnp.float32)], axis=0)


def spectrum_kernel(x_ref, f_ref, spectra_ref):
    steps, all_rows, tile = f_ref.shape
    half = x_ref.shape[0] // 2
    groups, span, channels = spectra_ref.shape
    sums = []
    for base in (0, half):
        total = None
        for step in range(steps):
            at = base + step * tile
            part = dot(f_ref[step], x_ref[at : at + tile, :])
            total = part if total is None else total + part
        sums.append(total)
    spectra = sums[0] + row_signs(all_rows, span, channels) * sums[1]
    spectra = spectra.astype(jnp.bfloat16)
    for at in range(groups):
        spectra_ref[at] = spectra[at * span : (at + 1) * span]


def message_kernel(pipes, spectra_ref, *refs):
    groups, span = spectra_ref.shape[0], spectra_ref.shape[1]
    msg_ref = refs[pipes]
    ends = jnp.concatenate([refs[step][0:2, :] for step in range(pipes)], axis=0)
    ends = ends.astype(jnp.bfloat16)
    for at in range(groups):
        msg_ref[at, 0:span, :] = spectra_ref[at]
        msg_ref[at, span:, :] = ends


def extra_rows(first, second, count, channels):
    parts = [first.astype(jnp.float32), second.astype(jnp.float32)]
    if count > 2:
        parts.append(jnp.zeros((count - 2, channels), jnp.float32))
    return jnp.concatenate(parts, axis=0).astype(jnp.bfloat16)


def mix_rows(backward, r_ref, real_ref, imag_ref, out_ref, x_ref, y_ref):
    groups, modes = r_ref.shape[0], real_ref.shape[0]
    span = 2 * modes
    for source in range(groups):
        put(x_ref, pl.ds(source * span, span), r_ref[source, 0:span, :].astype(jnp.float32))
    for mode in range(modes):
        first = pl.ds(mode, groups, stride=span)
        second = pl.ds(modes + mode, groups, stride=span)
        rows = jnp.concatenate([take(x_ref, first), take(x_ref, second)], axis=0).astype(
            jnp.bfloat16
        )
        dim = 1 if backward else 0
        by_real = dot(rows, real_ref[mode], 1, dim)
        by_imag = dot(rows, imag_ref[mode], 1, dim)
        if backward:
            put(y_ref, first, by_real[:groups] + by_imag[groups:])
            put(y_ref, second, by_real[groups:] - by_imag[:groups])
        else:
            put(y_ref, first, by_real[:groups] - by_imag[groups:])
            put(y_ref, second, by_imag[:groups] + by_real[groups:])
    for source in range(groups):
        rows = take(y_ref, pl.ds(source * span, span)).astype(jnp.bfloat16)
        out_ref[source] = rows


def mix_kernel(
    pipes,
    r_ref,
    real_ref,
    imag_ref,
    inlet_ref,
    outlet_ref,
    junc_weight_ref,
    junc_bias_ref,
    out_ref,
    cond_ref,
    slope_ref,
    x_ref,
    y_ref,
    first_ref,
    last_ref,
):
    groups, rows = r_ref.shape[0], r_ref.shape[1]
    span = rows - 2 * pipes
    column = lax.axis_index("pipe")
    ends = [r_ref[group, span:rows, :].astype(jnp.float32) for group in range(groups)]
    for step in range(pipes):
        at = pl.ds(lax.bitwise_xor(column, step), groups, stride=pipes)
        for side, ref in enumerate((first_ref, last_ref)):
            row = 2 * step + side
            put(ref, at, jnp.concatenate([part[row : row + 1] for part in ends], axis=0))
    picked_in, picked_out = selection(inlet_ref, outlet_ref, pipes)
    sums = dot(picked_in, whole(first_ref)) + dot(picked_out, whole(last_ref))
    act = dot(sums.astype(jnp.bfloat16), junc_weight_ref[...]) + junc_bias_ref[...]
    sigmoid_part = jax.nn.sigmoid(act)
    junc_rows = (act * sigmoid_part).astype(jnp.bfloat16).astype(jnp.float32)
    cond_ref[...] = COUPLING * (junc_rows[0:1] + junc_rows[1:2])
    slope_ref[...] = sigmoid_part * (1.0 + act * (1.0 - sigmoid_part))
    mix_rows(False, r_ref, real_ref, imag_ref, out_ref, x_ref, y_ref)


def mix_grad_kernel(
    r_ref, real_ref, imag_ref, early_ref, out_ref, copied_ref, sem, x_ref, y_ref
):
    copy = pltpu.make_async_copy(early_ref, copied_ref, sem)
    copy.start()
    mix_rows(True, r_ref, real_ref, imag_ref, out_ref, x_ref, y_ref)
    copy.wait()


def own_pipe(pipes):
    return lax.axis_index("len") * pipes + lax.axis_index("pipe")


def selection(inlet_ref, outlet_ref, pipes):
    count = inlet_ref.shape[1]
    lane = lax.broadcasted_iota(jnp.int32, (8, count), 1)
    row = lax.broadcasted_iota(jnp.int32, (8, count), 0)
    inlets = jnp.broadcast_to(inlet_ref[...], (8, count)).astype(jnp.float32)
    outlets = jnp.broadcast_to(outlet_ref[...], (8, count)).astype(jnp.float32)
    mine = jnp.where(row == 0, inlets, outlets)
    own = jnp.sum(jnp.where(lane == own_pipe(pipes), mine, 0.0), axis=1, keepdims=True)
    return (inlets == own).astype(jnp.bfloat16), (outlets == own).astype(jnp.bfloat16)


def whole(ref):
    return take(ref, pl.ds(0, ref.shape[1])).astype(jnp.bfloat16)


def started(copies):
    for copy in copies:
        copy.start()
    return copies


def wait(copies):
    for copy in copies:
        copy.wait()


def brought(pairs, sems, base=0):
    return started(
        [
            pltpu.make_async_copy(source, target, sems.at[base + place])
            for place, (source, target) in enumerate(pairs)
        ]
    )


def layer_kernel(
    x_ref,
    cot_ref,
    f_ref,
    ft_ref,
    weight_ref,
    bias_ref,
    cond_ref,
    modes_ref,
    out_ref,
    total_ref,
    msg_ref,
    low_ref,
    high_ref,
    summed_ref,
):
    steps, all_rows, tile = f_ref.shape
    half = steps * tile
    channels = x_ref.shape[1]
    groups, rows = msg_ref.shape[0], msg_ref.shape[1]
    span = all_rows // groups
    cond = cond_ref[...]
    row = lax.broadcasted_iota(jnp.int32, (all_rows, channels), 0)
    doubled = jnp.where((row == 0) | (row == span // 2), 1.0, 2.0).astype(jnp.float32)
    signs = row_signs(all_rows, span, channels)
    modes = jnp.concatenate(
        [modes_ref[at, 0:span, :].astype(jnp.float32) for at in range(groups)], axis=0
    )
    modes = modes * doubled
    modes = (modes.astype(jnp.bfloat16), (modes * signs).astype(jnp.bfloat16))
    weight = weight_ref[...]
    bias = bias_ref[...]
    for side, acc_ref in enumerate((low_ref, high_ref)):
        for step in range(steps):
            base = side * half + step * tile
            at = pl.ds(base, tile)
            pointwise = dot(x_ref[at, :], weight) + bias
            spectral = dot(ft_ref[pl.ds(step * tile, tile), :], modes[side])
            pre = (spectral + cond).astype(jnp.bfloat16).astype(jnp.float32)
            summed_ref[at, :] = pointwise + pre
            for piece in range(tile // PIECE):
                here = pl.ds(base + piece * PIECE, PIECE)
                summed = summed_ref[here, :]
                square = summed * summed
                part = 0.5 + 0.5 * jnp.tanh(summed * (GELU_S + (GELU_S * GELU_C) * square))
                result = summed * part
                out_ref[here, :] = result.astype(jnp.bfloat16)
                slope = part + result * (1.0 - part) * (
                    2.0 * GELU_S + (6.0 * GELU_S * GELU_C) * square
                )
                total = cot_ref[here, :].astype(jnp.float32) * slope
                total_ref[here, :] = total.astype(jnp.bfloat16)
            term = dot(f_ref[step], total_ref[at, :])
            if step == 0:
                acc_ref[...] = term
            else:
                acc_ref[...] += term
    acc = low_ref[...] + signs * high_ref[...]
    grad_cond = acc[0:1, :] * (1.0 / f_ref[0, 0:1, 0:1].astype(jnp.float32))
    upper = grad_cond.astype(jnp.bfloat16).astype(jnp.float32)
    extra = extra_rows(upper, grad_cond - upper, rows - span, channels)
    grad_spec = (acc * doubled).astype(jnp.bfloat16)
    for at in range(groups):
        msg_ref[at, 0:span, :] = grad_spec[at * span : (at + 1) * span]
        msg_ref[at, span:rows, :] = extra


def weight_grad_kernel(pipes, modes, per_copy, *refs):
    fields, grads, refs = refs[:pipes], refs[pipes : 2 * pipes], refs[2 * pipes :]
    (inlet_ref, outlet_ref, junc_weight_ref, slope_ref), refs = refs[:4], refs[4:]
    real_out, imag_out, rows_ref, x_ref, g_ref, real_ref, imag_ref = refs[:7]
    first_ref, last_ref, upper_ref, lower_ref, sems = refs[7:]
    groups, rows = grads[0].shape[0], grads[0].shape[1]
    span = 2 * modes
    for step in range(pipes):
        for source in range(groups):
            at = pl.ds((step * groups + source) * span, span)
            put(x_ref, at, fields[step][source, 0:span, :].astype(jnp.float32))
            put(g_ref, at, grads[step][source, 0:span, :].astype(jnp.float32))
    count = pipes * groups
    going = []
    for number in range(modes // per_copy):
        for mode in range(number * per_copy, (number + 1) * per_copy):
            first = pl.ds(mode, count, stride=span)
            second = pl.ds(modes + mode, count, stride=span)
            a, b = take(x_ref, first), take(x_ref, second)
            u, v = take(g_ref, first), take(g_ref, second)
            left = jnp.concatenate([a, b], axis=0).astype(jnp.bfloat16)
            right = jnp.concatenate([u, v], axis=0).astype(jnp.bfloat16)
            turned = jnp.concatenate([v, -u], axis=0).astype(jnp.bfloat16)
            real_ref[mode] = dot(left, right, 0, 0)
            imag_ref[mode] = dot(left, turned, 0, 0)
        at = pl.ds(number * per_copy, per_copy)
        going += started(
            [
                pltpu.make_async_copy(real_ref.at[at], real_out.at[at], sems.at[number, 0]),
                pltpu.make_async_copy(imag_ref.at[at], imag_out.at[at], sems.at[number, 1]),
            ]
        )
    column = lax.axis_index("pipe")
    for step in range(pipes):
        for group in range(groups):
            parts = grads[step][group, rows - 2 : rows, :].astype(jnp.float32)
            upper_ref[group : group + 1, :] = parts[0:1]
            lower_ref[group : group + 1, :] = parts[1:2]
        at = pl.ds(lax.bitwise_xor(column, step), groups, stride=pipes)
        put(first_ref, at, upper_ref[...])
        put(last_ref, at, lower_ref[...])
    picked_in, picked_out = selection(inlet_ref, outlet_ref, pipes)
    picked = picked_in + picked_out
    junc_grad = COUPLING * (dot(picked, whole(first_ref)) + dot(picked, whole(last_ref)))
    act_grad = (junc_grad * slope_ref[...]).astype(jnp.bfloat16)
    sums_grad = dot(act_grad, junc_weight_ref[...], 1, 1)
    rows_ref[...] = sums_grad.astype(jnp.bfloat16).astype(jnp.float32)
    wait(going)


def pack_kernel(first_ref, second_ref, out_ref):
    groups, rows = second_ref.shape[0], second_ref.shape[1]
    out_ref[0:groups] = first_ref[:, 0:rows, :]
    out_ref[groups : 2 * groups] = second_ref[...]


def split_kernel(both_ref, first_ref, second_ref):
    groups = first_ref.shape[0]
    first_ref[...] = both_ref[0:groups]
    second_ref[...] = both_ref[groups : 2 * groups]


def input_grad_kernel(
    total_ref, ft_ref, weight_ref, rows_ref, modes_ref, out_ref, tiles_ref, sems
):
    groups, span, channels = modes_ref.shape
    steps, tile = tiles_ref.shape[0], tiles_ref.shape[2]
    half, all_rows = steps * tile, groups * span
    back = jnp.concatenate(
        [modes_ref[at, 0:span, :].astype(jnp.float32) for at in range(groups)], axis=0
    )
    signs = row_signs(all_rows, span, channels)
    back = (back.astype(jnp.bfloat16), (back * signs).astype(jnp.bfloat16))
    weight = weight_ref[...]
    row = lax.broadcasted_iota(jnp.int32, (tile, channels), 0)
    going = []
    for side in range(2):
        for step in range(steps):
            at = pl.ds(side * half + step * tile, tile)
            grad_cells = dot(ft_ref[pl.ds(step * tile, tile), :], back[side])
            if step == 0 and side == 0:
                grad_cells = grad_cells + jnp.where(row == 0, rows_ref[0:1, :], 0.0)
            if step == steps - 1 and side == 1:
                grad_cells = grad_cells + jnp.where(row == tile - 1, rows_ref[1:2, :], 0.0)
            spread = grad_cells.astype(jnp.bfloat16).astype(jnp.float32)
            local = dot(total_ref[at, :], weight, 1, 1)
            tiles_ref[step, side] = (local + spread).astype(jnp.bfloat16)
            going += started(
                [
                    pltpu.make_async_copy(
                        tiles_ref.at[step, side], out_ref.at[at], sems.at[step, side]
                    )
                ]
            )
    wait(going)


def rows_of(count, channels):
    return pltpu.VMEM((channels // LANES, count, LANES), jnp.float32)


def call(kernel, outs, specs, scratch=(), out_specs=None, name=None, limit=8, busy=0):
    return pl.pallas_call(
        kernel,
        out_shape=outs,
        in_specs=specs,
        out_specs=out_specs if out_specs is not None else [VMEM] * len(outs),
        scratch_shapes=list(scratch),
        compiler_params=pltpu.CompilerParams(vmem_limit_bytes=limit * MIB),
        cost_estimate=pl.CostEstimate(
            flops=busy * 1_000_000_000, bytes_accessed=busy * MIB, transcendentals=0
        )
        if busy
        else None,
        name=name,
    )


def body(
    inputs,
    cotangent,
    point_weight,
    point_bias,
    spec_real,
    spec_imag,
    junc_weight,
    junc_bias,
    inlet_ids,
    outlet_ids,
):
    per_dev, cell_count, channels = inputs.shape
    assert per_dev == 1
    groups, pipes = lax.axis_size("len"), lax.axis_size("pipe")
    assert pipes == 4
    modes = spec_real.shape[0]
    span = 2 * modes
    all_rows = span * groups
    steps = cell_count // (2 * TILE)
    table = half_table(cell_count, modes * groups, groups)
    tiled = table.reshape(all_rows, steps, TILE).transpose(1, 0, 2)
    f_table = jnp.asarray(np.ascontiguousarray(tiled))
    ft_table = jnp.asarray(np.ascontiguousarray(table.T))
    field = inputs.reshape(cell_count, channels)
    cot = cotangent.reshape(cell_count, channels)
    bias_row = point_bias.reshape(1, channels)
    junc_bias_row = junc_bias.reshape(1, channels)
    shape = jax.ShapeDtypeStruct
    bf16, f32 = jnp.bfloat16, jnp.float32
    message = shape((groups, span + 2, channels), bf16)
    chunks = shape((groups, span, channels), bf16)
    dma = pltpu.SemaphoreType.DMA

    def exchange(value):
        return lax.all_to_all(value, "len", split_axis=0, concat_axis=0, tiled=True)

    def swap(value, step):
        return lax.ppermute(value, "pipe", [(i, i ^ step) for i in range(pipes)])

    mix_bufs = [rows_of(all_rows, channels)] * 2
    pipe_rows = [rows_of(pipes * groups, channels)] * 2
    inlet_row = inlet_ids.reshape(1, -1)
    outlet_row = outlet_ids.reshape(1, -1)
    (ends,) = call(
        ends_kernel,
        [shape((8, channels), f32)],
        [HBM],
        [pltpu.VMEM((2, 16, channels), bf16), dma((2,))],
        name="pipe_ends",
        limit=60,
        busy=4,
    )(field)
    ends = [ends] + [swap(ends, step) for step in range(1, pipes)]
    (spectra,) = call(spectrum_kernel, [chunks], [VMEM] * 2, name="spectrum", busy=12)(
        field, f_table
    )
    (sent,) = call(
        functools.partial(message_kernel, pipes),
        [shape((groups, span + 2 * pipes, channels), bf16)],
        [VMEM] * (1 + pipes),
        name="message",
    )(spectra, *ends)
    received = exchange(sent)
    mixed, cond, slope = call(
        functools.partial(mix_kernel, pipes),
        [chunks, shape((1, channels), f32), shape((8, channels), f32)],
        [VMEM] * 7,
        mix_bufs + pipe_rows,
        name="mix",
        busy=12,
    )(received, spec_real, spec_imag, inlet_row, outlet_row, junc_weight, junc_bias_row)
    returned = exchange(mixed)
    spectra = received
    early, total, sent = call(
        layer_kernel,
        [shape(field.shape, bf16)] * 2 + [message],
        [VMEM] * 8,
        [pltpu.VMEM((all_rows, channels), f32)] * 2 + [pltpu.VMEM(field.shape, f32)],
        name="layer",
        busy=12,
    )(field, cot, f_table, ft_table, point_weight, bias_row, cond, returned)
    received = exchange(sent)
    received, spectra = lax.optimization_barrier((received, spectra))
    (both,) = call(
        pack_kernel,
        [shape((2 * groups, span + 2, channels), bf16)],
        [VMEM] * 2,
        name="pack",
    )(spectra, received)
    mixed, outputs = call(
        mix_grad_kernel,
        [chunks, early],
        [VMEM] * 4,
        [dma] + mix_bufs,
        out_specs=[VMEM, HBM],
        name="mix_grad",
        busy=12,
    )(received, spec_real, spec_imag, early)
    both, behind = lax.optimization_barrier((swap(both, 2), mixed))
    across = call(split_kernel, [message] * 2, [VMEM], name="split")(both)
    spectra, received, _ = lax.optimization_barrier((spectra, received, behind))
    fields = [spectra, swap(spectra, 1), across[0], swap(across[0], 1)]
    grads = [received, swap(received, 1), across[1], swap(across[1], 1)]
    returned = exchange(mixed)
    big = shape((modes, channels, channels), f32)
    per_copy = math.gcd(modes, 2)
    grad_real, grad_imag, rows = call(
        functools.partial(weight_grad_kernel, pipes, modes, per_copy),
        [big, big, shape((8, channels), f32)],
        [VMEM] * (2 * pipes + 4),
        [rows_of(pipes * all_rows, channels)] * 2
        + [pltpu.VMEM(big.shape, f32)] * 2
        + pipe_rows
        + [pltpu.VMEM((groups, channels), f32)] * 2
        + [dma((modes // per_copy, 2))],
        out_specs=[HBM, HBM, VMEM],
        name="weight_grad",
        limit=16,
    )(*fields, *grads, inlet_row, outlet_row, junc_weight, slope)
    (grad_inputs,) = call(
        input_grad_kernel,
        [shape(field.shape, bf16)],
        [VMEM] * 5,
        [pltpu.VMEM((steps, 2, TILE, channels), bf16), dma((steps, 2))],
        out_specs=[HBM],
        name="input_grad",
    )(total, ft_table, point_weight, rows, returned)
    return (
        outputs.reshape(inputs.shape),
        grad_inputs.reshape(inputs.shape),
        grad_real,
        grad_imag,
    )


def solution(mesh):
    placed = (
        P(("len", "pipe"), None, None),
        P(("len", "pipe"), None, None),
        P(),
        P(),
        P("len", None, None),
        P("len", None, None),
        P(),
        P(),
        P(),
        P(),
    )
    return jax.shard_map(
        body,
        mesh=mesh,
        in_specs=placed,
        out_specs=(
            P(("len", "pipe"), None, None),
            P(("len", "pipe"), None, None),
            P("len", None, None),
            P("len", None, None),
        ),
        check_vma=False,
    )
```

```python
import functools
import math

import jax
import jax.numpy as jnp
import ml_dtypes
import numpy as np
from jax import lax
from jax.experimental import pallas as pl
from jax.experimental.pallas import tpu as pltpu
from jax.sharding import PartitionSpec as P

COUPLING = 0.125
TILE = 256
LANES = 128
GELU_S = math.sqrt(2.0 / math.pi)
GELU_C = 0.044715
VMEM = pl.BlockSpec(memory_space=pltpu.VMEM)
HBM = pl.BlockSpec(memory_space=pltpu.HBM)
MIB = 1024 * 1024


def half_table(cell_count, mode_count, groups):
    half = cell_count // 2
    product_index = np.arange(mode_count)[:, None] * np.arange(half)[None, :] % cell_count
    angles = product_index.astype(np.float32) * np.float32(2.0 * math.pi / cell_count)
    norm_scale = np.float32(1.0 / math.sqrt(cell_count))
    cosine = (np.cos(angles) * norm_scale).reshape(groups, -1, half)
    sine = (np.sin(angles) * norm_scale).reshape(groups, -1, half)
    table = np.concatenate([cosine, -sine], axis=1).reshape(2 * mode_count, half)
    return table.astype(ml_dtypes.bfloat16)


def row_signs(all_rows, span, channels):
    row = lax.broadcasted_iota(jnp.int32, (all_rows, channels), 0)
    per_owner = span // 2
    mode = (row // span) * per_owner + lax.rem(row, per_owner)
    return jnp.where(lax.rem(mode, 2) == 0, 1.0, -1.0).astype(jnp.float32)


def dot(left, right, left_dim=1, right_dim=0):
    return lax.dot_general(
        left,
        right,
        (((left_dim,), (right_dim,)), ((), ())),
        preferred_element_type=jnp.float32,
    )


def put(ref, at, value):
    for lane in range(ref.shape[0]):
        ref[lane, at, :] = value[:, lane * LANES : (lane + 1) * LANES]


def take(ref, at):
    return jnp.concatenate([ref[lane, at, :] for lane in range(ref.shape[0])], axis=1)


def ends_kernel(x_ref, ends_ref):
    cells, channels = x_ref.shape
    ends = [x_ref[0:1, :], x_ref[cells - 1 : cells, :], jnp.zeros((6, channels), x_ref.dtype)]
    ends_ref[...] = jnp.concatenate([part.astype(jnp.float32) for part in ends], axis=0)


def spectrum_kernel(x_ref, f_ref, spectra_ref):
    steps, all_rows, tile = f_ref.shape
    half = x_ref.shape[0] // 2
    groups, span, channels = spectra_ref.shape
    sums = []
    for base in (0, half):
        total = None
        for step in range(steps):
            at = base + step * tile
            part = dot(f_ref[step], x_ref[at : at + tile, :])
            total = part if total is None else total + part
        sums.append(total)
    spectra = sums[0] + row_signs(all_rows, span, channels) * sums[1]
    spectra = spectra.astype(jnp.bfloat16)
    for at in range(groups):
        spectra_ref[at] = spectra[at * span : (at + 1) * span]


def message_kernel(pipes, spectra_ref, *refs):
    groups, span = spectra_ref.shape[0], spectra_ref.shape[1]
    msg_ref = refs[pipes]
    ends = jnp.concatenate([refs[step][0:2, :] for step in range(pipes)], axis=0)
    ends = ends.astype(jnp.bfloat16)
    for at in range(groups):
        msg_ref[at, 0:span, :] = spectra_ref[at]
        msg_ref[at, span:, :] = ends


def extra_rows(first, second, count, channels):
    parts = [first.astype(jnp.float32), second.astype(jnp.float32)]
    if count > 2:
        parts.append(jnp.zeros((count - 2, channels), jnp.float32))
    return jnp.concatenate(parts, axis=0).astype(jnp.bfloat16)


def mix_rows(backward, r_ref, real_ref, imag_ref, out_ref, x_ref, y_ref):
    groups, modes = r_ref.shape[0], real_ref.shape[0]
    span = 2 * modes
    for source in range(groups):
        put(x_ref, pl.ds(source * span, span), r_ref[source, 0:span, :].astype(jnp.float32))
    for mode in range(modes):
        first = pl.ds(mode, groups, stride=span)
        second = pl.ds(modes + mode, groups, stride=span)
        rows = jnp.concatenate([take(x_ref, first), take(x_ref, second)], axis=0).astype(
            jnp.bfloat16
        )
        dim = 1 if backward else 0
        by_real = dot(rows, real_ref[mode], 1, dim)
        by_imag = dot(rows, imag_ref[mode], 1, dim)
        if backward:
            put(y_ref, first, by_real[:groups] + by_imag[groups:])
            put(y_ref, second, by_real[groups:] - by_imag[:groups])
        else:
            put(y_ref, first, by_real[:groups] - by_imag[groups:])
            put(y_ref, second, by_imag[:groups] + by_real[groups:])
    for source in range(groups):
        rows = take(y_ref, pl.ds(source * span, span)).astype(jnp.bfloat16)
        out_ref[source] = rows


def mix_kernel(
    pipes,
    r_ref,
    real_ref,
    imag_ref,
    inlet_ref,
    outlet_ref,
    junc_weight_ref,
    junc_bias_ref,
    out_ref,
    cond_ref,
    slope_ref,
    x_ref,
    y_ref,
    first_ref,
    last_ref,
):
    groups, rows = r_ref.shape[0], r_ref.shape[1]
    span = rows - 2 * pipes
    column = lax.axis_index("pipe")
    ends = [r_ref[group, span:rows, :].astype(jnp.float32) for group in range(groups)]
    for step in range(pipes):
        at = pl.ds(lax.bitwise_xor(column, step), groups, stride=pipes)
        for side, ref in enumerate((first_ref, last_ref)):
            row = 2 * step + side
            put(ref, at, jnp.concatenate([part[row : row + 1] for part in ends], axis=0))
    picked_in, picked_out = selection(inlet_ref, outlet_ref, pipes)
    sums = dot(picked_in, whole(first_ref)) + dot(picked_out, whole(last_ref))
    act = dot(sums.astype(jnp.bfloat16), junc_weight_ref[...]) + junc_bias_ref[...]
    sigmoid_part = jax.nn.sigmoid(act)
    junc_rows = (act * sigmoid_part).astype(jnp.bfloat16).astype(jnp.float32)
    cond_ref[...] = COUPLING * (junc_rows[0:1] + junc_rows[1:2])
    slope_ref[...] = sigmoid_part * (1.0 + act * (1.0 - sigmoid_part))
    mix_rows(False, r_ref, real_ref, imag_ref, out_ref, x_ref, y_ref)


def mix_grad_kernel(
    r_ref, real_ref, imag_ref, early_ref, out_ref, copied_ref, sem, x_ref, y_ref
):
    copy = pltpu.make_async_copy(early_ref, copied_ref, sem)
    copy.start()
    mix_rows(True, r_ref, real_ref, imag_ref, out_ref, x_ref, y_ref)
    copy.wait()


def own_pipe(pipes):
    return lax.axis_index("len") * pipes + lax.axis_index("pipe")


def selection(inlet_ref, outlet_ref, pipes):
    count = inlet_ref.shape[1]
    lane = lax.broadcasted_iota(jnp.int32, (8, count), 1)
    row = lax.broadcasted_iota(jnp.int32, (8, count), 0)
    inlets = jnp.broadcast_to(inlet_ref[...], (8, count)).astype(jnp.float32)
    outlets = jnp.broadcast_to(outlet_ref[...], (8, count)).astype(jnp.float32)
    mine = jnp.where(row == 0, inlets, outlets)
    own = jnp.sum(jnp.where(lane == own_pipe(pipes), mine, 0.0), axis=1, keepdims=True)
    return (inlets == own).astype(jnp.bfloat16), (outlets == own).astype(jnp.bfloat16)


def whole(ref):
    return take(ref, pl.ds(0, ref.shape[1])).astype(jnp.bfloat16)


def started(copies):
    for copy in copies:
        copy.start()
    return copies


def wait(copies):
    for copy in copies:
        copy.wait()


def brought(pairs, sems, base=0):
    return started(
        [
            pltpu.make_async_copy(source, target, sems.at[base + place])
            for place, (source, target) in enumerate(pairs)
        ]
    )


def layer_kernel(
    x_ref,
    cot_ref,
    f_ref,
    ft_ref,
    weight_ref,
    bias_ref,
    cond_ref,
    modes_ref,
    out_ref,
    total_ref,
    msg_ref,
    low_ref,
    high_ref,
):
    steps, all_rows, tile = f_ref.shape
    half = steps * tile
    channels = x_ref.shape[1]
    groups, rows = msg_ref.shape[0], msg_ref.shape[1]
    span = all_rows // groups
    cond = cond_ref[...]
    row = lax.broadcasted_iota(jnp.int32, (all_rows, channels), 0)
    doubled = jnp.where((row == 0) | (row == span // 2), 1.0, 2.0).astype(jnp.float32)
    signs = row_signs(all_rows, span, channels)
    modes = jnp.concatenate(
        [modes_ref[at, 0:span, :].astype(jnp.float32) for at in range(groups)], axis=0
    )
    modes = modes * doubled
    modes = (modes.astype(jnp.bfloat16), (modes * signs).astype(jnp.bfloat16))
    weight = weight_ref[...]
    bias = bias_ref[...]
    for side, acc_ref in enumerate((low_ref, high_ref)):
        for step in range(steps):
            at = pl.ds(side * half + step * tile, tile)
            pointwise = dot(x_ref[at, :], weight) + bias
            spectral = dot(ft_ref[pl.ds(step * tile, tile), :], modes[side])
            summed = pointwise + (spectral + cond).astype(jnp.bfloat16).astype(jnp.float32)
            square = summed * summed
            part = 0.5 + 0.5 * jnp.tanh(summed * (GELU_S + (GELU_S * GELU_C) * square))
            result = summed * part
            out_ref[at, :] = result.astype(jnp.bfloat16)
            slope = part + result * (1.0 - part) * (
                2.0 * GELU_S + (6.0 * GELU_S * GELU_C) * square
            )
            total = (cot_ref[at, :].astype(jnp.float32) * slope).astype(jnp.bfloat16)
            total_ref[at, :] = total
            term = dot(f_ref[step], total)
            if step == 0:
                acc_ref[...] = term
            else:
                acc_ref[...] += term
    acc = low_ref[...] + signs * high_ref[...]
    grad_cond = acc[0:1, :] * (1.0 / f_ref[0, 0:1, 0:1].astype(jnp.float32))
    upper = grad_cond.astype(jnp.bfloat16).astype(jnp.float32)
    extra = extra_rows(upper, grad_cond - upper, rows - span, channels)
    grad_spec = (acc * doubled).astype(jnp.bfloat16)
    for at in range(groups):
        msg_ref[at, 0:span, :] = grad_spec[at * span : (at + 1) * span]
        msg_ref[at, span:rows, :] = extra


def weight_grad_kernel(pipes, modes, per_copy, *refs):
    fields, grads, refs = refs[:pipes], refs[pipes : 2 * pipes], refs[2 * pipes :]
    (inlet_ref, outlet_ref, junc_weight_ref, slope_ref), refs = refs[:4], refs[4:]
    real_out, imag_out, rows_ref, x_ref, g_ref, real_ref, imag_ref = refs[:7]
    first_ref, last_ref, upper_ref, lower_ref, sems = refs[7:]
    groups, rows = grads[0].shape[0], grads[0].shape[1]
    span = 2 * modes
    for step in range(pipes):
        for source in range(groups):
            at = pl.ds((step * groups + source) * span, span)
            put(x_ref, at, fields[step][source, 0:span, :].astype(jnp.float32))
            put(g_ref, at, grads[step][source, 0:span, :].astype(jnp.float32))
    count = pipes * groups
    going = []
    for number in range(modes // per_copy):
        for mode in range(number * per_copy, (number + 1) * per_copy):
            first = pl.ds(mode, count, stride=span)
            second = pl.ds(modes + mode, count, stride=span)
            a, b = take(x_ref, first), take(x_ref, second)
            u, v = take(g_ref, first), take(g_ref, second)
            left = jnp.concatenate([a, b], axis=0).astype(jnp.bfloat16)
            right = jnp.concatenate([u, v], axis=0).astype(jnp.bfloat16)
            turned = jnp.concatenate([v, -u], axis=0).astype(jnp.bfloat16)
            real_ref[mode] = dot(left, right, 0, 0)
            imag_ref[mode] = dot(left, turned, 0, 0)
        at = pl.ds(number * per_copy, per_copy)
        going += started(
            [
                pltpu.make_async_copy(real_ref.at[at], real_out.at[at], sems.at[number, 0]),
                pltpu.make_async_copy(imag_ref.at[at], imag_out.at[at], sems.at[number, 1]),
            ]
        )
    column = lax.axis_index("pipe")
    for step in range(pipes):
        for group in range(groups):
            parts = grads[step][group, rows - 2 : rows, :].astype(jnp.float32)
            upper_ref[group : group + 1, :] = parts[0:1]
            lower_ref[group : group + 1, :] = parts[1:2]
        at = pl.ds(lax.bitwise_xor(column, step), groups, stride=pipes)
        put(first_ref, at, upper_ref[...])
        put(last_ref, at, lower_ref[...])
    picked_in, picked_out = selection(inlet_ref, outlet_ref, pipes)
    picked = picked_in + picked_out
    junc_grad = COUPLING * (dot(picked, whole(first_ref)) + dot(picked, whole(last_ref)))
    act_grad = (junc_grad * slope_ref[...]).astype(jnp.bfloat16)
    sums_grad = dot(act_grad, junc_weight_ref[...], 1, 1)
    rows_ref[...] = sums_grad.astype(jnp.bfloat16).astype(jnp.float32)
    wait(going)


def pick_kernel(r_ref, out_ref):
    other = 1 - lax.rem(lax.axis_index("len"), 2)
    for pair in range(out_ref.shape[0]):
        out_ref[pair] = r_ref[2 * pair + other]


def merge_kernel(r_ref, got_ref, out_ref):
    mine = lax.rem(lax.axis_index("len"), 2)
    for pair in range(got_ref.shape[0]):
        out_ref[2 * pair + mine] = r_ref[2 * pair + mine]
        out_ref[2 * pair + 1 - mine] = got_ref[pair]


def pack_kernel(first_ref, second_ref, out_ref):
    groups, rows = second_ref.shape[0], second_ref.shape[1]
    out_ref[0:groups] = first_ref[:, 0:rows, :]
    out_ref[groups : 2 * groups] = second_ref[...]


def split_kernel(both_ref, first_ref, second_ref):
    groups = first_ref.shape[0]
    first_ref[...] = both_ref[0:groups]
    second_ref[...] = both_ref[groups : 2 * groups]


def input_grad_kernel(
    total_ref, ft_ref, weight_ref, rows_ref, modes_ref, out_ref, tiles_ref, sems
):
    groups, span, channels = modes_ref.shape
    steps, tile = tiles_ref.shape[0], tiles_ref.shape[2]
    half, all_rows = steps * tile, groups * span
    back = jnp.concatenate(
        [modes_ref[at, 0:span, :].astype(jnp.float32) for at in range(groups)], axis=0
    )
    signs = row_signs(all_rows, span, channels)
    back = (back.astype(jnp.bfloat16), (back * signs).astype(jnp.bfloat16))
    weight = weight_ref[...]
    row = lax.broadcasted_iota(jnp.int32, (tile, channels), 0)
    going = []
    for side in range(2):
        for step in range(steps):
            at = pl.ds(side * half + step * tile, tile)
            grad_cells = dot(ft_ref[pl.ds(step * tile, tile), :], back[side])
            if step == 0 and side == 0:
                grad_cells = grad_cells + jnp.where(row == 0, rows_ref[0:1, :], 0.0)
            if step == steps - 1 and side == 1:
                grad_cells = grad_cells + jnp.where(row == tile - 1, rows_ref[1:2, :], 0.0)
            spread = grad_cells.astype(jnp.bfloat16).astype(jnp.float32)
            local = dot(total_ref[at, :], weight, 1, 1)
            tiles_ref[step, side] = (local + spread).astype(jnp.bfloat16)
            going += started(
                [
                    pltpu.make_async_copy(
                        tiles_ref.at[step, side], out_ref.at[at], sems.at[step, side]
                    )
                ]
            )
    wait(going)


def rows_of(count, channels):
    return pltpu.VMEM((channels // LANES, count, LANES), jnp.float32)


def call(kernel, outs, specs, scratch=(), out_specs=None, name=None, limit=8, busy=0):
    return pl.pallas_call(
        kernel,
        out_shape=outs,
        in_specs=specs,
        out_specs=out_specs if out_specs is not None else [VMEM] * len(outs),
        scratch_shapes=list(scratch),
        compiler_params=pltpu.CompilerParams(vmem_limit_bytes=limit * MIB),
        cost_estimate=pl.CostEstimate(
            flops=busy * 1_000_000_000, bytes_accessed=busy * MIB, transcendentals=0
        )
        if busy
        else None,
        name=name,
    )


def body(
    inputs,
    cotangent,
    point_weight,
    point_bias,
    spec_real,
    spec_imag,
    junc_weight,
    junc_bias,
    inlet_ids,
    outlet_ids,
):
    per_dev, cell_count, channels = inputs.shape
    assert per_dev == 1
    groups, pipes = lax.axis_size("len"), lax.axis_size("pipe")
    assert pipes == 4
    modes = spec_real.shape[0]
    span = 2 * modes
    all_rows = span * groups
    steps = cell_count // (2 * TILE)
    table = half_table(cell_count, modes * groups, groups)
    tiled = table.reshape(all_rows, steps, TILE).transpose(1, 0, 2)
    f_table = jnp.asarray(np.ascontiguousarray(tiled))
    ft_table = jnp.asarray(np.ascontiguousarray(table.T))
    field = inputs.reshape(cell_count, channels)
    cot = cotangent.reshape(cell_count, channels)
    bias_row = point_bias.reshape(1, channels)
    junc_bias_row = junc_bias.reshape(1, channels)
    shape = jax.ShapeDtypeStruct
    bf16, f32 = jnp.bfloat16, jnp.float32
    message = shape((groups, span + 2, channels), bf16)
    chunks = shape((groups, span, channels), bf16)
    dma = pltpu.SemaphoreType.DMA

    lines = [list(range(first, groups, 2)) for first in range(2)]

    def exchange(value):
        rows = value.shape[1]
        moved = lax.all_to_all(
            value, "len", split_axis=0, concat_axis=0, tiled=True, axis_index_groups=lines
        )
        half = shape((groups // 2, rows, channels), bf16)
        (passed,) = call(pick_kernel, [half], [VMEM], name="pick")(moved)
        got = lax.ppermute(passed, "len", [(i, i ^ 1) for i in range(groups)])
        return call(merge_kernel, [shape(value.shape, bf16)], [VMEM] * 2, name="merge")(
            moved, got
        )[0]

    def swap(value, step):
        return lax.ppermute(value, "pipe", [(i, i ^ step) for i in range(pipes)])

    mix_bufs = [rows_of(all_rows, channels)] * 2
    pipe_rows = [rows_of(pipes * groups, channels)] * 2
    inlet_row = inlet_ids.reshape(1, -1)
    outlet_row = outlet_ids.reshape(1, -1)
    (ends,) = call(
        ends_kernel, [shape((8, channels), f32)], [VMEM], name="pipe_ends", busy=4
    )(field)
    ends = [ends] + [swap(ends, step) for step in range(1, pipes)]
    (spectra,) = call(spectrum_kernel, [chunks], [VMEM] * 2, name="spectrum", busy=12)(
        field, f_table
    )
    (sent,) = call(
        functools.partial(message_kernel, pipes),
        [shape((groups, span + 2 * pipes, channels), bf16)],
        [VMEM] * (1 + pipes),
        name="message",
    )(spectra, *ends)
    received = exchange(sent)
    mixed, cond, slope = call(
        functools.partial(mix_kernel, pipes),
        [chunks, shape((1, channels), f32), shape((8, channels), f32)],
        [VMEM] * 7,
        mix_bufs + pipe_rows,
        name="mix",
        busy=12,
    )(received, spec_real, spec_imag, inlet_row, outlet_row, junc_weight, junc_bias_row)
    returned = exchange(mixed)
    spectra = received
    early, total, sent = call(
        layer_kernel,
        [shape(field.shape, bf16)] * 2 + [message],
        [VMEM] * 8,
        [pltpu.VMEM((all_rows, channels), f32)] * 2,
        name="layer",
        busy=12,
    )(field, cot, f_table, ft_table, point_weight, bias_row, cond, returned)
    received = exchange(sent)
    received, spectra = lax.optimization_barrier((received, spectra))
    (both,) = call(
        pack_kernel,
        [shape((2 * groups, span + 2, channels), bf16)],
        [VMEM] * 2,
        name="pack",
    )(spectra, received)
    mixed, outputs = call(
        mix_grad_kernel,
        [chunks, early],
        [VMEM] * 4,
        [dma] + mix_bufs,
        out_specs=[VMEM, HBM],
        name="mix_grad",
        busy=12,
    )(received, spec_real, spec_imag, early)
    both, behind = lax.optimization_barrier((swap(both, 2), mixed))
    across = call(split_kernel, [message] * 2, [VMEM], name="split")(both)
    spectra, received, _ = lax.optimization_barrier((spectra, received, behind))
    fields = [spectra, swap(spectra, 1), across[0], swap(across[0], 1)]
    grads = [received, swap(received, 1), across[1], swap(across[1], 1)]
    returned = exchange(mixed)
    big = shape((modes, channels, channels), f32)
    per_copy = math.gcd(modes, 2)
    grad_real, grad_imag, rows = call(
        functools.partial(weight_grad_kernel, pipes, modes, per_copy),
        [big, big, shape((8, channels), f32)],
        [VMEM] * (2 * pipes + 4),
        [rows_of(pipes * all_rows, channels)] * 2
        + [pltpu.VMEM(big.shape, f32)] * 2
        + pipe_rows
        + [pltpu.VMEM((groups, channels), f32)] * 2
        + [dma((modes // per_copy, 2))],
        out_specs=[HBM, HBM, VMEM],
        name="weight_grad",
        limit=16,
    )(*fields, *grads, inlet_row, outlet_row, junc_weight, slope)
    (grad_inputs,) = call(
        input_grad_kernel,
        [shape(field.shape, bf16)],
        [VMEM] * 5,
        [pltpu.VMEM((steps, 2, TILE, channels), bf16), dma((steps, 2))],
        out_specs=[HBM],
        name="input_grad",
    )(total, ft_table, point_weight, rows, returned)
    return (
        outputs.reshape(inputs.shape),
        grad_inputs.reshape(inputs.shape),
        grad_real,
        grad_imag,
    )


def solution(mesh):
    placed = (
        P(("len", "pipe"), None, None),
        P(("len", "pipe"), None, None),
        P(),
        P(),
        P("len", None, None),
        P("len", None, None),
        P(),
        P(),
        P(),
        P(),
    )
    return jax.shard_map(
        body,
        mesh=mesh,
        in_specs=placed,
        out_specs=(
            P(("len", "pipe"), None, None),
            P(("len", "pipe"), None, None),
            P("len", None, None),
            P("len", None, None),
        ),
        check_vma=False,
    )
```

```python
import functools
import math

import jax
import jax.numpy as jnp
import ml_dtypes
import numpy as np
from jax import lax
from jax.experimental import pallas as pl
from jax.experimental.pallas import tpu as pltpu
from jax.sharding import PartitionSpec as P

COUPLING = 0.125
TILE = 256
LANES = 128
GELU_S = math.sqrt(2.0 / math.pi)
GELU_C = 0.044715
VMEM = pl.BlockSpec(memory_space=pltpu.VMEM)
HBM = pl.BlockSpec(memory_space=pltpu.HBM)
MIB = 1024 * 1024


def half_table(cell_count, mode_count, groups):
    half = cell_count // 2
    product_index = np.arange(mode_count)[:, None] * np.arange(half)[None, :] % cell_count
    angles = product_index.astype(np.float32) * np.float32(2.0 * math.pi / cell_count)
    norm_scale = np.float32(1.0 / math.sqrt(cell_count))
    cosine = (np.cos(angles) * norm_scale).reshape(groups, -1, half)
    sine = (np.sin(angles) * norm_scale).reshape(groups, -1, half)
    table = np.concatenate([cosine, -sine], axis=1).reshape(2 * mode_count, half)
    return table.astype(ml_dtypes.bfloat16)


def row_signs(all_rows, span, channels):
    row = lax.broadcasted_iota(jnp.int32, (all_rows, channels), 0)
    per_owner = span // 2
    mode = (row // span) * per_owner + lax.rem(row, per_owner)
    return jnp.where(lax.rem(mode, 2) == 0, 1.0, -1.0).astype(jnp.float32)


def dot(left, right, left_dim=1, right_dim=0):
    return lax.dot_general(
        left,
        right,
        (((left_dim,), (right_dim,)), ((), ())),
        preferred_element_type=jnp.float32,
    )


def put(ref, at, value):
    for lane in range(ref.shape[0]):
        ref[lane, at, :] = value[:, lane * LANES : (lane + 1) * LANES]


def take(ref, at):
    return jnp.concatenate([ref[lane, at, :] for lane in range(ref.shape[0])], axis=1)


def ends_kernel(x_ref, ends_ref):
    cells, channels = x_ref.shape
    ends = [x_ref[0:1, :], x_ref[cells - 1 : cells, :], jnp.zeros((6, channels), x_ref.dtype)]
    ends_ref[...] = jnp.concatenate([part.astype(jnp.float32) for part in ends], axis=0)


def spectrum_kernel(x_ref, f_ref, weight_ref, bias_ref, spectra_ref, pointwise_ref):
    steps, all_rows, tile = f_ref.shape
    half = x_ref.shape[0] // 2
    groups, span, channels = spectra_ref.shape
    sums = []
    for base in (0, half):
        total = None
        for step in range(steps):
            at = base + step * tile
            part = dot(f_ref[step], x_ref[at : at + tile, :])
            total = part if total is None else total + part
        sums.append(total)
    spectra = sums[0] + row_signs(all_rows, span, channels) * sums[1]
    spectra = spectra.astype(jnp.bfloat16)
    for at in range(groups):
        spectra_ref[at] = spectra[at * span : (at + 1) * span]
    weight = weight_ref[...]
    bias = bias_ref[...]
    for step in range(2 * steps):
        at = pl.ds(step * tile, tile)
        pointwise_ref[at, :] = dot(x_ref[at, :], weight) + bias


def message_kernel(pipes, spectra_ref, *refs):
    groups, span = spectra_ref.shape[0], spectra_ref.shape[1]
    msg_ref = refs[pipes]
    ends = jnp.concatenate([refs[step][0:2, :] for step in range(pipes)], axis=0)
    ends = ends.astype(jnp.bfloat16)
    for at in range(groups):
        msg_ref[at, 0:span, :] = spectra_ref[at]
        msg_ref[at, span:, :] = ends


def extra_rows(first, second, count, channels):
    parts = [first.astype(jnp.float32), second.astype(jnp.float32)]
    if count > 2:
        parts.append(jnp.zeros((count - 2, channels), jnp.float32))
    return jnp.concatenate(parts, axis=0).astype(jnp.bfloat16)


def mix_rows(backward, r_ref, real_ref, imag_ref, out_ref, x_ref, y_ref):
    groups, modes = r_ref.shape[0], real_ref.shape[0]
    span = 2 * modes
    for source in range(groups):
        put(x_ref, pl.ds(source * span, span), r_ref[source, 0:span, :].astype(jnp.float32))
    for mode in range(modes):
        first = pl.ds(mode, groups, stride=span)
        second = pl.ds(modes + mode, groups, stride=span)
        rows = jnp.concatenate([take(x_ref, first), take(x_ref, second)], axis=0).astype(
            jnp.bfloat16
        )
        dim = 1 if backward else 0
        by_real = dot(rows, real_ref[mode], 1, dim)
        by_imag = dot(rows, imag_ref[mode], 1, dim)
        if backward:
            put(y_ref, first, by_real[:groups] + by_imag[groups:])
            put(y_ref, second, by_real[groups:] - by_imag[:groups])
        else:
            put(y_ref, first, by_real[:groups] - by_imag[groups:])
            put(y_ref, second, by_imag[:groups] + by_real[groups:])
    for source in range(groups):
        rows = take(y_ref, pl.ds(source * span, span)).astype(jnp.bfloat16)
        out_ref[source] = rows


def mix_kernel(
    pipes,
    r_ref,
    real_ref,
    imag_ref,
    inlet_ref,
    outlet_ref,
    junc_weight_ref,
    junc_bias_ref,
    out_ref,
    cond_ref,
    slope_ref,
    x_ref,
    y_ref,
    first_ref,
    last_ref,
):
    groups, rows = r_ref.shape[0], r_ref.shape[1]
    span = rows - 2 * pipes
    column = lax.axis_index("pipe")
    ends = [r_ref[group, span:rows, :].astype(jnp.float32) for group in range(groups)]
    for step in range(pipes):
        at = pl.ds(lax.bitwise_xor(column, step), groups, stride=pipes)
        for side, ref in enumerate((first_ref, last_ref)):
            row = 2 * step + side
            put(ref, at, jnp.concatenate([part[row : row + 1] for part in ends], axis=0))
    picked_in, picked_out = selection(inlet_ref, outlet_ref, pipes)
    sums = dot(picked_in, whole(first_ref)) + dot(picked_out, whole(last_ref))
    act = dot(sums.astype(jnp.bfloat16), junc_weight_ref[...]) + junc_bias_ref[...]
    sigmoid_part = jax.nn.sigmoid(act)
    junc_rows = (act * sigmoid_part).astype(jnp.bfloat16).astype(jnp.float32)
    cond_ref[...] = COUPLING * (junc_rows[0:1] + junc_rows[1:2])
    slope_ref[...] = sigmoid_part * (1.0 + act * (1.0 - sigmoid_part))
    mix_rows(False, r_ref, real_ref, imag_ref, out_ref, x_ref, y_ref)


def mix_grad_kernel(
    r_ref, real_ref, imag_ref, early_ref, out_ref, copied_ref, sem, x_ref, y_ref
):
    copy = pltpu.make_async_copy(early_ref, copied_ref, sem)
    copy.start()
    mix_rows(True, r_ref, real_ref, imag_ref, out_ref, x_ref, y_ref)
    copy.wait()


def own_pipe(pipes):
    return lax.axis_index("len") * pipes + lax.axis_index("pipe")


def selection(inlet_ref, outlet_ref, pipes):
    count = inlet_ref.shape[1]
    lane = lax.broadcasted_iota(jnp.int32, (8, count), 1)
    row = lax.broadcasted_iota(jnp.int32, (8, count), 0)
    inlets = jnp.broadcast_to(inlet_ref[...], (8, count)).astype(jnp.float32)
    outlets = jnp.broadcast_to(outlet_ref[...], (8, count)).astype(jnp.float32)
    mine = jnp.where(row == 0, inlets, outlets)
    own = jnp.sum(jnp.where(lane == own_pipe(pipes), mine, 0.0), axis=1, keepdims=True)
    return (inlets == own).astype(jnp.bfloat16), (outlets == own).astype(jnp.bfloat16)


def whole(ref):
    return take(ref, pl.ds(0, ref.shape[1])).astype(jnp.bfloat16)


def started(copies):
    for copy in copies:
        copy.start()
    return copies


def wait(copies):
    for copy in copies:
        copy.wait()


def brought(pairs, sems, base=0):
    return started(
        [
            pltpu.make_async_copy(source, target, sems.at[base + place])
            for place, (source, target) in enumerate(pairs)
        ]
    )


def layer_kernel(
    pointwise_ref,
    cot_ref,
    f_ref,
    ft_ref,
    cond_ref,
    modes_ref,
    out_ref,
    total_ref,
    msg_ref,
    low_ref,
    high_ref,
):
    steps, all_rows, tile = f_ref.shape
    half = steps * tile
    channels = cot_ref.shape[1]
    groups, rows = msg_ref.shape[0], msg_ref.shape[1]
    span = all_rows // groups
    cond = cond_ref[...]
    row = lax.broadcasted_iota(jnp.int32, (all_rows, channels), 0)
    doubled = jnp.where((row == 0) | (row == span // 2), 1.0, 2.0).astype(jnp.float32)
    signs = row_signs(all_rows, span, channels)
    modes = jnp.concatenate(
        [modes_ref[at, 0:span, :].astype(jnp.float32) for at in range(groups)], axis=0
    )
    modes = modes * doubled
    modes = (modes.astype(jnp.bfloat16), (modes * signs).astype(jnp.bfloat16))
    for side, acc_ref in enumerate((low_ref, high_ref)):
        for step in range(steps):
            at = pl.ds(side * half + step * tile, tile)
            spectral = dot(ft_ref[pl.ds(step * tile, tile), :], modes[side])
            summed = pointwise_ref[at, :] + (spectral + cond).astype(jnp.bfloat16).astype(jnp.float32)
            square = summed * summed
            part = 0.5 + 0.5 * jnp.tanh(summed * (GELU_S + (GELU_S * GELU_C) * square))
            result = summed * part
            out_ref[at, :] = result.astype(jnp.bfloat16)
            slope = part + result * (1.0 - part) * (
                2.0 * GELU_S + (6.0 * GELU_S * GELU_C) * square
            )
            total = (cot_ref[at, :].astype(jnp.float32) * slope).astype(jnp.bfloat16)
            total_ref[at, :] = total
            term = dot(f_ref[step], total)
            if step == 0:
                acc_ref[...] = term
            else:
                acc_ref[...] += term
    acc = low_ref[...] + signs * high_ref[...]
    grad_cond = acc[0:1, :] * (1.0 / f_ref[0, 0:1, 0:1].astype(jnp.float32))
    upper = grad_cond.astype(jnp.bfloat16).astype(jnp.float32)
    extra = extra_rows(upper, grad_cond - upper, rows - span, channels)
    grad_spec = (acc * doubled).astype(jnp.bfloat16)
    for at in range(groups):
        msg_ref[at, 0:span, :] = grad_spec[at * span : (at + 1) * span]
        msg_ref[at, span:rows, :] = extra


def weight_grad_kernel(pipes, modes, per_copy, *refs):
    fields, grads, refs = refs[:pipes], refs[pipes : 2 * pipes], refs[2 * pipes :]
    (inlet_ref, outlet_ref, junc_weight_ref, slope_ref), refs = refs[:4], refs[4:]
    real_out, imag_out, rows_ref, x_ref, g_ref, real_ref, imag_ref = refs[:7]
    first_ref, last_ref, upper_ref, lower_ref, sems = refs[7:]
    groups, rows = grads[0].shape[0], grads[0].shape[1]
    span = 2 * modes
    for step in range(pipes):
        for source in range(groups):
            at = pl.ds((step * groups + source) * span, span)
            put(x_ref, at, fields[step][source, 0:span, :].astype(jnp.float32))
            put(g_ref, at, grads[step][source, 0:span, :].astype(jnp.float32))
    count = pipes * groups
    going = []
    for number in range(modes // per_copy):
        for mode in range(number * per_copy, (number + 1) * per_copy):
            first = pl.ds(mode, count, stride=span)
            second = pl.ds(modes + mode, count, stride=span)
            a, b = take(x_ref, first), take(x_ref, second)
            u, v = take(g_ref, first), take(g_ref, second)
            left = jnp.concatenate([a, b], axis=0).astype(jnp.bfloat16)
            right = jnp.concatenate([u, v], axis=0).astype(jnp.bfloat16)
            turned = jnp.concatenate([v, -u], axis=0).astype(jnp.bfloat16)
            real_ref[mode] = dot(left, right, 0, 0)
            imag_ref[mode] = dot(left, turned, 0, 0)
        at = pl.ds(number * per_copy, per_copy)
        going += started(
            [
                pltpu.make_async_copy(real_ref.at[at], real_out.at[at], sems.at[number, 0]),
                pltpu.make_async_copy(imag_ref.at[at], imag_out.at[at], sems.at[number, 1]),
            ]
        )
    column = lax.axis_index("pipe")
    for step in range(pipes):
        for group in range(groups):
            parts = grads[step][group, rows - 2 : rows, :].astype(jnp.float32)
            upper_ref[group : group + 1, :] = parts[0:1]
            lower_ref[group : group + 1, :] = parts[1:2]
        at = pl.ds(lax.bitwise_xor(column, step), groups, stride=pipes)
        put(first_ref, at, upper_ref[...])
        put(last_ref, at, lower_ref[...])
    picked_in, picked_out = selection(inlet_ref, outlet_ref, pipes)
    picked = picked_in + picked_out
    junc_grad = COUPLING * (dot(picked, whole(first_ref)) + dot(picked, whole(last_ref)))
    act_grad = (junc_grad * slope_ref[...]).astype(jnp.bfloat16)
    sums_grad = dot(act_grad, junc_weight_ref[...], 1, 1)
    rows_ref[...] = sums_grad.astype(jnp.bfloat16).astype(jnp.float32)
    wait(going)


def pack_kernel(first_ref, second_ref, out_ref):
    groups, rows = second_ref.shape[0], second_ref.shape[1]
    out_ref[0:groups] = first_ref[:, 0:rows, :]
    out_ref[groups : 2 * groups] = second_ref[...]


def split_kernel(both_ref, first_ref, second_ref):
    groups = first_ref.shape[0]
    first_ref[...] = both_ref[0:groups]
    second_ref[...] = both_ref[groups : 2 * groups]


def input_grad_kernel(
    total_ref, ft_ref, weight_ref, rows_ref, modes_ref, out_ref, tiles_ref, sems
):
    groups, span, channels = modes_ref.shape
    steps, tile = tiles_ref.shape[0], tiles_ref.shape[2]
    half, all_rows = steps * tile, groups * span
    back = jnp.concatenate(
        [modes_ref[at, 0:span, :].astype(jnp.float32) for at in range(groups)], axis=0
    )
    signs = row_signs(all_rows, span, channels)
    back = (back.astype(jnp.bfloat16), (back * signs).astype(jnp.bfloat16))
    weight = weight_ref[...]
    row = lax.broadcasted_iota(jnp.int32, (tile, channels), 0)
    going = []
    for side in range(2):
        for step in range(steps):
            at = pl.ds(side * half + step * tile, tile)
            grad_cells = dot(ft_ref[pl.ds(step * tile, tile), :], back[side])
            if step == 0 and side == 0:
                grad_cells = grad_cells + jnp.where(row == 0, rows_ref[0:1, :], 0.0)
            if step == steps - 1 and side == 1:
                grad_cells = grad_cells + jnp.where(row == tile - 1, rows_ref[1:2, :], 0.0)
            spread = grad_cells.astype(jnp.bfloat16).astype(jnp.float32)
            local = dot(total_ref[at, :], weight, 1, 1)
            tiles_ref[step, side] = (local + spread).astype(jnp.bfloat16)
            going += started(
                [
                    pltpu.make_async_copy(
                        tiles_ref.at[step, side], out_ref.at[at], sems.at[step, side]
                    )
                ]
            )
    wait(going)


def rows_of(count, channels):
    return pltpu.VMEM((channels // LANES, count, LANES), jnp.float32)


def call(kernel, outs, specs, scratch=(), out_specs=None, name=None, limit=8, busy=0):
    return pl.pallas_call(
        kernel,
        out_shape=outs,
        in_specs=specs,
        out_specs=out_specs if out_specs is not None else [VMEM] * len(outs),
        scratch_shapes=list(scratch),
        compiler_params=pltpu.CompilerParams(vmem_limit_bytes=limit * MIB),
        cost_estimate=pl.CostEstimate(
            flops=busy * 1_000_000_000, bytes_accessed=busy * MIB, transcendentals=0
        )
        if busy
        else None,
        name=name,
    )


def body(
    inputs,
    cotangent,
    point_weight,
    point_bias,
    spec_real,
    spec_imag,
    junc_weight,
    junc_bias,
    inlet_ids,
    outlet_ids,
):
    per_dev, cell_count, channels = inputs.shape
    assert per_dev == 1
    groups, pipes = lax.axis_size("len"), lax.axis_size("pipe")
    assert pipes == 4
    modes = spec_real.shape[0]
    span = 2 * modes
    all_rows = span * groups
    steps = cell_count // (2 * TILE)
    table = half_table(cell_count, modes * groups, groups)
    tiled = table.reshape(all_rows, steps, TILE).transpose(1, 0, 2)
    f_table = jnp.asarray(np.ascontiguousarray(tiled))
    ft_table = jnp.asarray(np.ascontiguousarray(table.T))
    field = inputs.reshape(cell_count, channels)
    cot = cotangent.reshape(cell_count, channels)
    bias_row = point_bias.reshape(1, channels)
    junc_bias_row = junc_bias.reshape(1, channels)
    shape = jax.ShapeDtypeStruct
    bf16, f32 = jnp.bfloat16, jnp.float32
    message = shape((groups, span + 2, channels), bf16)
    chunks = shape((groups, span, channels), bf16)
    dma = pltpu.SemaphoreType.DMA

    def exchange(value):
        return lax.all_to_all(value, "len", split_axis=0, concat_axis=0, tiled=True)

    def swap(value, step):
        return lax.ppermute(value, "pipe", [(i, i ^ step) for i in range(pipes)])

    mix_bufs = [rows_of(all_rows, channels)] * 2
    pipe_rows = [rows_of(pipes * groups, channels)] * 2
    inlet_row = inlet_ids.reshape(1, -1)
    outlet_row = outlet_ids.reshape(1, -1)
    (ends,) = call(
        ends_kernel, [shape((8, channels), f32)], [VMEM], name="pipe_ends", busy=4
    )(field)
    ends = [ends] + [swap(ends, step) for step in range(1, pipes)]
    spectra, pointwise = call(
        spectrum_kernel,
        [chunks, shape(field.shape, f32)],
        [VMEM] * 4,
        name="spectrum",
        busy=12,
    )(field, f_table, point_weight, bias_row)
    (sent,) = call(
        functools.partial(message_kernel, pipes),
        [shape((groups, span + 2 * pipes, channels), bf16)],
        [VMEM] * (1 + pipes),
        name="message",
    )(spectra, *ends)
    received = exchange(sent)
    mixed, cond, slope = call(
        functools.partial(mix_kernel, pipes),
        [chunks, shape((1, channels), f32), shape((8, channels), f32)],
        [VMEM] * 7,
        mix_bufs + pipe_rows,
        name="mix",
        busy=12,
    )(received, spec_real, spec_imag, inlet_row, outlet_row, junc_weight, junc_bias_row)
    returned = exchange(mixed)
    spectra = received
    early, total, sent = call(
        layer_kernel,
        [shape(field.shape, bf16)] * 2 + [message],
        [VMEM] * 6,
        [pltpu.VMEM((all_rows, channels), f32)] * 2,
        name="layer",
        busy=12,
    )(pointwise, cot, f_table, ft_table, cond, returned)
    received = exchange(sent)
    received, spectra = lax.optimization_barrier((received, spectra))
    (both,) = call(
        pack_kernel,
        [shape((2 * groups, span + 2, channels), bf16)],
        [VMEM] * 2,
        name="pack",
    )(spectra, received)
    mixed, outputs = call(
        mix_grad_kernel,
        [chunks, early],
        [VMEM] * 4,
        [dma] + mix_bufs,
        out_specs=[VMEM, HBM],
        name="mix_grad",
        busy=12,
    )(received, spec_real, spec_imag, early)
    both, behind = lax.optimization_barrier((swap(both, 2), mixed))
    across = call(split_kernel, [message] * 2, [VMEM], name="split")(both)
    spectra, received, _ = lax.optimization_barrier((spectra, received, behind))
    fields = [spectra, swap(spectra, 1), across[0], swap(across[0], 1)]
    grads = [received, swap(received, 1), across[1], swap(across[1], 1)]
    returned = exchange(mixed)
    big = shape((modes, channels, channels), f32)
    per_copy = math.gcd(modes, 2)
    grad_real, grad_imag, rows = call(
        functools.partial(weight_grad_kernel, pipes, modes, per_copy),
        [big, big, shape((8, channels), f32)],
        [VMEM] * (2 * pipes + 4),
        [rows_of(pipes * all_rows, channels)] * 2
        + [pltpu.VMEM(big.shape, f32)] * 2
        + pipe_rows
        + [pltpu.VMEM((groups, channels), f32)] * 2
        + [dma((modes // per_copy, 2))],
        out_specs=[HBM, HBM, VMEM],
        name="weight_grad",
        limit=16,
    )(*fields, *grads, inlet_row, outlet_row, junc_weight, slope)
    (grad_inputs,) = call(
        input_grad_kernel,
        [shape(field.shape, bf16)],
        [VMEM] * 5,
        [pltpu.VMEM((steps, 2, TILE, channels), bf16), dma((steps, 2))],
        out_specs=[HBM],
        name="input_grad",
    )(total, ft_table, point_weight, rows, returned)
    return (
        outputs.reshape(inputs.shape),
        grad_inputs.reshape(inputs.shape),
        grad_real,
        grad_imag,
    )


def solution(mesh):
    placed = (
        P(("len", "pipe"), None, None),
        P(("len", "pipe"), None, None),
        P(),
        P(),
        P("len", None, None),
        P("len", None, None),
        P(),
        P(),
        P(),
        P(),
    )
    return jax.shard_map(
        body,
        mesh=mesh,
        in_specs=placed,
        out_specs=(
            P(("len", "pipe"), None, None),
            P(("len", "pipe"), None, None),
            P("len", None, None),
            P("len", None, None),
        ),
        check_vma=False,
    )
```

```python
import functools
import math

import jax
import jax.numpy as jnp
import ml_dtypes
import numpy as np
from jax import lax
from jax.experimental import pallas as pl
from jax.experimental.pallas import tpu as pltpu
from jax.sharding import PartitionSpec as P

COUPLING = 0.125
TILE = 256
LANES = 128
GELU_S = math.sqrt(2.0 / math.pi)
GELU_C = 0.044715
VMEM = pl.BlockSpec(memory_space=pltpu.VMEM)
HBM = pl.BlockSpec(memory_space=pltpu.HBM)
MIB = 1024 * 1024


def half_table(cell_count, mode_count, groups):
    half = cell_count // 2
    product_index = np.arange(mode_count)[:, None] * np.arange(half)[None, :] % cell_count
    angles = product_index.astype(np.float32) * np.float32(2.0 * math.pi / cell_count)
    norm_scale = np.float32(1.0 / math.sqrt(cell_count))
    cosine = (np.cos(angles) * norm_scale).reshape(groups, -1, half)
    sine = (np.sin(angles) * norm_scale).reshape(groups, -1, half)
    table = np.concatenate([cosine, -sine], axis=1).reshape(2 * mode_count, half)
    return table.astype(ml_dtypes.bfloat16)


def row_signs(all_rows, span, channels):
    row = lax.broadcasted_iota(jnp.int32, (all_rows, channels), 0)
    per_owner = span // 2
    mode = (row // span) * per_owner + lax.rem(row, per_owner)
    return jnp.where(lax.rem(mode, 2) == 0, 1.0, -1.0).astype(jnp.float32)


def dot(left, right, left_dim=1, right_dim=0):
    return lax.dot_general(
        left,
        right,
        (((left_dim,), (right_dim,)), ((), ())),
        preferred_element_type=jnp.float32,
    )


def put(ref, at, value):
    for lane in range(ref.shape[0]):
        ref[lane, at, :] = value[:, lane * LANES : (lane + 1) * LANES]


def take(ref, at):
    return jnp.concatenate([ref[lane, at, :] for lane in range(ref.shape[0])], axis=1)


def ends_kernel(x_ref, ends_ref):
    cells, channels = x_ref.shape
    ends = [x_ref[0:1, :], x_ref[cells - 1 : cells, :], jnp.zeros((6, channels), x_ref.dtype)]
    ends_ref[...] = jnp.concatenate([part.astype(jnp.float32) for part in ends], axis=0)


def spectrum_kernel(x_ref, f_ref, weight_ref, bias_ref, spectra_ref, pointwise_ref):
    steps, all_rows, tile = f_ref.shape
    half = x_ref.shape[0] // 2
    groups, span, channels = spectra_ref.shape
    sums = []
    for base in (0, half):
        total = None
        for step in range(steps):
            at = base + step * tile
            part = dot(f_ref[step], x_ref[at : at + tile, :])
            total = part if total is None else total + part
        sums.append(total)
    spectra = sums[0] + row_signs(all_rows, span, channels) * sums[1]
    spectra = spectra.astype(jnp.bfloat16)
    for at in range(groups):
        spectra_ref[at] = spectra[at * span : (at + 1) * span]
    weight = weight_ref[...]
    bias = bias_ref[...]
    for step in range(2 * steps):
        at = pl.ds(step * tile, tile)
        pointwise_ref[at, :] = dot(x_ref[at, :], weight) + bias


def message_kernel(pipes, spectra_ref, *refs):
    groups, span = spectra_ref.shape[0], spectra_ref.shape[1]
    msg_ref = refs[pipes]
    ends = jnp.concatenate([refs[step][0:2, :] for step in range(pipes)], axis=0)
    ends = ends.astype(jnp.bfloat16)
    for at in range(groups):
        msg_ref[at, 0:span, :] = spectra_ref[at]
        msg_ref[at, span:, :] = ends


def extra_rows(first, second, count, channels):
    parts = [first.astype(jnp.float32), second.astype(jnp.float32)]
    if count > 2:
        parts.append(jnp.zeros((count - 2, channels), jnp.float32))
    return jnp.concatenate(parts, axis=0).astype(jnp.bfloat16)


def mix_rows(backward, r_ref, real_ref, imag_ref, out_ref, x_ref, y_ref):
    groups, modes = r_ref.shape[0], real_ref.shape[0]
    span = 2 * modes
    for source in range(groups):
        put(x_ref, pl.ds(source * span, span), r_ref[source, 0:span, :].astype(jnp.float32))
    for mode in range(modes):
        first = pl.ds(mode, groups, stride=span)
        second = pl.ds(modes + mode, groups, stride=span)
        rows = jnp.concatenate([take(x_ref, first), take(x_ref, second)], axis=0).astype(
            jnp.bfloat16
        )
        dim = 1 if backward else 0
        by_real = dot(rows, real_ref[mode], 1, dim)
        by_imag = dot(rows, imag_ref[mode], 1, dim)
        if backward:
            put(y_ref, first, by_real[:groups] + by_imag[groups:])
            put(y_ref, second, by_real[groups:] - by_imag[:groups])
        else:
            put(y_ref, first, by_real[:groups] - by_imag[groups:])
            put(y_ref, second, by_imag[:groups] + by_real[groups:])
    for source in range(groups):
        rows = take(y_ref, pl.ds(source * span, span)).astype(jnp.bfloat16)
        out_ref[source] = rows


def mix_kernel(
    pipes,
    r_ref,
    real_ref,
    imag_ref,
    inlet_ref,
    outlet_ref,
    junc_weight_ref,
    junc_bias_ref,
    out_ref,
    cond_ref,
    slope_ref,
    x_ref,
    y_ref,
    first_ref,
    last_ref,
):
    groups, rows = r_ref.shape[0], r_ref.shape[1]
    span = rows - 2 * pipes
    column = lax.axis_index("pipe")
    ends = [r_ref[group, span:rows, :].astype(jnp.float32) for group in range(groups)]
    for step in range(pipes):
        at = pl.ds(lax.bitwise_xor(column, step), groups, stride=pipes)
        for side, ref in enumerate((first_ref, last_ref)):
            row = 2 * step + side
            put(ref, at, jnp.concatenate([part[row : row + 1] for part in ends], axis=0))
    picked_in, picked_out = selection(inlet_ref, outlet_ref, pipes)
    sums = dot(picked_in, whole(first_ref)) + dot(picked_out, whole(last_ref))
    act = dot(sums.astype(jnp.bfloat16), junc_weight_ref[...]) + junc_bias_ref[...]
    sigmoid_part = jax.nn.sigmoid(act)
    junc_rows = (act * sigmoid_part).astype(jnp.bfloat16).astype(jnp.float32)
    cond_ref[...] = COUPLING * (junc_rows[0:1] + junc_rows[1:2])
    slope_ref[...] = sigmoid_part * (1.0 + act * (1.0 - sigmoid_part))
    mix_rows(False, r_ref, real_ref, imag_ref, out_ref, x_ref, y_ref)


def mix_grad_kernel(
    r_ref, real_ref, imag_ref, early_ref, out_ref, copied_ref, sem, x_ref, y_ref
):
    copy = pltpu.make_async_copy(early_ref, copied_ref, sem)
    copy.start()
    mix_rows(True, r_ref, real_ref, imag_ref, out_ref, x_ref, y_ref)
    copy.wait()


def own_pipe(pipes):
    return lax.axis_index("len") * pipes + lax.axis_index("pipe")


def selection(inlet_ref, outlet_ref, pipes):
    count = inlet_ref.shape[1]
    lane = lax.broadcasted_iota(jnp.int32, (8, count), 1)
    row = lax.broadcasted_iota(jnp.int32, (8, count), 0)
    inlets = jnp.broadcast_to(inlet_ref[...], (8, count)).astype(jnp.float32)
    outlets = jnp.broadcast_to(outlet_ref[...], (8, count)).astype(jnp.float32)
    mine = jnp.where(row == 0, inlets, outlets)
    own = jnp.sum(jnp.where(lane == own_pipe(pipes), mine, 0.0), axis=1, keepdims=True)
    return (inlets == own).astype(jnp.bfloat16), (outlets == own).astype(jnp.bfloat16)


def whole(ref):
    return take(ref, pl.ds(0, ref.shape[1])).astype(jnp.bfloat16)


def started(copies):
    for copy in copies:
        copy.start()
    return copies


def wait(copies):
    for copy in copies:
        copy.wait()


def brought(pairs, sems, base=0):
    return started(
        [
            pltpu.make_async_copy(source, target, sems.at[base + place])
            for place, (source, target) in enumerate(pairs)
        ]
    )


def layer_kernel(
    pointwise_ref,
    cot_ref,
    f_ref,
    ft_ref,
    cond_ref,
    modes_ref,
    out_ref,
    total_ref,
    msg_ref,
    spectral_ref,
):
    steps, all_rows, tile = f_ref.shape
    half = steps * tile
    channels = cot_ref.shape[1]
    groups, rows = msg_ref.shape[0], msg_ref.shape[1]
    span = all_rows // groups
    cond = cond_ref[...]
    row = lax.broadcasted_iota(jnp.int32, (all_rows, channels), 0)
    doubled = jnp.where((row == 0) | (row == span // 2), 1.0, 2.0).astype(jnp.float32)
    signs = row_signs(all_rows, span, channels)
    modes = jnp.concatenate(
        [modes_ref[at, 0:span, :].astype(jnp.float32) for at in range(groups)], axis=0
    )
    modes = modes * doubled
    modes = (modes.astype(jnp.bfloat16), (modes * signs).astype(jnp.bfloat16))
    for side in range(2):
        spectral_ref[side * half : (side + 1) * half, :] = dot(ft_ref[...], modes[side])
    sums = []
    for side in range(2):
        terms = None
        for step in range(steps):
            at = pl.ds(side * half + step * tile, tile)
            pre = (spectral_ref[at, :] + cond).astype(jnp.bfloat16).astype(jnp.float32)
            summed = pointwise_ref[at, :] + pre
            square = summed * summed
            part = 0.5 + 0.5 * jnp.tanh(summed * (GELU_S + (GELU_S * GELU_C) * square))
            result = summed * part
            out_ref[at, :] = result.astype(jnp.bfloat16)
            slope = part + result * (1.0 - part) * (
                2.0 * GELU_S + (6.0 * GELU_S * GELU_C) * square
            )
            total = (cot_ref[at, :].astype(jnp.float32) * slope).astype(jnp.bfloat16)
            total_ref[at, :] = total
        for step in range(steps):
            at = pl.ds(side * half + step * tile, tile)
            term = dot(f_ref[step], total_ref[at, :])
            terms = term if terms is None else terms + term
        sums.append(terms)
    acc = sums[0] + signs * sums[1]
    grad_cond = acc[0:1, :] * (1.0 / f_ref[0, 0:1, 0:1].astype(jnp.float32))
    upper = grad_cond.astype(jnp.bfloat16).astype(jnp.float32)
    extra = extra_rows(upper, grad_cond - upper, rows - span, channels)
    grad_spec = (acc * doubled).astype(jnp.bfloat16)
    for at in range(groups):
        msg_ref[at, 0:span, :] = grad_spec[at * span : (at + 1) * span]
        msg_ref[at, span:rows, :] = extra


def weight_grad_kernel(pipes, modes, per_copy, *refs):
    fields, grads, refs = refs[:pipes], refs[pipes : 2 * pipes], refs[2 * pipes :]
    (inlet_ref, outlet_ref, junc_weight_ref, slope_ref), refs = refs[:4], refs[4:]
    total_ref, weight_ref, real_out, imag_out, rows_ref, local_ref = refs[:6]
    x_ref, g_ref, real_ref, imag_ref = refs[6:10]
    first_ref, last_ref, upper_ref, lower_ref, sems = refs[10:]
    groups, rows = grads[0].shape[0], grads[0].shape[1]
    span = 2 * modes
    for step in range(pipes):
        for source in range(groups):
            at = pl.ds((step * groups + source) * span, span)
            put(x_ref, at, fields[step][source, 0:span, :].astype(jnp.float32))
            put(g_ref, at, grads[step][source, 0:span, :].astype(jnp.float32))
    count = pipes * groups
    going = []
    for number in range(modes // per_copy):
        for mode in range(number * per_copy, (number + 1) * per_copy):
            first = pl.ds(mode, count, stride=span)
            second = pl.ds(modes + mode, count, stride=span)
            a, b = take(x_ref, first), take(x_ref, second)
            u, v = take(g_ref, first), take(g_ref, second)
            left = jnp.concatenate([a, b], axis=0).astype(jnp.bfloat16)
            right = jnp.concatenate([u, v], axis=0).astype(jnp.bfloat16)
            turned = jnp.concatenate([v, -u], axis=0).astype(jnp.bfloat16)
            real_ref[mode] = dot(left, right, 0, 0)
            imag_ref[mode] = dot(left, turned, 0, 0)
        at = pl.ds(number * per_copy, per_copy)
        going += started(
            [
                pltpu.make_async_copy(real_ref.at[at], real_out.at[at], sems.at[number, 0]),
                pltpu.make_async_copy(imag_ref.at[at], imag_out.at[at], sems.at[number, 1]),
            ]
        )
    column = lax.axis_index("pipe")
    for step in range(pipes):
        for group in range(groups):
            parts = grads[step][group, rows - 2 : rows, :].astype(jnp.float32)
            upper_ref[group : group + 1, :] = parts[0:1]
            lower_ref[group : group + 1, :] = parts[1:2]
        at = pl.ds(lax.bitwise_xor(column, step), groups, stride=pipes)
        put(first_ref, at, upper_ref[...])
        put(last_ref, at, lower_ref[...])
    picked_in, picked_out = selection(inlet_ref, outlet_ref, pipes)
    picked = picked_in + picked_out
    junc_grad = COUPLING * (dot(picked, whole(first_ref)) + dot(picked, whole(last_ref)))
    act_grad = (junc_grad * slope_ref[...]).astype(jnp.bfloat16)
    sums_grad = dot(act_grad, junc_weight_ref[...], 1, 1)
    rows_ref[...] = sums_grad.astype(jnp.bfloat16).astype(jnp.float32)
    local_ref[...] = dot(total_ref[...], weight_ref[...], 1, 1)
    wait(going)


def pack_kernel(first_ref, second_ref, out_ref):
    groups, rows = second_ref.shape[0], second_ref.shape[1]
    out_ref[0:groups] = first_ref[:, 0:rows, :]
    out_ref[groups : 2 * groups] = second_ref[...]


def split_kernel(both_ref, first_ref, second_ref):
    groups = first_ref.shape[0]
    first_ref[...] = both_ref[0:groups]
    second_ref[...] = both_ref[groups : 2 * groups]


def input_grad_kernel(
    local_ref, ft_ref, rows_ref, modes_ref, out_ref, cells_ref, tiles_ref, sems
):
    groups, span, channels = modes_ref.shape
    steps, tile = tiles_ref.shape[0], tiles_ref.shape[2]
    half, all_rows = steps * tile, groups * span
    back = jnp.concatenate(
        [modes_ref[at, 0:span, :].astype(jnp.float32) for at in range(groups)], axis=0
    )
    signs = row_signs(all_rows, span, channels)
    back = (back.astype(jnp.bfloat16), (back * signs).astype(jnp.bfloat16))
    row = lax.broadcasted_iota(jnp.int32, (tile, channels), 0)
    for side in range(2):
        cells_ref[side * half : (side + 1) * half, :] = dot(ft_ref[...], back[side])
    going = []
    for side in range(2):
        for step in range(steps):
            at = pl.ds(side * half + step * tile, tile)
            grad_cells = cells_ref[at, :]
            if step == 0 and side == 0:
                grad_cells = grad_cells + jnp.where(row == 0, rows_ref[0:1, :], 0.0)
            if step == steps - 1 and side == 1:
                grad_cells = grad_cells + jnp.where(row == tile - 1, rows_ref[1:2, :], 0.0)
            spread = grad_cells.astype(jnp.bfloat16).astype(jnp.float32)
            tiles_ref[step, side] = (local_ref[at, :] + spread).astype(jnp.bfloat16)
            going += started(
                [
                    pltpu.make_async_copy(
                        tiles_ref.at[step, side], out_ref.at[at], sems.at[step, side]
                    )
                ]
            )
    wait(going)


def rows_of(count, channels):
    return pltpu.VMEM((channels // LANES, count, LANES), jnp.float32)


def call(kernel, outs, specs, scratch=(), out_specs=None, name=None, limit=8, busy=0):
    return pl.pallas_call(
        kernel,
        out_shape=outs,
        in_specs=specs,
        out_specs=out_specs if out_specs is not None else [VMEM] * len(outs),
        scratch_shapes=list(scratch),
        compiler_params=pltpu.CompilerParams(vmem_limit_bytes=limit * MIB),
        cost_estimate=pl.CostEstimate(
            flops=busy * 1_000_000_000, bytes_accessed=busy * MIB, transcendentals=0
        )
        if busy
        else None,
        name=name,
    )


def body(
    inputs,
    cotangent,
    point_weight,
    point_bias,
    spec_real,
    spec_imag,
    junc_weight,
    junc_bias,
    inlet_ids,
    outlet_ids,
):
    per_dev, cell_count, channels = inputs.shape
    assert per_dev == 1
    groups, pipes = lax.axis_size("len"), lax.axis_size("pipe")
    assert pipes == 4
    modes = spec_real.shape[0]
    span = 2 * modes
    all_rows = span * groups
    steps = cell_count // (2 * TILE)
    table = half_table(cell_count, modes * groups, groups)
    tiled = table.reshape(all_rows, steps, TILE).transpose(1, 0, 2)
    f_table = jnp.asarray(np.ascontiguousarray(tiled))
    ft_table = jnp.asarray(np.ascontiguousarray(table.T))
    field = inputs.reshape(cell_count, channels)
    cot = cotangent.reshape(cell_count, channels)
    bias_row = point_bias.reshape(1, channels)
    junc_bias_row = junc_bias.reshape(1, channels)
    shape = jax.ShapeDtypeStruct
    bf16, f32 = jnp.bfloat16, jnp.float32
    message = shape((groups, span + 2, channels), bf16)
    chunks = shape((groups, span, channels), bf16)
    dma = pltpu.SemaphoreType.DMA

    def exchange(value):
        return lax.all_to_all(value, "len", split_axis=0, concat_axis=0, tiled=True)

    def swap(value, step):
        return lax.ppermute(value, "pipe", [(i, i ^ step) for i in range(pipes)])

    mix_bufs = [rows_of(all_rows, channels)] * 2
    pipe_rows = [rows_of(pipes * groups, channels)] * 2
    inlet_row = inlet_ids.reshape(1, -1)
    outlet_row = outlet_ids.reshape(1, -1)
    (ends,) = call(
        ends_kernel, [shape((8, channels), f32)], [VMEM], name="pipe_ends", busy=4
    )(field)
    ends = [ends] + [swap(ends, step) for step in range(1, pipes)]
    spectra, pointwise = call(
        spectrum_kernel,
        [chunks, shape(field.shape, f32)],
        [VMEM] * 4,
        name="spectrum",
        busy=12,
    )(field, f_table, point_weight, bias_row)
    (sent,) = call(
        functools.partial(message_kernel, pipes),
        [shape((groups, span + 2 * pipes, channels), bf16)],
        [VMEM] * (1 + pipes),
        name="message",
    )(spectra, *ends)
    received = exchange(sent)
    mixed, cond, slope = call(
        functools.partial(mix_kernel, pipes),
        [chunks, shape((1, channels), f32), shape((8, channels), f32)],
        [VMEM] * 7,
        mix_bufs + pipe_rows,
        name="mix",
        busy=12,
    )(received, spec_real, spec_imag, inlet_row, outlet_row, junc_weight, junc_bias_row)
    returned = exchange(mixed)
    spectra = received
    early, total, sent = call(
        layer_kernel,
        [shape(field.shape, bf16)] * 2 + [message],
        [VMEM] * 6,
        [pltpu.VMEM(field.shape, f32)],
        name="layer",
        busy=12,
    )(pointwise, cot, f_table, ft_table, cond, returned)
    received = exchange(sent)
    received, spectra = lax.optimization_barrier((received, spectra))
    (both,) = call(
        pack_kernel,
        [shape((2 * groups, span + 2, channels), bf16)],
        [VMEM] * 2,
        name="pack",
    )(spectra, received)
    mixed, outputs = call(
        mix_grad_kernel,
        [chunks, early],
        [VMEM] * 4,
        [dma] + mix_bufs,
        out_specs=[VMEM, HBM],
        name="mix_grad",
        busy=12,
    )(received, spec_real, spec_imag, early)
    both, behind = lax.optimization_barrier((swap(both, 2), mixed))
    across = call(split_kernel, [message] * 2, [VMEM], name="split")(both)
    spectra, received, _ = lax.optimization_barrier((spectra, received, behind))
    fields = [spectra, swap(spectra, 1), across[0], swap(across[0], 1)]
    grads = [received, swap(received, 1), across[1], swap(across[1], 1)]
    returned = exchange(mixed)
    big = shape((modes, channels, channels), f32)
    per_copy = math.gcd(modes, 2)
    grad_real, grad_imag, rows, local = call(
        functools.partial(weight_grad_kernel, pipes, modes, per_copy),
        [big, big, shape((8, channels), f32), shape(field.shape, f32)],
        [VMEM] * (2 * pipes + 6),
        [rows_of(pipes * all_rows, channels)] * 2
        + [pltpu.VMEM(big.shape, f32)] * 2
        + pipe_rows
        + [pltpu.VMEM((groups, channels), f32)] * 2
        + [dma((modes // per_copy, 2))],
        out_specs=[HBM, HBM, VMEM, VMEM],
        name="weight_grad",
        limit=16,
    )(*fields, *grads, inlet_row, outlet_row, junc_weight, slope, total, point_weight)
    (grad_inputs,) = call(
        input_grad_kernel,
        [shape(field.shape, bf16)],
        [VMEM] * 4,
        [pltpu.VMEM(field.shape, f32)]
        + [pltpu.VMEM((steps, 2, TILE, channels), bf16), dma((steps, 2))],
        out_specs=[HBM],
        name="input_grad",
    )(local, ft_table, rows, returned)
    return (
        outputs.reshape(inputs.shape),
        grad_inputs.reshape(inputs.shape),
        grad_real,
        grad_imag,
    )


def solution(mesh):
    placed = (
        P(("len", "pipe"), None, None),
        P(("len", "pipe"), None, None),
        P(),
        P(),
        P("len", None, None),
        P("len", None, None),
        P(),
        P(),
        P(),
        P(),
    )
    return jax.shard_map(
        body,
        mesh=mesh,
        in_specs=placed,
        out_specs=(
            P(("len", "pipe"), None, None),
            P(("len", "pipe"), None, None),
            P("len", None, None),
            P("len", None, None),
        ),
        check_vma=False,
    )
```

```python
import functools
import math

import jax
import jax.numpy as jnp
import ml_dtypes
import numpy as np
from jax import lax
from jax.experimental import pallas as pl
from jax.experimental.pallas import tpu as pltpu
from jax.sharding import PartitionSpec as P

COUPLING = 0.125
TILE = 256
LANES = 128
GELU_S = math.sqrt(2.0 / math.pi)
GELU_C = 0.044715
VMEM = pl.BlockSpec(memory_space=pltpu.VMEM)
HBM = pl.BlockSpec(memory_space=pltpu.HBM)
MIB = 1024 * 1024


def half_table(cell_count, mode_count, groups):
    half = cell_count // 2
    product_index = np.arange(mode_count)[:, None] * np.arange(half)[None, :] % cell_count
    angles = product_index.astype(np.float32) * np.float32(2.0 * math.pi / cell_count)
    norm_scale = np.float32(1.0 / math.sqrt(cell_count))
    cosine = (np.cos(angles) * norm_scale).reshape(groups, -1, half)
    sine = (np.sin(angles) * norm_scale).reshape(groups, -1, half)
    table = np.concatenate([cosine, -sine], axis=1).reshape(2 * mode_count, half)
    return table.astype(ml_dtypes.bfloat16)


def row_signs(all_rows, span, channels):
    row = lax.broadcasted_iota(jnp.int32, (all_rows, channels), 0)
    per_owner = span // 2
    mode = (row // span) * per_owner + lax.rem(row, per_owner)
    return jnp.where(lax.rem(mode, 2) == 0, 1.0, -1.0).astype(jnp.float32)


def dot(left, right, left_dim=1, right_dim=0):
    return lax.dot_general(
        left,
        right,
        (((left_dim,), (right_dim,)), ((), ())),
        preferred_element_type=jnp.float32,
    )


def put(ref, at, value):
    for lane in range(ref.shape[0]):
        ref[lane, at, :] = value[:, lane * LANES : (lane + 1) * LANES]


def take(ref, at):
    return jnp.concatenate([ref[lane, at, :] for lane in range(ref.shape[0])], axis=1)


def ends_kernel(x_ref, ends_ref):
    cells, channels = x_ref.shape
    ends = [x_ref[0:1, :], x_ref[cells - 1 : cells, :], jnp.zeros((6, channels), x_ref.dtype)]
    ends_ref[...] = jnp.concatenate([part.astype(jnp.float32) for part in ends], axis=0)


def spectrum_kernel(x_ref, f_ref, weight_ref, bias_ref, spectra_ref, pointwise_ref):
    steps, all_rows, tile = f_ref.shape
    half = x_ref.shape[0] // 2
    groups, span, channels = spectra_ref.shape
    sums = []
    for base in (0, half):
        total = None
        for step in range(steps):
            at = base + step * tile
            part = dot(f_ref[step], x_ref[at : at + tile, :])
            total = part if total is None else total + part
        sums.append(total)
    spectra = sums[0] + row_signs(all_rows, span, channels) * sums[1]
    spectra = spectra.astype(jnp.bfloat16)
    for at in range(groups):
        spectra_ref[at] = spectra[at * span : (at + 1) * span]
    weight = weight_ref[...]
    bias = bias_ref[...]
    for step in range(2 * steps):
        at = pl.ds(step * tile, tile)
        pointwise_ref[at, :] = dot(x_ref[at, :], weight) + bias


def message_kernel(pipes, spectra_ref, *refs):
    groups, span = spectra_ref.shape[0], spectra_ref.shape[1]
    msg_ref = refs[pipes]
    ends = jnp.concatenate([refs[step][0:2, :] for step in range(pipes)], axis=0)
    ends = ends.astype(jnp.bfloat16)
    for at in range(groups):
        msg_ref[at, 0:span, :] = spectra_ref[at]
        msg_ref[at, span:, :] = ends


def extra_rows(first, second, count, channels):
    parts = [first.astype(jnp.float32), second.astype(jnp.float32)]
    if count > 2:
        parts.append(jnp.zeros((count - 2, channels), jnp.float32))
    return jnp.concatenate(parts, axis=0).astype(jnp.bfloat16)


def mix_rows(backward, r_ref, real_ref, imag_ref, out_ref, x_ref, y_ref):
    groups, modes = r_ref.shape[0], real_ref.shape[0]
    span = 2 * modes
    for source in range(groups):
        put(x_ref, pl.ds(source * span, span), r_ref[source, 0:span, :].astype(jnp.float32))
    for mode in range(modes):
        first = pl.ds(mode, groups, stride=span)
        second = pl.ds(modes + mode, groups, stride=span)
        rows = jnp.concatenate([take(x_ref, first), take(x_ref, second)], axis=0).astype(
            jnp.bfloat16
        )
        dim = 1 if backward else 0
        by_real = dot(rows, real_ref[mode], 1, dim)
        by_imag = dot(rows, imag_ref[mode], 1, dim)
        if backward:
            put(y_ref, first, by_real[:groups] + by_imag[groups:])
            put(y_ref, second, by_real[groups:] - by_imag[:groups])
        else:
            put(y_ref, first, by_real[:groups] - by_imag[groups:])
            put(y_ref, second, by_imag[:groups] + by_real[groups:])
    for source in range(groups):
        rows = take(y_ref, pl.ds(source * span, span)).astype(jnp.bfloat16)
        out_ref[source] = rows


def mix_kernel(
    pipes,
    r_ref,
    real_ref,
    imag_ref,
    inlet_ref,
    outlet_ref,
    junc_weight_ref,
    junc_bias_ref,
    out_ref,
    cond_ref,
    slope_ref,
    x_ref,
    y_ref,
    first_ref,
    last_ref,
):
    groups, rows = r_ref.shape[0], r_ref.shape[1]
    span = rows - 2 * pipes
    column = lax.axis_index("pipe")
    ends = [r_ref[group, span:rows, :].astype(jnp.float32) for group in range(groups)]
    for step in range(pipes):
        at = pl.ds(lax.bitwise_xor(column, step), groups, stride=pipes)
        for side, ref in enumerate((first_ref, last_ref)):
            row = 2 * step + side
            put(ref, at, jnp.concatenate([part[row : row + 1] for part in ends], axis=0))
    picked_in, picked_out = selection(inlet_ref, outlet_ref, pipes)
    sums = dot(picked_in, whole(first_ref)) + dot(picked_out, whole(last_ref))
    act = dot(sums.astype(jnp.bfloat16), junc_weight_ref[...]) + junc_bias_ref[...]
    sigmoid_part = jax.nn.sigmoid(act)
    junc_rows = (act * sigmoid_part).astype(jnp.bfloat16).astype(jnp.float32)
    cond_ref[...] = COUPLING * (junc_rows[0:1] + junc_rows[1:2])
    slope_ref[...] = sigmoid_part * (1.0 + act * (1.0 - sigmoid_part))
    mix_rows(False, r_ref, real_ref, imag_ref, out_ref, x_ref, y_ref)


def mix_grad_kernel(
    r_ref, real_ref, imag_ref, early_ref, out_ref, copied_ref, sem, x_ref, y_ref
):
    copy = pltpu.make_async_copy(early_ref, copied_ref, sem)
    copy.start()
    mix_rows(True, r_ref, real_ref, imag_ref, out_ref, x_ref, y_ref)
    copy.wait()


def own_pipe(pipes):
    return lax.axis_index("len") * pipes + lax.axis_index("pipe")


def selection(inlet_ref, outlet_ref, pipes):
    count = inlet_ref.shape[1]
    lane = lax.broadcasted_iota(jnp.int32, (8, count), 1)
    row = lax.broadcasted_iota(jnp.int32, (8, count), 0)
    inlets = jnp.broadcast_to(inlet_ref[...], (8, count)).astype(jnp.float32)
    outlets = jnp.broadcast_to(outlet_ref[...], (8, count)).astype(jnp.float32)
    mine = jnp.where(row == 0, inlets, outlets)
    own = jnp.sum(jnp.where(lane == own_pipe(pipes), mine, 0.0), axis=1, keepdims=True)
    return (inlets == own).astype(jnp.bfloat16), (outlets == own).astype(jnp.bfloat16)


def whole(ref):
    return take(ref, pl.ds(0, ref.shape[1])).astype(jnp.bfloat16)


def started(copies):
    for copy in copies:
        copy.start()
    return copies


def wait(copies):
    for copy in copies:
        copy.wait()


def brought(pairs, sems, base=0):
    return started(
        [
            pltpu.make_async_copy(source, target, sems.at[base + place])
            for place, (source, target) in enumerate(pairs)
        ]
    )


def layer_kernel(
    pointwise_ref,
    cot_ref,
    f_ref,
    ft_ref,
    cond_ref,
    modes_ref,
    out_ref,
    total_ref,
    msg_ref,
    spectral_ref,
):
    steps, all_rows, tile = f_ref.shape
    half = steps * tile
    channels = cot_ref.shape[1]
    groups, rows = msg_ref.shape[0], msg_ref.shape[1]
    span = all_rows // groups
    cond = cond_ref[...]
    row = lax.broadcasted_iota(jnp.int32, (all_rows, channels), 0)
    doubled = jnp.where((row == 0) | (row == span // 2), 1.0, 2.0).astype(jnp.float32)
    signs = row_signs(all_rows, span, channels)
    modes = jnp.concatenate(
        [modes_ref[at, 0:span, :].astype(jnp.float32) for at in range(groups)], axis=0
    )
    modes = modes * doubled
    modes = (modes.astype(jnp.bfloat16), (modes * signs).astype(jnp.bfloat16))
    for side in range(2):
        spectral_ref[side * half : (side + 1) * half, :] = dot(ft_ref[...], modes[side])
    sums = []
    for side in range(2):
        terms = None
        for step in range(steps):
            at = pl.ds(side * half + step * tile, tile)
            pre = (spectral_ref[at, :] + cond).astype(jnp.bfloat16).astype(jnp.float32)
            summed = pointwise_ref[at, :] + pre
            square = summed * summed
            part = 0.5 + 0.5 * jnp.tanh(summed * (GELU_S + (GELU_S * GELU_C) * square))
            result = summed * part
            out_ref[at, :] = result.astype(jnp.bfloat16)
            slope = part + result * (1.0 - part) * (
                2.0 * GELU_S + (6.0 * GELU_S * GELU_C) * square
            )
            total = (cot_ref[at, :].astype(jnp.float32) * slope).astype(jnp.bfloat16)
            total_ref[at, :] = total
        for step in range(steps):
            at = pl.ds(side * half + step * tile, tile)
            term = dot(f_ref[step], total_ref[at, :])
            terms = term if terms is None else terms + term
        sums.append(terms)
    acc = sums[0] + signs * sums[1]
    grad_cond = acc[0:1, :] * (1.0 / f_ref[0, 0:1, 0:1].astype(jnp.float32))
    upper = grad_cond.astype(jnp.bfloat16).astype(jnp.float32)
    extra = extra_rows(upper, grad_cond - upper, rows - span, channels)
    grad_spec = (acc * doubled).astype(jnp.bfloat16)
    for at in range(groups):
        msg_ref[at, 0:span, :] = grad_spec[at * span : (at + 1) * span]
        msg_ref[at, span:rows, :] = extra


def weight_grad_kernel(pipes, modes, per_copy, *refs):
    fields, grads, refs = refs[:pipes], refs[pipes : 2 * pipes], refs[2 * pipes :]
    (inlet_ref, outlet_ref, junc_weight_ref, slope_ref), refs = refs[:4], refs[4:]
    total_ref, weight_ref, real_out, imag_out, rows_ref, local_ref = refs[:6]
    x_ref, g_ref, real_ref, imag_ref = refs[6:10]
    first_ref, last_ref, upper_ref, lower_ref, sems = refs[10:]
    groups, rows = grads[0].shape[0], grads[0].shape[1]
    span = 2 * modes
    for step in range(pipes):
        for source in range(groups):
            at = pl.ds((step * groups + source) * span, span)
            put(x_ref, at, fields[step][source, 0:span, :].astype(jnp.float32))
            put(g_ref, at, grads[step][source, 0:span, :].astype(jnp.float32))
    count = pipes * groups
    going = []
    for number in range(modes // per_copy):
        for mode in range(number * per_copy, (number + 1) * per_copy):
            first = pl.ds(mode, count, stride=span)
            second = pl.ds(modes + mode, count, stride=span)
            a, b = take(x_ref, first), take(x_ref, second)
            u, v = take(g_ref, first), take(g_ref, second)
            left = jnp.concatenate([a, b], axis=0).astype(jnp.bfloat16)
            right = jnp.concatenate([u, v], axis=0).astype(jnp.bfloat16)
            turned = jnp.concatenate([v, -u], axis=0).astype(jnp.bfloat16)
            real_ref[mode] = dot(left, right, 0, 0)
            imag_ref[mode] = dot(left, turned, 0, 0)
        at = pl.ds(number * per_copy, per_copy)
        going += started(
            [
                pltpu.make_async_copy(real_ref.at[at], real_out.at[at], sems.at[number, 0]),
                pltpu.make_async_copy(imag_ref.at[at], imag_out.at[at], sems.at[number, 1]),
            ]
        )
    column = lax.axis_index("pipe")
    for step in range(pipes):
        for group in range(groups):
            parts = grads[step][group, rows - 2 : rows, :].astype(jnp.float32)
            upper_ref[group : group + 1, :] = parts[0:1]
            lower_ref[group : group + 1, :] = parts[1:2]
        at = pl.ds(lax.bitwise_xor(column, step), groups, stride=pipes)
        put(first_ref, at, upper_ref[...])
        put(last_ref, at, lower_ref[...])
    picked_in, picked_out = selection(inlet_ref, outlet_ref, pipes)
    picked = picked_in + picked_out
    junc_grad = COUPLING * (dot(picked, whole(first_ref)) + dot(picked, whole(last_ref)))
    act_grad = (junc_grad * slope_ref[...]).astype(jnp.bfloat16)
    sums_grad = dot(act_grad, junc_weight_ref[...], 1, 1)
    rows_ref[...] = sums_grad.astype(jnp.bfloat16).astype(jnp.float32)
    local_ref[...] = dot(total_ref[...], weight_ref[...], 1, 1).astype(jnp.bfloat16)
    wait(going)


def pack_kernel(first_ref, second_ref, out_ref):
    groups, rows = second_ref.shape[0], second_ref.shape[1]
    out_ref[0:groups] = first_ref[:, 0:rows, :]
    out_ref[groups : 2 * groups] = second_ref[...]


def split_kernel(both_ref, first_ref, second_ref):
    groups = first_ref.shape[0]
    first_ref[...] = both_ref[0:groups]
    second_ref[...] = both_ref[groups : 2 * groups]


def input_grad_kernel(
    local_ref, ft_ref, rows_ref, modes_ref, out_ref, cells_ref, tiles_ref, sems
):
    groups, span, channels = modes_ref.shape
    steps, tile = tiles_ref.shape[0], tiles_ref.shape[2]
    half, all_rows = steps * tile, groups * span
    back = jnp.concatenate(
        [modes_ref[at, 0:span, :].astype(jnp.float32) for at in range(groups)], axis=0
    )
    signs = row_signs(all_rows, span, channels)
    back = (back.astype(jnp.bfloat16), (back * signs).astype(jnp.bfloat16))
    row = lax.broadcasted_iota(jnp.int32, (tile, channels), 0)
    for side in range(2):
        cells_ref[side * half : (side + 1) * half, :] = dot(ft_ref[...], back[side])
    going = []
    for side in range(2):
        for step in range(steps):
            at = pl.ds(side * half + step * tile, tile)
            grad_cells = cells_ref[at, :]
            if step == 0 and side == 0:
                grad_cells = grad_cells + jnp.where(row == 0, rows_ref[0:1, :], 0.0)
            if step == steps - 1 and side == 1:
                grad_cells = grad_cells + jnp.where(row == tile - 1, rows_ref[1:2, :], 0.0)
            spread = grad_cells.astype(jnp.bfloat16).astype(jnp.float32)
            tiles_ref[step, side] = (local_ref[at, :].astype(jnp.float32) + spread).astype(
                jnp.bfloat16
            )
            going += started(
                [
                    pltpu.make_async_copy(
                        tiles_ref.at[step, side], out_ref.at[at], sems.at[step, side]
                    )
                ]
            )
    wait(going)


def rows_of(count, channels):
    return pltpu.VMEM((channels // LANES, count, LANES), jnp.float32)


def call(kernel, outs, specs, scratch=(), out_specs=None, name=None, limit=8, busy=0):
    return pl.pallas_call(
        kernel,
        out_shape=outs,
        in_specs=specs,
        out_specs=out_specs if out_specs is not None else [VMEM] * len(outs),
        scratch_shapes=list(scratch),
        compiler_params=pltpu.CompilerParams(vmem_limit_bytes=limit * MIB),
        cost_estimate=pl.CostEstimate(
            flops=busy * 1_000_000_000, bytes_accessed=busy * MIB, transcendentals=0
        )
        if busy
        else None,
        name=name,
    )


def body(
    inputs,
    cotangent,
    point_weight,
    point_bias,
    spec_real,
    spec_imag,
    junc_weight,
    junc_bias,
    inlet_ids,
    outlet_ids,
):
    per_dev, cell_count, channels = inputs.shape
    assert per_dev == 1
    groups, pipes = lax.axis_size("len"), lax.axis_size("pipe")
    assert pipes == 4
    modes = spec_real.shape[0]
    span = 2 * modes
    all_rows = span * groups
    steps = cell_count // (2 * TILE)
    table = half_table(cell_count, modes * groups, groups)
    tiled = table.reshape(all_rows, steps, TILE).transpose(1, 0, 2)
    f_table = jnp.asarray(np.ascontiguousarray(tiled))
    ft_table = jnp.asarray(np.ascontiguousarray(table.T))
    field = inputs.reshape(cell_count, channels)
    cot = cotangent.reshape(cell_count, channels)
    bias_row = point_bias.reshape(1, channels)
    junc_bias_row = junc_bias.reshape(1, channels)
    shape = jax.ShapeDtypeStruct
    bf16, f32 = jnp.bfloat16, jnp.float32
    message = shape((groups, span + 2, channels), bf16)
    chunks = shape((groups, span, channels), bf16)
    dma = pltpu.SemaphoreType.DMA

    def exchange(value):
        return lax.all_to_all(value, "len", split_axis=0, concat_axis=0, tiled=True)

    def swap(value, step):
        return lax.ppermute(value, "pipe", [(i, i ^ step) for i in range(pipes)])

    mix_bufs = [rows_of(all_rows, channels)] * 2
    pipe_rows = [rows_of(pipes * groups, channels)] * 2
    inlet_row = inlet_ids.reshape(1, -1)
    outlet_row = outlet_ids.reshape(1, -1)
    (ends,) = call(
        ends_kernel, [shape((8, channels), f32)], [VMEM], name="pipe_ends", busy=4
    )(field)
    ends = [ends] + [swap(ends, step) for step in range(1, pipes)]
    spectra, pointwise = call(
        spectrum_kernel,
        [chunks, shape(field.shape, f32)],
        [VMEM] * 4,
        name="spectrum",
        busy=12,
    )(field, f_table, point_weight, bias_row)
    (sent,) = call(
        functools.partial(message_kernel, pipes),
        [shape((groups, span + 2 * pipes, channels), bf16)],
        [VMEM] * (1 + pipes),
        name="message",
    )(spectra, *ends)
    received = exchange(sent)
    mixed, cond, slope = call(
        functools.partial(mix_kernel, pipes),
        [chunks, shape((1, channels), f32), shape((8, channels), f32)],
        [VMEM] * 7,
        mix_bufs + pipe_rows,
        name="mix",
        busy=12,
    )(received, spec_real, spec_imag, inlet_row, outlet_row, junc_weight, junc_bias_row)
    returned = exchange(mixed)
    spectra = received
    early, total, sent = call(
        layer_kernel,
        [shape(field.shape, bf16)] * 2 + [message],
        [VMEM] * 6,
        [pltpu.VMEM(field.shape, f32)],
        name="layer",
        busy=12,
    )(pointwise, cot, f_table, ft_table, cond, returned)
    received = exchange(sent)
    received, spectra = lax.optimization_barrier((received, spectra))
    (both,) = call(
        pack_kernel,
        [shape((2 * groups, span + 2, channels), bf16)],
        [VMEM] * 2,
        name="pack",
    )(spectra, received)
    mixed, outputs = call(
        mix_grad_kernel,
        [chunks, early],
        [VMEM] * 4,
        [dma] + mix_bufs,
        out_specs=[VMEM, HBM],
        name="mix_grad",
        busy=12,
    )(received, spec_real, spec_imag, early)
    both, behind = lax.optimization_barrier((swap(both, 2), mixed))
    across = call(split_kernel, [message] * 2, [VMEM], name="split")(both)
    spectra, received, _ = lax.optimization_barrier((spectra, received, behind))
    fields = [spectra, swap(spectra, 1), across[0], swap(across[0], 1)]
    grads = [received, swap(received, 1), across[1], swap(across[1], 1)]
    returned = exchange(mixed)
    big = shape((modes, channels, channels), f32)
    per_copy = math.gcd(modes, 2)
    grad_real, grad_imag, rows, local = call(
        functools.partial(weight_grad_kernel, pipes, modes, per_copy),
        [big, big, shape((8, channels), f32), shape(field.shape, bf16)],
        [VMEM] * (2 * pipes + 6),
        [rows_of(pipes * all_rows, channels)] * 2
        + [pltpu.VMEM(big.shape, f32)] * 2
        + pipe_rows
        + [pltpu.VMEM((groups, channels), f32)] * 2
        + [dma((modes // per_copy, 2))],
        out_specs=[HBM, HBM, VMEM, VMEM],
        name="weight_grad",
        limit=16,
    )(*fields, *grads, inlet_row, outlet_row, junc_weight, slope, total, point_weight)
    (grad_inputs,) = call(
        input_grad_kernel,
        [shape(field.shape, bf16)],
        [VMEM] * 4,
        [pltpu.VMEM(field.shape, f32)]
        + [pltpu.VMEM((steps, 2, TILE, channels), bf16), dma((steps, 2))],
        out_specs=[HBM],
        name="input_grad",
    )(local, ft_table, rows, returned)
    return (
        outputs.reshape(inputs.shape),
        grad_inputs.reshape(inputs.shape),
        grad_real,
        grad_imag,
    )


def solution(mesh):
    placed = (
        P(("len", "pipe"), None, None),
        P(("len", "pipe"), None, None),
        P(),
        P(),
        P("len", None, None),
        P("len", None, None),
        P(),
        P(),
        P(),
        P(),
    )
    return jax.shard_map(
        body,
        mesh=mesh,
        in_specs=placed,
        out_specs=(
            P(("len", "pipe"), None, None),
            P(("len", "pipe"), None, None),
            P("len", None, None),
            P("len", None, None),
        ),
        check_vma=False,
    )
```

```python
import functools
import math

import jax
import jax.numpy as jnp
import ml_dtypes
import numpy as np
from jax import lax
from jax.experimental import pallas as pl
from jax.experimental.pallas import tpu as pltpu
from jax.sharding import PartitionSpec as P

COUPLING = 0.125
TILE = 256
LANES = 128
GELU_S = math.sqrt(2.0 / math.pi)
GELU_C = 0.044715
VMEM = pl.BlockSpec(memory_space=pltpu.VMEM)
HBM = pl.BlockSpec(memory_space=pltpu.HBM)
MIB = 1024 * 1024


def half_table(cell_count, mode_count, groups):
    half = cell_count // 2
    product_index = np.arange(mode_count)[:, None] * np.arange(half)[None, :] % cell_count
    angles = product_index.astype(np.float32) * np.float32(2.0 * math.pi / cell_count)
    norm_scale = np.float32(1.0 / math.sqrt(cell_count))
    cosine = (np.cos(angles) * norm_scale).reshape(groups, -1, half)
    sine = (np.sin(angles) * norm_scale).reshape(groups, -1, half)
    table = np.concatenate([cosine, -sine], axis=1).reshape(2 * mode_count, half)
    return table.astype(ml_dtypes.bfloat16)


def row_signs(all_rows, span, channels):
    row = lax.broadcasted_iota(jnp.int32, (all_rows, channels), 0)
    per_owner = span // 2
    mode = (row // span) * per_owner + lax.rem(row, per_owner)
    return jnp.where(lax.rem(mode, 2) == 0, 1.0, -1.0).astype(jnp.float32)


def dot(left, right, left_dim=1, right_dim=0):
    return lax.dot_general(
        left,
        right,
        (((left_dim,), (right_dim,)), ((), ())),
        preferred_element_type=jnp.float32,
    )


def put(ref, at, value):
    for lane in range(ref.shape[0]):
        ref[lane, at, :] = value[:, lane * LANES : (lane + 1) * LANES]


def take(ref, at):
    return jnp.concatenate([ref[lane, at, :] for lane in range(ref.shape[0])], axis=1)


def ends_kernel(x_ref, ends_ref):
    cells, channels = x_ref.shape
    ends = [x_ref[0:1, :], x_ref[cells - 1 : cells, :], jnp.zeros((6, channels), x_ref.dtype)]
    ends_ref[...] = jnp.concatenate([part.astype(jnp.float32) for part in ends], axis=0)


def spectrum_kernel(x_ref, f_ref, weight_ref, bias_ref, spectra_ref, pointwise_ref):
    steps, all_rows, tile = f_ref.shape
    half = x_ref.shape[0] // 2
    groups, span, channels = spectra_ref.shape
    sums = []
    for base in (0, half):
        total = None
        for step in range(steps):
            at = base + step * tile
            part = dot(f_ref[step], x_ref[at : at + tile, :])
            total = part if total is None else total + part
        sums.append(total)
    spectra = sums[0] + row_signs(all_rows, span, channels) * sums[1]
    spectra = spectra.astype(jnp.bfloat16)
    for at in range(groups):
        spectra_ref[at] = spectra[at * span : (at + 1) * span]
    weight = weight_ref[...]
    bias = bias_ref[...]
    for step in range(2 * steps):
        at = pl.ds(step * tile, tile)
        pointwise_ref[at, :] = dot(x_ref[at, :], weight) + bias


def message_kernel(order, spectra_ref, *refs):
    groups, span = spectra_ref.shape[0], spectra_ref.shape[1]
    pipes = len(order)
    msg_ref = refs[pipes]
    ends = jnp.concatenate([refs[order.index(step)][0:2, :] for step in range(pipes)], axis=0)
    ends = ends.astype(jnp.bfloat16)
    for at in range(groups):
        msg_ref[at, 0:span, :] = spectra_ref[at]
        msg_ref[at, span:, :] = ends


def extra_rows(first, second, count, channels):
    parts = [first.astype(jnp.float32), second.astype(jnp.float32)]
    if count > 2:
        parts.append(jnp.zeros((count - 2, channels), jnp.float32))
    return jnp.concatenate(parts, axis=0).astype(jnp.bfloat16)


def mix_rows(backward, r_ref, real_ref, imag_ref, out_ref, x_ref, y_ref):
    groups, modes = r_ref.shape[0], real_ref.shape[0]
    span = 2 * modes
    for source in range(groups):
        put(x_ref, pl.ds(source * span, span), r_ref[source, 0:span, :].astype(jnp.float32))
    for mode in range(modes):
        first = pl.ds(mode, groups, stride=span)
        second = pl.ds(modes + mode, groups, stride=span)
        rows = jnp.concatenate([take(x_ref, first), take(x_ref, second)], axis=0).astype(
            jnp.bfloat16
        )
        dim = 1 if backward else 0
        by_real = dot(rows, real_ref[mode], 1, dim)
        by_imag = dot(rows, imag_ref[mode], 1, dim)
        if backward:
            put(y_ref, first, by_real[:groups] + by_imag[groups:])
            put(y_ref, second, by_real[groups:] - by_imag[:groups])
        else:
            put(y_ref, first, by_real[:groups] - by_imag[groups:])
            put(y_ref, second, by_imag[:groups] + by_real[groups:])
    for source in range(groups):
        rows = take(y_ref, pl.ds(source * span, span)).astype(jnp.bfloat16)
        out_ref[source] = rows


def mix_kernel(
    pipes,
    r_ref,
    real_ref,
    imag_ref,
    inlet_ref,
    outlet_ref,
    junc_weight_ref,
    junc_bias_ref,
    out_ref,
    cond_ref,
    slope_ref,
    x_ref,
    y_ref,
    first_ref,
    last_ref,
):
    groups, rows = r_ref.shape[0], r_ref.shape[1]
    span = rows - 2 * pipes
    column = lax.axis_index("pipe")
    ends = [r_ref[group, span:rows, :].astype(jnp.float32) for group in range(groups)]
    for step in range(pipes):
        at = pl.ds(lax.bitwise_xor(column, step), groups, stride=pipes)
        for side, ref in enumerate((first_ref, last_ref)):
            row = 2 * step + side
            put(ref, at, jnp.concatenate([part[row : row + 1] for part in ends], axis=0))
    picked_in, picked_out = selection(inlet_ref, outlet_ref, pipes)
    sums = dot(picked_in, whole(first_ref)) + dot(picked_out, whole(last_ref))
    act = dot(sums.astype(jnp.bfloat16), junc_weight_ref[...]) + junc_bias_ref[...]
    sigmoid_part = jax.nn.sigmoid(act)
    junc_rows = (act * sigmoid_part).astype(jnp.bfloat16).astype(jnp.float32)
    cond_ref[...] = COUPLING * (junc_rows[0:1] + junc_rows[1:2])
    slope_ref[...] = sigmoid_part * (1.0 + act * (1.0 - sigmoid_part))
    mix_rows(False, r_ref, real_ref, imag_ref, out_ref, x_ref, y_ref)


def mix_grad_kernel(
    r_ref, real_ref, imag_ref, early_ref, out_ref, copied_ref, sem, x_ref, y_ref
):
    copy = pltpu.make_async_copy(early_ref, copied_ref, sem)
    copy.start()
    mix_rows(True, r_ref, real_ref, imag_ref, out_ref, x_ref, y_ref)
    copy.wait()


def own_pipe(pipes):
    return lax.axis_index("len") * pipes + lax.axis_index("pipe")


def selection(inlet_ref, outlet_ref, pipes):
    count = inlet_ref.shape[1]
    lane = lax.broadcasted_iota(jnp.int32, (8, count), 1)
    row = lax.broadcasted_iota(jnp.int32, (8, count), 0)
    inlets = jnp.broadcast_to(inlet_ref[...], (8, count)).astype(jnp.float32)
    outlets = jnp.broadcast_to(outlet_ref[...], (8, count)).astype(jnp.float32)
    mine = jnp.where(row == 0, inlets, outlets)
    own = jnp.sum(jnp.where(lane == own_pipe(pipes), mine, 0.0), axis=1, keepdims=True)
    return (inlets == own).astype(jnp.bfloat16), (outlets == own).astype(jnp.bfloat16)


def whole(ref):
    return take(ref, pl.ds(0, ref.shape[1])).astype(jnp.bfloat16)


def started(copies):
    for copy in copies:
        copy.start()
    return copies


def wait(copies):
    for copy in copies:
        copy.wait()


def brought(pairs, sems, base=0):
    return started(
        [
            pltpu.make_async_copy(source, target, sems.at[base + place])
            for place, (source, target) in enumerate(pairs)
        ]
    )


def layer_kernel(
    pointwise_ref,
    cot_ref,
    f_ref,
    ft_ref,
    cond_ref,
    modes_ref,
    out_ref,
    total_ref,
    msg_ref,
    spectral_ref,
):
    steps, all_rows, tile = f_ref.shape
    half = steps * tile
    channels = cot_ref.shape[1]
    groups, rows = msg_ref.shape[0], msg_ref.shape[1]
    span = all_rows // groups
    cond = cond_ref[...]
    row = lax.broadcasted_iota(jnp.int32, (all_rows, channels), 0)
    doubled = jnp.where((row == 0) | (row == span // 2), 1.0, 2.0).astype(jnp.float32)
    signs = row_signs(all_rows, span, channels)
    modes = jnp.concatenate(
        [modes_ref[at, 0:span, :].astype(jnp.float32) for at in range(groups)], axis=0
    )
    modes = modes * doubled
    modes = (modes.astype(jnp.bfloat16), (modes * signs).astype(jnp.bfloat16))
    for side in range(2):
        spectral_ref[side * half : (side + 1) * half, :] = dot(ft_ref[...], modes[side])
    sums = []
    for side in range(2):
        terms = None
        for step in range(steps):
            at = pl.ds(side * half + step * tile, tile)
            pre = (spectral_ref[at, :] + cond).astype(jnp.bfloat16).astype(jnp.float32)
            summed = pointwise_ref[at, :] + pre
            square = summed * summed
            part = 0.5 + 0.5 * jnp.tanh(summed * (GELU_S + (GELU_S * GELU_C) * square))
            result = summed * part
            out_ref[at, :] = result.astype(jnp.bfloat16)
            slope = part + result * (1.0 - part) * (
                2.0 * GELU_S + (6.0 * GELU_S * GELU_C) * square
            )
            total = (cot_ref[at, :].astype(jnp.float32) * slope).astype(jnp.bfloat16)
            total_ref[at, :] = total
        for step in range(steps):
            at = pl.ds(side * half + step * tile, tile)
            term = dot(f_ref[step], total_ref[at, :])
            terms = term if terms is None else terms + term
        sums.append(terms)
    acc = sums[0] + signs * sums[1]
    grad_cond = acc[0:1, :] * (1.0 / f_ref[0, 0:1, 0:1].astype(jnp.float32))
    upper = grad_cond.astype(jnp.bfloat16).astype(jnp.float32)
    extra = extra_rows(upper, grad_cond - upper, rows - span, channels)
    grad_spec = (acc * doubled).astype(jnp.bfloat16)
    for at in range(groups):
        msg_ref[at, 0:span, :] = grad_spec[at * span : (at + 1) * span]
        msg_ref[at, span:rows, :] = extra


def weight_grad_kernel(pipes, modes, per_copy, *refs):
    fields, grads, refs = refs[:pipes], refs[pipes : 2 * pipes], refs[2 * pipes :]
    (inlet_ref, outlet_ref, junc_weight_ref, slope_ref), refs = refs[:4], refs[4:]
    total_ref, weight_ref, real_out, imag_out, rows_ref, local_ref = refs[:6]
    x_ref, g_ref, real_ref, imag_ref = refs[6:10]
    first_ref, last_ref, upper_ref, lower_ref, sems = refs[10:]
    groups, rows = grads[0].shape[0], grads[0].shape[1]
    span = 2 * modes
    for step in range(pipes):
        for source in range(groups):
            at = pl.ds((step * groups + source) * span, span)
            put(x_ref, at, fields[step][source, 0:span, :].astype(jnp.float32))
            put(g_ref, at, grads[step][source, 0:span, :].astype(jnp.float32))
    count = pipes * groups
    going = []
    for number in range(modes // per_copy):
        for mode in range(number * per_copy, (number + 1) * per_copy):
            first = pl.ds(mode, count, stride=span)
            second = pl.ds(modes + mode, count, stride=span)
            a, b = take(x_ref, first), take(x_ref, second)
            u, v = take(g_ref, first), take(g_ref, second)
            left = jnp.concatenate([a, b], axis=0).astype(jnp.bfloat16)
            right = jnp.concatenate([u, v], axis=0).astype(jnp.bfloat16)
            turned = jnp.concatenate([v, -u], axis=0).astype(jnp.bfloat16)
            real_ref[mode] = dot(left, right, 0, 0)
            imag_ref[mode] = dot(left, turned, 0, 0)
        at = pl.ds(number * per_copy, per_copy)
        going += started(
            [
                pltpu.make_async_copy(real_ref.at[at], real_out.at[at], sems.at[number, 0]),
                pltpu.make_async_copy(imag_ref.at[at], imag_out.at[at], sems.at[number, 1]),
            ]
        )
    column = lax.axis_index("pipe")
    for step in range(pipes):
        for group in range(groups):
            parts = grads[step][group, rows - 2 : rows, :].astype(jnp.float32)
            upper_ref[group : group + 1, :] = parts[0:1]
            lower_ref[group : group + 1, :] = parts[1:2]
        at = pl.ds(lax.bitwise_xor(column, step), groups, stride=pipes)
        put(first_ref, at, upper_ref[...])
        put(last_ref, at, lower_ref[...])
    picked_in, picked_out = selection(inlet_ref, outlet_ref, pipes)
    picked = picked_in + picked_out
    junc_grad = COUPLING * (dot(picked, whole(first_ref)) + dot(picked, whole(last_ref)))
    act_grad = (junc_grad * slope_ref[...]).astype(jnp.bfloat16)
    sums_grad = dot(act_grad, junc_weight_ref[...], 1, 1)
    rows_ref[...] = sums_grad.astype(jnp.bfloat16).astype(jnp.float32)
    local_ref[...] = dot(total_ref[...], weight_ref[...], 1, 1).astype(jnp.bfloat16)
    wait(going)


def pack_kernel(first_ref, second_ref, out_ref):
    groups, rows = second_ref.shape[0], second_ref.shape[1]
    out_ref[0:groups] = first_ref[:, 0:rows, :]
    out_ref[groups : 2 * groups] = second_ref[...]


def split_kernel(both_ref, first_ref, second_ref):
    groups = first_ref.shape[0]
    first_ref[...] = both_ref[0:groups]
    second_ref[...] = both_ref[groups : 2 * groups]


def input_grad_kernel(
    local_ref, ft_ref, rows_ref, modes_ref, out_ref, cells_ref, tiles_ref, sems
):
    groups, span, channels = modes_ref.shape
    steps, tile = tiles_ref.shape[0], tiles_ref.shape[2]
    half, all_rows = steps * tile, groups * span
    back = jnp.concatenate(
        [modes_ref[at, 0:span, :].astype(jnp.float32) for at in range(groups)], axis=0
    )
    signs = row_signs(all_rows, span, channels)
    back = (back.astype(jnp.bfloat16), (back * signs).astype(jnp.bfloat16))
    row = lax.broadcasted_iota(jnp.int32, (tile, channels), 0)
    for side in range(2):
        cells_ref[side * half : (side + 1) * half, :] = dot(ft_ref[...], back[side])
    going = []
    for side in range(2):
        for step in range(steps):
            at = pl.ds(side * half + step * tile, tile)
            grad_cells = cells_ref[at, :]
            if step == 0 and side == 0:
                grad_cells = grad_cells + jnp.where(row == 0, rows_ref[0:1, :], 0.0)
            if step == steps - 1 and side == 1:
                grad_cells = grad_cells + jnp.where(row == tile - 1, rows_ref[1:2, :], 0.0)
            spread = grad_cells.astype(jnp.bfloat16).astype(jnp.float32)
            tiles_ref[step, side] = (local_ref[at, :].astype(jnp.float32) + spread).astype(
                jnp.bfloat16
            )
            going += started(
                [
                    pltpu.make_async_copy(
                        tiles_ref.at[step, side], out_ref.at[at], sems.at[step, side]
                    )
                ]
            )
    wait(going)


def rows_of(count, channels):
    return pltpu.VMEM((channels // LANES, count, LANES), jnp.float32)


def call(kernel, outs, specs, scratch=(), out_specs=None, name=None, limit=8, busy=0):
    return pl.pallas_call(
        kernel,
        out_shape=outs,
        in_specs=specs,
        out_specs=out_specs if out_specs is not None else [VMEM] * len(outs),
        scratch_shapes=list(scratch),
        compiler_params=pltpu.CompilerParams(vmem_limit_bytes=limit * MIB),
        cost_estimate=pl.CostEstimate(
            flops=busy * 1_000_000_000, bytes_accessed=busy * MIB, transcendentals=0
        )
        if busy
        else None,
        name=name,
    )


def body(
    inputs,
    cotangent,
    point_weight,
    point_bias,
    spec_real,
    spec_imag,
    junc_weight,
    junc_bias,
    inlet_ids,
    outlet_ids,
):
    per_dev, cell_count, channels = inputs.shape
    assert per_dev == 1
    groups, pipes = lax.axis_size("len"), lax.axis_size("pipe")
    assert pipes == 4
    modes = spec_real.shape[0]
    span = 2 * modes
    all_rows = span * groups
    steps = cell_count // (2 * TILE)
    table = half_table(cell_count, modes * groups, groups)
    tiled = table.reshape(all_rows, steps, TILE).transpose(1, 0, 2)
    f_table = jnp.asarray(np.ascontiguousarray(tiled))
    ft_table = jnp.asarray(np.ascontiguousarray(table.T))
    field = inputs.reshape(cell_count, channels)
    cot = cotangent.reshape(cell_count, channels)
    bias_row = point_bias.reshape(1, channels)
    junc_bias_row = junc_bias.reshape(1, channels)
    shape = jax.ShapeDtypeStruct
    bf16, f32 = jnp.bfloat16, jnp.float32
    message = shape((groups, span + 2, channels), bf16)
    chunks = shape((groups, span, channels), bf16)
    dma = pltpu.SemaphoreType.DMA

    def exchange(value):
        return lax.all_to_all(value, "len", split_axis=0, concat_axis=0, tiled=True)

    def swap(value, step):
        return lax.ppermute(value, "pipe", [(i, i ^ step) for i in range(pipes)])

    mix_bufs = [rows_of(all_rows, channels)] * 2
    pipe_rows = [rows_of(pipes * groups, channels)] * 2
    inlet_row = inlet_ids.reshape(1, -1)
    outlet_row = outlet_ids.reshape(1, -1)
    (ends,) = call(
        ends_kernel, [shape((8, channels), f32)], [VMEM], name="pipe_ends", busy=4
    )(field)
    order = [0, 1, 3, 2]
    ends = [swap(ends, step) if step else ends for step in order]
    spectra, pointwise = call(
        spectrum_kernel,
        [chunks, shape(field.shape, f32)],
        [VMEM] * 4,
        name="spectrum",
        busy=12,
    )(field, f_table, point_weight, bias_row)
    (sent,) = call(
        functools.partial(message_kernel, order),
        [shape((groups, span + 2 * pipes, channels), bf16)],
        [VMEM] * (1 + pipes),
        name="message",
    )(spectra, *ends)
    received = exchange(sent)
    mixed, cond, slope = call(
        functools.partial(mix_kernel, pipes),
        [chunks, shape((1, channels), f32), shape((8, channels), f32)],
        [VMEM] * 7,
        mix_bufs + pipe_rows,
        name="mix",
        busy=12,
    )(received, spec_real, spec_imag, inlet_row, outlet_row, junc_weight, junc_bias_row)
    returned = exchange(mixed)
    spectra = received
    early, total, sent = call(
        layer_kernel,
        [shape(field.shape, bf16)] * 2 + [message],
        [VMEM] * 6,
        [pltpu.VMEM(field.shape, f32)],
        name="layer",
        busy=12,
    )(pointwise, cot, f_table, ft_table, cond, returned)
    received = exchange(sent)
    received, spectra = lax.optimization_barrier((received, spectra))
    (both,) = call(
        pack_kernel,
        [shape((2 * groups, span + 2, channels), bf16)],
        [VMEM] * 2,
        name="pack",
    )(spectra, received)
    mixed, outputs = call(
        mix_grad_kernel,
        [chunks, early],
        [VMEM] * 4,
        [dma] + mix_bufs,
        out_specs=[VMEM, HBM],
        name="mix_grad",
        busy=12,
    )(received, spec_real, spec_imag, early)
    both, behind = lax.optimization_barrier((swap(both, 2), mixed))
    across = call(split_kernel, [message] * 2, [VMEM], name="split")(both)
    spectra, received, _ = lax.optimization_barrier((spectra, received, behind))
    fields = [spectra, swap(spectra, 1), across[0], swap(across[0], 1)]
    grads = [received, swap(received, 1), across[1], swap(across[1], 1)]
    returned = exchange(mixed)
    big = shape((modes, channels, channels), f32)
    per_copy = math.gcd(modes, 2)
    grad_real, grad_imag, rows, local = call(
        functools.partial(weight_grad_kernel, pipes, modes, per_copy),
        [big, big, shape((8, channels), f32), shape(field.shape, bf16)],
        [VMEM] * (2 * pipes + 6),
        [rows_of(pipes * all_rows, channels)] * 2
        + [pltpu.VMEM(big.shape, f32)] * 2
        + pipe_rows
        + [pltpu.VMEM((groups, channels), f32)] * 2
        + [dma((modes // per_copy, 2))],
        out_specs=[HBM, HBM, VMEM, VMEM],
        name="weight_grad",
        limit=16,
    )(*fields, *grads, inlet_row, outlet_row, junc_weight, slope, total, point_weight)
    (grad_inputs,) = call(
        input_grad_kernel,
        [shape(field.shape, bf16)],
        [VMEM] * 4,
        [pltpu.VMEM(field.shape, f32)]
        + [pltpu.VMEM((steps, 2, TILE, channels), bf16), dma((steps, 2))],
        out_specs=[HBM],
        name="input_grad",
    )(local, ft_table, rows, returned)
    return (
        outputs.reshape(inputs.shape),
        grad_inputs.reshape(inputs.shape),
        grad_real,
        grad_imag,
    )


def solution(mesh):
    placed = (
        P(("len", "pipe"), None, None),
        P(("len", "pipe"), None, None),
        P(),
        P(),
        P("len", None, None),
        P("len", None, None),
        P(),
        P(),
        P(),
        P(),
    )
    return jax.shard_map(
        body,
        mesh=mesh,
        in_specs=placed,
        out_specs=(
            P(("len", "pipe"), None, None),
            P(("len", "pipe"), None, None),
            P("len", None, None),
            P("len", None, None),
        ),
        check_vma=False,
    )
```

```python
import functools
import math

import jax
import jax.numpy as jnp
import ml_dtypes
import numpy as np
from jax import lax
from jax.experimental import pallas as pl
from jax.experimental.pallas import tpu as pltpu
from jax.sharding import PartitionSpec as P

COUPLING = 0.125
TILE = 256
LANES = 128
GELU_S = math.sqrt(2.0 / math.pi)
GELU_C = 0.044715
VMEM = pl.BlockSpec(memory_space=pltpu.VMEM)
HBM = pl.BlockSpec(memory_space=pltpu.HBM)
MIB = 1024 * 1024


def half_table(cell_count, mode_count, groups):
    half = cell_count // 2
    product_index = np.arange(mode_count)[:, None] * np.arange(half)[None, :] % cell_count
    angles = product_index.astype(np.float32) * np.float32(2.0 * math.pi / cell_count)
    norm_scale = np.float32(1.0 / math.sqrt(cell_count))
    cosine = (np.cos(angles) * norm_scale).reshape(groups, -1, half)
    sine = (np.sin(angles) * norm_scale).reshape(groups, -1, half)
    table = np.concatenate([cosine, -sine], axis=1).reshape(2 * mode_count, half)
    return table.astype(ml_dtypes.bfloat16)


def row_signs(all_rows, span, channels):
    row = lax.broadcasted_iota(jnp.int32, (all_rows, channels), 0)
    per_owner = span // 2
    mode = (row // span) * per_owner + lax.rem(row, per_owner)
    return jnp.where(lax.rem(mode, 2) == 0, 1.0, -1.0).astype(jnp.float32)


def dot(left, right, left_dim=1, right_dim=0):
    return lax.dot_general(
        left,
        right,
        (((left_dim,), (right_dim,)), ((), ())),
        preferred_element_type=jnp.float32,
    )


def put(ref, at, value):
    for lane in range(ref.shape[0]):
        ref[lane, at, :] = value[:, lane * LANES : (lane + 1) * LANES]


def take(ref, at):
    return jnp.concatenate([ref[lane, at, :] for lane in range(ref.shape[0])], axis=1)


def ends_kernel(x_ref, ends_ref):
    cells, channels = x_ref.shape
    ends = [x_ref[0:1, :], x_ref[cells - 1 : cells, :], jnp.zeros((6, channels), x_ref.dtype)]
    ends_ref[...] = jnp.concatenate([part.astype(jnp.float32) for part in ends], axis=0)


def spectrum_kernel(x_ref, f_ref, weight_ref, bias_ref, spectra_ref, pointwise_ref):
    steps, all_rows, tile = f_ref.shape
    half = x_ref.shape[0] // 2
    groups, span, channels = spectra_ref.shape
    sums = []
    for base in (0, half):
        total = None
        for step in range(steps):
            at = base + step * tile
            part = dot(f_ref[step], x_ref[at : at + tile, :])
            total = part if total is None else total + part
        sums.append(total)
    spectra = sums[0] + row_signs(all_rows, span, channels) * sums[1]
    spectra = spectra.astype(jnp.bfloat16)
    for at in range(groups):
        spectra_ref[at] = spectra[at * span : (at + 1) * span]
    weight = weight_ref[...]
    bias = bias_ref[...]
    for step in range(2 * steps):
        at = pl.ds(step * tile, tile)
        pointwise_ref[at, :] = dot(x_ref[at, :], weight) + bias


def message_kernel(pipes, spectra_ref, *refs):
    groups, span = spectra_ref.shape[0], spectra_ref.shape[1]
    msg_ref = refs[pipes]
    ends = jnp.concatenate([refs[step][0:2, :] for step in range(pipes)], axis=0)
    ends = ends.astype(jnp.bfloat16)
    for at in range(groups):
        msg_ref[at, 0:span, :] = spectra_ref[at]
        msg_ref[at, span:, :] = ends


def extra_rows(first, second, count, channels):
    parts = [first.astype(jnp.float32), second.astype(jnp.float32)]
    if count > 2:
        parts.append(jnp.zeros((count - 2, channels), jnp.float32))
    return jnp.concatenate(parts, axis=0).astype(jnp.bfloat16)


def mix_rows(backward, r_ref, real_ref, imag_ref, out_ref, x_ref, y_ref):
    groups, modes = r_ref.shape[0], real_ref.shape[0]
    span = 2 * modes
    for source in range(groups):
        put(x_ref, pl.ds(source * span, span), r_ref[source, 0:span, :].astype(jnp.float32))
    for mode in range(modes):
        first = pl.ds(mode, groups, stride=span)
        second = pl.ds(modes + mode, groups, stride=span)
        rows = jnp.concatenate([take(x_ref, first), take(x_ref, second)], axis=0).astype(
            jnp.bfloat16
        )
        dim = 1 if backward else 0
        by_real = dot(rows, real_ref[mode], 1, dim)
        by_imag = dot(rows, imag_ref[mode], 1, dim)
        if backward:
            put(y_ref, first, by_real[:groups] + by_imag[groups:])
            put(y_ref, second, by_real[groups:] - by_imag[:groups])
        else:
            put(y_ref, first, by_real[:groups] - by_imag[groups:])
            put(y_ref, second, by_imag[:groups] + by_real[groups:])
    for source in range(groups):
        rows = take(y_ref, pl.ds(source * span, span)).astype(jnp.bfloat16)
        out_ref[source] = rows


def mix_kernel(
    pipes,
    r_ref,
    real_ref,
    imag_ref,
    inlet_ref,
    outlet_ref,
    junc_weight_ref,
    junc_bias_ref,
    out_ref,
    cond_ref,
    slope_ref,
    x_ref,
    y_ref,
    first_ref,
    last_ref,
):
    mix_rows(False, r_ref, real_ref, imag_ref, out_ref, x_ref, y_ref)
    groups, rows = r_ref.shape[0], r_ref.shape[1]
    span = rows - 2 * pipes
    column = lax.axis_index("pipe")
    ends = [r_ref[group, span:rows, :].astype(jnp.float32) for group in range(groups)]
    for step in range(pipes):
        at = pl.ds(lax.bitwise_xor(column, step), groups, stride=pipes)
        for side, ref in enumerate((first_ref, last_ref)):
            row = 2 * step + side
            put(ref, at, jnp.concatenate([part[row : row + 1] for part in ends], axis=0))
    picked_in, picked_out = selection(inlet_ref, outlet_ref, pipes)
    sums = dot(picked_in, whole(first_ref)) + dot(picked_out, whole(last_ref))
    act = dot(sums.astype(jnp.bfloat16), junc_weight_ref[...]) + junc_bias_ref[...]
    sigmoid_part = jax.nn.sigmoid(act)
    junc_rows = (act * sigmoid_part).astype(jnp.bfloat16).astype(jnp.float32)
    cond_ref[...] = COUPLING * (junc_rows[0:1] + junc_rows[1:2])
    slope_ref[...] = sigmoid_part * (1.0 + act * (1.0 - sigmoid_part))


def mix_grad_kernel(
    r_ref, real_ref, imag_ref, early_ref, out_ref, copied_ref, sem, x_ref, y_ref
):
    copy = pltpu.make_async_copy(early_ref, copied_ref, sem)
    copy.start()
    mix_rows(True, r_ref, real_ref, imag_ref, out_ref, x_ref, y_ref)
    copy.wait()


def own_pipe(pipes):
    return lax.axis_index("len") * pipes + lax.axis_index("pipe")


def selection(inlet_ref, outlet_ref, pipes):
    count = inlet_ref.shape[1]
    lane = lax.broadcasted_iota(jnp.int32, (8, count), 1)
    row = lax.broadcasted_iota(jnp.int32, (8, count), 0)
    inlets = jnp.broadcast_to(inlet_ref[...], (8, count)).astype(jnp.float32)
    outlets = jnp.broadcast_to(outlet_ref[...], (8, count)).astype(jnp.float32)
    mine = jnp.where(row == 0, inlets, outlets)
    own = jnp.sum(jnp.where(lane == own_pipe(pipes), mine, 0.0), axis=1, keepdims=True)
    return (inlets == own).astype(jnp.bfloat16), (outlets == own).astype(jnp.bfloat16)


def whole(ref):
    return take(ref, pl.ds(0, ref.shape[1])).astype(jnp.bfloat16)


def started(copies):
    for copy in copies:
        copy.start()
    return copies


def wait(copies):
    for copy in copies:
        copy.wait()


def brought(pairs, sems, base=0):
    return started(
        [
            pltpu.make_async_copy(source, target, sems.at[base + place])
            for place, (source, target) in enumerate(pairs)
        ]
    )


def layer_kernel(
    pointwise_ref,
    cot_ref,
    f_ref,
    ft_ref,
    cond_ref,
    modes_ref,
    out_ref,
    total_ref,
    msg_ref,
    spectral_ref,
):
    steps, all_rows, tile = f_ref.shape
    half = steps * tile
    channels = cot_ref.shape[1]
    groups, rows = msg_ref.shape[0], msg_ref.shape[1]
    span = all_rows // groups
    cond = cond_ref[...]
    row = lax.broadcasted_iota(jnp.int32, (all_rows, channels), 0)
    doubled = jnp.where((row == 0) | (row == span // 2), 1.0, 2.0).astype(jnp.float32)
    signs = row_signs(all_rows, span, channels)
    modes = jnp.concatenate(
        [modes_ref[at, 0:span, :].astype(jnp.float32) for at in range(groups)], axis=0
    )
    modes = modes * doubled
    modes = (modes.astype(jnp.bfloat16), (modes * signs).astype(jnp.bfloat16))
    for side in range(2):
        spectral_ref[side * half : (side + 1) * half, :] = dot(ft_ref[...], modes[side])
    sums = []
    for side in range(2):
        terms = None
        for step in range(steps):
            at = pl.ds(side * half + step * tile, tile)
            pre = (spectral_ref[at, :] + cond).astype(jnp.bfloat16).astype(jnp.float32)
            summed = pointwise_ref[at, :] + pre
            square = summed * summed
            part = 0.5 + 0.5 * jnp.tanh(summed * (GELU_S + (GELU_S * GELU_C) * square))
            result = summed * part
            out_ref[at, :] = result.astype(jnp.bfloat16)
            slope = part + result * (1.0 - part) * (
                2.0 * GELU_S + (6.0 * GELU_S * GELU_C) * square
            )
            total = (cot_ref[at, :].astype(jnp.float32) * slope).astype(jnp.bfloat16)
            total_ref[at, :] = total
        for step in range(steps):
            at = pl.ds(side * half + step * tile, tile)
            term = dot(f_ref[step], total_ref[at, :])
            terms = term if terms is None else terms + term
        sums.append(terms)
    acc = sums[0] + signs * sums[1]
    grad_cond = acc[0:1, :] * (1.0 / f_ref[0, 0:1, 0:1].astype(jnp.float32))
    upper = grad_cond.astype(jnp.bfloat16).astype(jnp.float32)
    extra = extra_rows(upper, grad_cond - upper, rows - span, channels)
    grad_spec = (acc * doubled).astype(jnp.bfloat16)
    for at in range(groups):
        msg_ref[at, 0:span, :] = grad_spec[at * span : (at + 1) * span]
        msg_ref[at, span:rows, :] = extra


def weight_grad_kernel(pipes, modes, per_copy, *refs):
    fields, grads, refs = refs[:pipes], refs[pipes : 2 * pipes], refs[2 * pipes :]
    (inlet_ref, outlet_ref, junc_weight_ref, slope_ref), refs = refs[:4], refs[4:]
    total_ref, weight_ref, real_out, imag_out, rows_ref, local_ref = refs[:6]
    x_ref, g_ref, real_ref, imag_ref = refs[6:10]
    first_ref, last_ref, upper_ref, lower_ref, sems = refs[10:]
    groups, rows = grads[0].shape[0], grads[0].shape[1]
    span = 2 * modes
    for step in range(pipes):
        for source in range(groups):
            at = pl.ds((step * groups + source) * span, span)
            put(x_ref, at, fields[step][source, 0:span, :].astype(jnp.float32))
            put(g_ref, at, grads[step][source, 0:span, :].astype(jnp.float32))
    count = pipes * groups
    going = []
    for number in range(modes // per_copy):
        for mode in range(number * per_copy, (number + 1) * per_copy):
            first = pl.ds(mode, count, stride=span)
            second = pl.ds(modes + mode, count, stride=span)
            a, b = take(x_ref, first), take(x_ref, second)
            u, v = take(g_ref, first), take(g_ref, second)
            left = jnp.concatenate([a, b], axis=0).astype(jnp.bfloat16)
            right = jnp.concatenate([u, v], axis=0).astype(jnp.bfloat16)
            turned = jnp.concatenate([v, -u], axis=0).astype(jnp.bfloat16)
            real_ref[mode] = dot(left, right, 0, 0)
            imag_ref[mode] = dot(left, turned, 0, 0)
        at = pl.ds(number * per_copy, per_copy)
        going += started(
            [
                pltpu.make_async_copy(real_ref.at[at], real_out.at[at], sems.at[number, 0]),
                pltpu.make_async_copy(imag_ref.at[at], imag_out.at[at], sems.at[number, 1]),
            ]
        )
    column = lax.axis_index("pipe")
    for step in range(pipes):
        for group in range(groups):
            parts = grads[step][group, rows - 2 : rows, :].astype(jnp.float32)
            upper_ref[group : group + 1, :] = parts[0:1]
            lower_ref[group : group + 1, :] = parts[1:2]
        at = pl.ds(lax.bitwise_xor(column, step), groups, stride=pipes)
        put(first_ref, at, upper_ref[...])
        put(last_ref, at, lower_ref[...])
    picked_in, picked_out = selection(inlet_ref, outlet_ref, pipes)
    picked = picked_in + picked_out
    junc_grad = COUPLING * (dot(picked, whole(first_ref)) + dot(picked, whole(last_ref)))
    act_grad = (junc_grad * slope_ref[...]).astype(jnp.bfloat16)
    sums_grad = dot(act_grad, junc_weight_ref[...], 1, 1)
    rows_ref[...] = sums_grad.astype(jnp.bfloat16).astype(jnp.float32)
    local_ref[...] = dot(total_ref[...], weight_ref[...], 1, 1).astype(jnp.bfloat16)
    wait(going)


def pack_kernel(first_ref, second_ref, out_ref):
    groups, rows = second_ref.shape[0], second_ref.shape[1]
    out_ref[0:groups] = first_ref[:, 0:rows, :]
    out_ref[groups : 2 * groups] = second_ref[...]


def split_kernel(both_ref, first_ref, second_ref):
    groups = first_ref.shape[0]
    first_ref[...] = both_ref[0:groups]
    second_ref[...] = both_ref[groups : 2 * groups]


def input_grad_kernel(
    local_ref, ft_ref, rows_ref, modes_ref, out_ref, cells_ref, tiles_ref, sems
):
    groups, span, channels = modes_ref.shape
    steps, tile = tiles_ref.shape[0], tiles_ref.shape[2]
    half, all_rows = steps * tile, groups * span
    back = jnp.concatenate(
        [modes_ref[at, 0:span, :].astype(jnp.float32) for at in range(groups)], axis=0
    )
    signs = row_signs(all_rows, span, channels)
    back = (back.astype(jnp.bfloat16), (back * signs).astype(jnp.bfloat16))
    row = lax.broadcasted_iota(jnp.int32, (tile, channels), 0)
    for side in range(2):
        cells_ref[side * half : (side + 1) * half, :] = dot(ft_ref[...], back[side])
    going = []
    for side in range(2):
        for step in range(steps):
            at = pl.ds(side * half + step * tile, tile)
            grad_cells = cells_ref[at, :]
            if step == 0 and side == 0:
                grad_cells = grad_cells + jnp.where(row == 0, rows_ref[0:1, :], 0.0)
            if step == steps - 1 and side == 1:
                grad_cells = grad_cells + jnp.where(row == tile - 1, rows_ref[1:2, :], 0.0)
            spread = grad_cells.astype(jnp.bfloat16).astype(jnp.float32)
            tiles_ref[step, side] = (local_ref[at, :].astype(jnp.float32) + spread).astype(
                jnp.bfloat16
            )
            going += started(
                [
                    pltpu.make_async_copy(
                        tiles_ref.at[step, side], out_ref.at[at], sems.at[step, side]
                    )
                ]
            )
    wait(going)


def rows_of(count, channels):
    return pltpu.VMEM((channels // LANES, count, LANES), jnp.float32)


def call(kernel, outs, specs, scratch=(), out_specs=None, name=None, limit=8, busy=0):
    return pl.pallas_call(
        kernel,
        out_shape=outs,
        in_specs=specs,
        out_specs=out_specs if out_specs is not None else [VMEM] * len(outs),
        scratch_shapes=list(scratch),
        compiler_params=pltpu.CompilerParams(vmem_limit_bytes=limit * MIB),
        cost_estimate=pl.CostEstimate(
            flops=busy * 1_000_000_000, bytes_accessed=busy * MIB, transcendentals=0
        )
        if busy
        else None,
        name=name,
    )


def body(
    inputs,
    cotangent,
    point_weight,
    point_bias,
    spec_real,
    spec_imag,
    junc_weight,
    junc_bias,
    inlet_ids,
    outlet_ids,
):
    per_dev, cell_count, channels = inputs.shape
    assert per_dev == 1
    groups, pipes = lax.axis_size("len"), lax.axis_size("pipe")
    assert pipes == 4
    modes = spec_real.shape[0]
    span = 2 * modes
    all_rows = span * groups
    steps = cell_count // (2 * TILE)
    table = half_table(cell_count, modes * groups, groups)
    tiled = table.reshape(all_rows, steps, TILE).transpose(1, 0, 2)
    f_table = jnp.asarray(np.ascontiguousarray(tiled))
    ft_table = jnp.asarray(np.ascontiguousarray(table.T))
    field = inputs.reshape(cell_count, channels)
    cot = cotangent.reshape(cell_count, channels)
    bias_row = point_bias.reshape(1, channels)
    junc_bias_row = junc_bias.reshape(1, channels)
    shape = jax.ShapeDtypeStruct
    bf16, f32 = jnp.bfloat16, jnp.float32
    message = shape((groups, span + 2, channels), bf16)
    chunks = shape((groups, span, channels), bf16)
    dma = pltpu.SemaphoreType.DMA

    def exchange(value):
        return lax.all_to_all(value, "len", split_axis=0, concat_axis=0, tiled=True)

    def swap(value, step):
        return lax.ppermute(value, "pipe", [(i, i ^ step) for i in range(pipes)])

    mix_bufs = [rows_of(all_rows, channels)] * 2
    pipe_rows = [rows_of(pipes * groups, channels)] * 2
    inlet_row = inlet_ids.reshape(1, -1)
    outlet_row = outlet_ids.reshape(1, -1)
    (ends,) = call(
        ends_kernel, [shape((8, channels), f32)], [VMEM], name="pipe_ends", busy=4
    )(field)
    ends = [ends] + [swap(ends, step) for step in range(1, pipes)]
    spectra, pointwise = call(
        spectrum_kernel,
        [chunks, shape(field.shape, f32)],
        [VMEM] * 4,
        name="spectrum",
        busy=12,
    )(field, f_table, point_weight, bias_row)
    (sent,) = call(
        functools.partial(message_kernel, pipes),
        [shape((groups, span + 2 * pipes, channels), bf16)],
        [VMEM] * (1 + pipes),
        name="message",
    )(spectra, *ends)
    received = exchange(sent)
    mixed, cond, slope = call(
        functools.partial(mix_kernel, pipes),
        [chunks, shape((1, channels), f32), shape((8, channels), f32)],
        [VMEM] * 7,
        mix_bufs + pipe_rows,
        name="mix",
        busy=12,
    )(received, spec_real, spec_imag, inlet_row, outlet_row, junc_weight, junc_bias_row)
    returned = exchange(mixed)
    spectra = received
    early, total, sent = call(
        layer_kernel,
        [shape(field.shape, bf16)] * 2 + [message],
        [VMEM] * 6,
        [pltpu.VMEM(field.shape, f32)],
        name="layer",
        busy=12,
    )(pointwise, cot, f_table, ft_table, cond, returned)
    received = exchange(sent)
    received, spectra = lax.optimization_barrier((received, spectra))
    (both,) = call(
        pack_kernel,
        [shape((2 * groups, span + 2, channels), bf16)],
        [VMEM] * 2,
        name="pack",
    )(spectra, received)
    mixed, outputs = call(
        mix_grad_kernel,
        [chunks, early],
        [VMEM] * 4,
        [dma] + mix_bufs,
        out_specs=[VMEM, HBM],
        name="mix_grad",
        busy=12,
    )(received, spec_real, spec_imag, early)
    both, behind = lax.optimization_barrier((swap(both, 2), mixed))
    across = call(split_kernel, [message] * 2, [VMEM], name="split")(both)
    spectra, received, _ = lax.optimization_barrier((spectra, received, behind))
    fields = [spectra, swap(spectra, 1), across[0], swap(across[0], 1)]
    grads = [received, swap(received, 1), across[1], swap(across[1], 1)]
    returned = exchange(mixed)
    big = shape((modes, channels, channels), f32)
    per_copy = math.gcd(modes, 2)
    grad_real, grad_imag, rows, local = call(
        functools.partial(weight_grad_kernel, pipes, modes, per_copy),
        [big, big, shape((8, channels), f32), shape(field.shape, bf16)],
        [VMEM] * (2 * pipes + 6),
        [rows_of(pipes * all_rows, channels)] * 2
        + [pltpu.VMEM(big.shape, f32)] * 2
        + pipe_rows
        + [pltpu.VMEM((groups, channels), f32)] * 2
        + [dma((modes // per_copy, 2))],
        out_specs=[HBM, HBM, VMEM, VMEM],
        name="weight_grad",
        limit=16,
    )(*fields, *grads, inlet_row, outlet_row, junc_weight, slope, total, point_weight)
    (grad_inputs,) = call(
        input_grad_kernel,
        [shape(field.shape, bf16)],
        [VMEM] * 4,
        [pltpu.VMEM(field.shape, f32)]
        + [pltpu.VMEM((steps, 2, TILE, channels), bf16), dma((steps, 2))],
        out_specs=[HBM],
        name="input_grad",
    )(local, ft_table, rows, returned)
    return (
        outputs.reshape(inputs.shape),
        grad_inputs.reshape(inputs.shape),
        grad_real,
        grad_imag,
    )


def solution(mesh):
    placed = (
        P(("len", "pipe"), None, None),
        P(("len", "pipe"), None, None),
        P(),
        P(),
        P("len", None, None),
        P("len", None, None),
        P(),
        P(),
        P(),
        P(),
    )
    return jax.shard_map(
        body,
        mesh=mesh,
        in_specs=placed,
        out_specs=(
            P(("len", "pipe"), None, None),
            P(("len", "pipe"), None, None),
            P("len", None, None),
            P("len", None, None),
        ),
        check_vma=False,
    )
```

```python
import functools
import math

import jax
import jax.numpy as jnp
import ml_dtypes
import numpy as np
from jax import lax
from jax.experimental import pallas as pl
from jax.experimental.pallas import tpu as pltpu
from jax.sharding import PartitionSpec as P

COUPLING = 0.125
TILE = 256
LANES = 128
GELU_S = math.sqrt(2.0 / math.pi)
GELU_C = 0.044715
VMEM = pl.BlockSpec(memory_space=pltpu.VMEM)
HBM = pl.BlockSpec(memory_space=pltpu.HBM)
MIB = 1024 * 1024


def half_table(cell_count, mode_count, groups):
    half = cell_count // 2
    product_index = np.arange(mode_count)[:, None] * np.arange(half)[None, :] % cell_count
    angles = product_index.astype(np.float32) * np.float32(2.0 * math.pi / cell_count)
    norm_scale = np.float32(1.0 / math.sqrt(cell_count))
    cosine = (np.cos(angles) * norm_scale).reshape(groups, -1, half)
    sine = (np.sin(angles) * norm_scale).reshape(groups, -1, half)
    table = np.concatenate([cosine, -sine], axis=1).reshape(2 * mode_count, half)
    return table.astype(ml_dtypes.bfloat16)


def row_signs(all_rows, span, channels):
    row = lax.broadcasted_iota(jnp.int32, (all_rows, channels), 0)
    per_owner = span // 2
    mode = (row // span) * per_owner + lax.rem(row, per_owner)
    return jnp.where(lax.rem(mode, 2) == 0, 1.0, -1.0).astype(jnp.float32)


def dot(left, right, left_dim=1, right_dim=0):
    return lax.dot_general(
        left,
        right,
        (((left_dim,), (right_dim,)), ((), ())),
        preferred_element_type=jnp.float32,
    )


def put(ref, at, value):
    for lane in range(ref.shape[0]):
        ref[lane, at, :] = value[:, lane * LANES : (lane + 1) * LANES]


def take(ref, at):
    return jnp.concatenate([ref[lane, at, :] for lane in range(ref.shape[0])], axis=1)


def ends_kernel(x_ref, ends_ref):
    cells, channels = x_ref.shape
    ends = [x_ref[0:1, :], x_ref[cells - 1 : cells, :], jnp.zeros((6, channels), x_ref.dtype)]
    ends_ref[...] = jnp.concatenate([part.astype(jnp.float32) for part in ends], axis=0)


def spectrum_kernel(x_ref, f_ref, weight_ref, bias_ref, spectra_ref, pointwise_ref):
    steps, all_rows, tile = f_ref.shape
    half = x_ref.shape[0] // 2
    groups, span, channels = spectra_ref.shape
    sums = []
    for base in (0, half):
        total = None
        for step in range(steps):
            at = base + step * tile
            part = dot(f_ref[step], x_ref[at : at + tile, :])
            total = part if total is None else total + part
        sums.append(total)
    spectra = sums[0] + row_signs(all_rows, span, channels) * sums[1]
    spectra = spectra.astype(jnp.bfloat16)
    for at in range(groups):
        spectra_ref[at] = spectra[at * span : (at + 1) * span]
    weight = weight_ref[...]
    bias = bias_ref[...]
    for step in range(2 * steps):
        at = pl.ds(step * tile, tile)
        pointwise_ref[at, :] = dot(x_ref[at, :], weight) + bias


def message_kernel(pipes, spectra_ref, *refs):
    groups, span = spectra_ref.shape[0], spectra_ref.shape[1]
    msg_ref = refs[pipes]
    ends = jnp.concatenate([refs[step][0:2, :] for step in range(pipes)], axis=0)
    ends = ends.astype(jnp.bfloat16)
    for at in range(groups):
        msg_ref[at, 0:span, :] = spectra_ref[at]
        msg_ref[at, span:, :] = ends


def extra_rows(first, second, count, channels):
    parts = [first.astype(jnp.float32), second.astype(jnp.float32)]
    if count > 2:
        parts.append(jnp.zeros((count - 2, channels), jnp.float32))
    return jnp.concatenate(parts, axis=0).astype(jnp.bfloat16)


def mix_rows(backward, r_ref, real_ref, imag_ref, out_ref, x_ref, y_ref):
    groups, modes = r_ref.shape[0], real_ref.shape[0]
    span = 2 * modes
    for source in range(groups):
        put(x_ref, pl.ds(source * span, span), r_ref[source, 0:span, :].astype(jnp.float32))
    for mode in range(modes):
        first = pl.ds(mode, groups, stride=span)
        second = pl.ds(modes + mode, groups, stride=span)
        rows = jnp.concatenate([take(x_ref, first), take(x_ref, second)], axis=0).astype(
            jnp.bfloat16
        )
        dim = 1 if backward else 0
        by_real = dot(rows, real_ref[mode], 1, dim)
        by_imag = dot(rows, imag_ref[mode], 1, dim)
        if backward:
            put(y_ref, first, by_real[:groups] + by_imag[groups:])
            put(y_ref, second, by_real[groups:] - by_imag[:groups])
        else:
            put(y_ref, first, by_real[:groups] - by_imag[groups:])
            put(y_ref, second, by_imag[:groups] + by_real[groups:])
    for source in range(groups):
        rows = take(y_ref, pl.ds(source * span, span)).astype(jnp.bfloat16)
        out_ref[source] = rows


def mix_kernel(
    pipes,
    r_ref,
    real_ref,
    imag_ref,
    inlet_ref,
    outlet_ref,
    junc_weight_ref,
    junc_bias_ref,
    out_ref,
    cond_ref,
    slope_ref,
    x_ref,
    y_ref,
    first_ref,
    last_ref,
):
    mix_rows(False, r_ref, real_ref, imag_ref, out_ref, x_ref, y_ref)
    groups, rows = r_ref.shape[0], r_ref.shape[1]
    span = rows - 2 * pipes
    column = lax.axis_index("pipe")
    ends = [r_ref[group, span:rows, :].astype(jnp.float32) for group in range(groups)]
    for step in range(pipes):
        at = pl.ds(lax.bitwise_xor(column, step), groups, stride=pipes)
        for side, ref in enumerate((first_ref, last_ref)):
            row = 2 * step + side
            put(ref, at, jnp.concatenate([part[row : row + 1] for part in ends], axis=0))
    picked_in, picked_out = selection(inlet_ref, outlet_ref, pipes)
    count = pipes * groups
    sums = dot(picked_in, whole(first_ref, count)) + dot(picked_out, whole(last_ref, count))
    act = dot(sums.astype(jnp.bfloat16), junc_weight_ref[...]) + junc_bias_ref[...]
    sigmoid_part = jax.nn.sigmoid(act)
    junc_rows = (act * sigmoid_part).astype(jnp.bfloat16).astype(jnp.float32)
    cond_ref[...] = COUPLING * (junc_rows[0:1] + junc_rows[1:2])
    slope_ref[...] = sigmoid_part * (1.0 + act * (1.0 - sigmoid_part))


def mix_grad_kernel(
    r_ref, real_ref, imag_ref, early_ref, out_ref, copied_ref, sem, x_ref, y_ref
):
    copy = pltpu.make_async_copy(early_ref, copied_ref, sem)
    copy.start()
    mix_rows(True, r_ref, real_ref, imag_ref, out_ref, x_ref, y_ref)
    copy.wait()


def own_pipe(pipes):
    return lax.axis_index("len") * pipes + lax.axis_index("pipe")


def selection(inlet_ref, outlet_ref, pipes):
    count = inlet_ref.shape[1]
    lane = lax.broadcasted_iota(jnp.int32, (8, count), 1)
    row = lax.broadcasted_iota(jnp.int32, (8, count), 0)
    inlets = jnp.broadcast_to(inlet_ref[...], (8, count)).astype(jnp.float32)
    outlets = jnp.broadcast_to(outlet_ref[...], (8, count)).astype(jnp.float32)
    mine = jnp.where(row == 0, inlets, outlets)
    own = jnp.sum(jnp.where(lane == own_pipe(pipes), mine, 0.0), axis=1, keepdims=True)
    return (inlets == own).astype(jnp.bfloat16), (outlets == own).astype(jnp.bfloat16)


def whole(ref, count):
    return take(ref, pl.ds(0, count)).astype(jnp.bfloat16)


def started(copies):
    for copy in copies:
        copy.start()
    return copies


def wait(copies):
    for copy in copies:
        copy.wait()


def brought(pairs, sems, base=0):
    return started(
        [
            pltpu.make_async_copy(source, target, sems.at[base + place])
            for place, (source, target) in enumerate(pairs)
        ]
    )


def layer_kernel(
    pointwise_ref,
    cot_ref,
    f_ref,
    ft_ref,
    cond_ref,
    modes_ref,
    out_ref,
    total_ref,
    msg_ref,
    spectral_ref,
):
    steps, all_rows, tile = f_ref.shape
    half = steps * tile
    channels = cot_ref.shape[1]
    groups, rows = msg_ref.shape[0], msg_ref.shape[1]
    span = all_rows // groups
    cond = cond_ref[...]
    row = lax.broadcasted_iota(jnp.int32, (all_rows, channels), 0)
    doubled = jnp.where((row == 0) | (row == span // 2), 1.0, 2.0).astype(jnp.float32)
    signs = row_signs(all_rows, span, channels)
    modes = jnp.concatenate(
        [modes_ref[at, 0:span, :].astype(jnp.float32) for at in range(groups)], axis=0
    )
    modes = modes * doubled
    modes = (modes.astype(jnp.bfloat16), (modes * signs).astype(jnp.bfloat16))
    for side in range(2):
        spectral_ref[side * half : (side + 1) * half, :] = dot(ft_ref[...], modes[side])
    sums = []
    for side in range(2):
        terms = None
        for step in range(steps):
            at = pl.ds(side * half + step * tile, tile)
            pre = (spectral_ref[at, :] + cond).astype(jnp.bfloat16).astype(jnp.float32)
            summed = pointwise_ref[at, :] + pre
            square = summed * summed
            part = 0.5 + 0.5 * jnp.tanh(summed * (GELU_S + (GELU_S * GELU_C) * square))
            result = summed * part
            out_ref[at, :] = result.astype(jnp.bfloat16)
            slope = part + result * (1.0 - part) * (
                2.0 * GELU_S + (6.0 * GELU_S * GELU_C) * square
            )
            total = (cot_ref[at, :].astype(jnp.float32) * slope).astype(jnp.bfloat16)
            total_ref[at, :] = total
        for step in range(steps):
            at = pl.ds(side * half + step * tile, tile)
            term = dot(f_ref[step], total_ref[at, :])
            terms = term if terms is None else terms + term
        sums.append(terms)
    acc = sums[0] + signs * sums[1]
    grad_cond = acc[0:1, :] * (1.0 / f_ref[0, 0:1, 0:1].astype(jnp.float32))
    upper = grad_cond.astype(jnp.bfloat16).astype(jnp.float32)
    extra = extra_rows(upper, grad_cond - upper, rows - span, channels)
    grad_spec = (acc * doubled).astype(jnp.bfloat16)
    for at in range(groups):
        msg_ref[at, 0:span, :] = grad_spec[at * span : (at + 1) * span]
        msg_ref[at, span:rows, :] = extra


def weight_grad_kernel(pipes, modes, per_copy, *refs):
    fields, grads, refs = refs[:pipes], refs[pipes : 2 * pipes], refs[2 * pipes :]
    (inlet_ref, outlet_ref, junc_weight_ref, slope_ref), refs = refs[:4], refs[4:]
    total_ref, weight_ref, real_out, imag_out, rows_ref, local_ref = refs[:6]
    x_ref, g_ref, real_ref, imag_ref = refs[6:10]
    first_ref, last_ref, upper_ref, lower_ref, sems = refs[10:]
    groups, rows = grads[0].shape[0], grads[0].shape[1]
    span = 2 * modes
    for step in range(pipes):
        for source in range(groups):
            at = pl.ds((step * groups + source) * span, span)
            put(x_ref, at, fields[step][source, 0:span, :].astype(jnp.float32))
            put(g_ref, at, grads[step][source, 0:span, :].astype(jnp.float32))
    count = pipes * groups
    going = []
    for number in range(modes // per_copy):
        for mode in range(number * per_copy, (number + 1) * per_copy):
            first = pl.ds(mode, count, stride=span)
            second = pl.ds(modes + mode, count, stride=span)
            a, b = take(x_ref, first), take(x_ref, second)
            u, v = take(g_ref, first), take(g_ref, second)
            left = jnp.concatenate([a, b], axis=0).astype(jnp.bfloat16)
            right = jnp.concatenate([u, v], axis=0).astype(jnp.bfloat16)
            turned = jnp.concatenate([v, -u], axis=0).astype(jnp.bfloat16)
            real_ref[mode] = dot(left, right, 0, 0)
            imag_ref[mode] = dot(left, turned, 0, 0)
        at = pl.ds(number * per_copy, per_copy)
        going += started(
            [
                pltpu.make_async_copy(real_ref.at[at], real_out.at[at], sems.at[number, 0]),
                pltpu.make_async_copy(imag_ref.at[at], imag_out.at[at], sems.at[number, 1]),
            ]
        )
    column = lax.axis_index("pipe")
    for step in range(pipes):
        for group in range(groups):
            parts = grads[step][group, rows - 2 : rows, :].astype(jnp.float32)
            upper_ref[group : group + 1, :] = parts[0:1]
            lower_ref[group : group + 1, :] = parts[1:2]
        at = pl.ds(lax.bitwise_xor(column, step), groups, stride=pipes)
        put(first_ref, at, upper_ref[...])
        put(last_ref, at, lower_ref[...])
    picked_in, picked_out = selection(inlet_ref, outlet_ref, pipes)
    picked = picked_in + picked_out
    sums = dot(picked, whole(first_ref, count)) + dot(picked, whole(last_ref, count))
    junc_grad = COUPLING * sums
    act_grad = (junc_grad * slope_ref[...]).astype(jnp.bfloat16)
    sums_grad = dot(act_grad, junc_weight_ref[...], 1, 1)
    rows_ref[...] = sums_grad.astype(jnp.bfloat16).astype(jnp.float32)
    local_ref[...] = dot(total_ref[...], weight_ref[...], 1, 1).astype(jnp.bfloat16)
    wait(going)


def pack_kernel(first_ref, second_ref, out_ref):
    groups, rows = second_ref.shape[0], second_ref.shape[1]
    out_ref[0:groups] = first_ref[:, 0:rows, :]
    out_ref[groups : 2 * groups] = second_ref[...]


def split_kernel(both_ref, first_ref, second_ref):
    groups = first_ref.shape[0]
    first_ref[...] = both_ref[0:groups]
    second_ref[...] = both_ref[groups : 2 * groups]


def input_grad_kernel(
    local_ref, ft_ref, rows_ref, modes_ref, out_ref, cells_ref, tiles_ref, sems
):
    groups, span, channels = modes_ref.shape
    steps, tile = tiles_ref.shape[0], tiles_ref.shape[2]
    half, all_rows = steps * tile, groups * span
    back = jnp.concatenate(
        [modes_ref[at, 0:span, :].astype(jnp.float32) for at in range(groups)], axis=0
    )
    signs = row_signs(all_rows, span, channels)
    back = (back.astype(jnp.bfloat16), (back * signs).astype(jnp.bfloat16))
    row = lax.broadcasted_iota(jnp.int32, (tile, channels), 0)
    for side in range(2):
        cells_ref[side * half : (side + 1) * half, :] = dot(ft_ref[...], back[side])
    going = []
    for side in range(2):
        for step in range(steps):
            at = pl.ds(side * half + step * tile, tile)
            grad_cells = cells_ref[at, :]
            if step == 0 and side == 0:
                grad_cells = grad_cells + jnp.where(row == 0, rows_ref[0:1, :], 0.0)
            if step == steps - 1 and side == 1:
                grad_cells = grad_cells + jnp.where(row == tile - 1, rows_ref[1:2, :], 0.0)
            spread = grad_cells.astype(jnp.bfloat16).astype(jnp.float32)
            tiles_ref[step, side] = (local_ref[at, :].astype(jnp.float32) + spread).astype(
                jnp.bfloat16
            )
            going += started(
                [
                    pltpu.make_async_copy(
                        tiles_ref.at[step, side], out_ref.at[at], sems.at[step, side]
                    )
                ]
            )
    wait(going)


def rows_of(count, stride, channels):
    rows = -(-(count + stride) // 8) * 8
    return pltpu.VMEM((channels // LANES, rows, LANES), jnp.float32)


def call(kernel, outs, specs, scratch=(), out_specs=None, name=None, limit=8, busy=0):
    return pl.pallas_call(
        kernel,
        out_shape=outs,
        in_specs=specs,
        out_specs=out_specs if out_specs is not None else [VMEM] * len(outs),
        scratch_shapes=list(scratch),
        compiler_params=pltpu.CompilerParams(vmem_limit_bytes=limit * MIB),
        cost_estimate=pl.CostEstimate(
            flops=busy * 1_000_000_000, bytes_accessed=busy * MIB, transcendentals=0
        )
        if busy
        else None,
        name=name,
    )


def body(
    inputs,
    cotangent,
    point_weight,
    point_bias,
    spec_real,
    spec_imag,
    junc_weight,
    junc_bias,
    inlet_ids,
    outlet_ids,
):
    per_dev, cell_count, channels = inputs.shape
    assert per_dev == 1
    groups, pipes = lax.axis_size("len"), lax.axis_size("pipe")
    assert pipes == 4
    modes = spec_real.shape[0]
    span = 2 * modes
    all_rows = span * groups
    steps = cell_count // (2 * TILE)
    table = half_table(cell_count, modes * groups, groups)
    tiled = table.reshape(all_rows, steps, TILE).transpose(1, 0, 2)
    f_table = jnp.asarray(np.ascontiguousarray(tiled))
    ft_table = jnp.asarray(np.ascontiguousarray(table.T))
    field = inputs.reshape(cell_count, channels)
    cot = cotangent.reshape(cell_count, channels)
    bias_row = point_bias.reshape(1, channels)
    junc_bias_row = junc_bias.reshape(1, channels)
    shape = jax.ShapeDtypeStruct
    bf16, f32 = jnp.bfloat16, jnp.float32
    message = shape((groups, span + 2, channels), bf16)
    chunks = shape((groups, span, channels), bf16)
    dma = pltpu.SemaphoreType.DMA

    def exchange(value):
        return lax.all_to_all(value, "len", split_axis=0, concat_axis=0, tiled=True)

    def swap(value, step):
        return lax.ppermute(value, "pipe", [(i, i ^ step) for i in range(pipes)])

    mix_bufs = [rows_of(all_rows, span, channels)] * 2
    pipe_rows = [rows_of(pipes * groups, pipes, channels)] * 2
    inlet_row = inlet_ids.reshape(1, -1)
    outlet_row = outlet_ids.reshape(1, -1)
    (ends,) = call(
        ends_kernel, [shape((8, channels), f32)], [VMEM], name="pipe_ends", busy=4
    )(field)
    ends = [ends] + [swap(ends, step) for step in range(1, pipes)]
    spectra, pointwise = call(
        spectrum_kernel,
        [chunks, shape(field.shape, f32)],
        [VMEM] * 4,
        name="spectrum",
        busy=12,
    )(field, f_table, point_weight, bias_row)
    (sent,) = call(
        functools.partial(message_kernel, pipes),
        [shape((groups, span + 2 * pipes, channels), bf16)],
        [VMEM] * (1 + pipes),
        name="message",
    )(spectra, *ends)
    received = exchange(sent)
    mixed, cond, slope = call(
        functools.partial(mix_kernel, pipes),
        [chunks, shape((1, channels), f32), shape((8, channels), f32)],
        [VMEM] * 7,
        mix_bufs + pipe_rows,
        name="mix",
        busy=12,
    )(received, spec_real, spec_imag, inlet_row, outlet_row, junc_weight, junc_bias_row)
    returned = exchange(mixed)
    spectra = received
    early, total, sent = call(
        layer_kernel,
        [shape(field.shape, bf16)] * 2 + [message],
        [VMEM] * 6,
        [pltpu.VMEM(field.shape, f32)],
        name="layer",
        busy=12,
    )(pointwise, cot, f_table, ft_table, cond, returned)
    received = exchange(sent)
    received, spectra = lax.optimization_barrier((received, spectra))
    (both,) = call(
        pack_kernel,
        [shape((2 * groups, span + 2, channels), bf16)],
        [VMEM] * 2,
        name="pack",
    )(spectra, received)
    mixed, outputs = call(
        mix_grad_kernel,
        [chunks, early],
        [VMEM] * 4,
        [dma] + mix_bufs,
        out_specs=[VMEM, HBM],
        name="mix_grad",
        busy=12,
    )(received, spec_real, spec_imag, early)
    both, behind = lax.optimization_barrier((swap(both, 2), mixed))
    across = call(split_kernel, [message] * 2, [VMEM], name="split")(both)
    spectra, received, _ = lax.optimization_barrier((spectra, received, behind))
    fields = [spectra, swap(spectra, 1), across[0], swap(across[0], 1)]
    grads = [received, swap(received, 1), across[1], swap(across[1], 1)]
    returned = exchange(mixed)
    big = shape((modes, channels, channels), f32)
    per_copy = math.gcd(modes, 2)
    grad_real, grad_imag, rows, local = call(
        functools.partial(weight_grad_kernel, pipes, modes, per_copy),
        [big, big, shape((8, channels), f32), shape(field.shape, bf16)],
        [VMEM] * (2 * pipes + 6),
        [rows_of(pipes * all_rows, span, channels)] * 2
        + [pltpu.VMEM(big.shape, f32)] * 2
        + pipe_rows
        + [pltpu.VMEM((groups, channels), f32)] * 2
        + [dma((modes // per_copy, 2))],
        out_specs=[HBM, HBM, VMEM, VMEM],
        name="weight_grad",
        limit=16,
    )(*fields, *grads, inlet_row, outlet_row, junc_weight, slope, total, point_weight)
    (grad_inputs,) = call(
        input_grad_kernel,
        [shape(field.shape, bf16)],
        [VMEM] * 4,
        [pltpu.VMEM(field.shape, f32)]
        + [pltpu.VMEM((steps, 2, TILE, channels), bf16), dma((steps, 2))],
        out_specs=[HBM],
        name="input_grad",
    )(local, ft_table, rows, returned)
    return (
        outputs.reshape(inputs.shape),
        grad_inputs.reshape(inputs.shape),
        grad_real,
        grad_imag,
    )


def solution(mesh):
    placed = (
        P(("len", "pipe"), None, None),
        P(("len", "pipe"), None, None),
        P(),
        P(),
        P("len", None, None),
        P("len", None, None),
        P(),
        P(),
        P(),
        P(),
    )
    return jax.shard_map(
        body,
        mesh=mesh,
        in_specs=placed,
        out_specs=(
            P(("len", "pipe"), None, None),
            P(("len", "pipe"), None, None),
            P("len", None, None),
            P("len", None, None),
        ),
        check_vma=False,
    )
```
